32 devices in a mesh: asc: 8 (over y, x, core), desc: 4 (over z).
Axes of the slice: x: 2, y: 2, z: 4, core: 2. Of those that a mesh axis runs over, the one named last changes fastest.
Arguments:
- coef_asc: float32 [1024, 128], P(('asc', 'desc')), may hold values from -0.3 to 0.3
- coef_desc: float32 [1024, 128], P(('asc', 'desc')), may hold values from -0.3 to 0.3
- cross_asc: int32 [2048, 128], P(('asc', 'desc')), may hold values from 0 to 1023, as said below
- cross_desc: int32 [2048, 128], P(('asc', 'desc')), may hold values from 0 to 1023, as said below
- time_asc: float32 [2048, 128], P(('asc', 'desc')), may hold values from 0 to 1
- time_desc: float32 [2048, 128], P(('asc', 'desc')), may hold values from 0 to 1
- height: float32 [2048, 128], P(('asc', 'desc')), may hold values from -18 to 18
- block_fill: int32 [2048], P(('asc', 'desc')), may hold values from 0 to 128, as said below
Outputs:
- adjusted_asc: float32 [1024, 128], P(('asc', 'desc'))
- adjusted_desc: float32 [1024, 128], P(('asc', 'desc'))
The draws below stay inside these ranges and needn't reach their ends.
Inputs may be any that keep to these rules, and one draw needn't show every extreme that they name: `cross_asc`: every crossover slot stored on a device of asc index p names an ascending arc a with a // 128 == p; slot s of every block names an arc a with (a // 32) % 4 == s % 4. `cross_desc`: every crossover slot stored on a device of desc index q names a descending arc d with (d // 32) % 4 == q; slot s of every block names an arc d with d // 128 == s % 8. `block_fill`: the slots in use stand first in each block; on each device the blocks with a nonzero count stand first and the first block is full; on some device all 64 blocks are in use.
All inputs are finite; a program needn't handle non-finite values.
Results may differ from the reference program's by a relative error of at most 0.0003.
Values sent between devices are 32-bit elements; how exact they have to be, the bound alone decides.
No kernel may reach another device: no remote copies, remote signals or barrier semaphores. Data moves between devices by JAX's collectives and lax.ppermute only.
A program may use at most 64 MiB of HBM per device.

```python
import jax
import jax.numpy as jnp
from jax import lax

K = 128
BLOCK = 128
MAXB = 64
ARC_A_DEV = 32
ARC_D_DEV = 32
GN_STEPS = 2
CG_STEPS = 3
GROUP_A = 128
GROUP_D = 256
NA = 1024
ND = 1024
XROWS = 2048
N_ASC = 8
N_DESC = 4


def draw_cross_asc(key, part):
    row_device = jnp.arange(XROWS, dtype=jnp.int32) // MAXB
    desc_count = GROUP_A // ARC_A_DEV
    asc_group = row_device // desc_count
    column_owner = jnp.arange(BLOCK, dtype=jnp.int32) % desc_count
    within = jax.random.randint(jax.random.fold_in(key, 31), (XROWS, BLOCK), 0, ARC_A_DEV)
    return (asc_group[:, None] * GROUP_A + column_owner[None, :] * ARC_A_DEV + within).astype(jnp.int32)


def draw_cross_desc(key, part):
    row_device = jnp.arange(XROWS, dtype=jnp.int32) // MAXB
    desc_count = GROUP_A // ARC_A_DEV
    asc_count = GROUP_D // ARC_D_DEV
    desc_group = row_device % desc_count
    owner = (jnp.arange(BLOCK, dtype=jnp.int32) % asc_count)[None, :]
    within = jax.random.randint(jax.random.fold_in(key, 37), (XROWS, BLOCK), 0, ARC_D_DEV)
    return ((owner * desc_count + desc_group[:, None]) * ARC_D_DEV + within).astype(jnp.int32)


def draw_block_fill(key, part):
    device_count = XROWS // MAXB
    key_used, key_busy, key_fill = jax.random.split(jax.random.fold_in(key, 41), 3)
    used_blocks = jax.random.randint(key_used, (device_count,), MAXB // 4, MAXB // 2 + 1)
    busiest = jax.random.randint(key_busy, (), 0, device_count)
    used_blocks = jnp.where(jnp.arange(device_count) == busiest, MAXB, used_blocks)
    counts = jax.random.randint(key_fill, (device_count, MAXB), BLOCK // 2, BLOCK + 1)
    position = jnp.arange(MAXB)[None, :]
    counts = jnp.where(position == 0, BLOCK, counts)
    counts = jnp.where(position < used_blocks[:, None], counts, 0)
    return counts.reshape(-1).astype(jnp.int32)


def draw_height(key, part):
    key_scale, key_value = jax.random.split(jax.random.fold_in(key, 53))
    row_scale = jnp.exp(jax.random.uniform(key_scale, (XROWS, 1), minval=jnp.log(0.3), maxval=jnp.log(3.0)))
    base = jnp.clip(jax.random.normal(key_value, (XROWS, BLOCK)), -6.0, 6.0)
    return (row_scale * base).astype(jnp.float32)


def shard_levels(own_key, dims, shards, smallest, high):
    loudness, own = 1.0, jax.random.fold_in(own_key, 6)
    for dim, parts in shards:
        draws = jnp.exp(jax.random.uniform(jax.random.fold_in(own, dim), (parts,), jnp.float32, smallest / len(shards), high / len(shards)))
        loudness = loudness * jnp.repeat(draws, dims[dim] // parts).reshape([-1 if axis == dim else 1 for axis in range(len(dims))])
    return loudness


def scatter_about(key, shape, width, most, pieces=(), kind=jnp.bfloat16):
    gain = shard_levels(key, shape, pieces, -0.22, 0.18) if pieces else 1.0
    entries = jax.random.normal(key, shape, jnp.float32) * width * gain
    return jnp.minimum(jnp.maximum(entries, -most), most).astype(kind)


def setup_inputs(seed: int = 0) -> dict:
    streams_of = jax.random.split(jax.random.key(seed), 9)
    coef_asc = scatter_about(streams_of[0], (NA, K), 0.05, 0.3, ((0, 32),), jnp.float32)
    coef_desc = scatter_about(streams_of[1], (ND, K), 0.05, 0.3, ((0, 32),), jnp.float32)
    cross_asc = draw_cross_asc(jax.random.fold_in(streams_of[8], 71), 0)
    cross_desc = draw_cross_desc(jax.random.fold_in(streams_of[8], 71), 0)
    time_asc = jnp.clip(1.0 * jax.random.uniform(streams_of[4], (XROWS, BLOCK), jnp.float32) ** shard_levels(streams_of[4], (XROWS, BLOCK), ((0, 32),), -0.2, 0.2), 0.0, 1.0)
    time_desc = jnp.clip(1.0 * jax.random.uniform(streams_of[5], (XROWS, BLOCK), jnp.float32) ** shard_levels(streams_of[5], (XROWS, BLOCK), ((0, 32),), -0.2, 0.2), 0.0, 1.0)
    height = draw_height(jax.random.fold_in(streams_of[8], 71), 0)
    block_fill = draw_block_fill(jax.random.fold_in(streams_of[8], 71), 0)
    return dict(coef_asc=coef_asc, coef_desc=coef_desc, cross_asc=cross_asc, cross_desc=cross_desc, time_asc=time_asc, time_desc=time_desc, height=height, block_fill=block_fill)


damping = 2.0
cauchy_square = 2.25


def harmonics(times, term_count):
    half_terms = term_count // 2
    frequency = (lax.iota(jnp.int32, half_terms) + 1).astype(times.dtype)
    phases = jnp.pi * times[:, None] * frequency[None, :]
    return jnp.concatenate([jnp.cos(phases), jnp.sin(phases)], axis=1)


def device_rows(array, device):
    return lax.dynamic_slice_in_dim(array, (device * MAXB).astype(jnp.int32), MAXB, 0)


def crossover_pass(field_asc, field_desc, cross_asc, cross_desc, time_asc, time_desc, height, block_fill, weights, first_pass):
    def one_device(state_carry, device):
        grad_asc, grad_desc = state_carry
        ids_asc = device_rows(cross_asc, device).reshape(-1)
        ids_desc = device_rows(cross_desc, device).reshape(-1)
        basis_asc = harmonics(device_rows(time_asc, device).reshape(-1), K)
        basis_desc = harmonics(device_rows(time_desc, device).reshape(-1), K)
        block_counts = device_rows(block_fill, device)
        position = lax.broadcasted_iota(jnp.int32, (MAXB, BLOCK), 1)
        live_mask = (position < block_counts[:, None]).astype(field_asc.dtype).reshape(-1)
        modelled = jnp.sum(basis_asc * jnp.take(field_asc, ids_asc, axis=0), axis=1) - jnp.sum(
            basis_desc * jnp.take(field_desc, ids_desc, axis=0), axis=1)
        if first_pass:
            observed = device_rows(height, device).reshape(-1)
            misfit = live_mask * (observed - modelled)
            weight = live_mask / (1.0 + misfit * misfit / cauchy_square)
            weighted = weight * misfit
        else:
            weight = weights[device]
            weighted = weight * modelled
        grad_asc = grad_asc + jax.ops.segment_sum(weighted[:, None] * basis_asc, ids_asc, num_segments=NA)
        grad_desc = grad_desc - jax.ops.segment_sum(weighted[:, None] * basis_desc, ids_desc, num_segments=ND)
        return (grad_asc, grad_desc), weight

    start = (jnp.zeros((NA, K), field_asc.dtype), jnp.zeros((ND, K), field_asc.dtype))
    devices_all = jnp.arange(N_ASC * N_DESC, dtype=jnp.int32)
    (grad_asc, grad_desc), all_weights = lax.scan(one_device, start, devices_all)
    return grad_asc, grad_desc, all_weights


def pair_inner(first, second):
    return jnp.sum(first[0] * second[0]) + jnp.sum(first[1] * second[1])


def reference(coef_asc, coef_desc, cross_asc, cross_desc, time_asc, time_desc, height, block_fill):
    state_asc, state_desc = coef_asc, coef_desc
    for outer_step in range(GN_STEPS):
        grad_asc, grad_desc, weights = crossover_pass(state_asc, state_desc, cross_asc, cross_desc,
                                                      time_asc, time_desc, height, block_fill, None, True)
        remainder = (grad_asc - damping * state_asc, grad_desc - damping * state_desc)
        direction = remainder
        step_sum = (jnp.zeros_like(state_asc), jnp.zeros_like(state_desc))
        norm_now = pair_inner(remainder, remainder)
        for inner_step in range(CG_STEPS):
            part_asc, part_desc, unused = crossover_pass(direction[0], direction[1], cross_asc, cross_desc,
                                                         time_asc, time_desc, height, block_fill, weights, False)
            image_pair = (part_asc + damping * direction[0], part_desc + damping * direction[1])
            step_length = norm_now / pair_inner(direction, image_pair)
            step_sum = (step_sum[0] + step_length * direction[0], step_sum[1] + step_length * direction[1])
            if inner_step + 1 < CG_STEPS:
                remainder = (remainder[0] - step_length * image_pair[0], remainder[1] - step_length * image_pair[1])
                norm_next = pair_inner(remainder, remainder)
                ratio = norm_next / norm_now
                direction = (remainder[0] + ratio * direction[0], remainder[1] + ratio * direction[1])
                norm_now = norm_next
        state_asc = state_asc + step_sum[0]
        state_desc = state_desc + step_sum[1]
    return state_asc, state_desc
```

```python
import functools
import math

import jax
import jax.numpy as jnp
from jax import lax
from jax.experimental import pallas as pl
from jax.experimental.pallas import tpu as pltpu
from jax.sharding import PartitionSpec as P

GN_STEPS = 2
damping = 2.0
cauchy_square = 2.25

LANES = 128
STEP_ROWS = 2
UNROLL = 2
SCALE = 1.0 / 128.0
FIELDS = 6
PIVOT_FLOOR = 1e-6
F32 = jnp.float32
BF16 = jnp.bfloat16

COS_TERMS = [(-1.0) ** i * math.pi ** (2 * i) / math.factorial(2 * i) for i in range(8)]
SIN_TERMS = [(-1.0) ** i * math.pi ** (2 * i + 1) / math.factorial(2 * i + 1) for i in range(7)]


def params():
    return pltpu.CompilerParams(vmem_limit_bytes=32 * 1024 * 1024)


def whole(count):
    return [pl.BlockSpec(memory_space=pltpu.VMEM)] * count


def split(x):
    high = x.astype(BF16)
    low = (x - high.astype(F32)).astype(BF16)
    return high, low


def flat(ref, field, chunks):
    return jnp.concatenate([ref[j, field] for j in range(chunks)], axis=0)


def local_id(ids, owned):
    if owned & (owned - 1) == 0:
        return ids & (owned - 1)
    return lax.rem(ids, owned)


def pack_kernel(na, nd, owned_asc, owned_desc, ca, cd, ta, td, height, fill, out, turned):
    blocks, width = ca.shape
    group = width // na
    rows = blocks // na
    fill_row = fill[...]
    row_id = lax.broadcasted_iota(jnp.int32, (blocks, blocks), 0)
    col_id = lax.broadcasted_iota(jnp.int32, (blocks, blocks), 1)
    fill_col = jnp.sum(
        jnp.where(row_id == col_id, fill_row, 0).astype(F32), axis=1, keepdims=True
    )
    lane = lax.broadcasted_iota(jnp.int32, (blocks, width), 1)
    live = (lane.astype(F32) < fill_col).astype(F32)
    fields = [
        local_id(ca[...], owned_asc).astype(F32),
        ta[...],
        local_id(cd[...], owned_desc).astype(F32),
        td[...],
        height[...],
        live,
    ]
    source = lax.broadcasted_iota(jnp.int32, (width, width), 0)
    target = lax.broadcasted_iota(jnp.int32, (width, width), 1)
    owner = target // group
    place = target - owner * group
    order = (source == place * na + owner).astype(F32).astype(BF16)
    for f, x in enumerate(fields):
        high = x.astype(BF16)
        rest = x - high.astype(F32)
        middle = rest.astype(BF16)
        low = (rest - middle.astype(F32)).astype(BF16)
        turned[f] = (
            jnp.dot(high, order, preferred_element_type=F32)
            + jnp.dot(middle, order, preferred_element_type=F32)
        ) + jnp.dot(low, order, preferred_element_type=F32)
    lane_group = lax.broadcasted_iota(jnp.int32, (rows, width), 1) // group
    for f in range(FIELDS):
        parts = [None] * na
        for k in range(na):
            piece = turned[f, pl.ds(k, rows, stride=na), :]
            for r in range(na):
                amount = ((k - r) * group) % width
                moved = pltpu.roll(piece, amount, 1) if amount else piece
                parts[r] = moved if k == 0 else jnp.where(lane_group == k, moved, parts[r])
        for r in range(na):
            out[r % nd, r // nd, f] = parts[r]


def cos_sin_pi(x):
    turns = jnp.floor(x + 0.5)
    f = x - turns
    sign = 1.0 - 2.0 * (turns - 2.0 * jnp.floor(turns * 0.5))
    u = f * f
    c = COS_TERMS[-1]
    for term in COS_TERMS[-2::-1]:
        c = c * u + term
    s = SIN_TERMS[-1]
    for term in SIN_TERMS[-2::-1]:
        s = s * u + term
    return c * sign, s * (f * sign)


def rows_pair(ref, start):
    return jnp.concatenate([ref[pl.ds(start + i, 1), :] for i in range(STEP_ROWS)], axis=1)


def stacked(field):
    high, low = split(field)
    top = jnp.concatenate([high, high], axis=1)
    bottom = jnp.concatenate([low, jnp.zeros_like(low)], axis=1)
    return jnp.concatenate([top, bottom], axis=0)


def forward_step(stack, phi, ids_row, row_iota, owned):
    both = jnp.dot(stack, phi, preferred_element_type=F32)
    value = both[:owned] + both[owned:]
    return jnp.sum(jnp.where(row_iota == ids_row, value, 0.0), axis=0, keepdims=True)


def store_rows(ref, start, value):
    for i in range(STEP_ROWS):
        ref[pl.ds(start + i, 1), :] = value[:, i * LANES : (i + 1) * LANES]


def basis_loop(ids_ref, time_ref, coef, phi_ref, value_ref):
    owned, terms = coef.shape
    half = terms // 2
    steps = phi_ref.shape[0]
    width = phi_ref.shape[2]
    stack = stacked(coef)
    row_iota = lax.broadcasted_iota(jnp.int32, (owned, width), 0).astype(F32)
    fine = (lax.broadcasted_iota(jnp.int32, (8, width), 0) + 1).astype(F32)
    coarse = (lax.broadcasted_iota(jnp.int32, (half // 8, width), 0) * 8).astype(F32)

    def step(n):
        start = n * STEP_ROWS
        times = rows_pair(time_ref, start)
        cos_fine, sin_fine = cos_sin_pi(fine * times)
        cos_coarse, sin_coarse = cos_sin_pi(coarse * times)
        cos_parts, sin_parts = [], []
        for j in range(half // 8):
            cj = cos_coarse[j : j + 1]
            sj = sin_coarse[j : j + 1]
            cos_parts.append(cj * cos_fine - sj * sin_fine)
            sin_parts.append(sj * cos_fine + cj * sin_fine)
        high, low = split(jnp.concatenate(cos_parts + sin_parts, axis=0))
        phi = jnp.concatenate([high, low], axis=0)
        phi_ref[n] = phi
        value = forward_step(stack, phi, rows_pair(ids_ref, start), row_iota, owned)
        store_rows(value_ref, start, value)

    def block(i, carry):
        for u in range(UNROLL):
            step(i * UNROLL + u)
        return carry

    lax.fori_loop(0, steps // UNROLL, block, 0)


def setup_asc_kernel(chunks, packed, coef, phi, value, meta, times):
    meta[0] = flat(packed, 0, chunks)
    times[...] = flat(packed, 1, chunks)
    meta[1] = flat(packed, 4, chunks)
    meta[2] = flat(packed, 5, chunks)
    basis_loop(meta.at[0], times, coef[...], phi, value)


def setup_desc_kernel(chunks, packed, coef, value_asc, phi, meta, send, times, value):
    rows = send.shape[2]
    meta[0] = flat(packed, 2, chunks)
    times[...] = flat(packed, 3, chunks)
    meta[1] = flat(packed, 4, chunks)
    meta[2] = flat(packed, 5, chunks)
    basis_loop(meta.at[0], times, coef[...], phi, value)
    for j in range(chunks):
        send[j, 0] = value_asc[j * rows : (j + 1) * rows, :]
        send[j, 1] = value[j * rows : (j + 1) * rows, :]


def backward_forward(chunks, ids, z_ref, phis, finish, send, value_ref):
    owned = finish.owned
    steps, double, width = phis[0].shape
    terms = double // 2
    row_iota = lax.broadcasted_iota(jnp.int32, (owned, width), 0).astype(F32)

    def gather(role, n):
        start = n * STEP_ROWS
        hit = row_iota == rows_pair(ids[role], start)
        high = jnp.where(hit, rows_pair(z_ref.at[2 * role], start), 0.0).astype(BF16)
        low = jnp.where(hit, rows_pair(z_ref.at[2 * role + 1], start), 0.0).astype(BF16)
        return lax.dot_general(
            jnp.concatenate([high, low], axis=0),
            phis[role][n],
            (((1,), (1,)), ((), ())),
            preferred_element_type=F32,
        )

    def back(i, carry):
        asc, desc = carry
        for u in range(UNROLL):
            asc = asc + gather(0, i * UNROLL + u)
            desc = desc + gather(1, i * UNROLL + u)
        return asc, desc

    zero = jnp.zeros((2 * owned, double), F32)
    sums = lax.fori_loop(0, steps // UNROLL, back, (zero, zero))
    grads = [g[:owned, :terms] + (g[:owned, terms:] + g[owned:, :terms]) for g in sums]
    fields = finish(grads[0], -grads[1])
    stacks = [stacked(f) for f in fields]

    def ahead(i, carry):
        for u in range(UNROLL):
            n = i * UNROLL + u
            start = n * STEP_ROWS
            for role in range(2):
                value = forward_step(
                    stacks[role], phis[role][n], rows_pair(ids[role], start), row_iota, owned
                )
                store_rows(value_ref.at[role], start, value)
        return carry

    lax.fori_loop(0, steps // UNROLL, ahead, 0)
    rows = send.shape[2]
    for j in range(chunks):
        for role in range(2):
            send[j, role] = value_ref[role, j * rows : (j + 1) * rows, :]


class Finish:
    def __init__(self, owned, call):
        self.owned = owned
        self.call = call

    def __call__(self, asc, desc):
        return self.call(asc, desc)


def store_split(z_ref, role, z):
    high = z.astype(BF16).astype(F32)
    z_ref[2 * role] = high
    z_ref[2 * role + 1] = z - high


def cross_values(chunks, got, sent, role):
    if role == 0:
        return flat(sent, 0, chunks) - flat(got, 1, chunks)
    return flat(got, 0, chunks) - flat(sent, 1, chunks)


def weigh(model, meta, role, weights, z_ref):
    height, live = meta[1], meta[2]
    misfit = jnp.where(live > 0.0, height - model, 0.0)
    weight = live / (1.0 + misfit * misfit / cauchy_square)
    weights[role] = weight
    store_split(z_ref, role, weight * misfit)


def first_kernel(
    chunks, got, sent, meta_a, meta_d, phi_a, phi_d, state_a, state_d,
    model, weights, basis, send, z_ref, value_ref,
):
    for role, meta in enumerate((meta_a, meta_d)):
        values = cross_values(chunks, got, sent, role)
        model[role] = values
        weigh(values, meta, role, weights, z_ref)

    def finish(asc, desc):
        new = (asc - damping * state_a[...], desc - damping * state_d[...])
        basis[0], basis[1] = new
        return new

    backward_forward(
        chunks, (meta_a.at[0], meta_d.at[0]), z_ref, (phi_a, phi_d),
        Finish(state_a.shape[0], finish), send, value_ref,
    )


def image_kernel(
    chunks, got, sent, meta_a, meta_d, phi_a, phi_d, weights, before,
    crossed, basis, send, z_ref, value_ref,
):
    for role, meta in enumerate((meta_a, meta_d)):
        values = cross_values(chunks, got, sent, role)
        crossed[role] = values
        store_split(z_ref, role, weights[role] * values)

    def finish(asc, desc):
        new = (
            SCALE * (asc + damping * before[0]),
            SCALE * (desc + damping * before[1]),
        )
        basis[0], basis[1] = new
        return new

    backward_forward(
        chunks, (meta_a.at[0], meta_d.at[0]), z_ref, (phi_a, phi_d),
        Finish(before.shape[1], finish), send, value_ref,
    )


def total(x):
    return jnp.sum(jnp.sum(x, axis=0, keepdims=True), axis=1, keepdims=True)


PAIRS = [(0, 0), (0, 1), (0, 2), (1, 1), (1, 2), (2, 2)]


def gram_kernel(
    chunks, got, sent, weights, crossed_0, crossed_1, basis_0, basis_1, basis_2,
    crossed_2, scalars,
):
    for role in range(2):
        crossed_2[role] = cross_values(chunks, got, sent, role)
    weight = weights[0]
    values = [crossed_0[0], crossed_1[0], crossed_2[0]]
    bases = [basis_0, basis_1, basis_2]
    lane = lax.broadcasted_iota(jnp.int32, (1, LANES), 1)
    line = jnp.zeros((1, LANES), F32)
    for place, (i, j) in enumerate(PAIRS):
        dots = total(bases[i][0] * bases[j][0] + bases[i][1] * bases[j][1])
        curve = total(weight * values[i] * values[j]) + damping * dots
        line = jnp.where(lane == place, curve, line)
        if i == 0:
            line = jnp.where(lane == len(PAIRS) + j, dots, line)
    for d in range(scalars.shape[0]):
        scalars[d] = jnp.broadcast_to(line, scalars.shape[1:])


def solve(scalars):
    summed = scalars[0]
    for d in range(1, scalars.shape[0]):
        summed = summed + scalars[d]
    line = summed[0:1]
    lane = lax.broadcasted_iota(jnp.int32, (1, LANES), 1)

    def pick(place):
        return jnp.sum(jnp.where(lane == place, line, 0.0), axis=1, keepdims=True)

    g = {pair: pick(place) for place, pair in enumerate(PAIRS)}
    right = [pick(len(PAIRS) + i) for i in range(3)]
    s = [
        jnp.where(g[i, i] > 0.0, lax.rsqrt(jnp.maximum(g[i, i], 1e-37)), 0.0) for i in range(3)
    ]
    l10 = g[0, 1] * s[0] * s[1]
    l20 = g[0, 2] * s[0] * s[2]
    g21 = g[1, 2] * s[1] * s[2]
    c = [right[i] * s[i] for i in range(3)]

    def inverse(pivot):
        good = pivot > PIVOT_FLOOR
        return jnp.where(good, 1.0 / jnp.where(good, pivot, 1.0), 0.0)

    inv1 = inverse(1.0 - l10 * l10)
    t21 = g21 - l20 * l10
    l21 = t21 * inv1
    inv2 = inverse(1.0 - l20 * l20 - l21 * t21)
    u1 = c[1] - l10 * c[0]
    u2 = c[2] - l20 * c[0] - l21 * u1
    x2 = u2 * inv2
    x1 = u1 * inv1 - l21 * x2
    x0 = c[0] - l10 * x1 - l20 * x2
    return [x0 * s[0], x1 * s[1], x2 * s[2]]


def combine(y, parts):
    return y[0] * parts[0] + (y[1] * parts[1] + y[2] * parts[2])


def next_kernel(
    chunks, scalars, meta_a, meta_d, phi_a, phi_d, state_a, state_d, model,
    crossed_0, crossed_1, crossed_2, basis_0, basis_1, basis_2,
    new_state_a, new_state_d, new_model, weights, basis, send, z_ref, value_ref,
):
    y = solve(scalars)
    for role, meta in enumerate((meta_a, meta_d)):
        values = model[role] + combine(y, [crossed_0[role], crossed_1[role], crossed_2[role]])
        new_model[role] = values
        weigh(values, meta, role, weights, z_ref)
    new_state_a[...] = state_a[...] + combine(y, [basis_0[0], basis_1[0], basis_2[0]])
    new_state_d[...] = state_d[...] + combine(y, [basis_0[1], basis_1[1], basis_2[1]])

    def finish(asc, desc):
        new = (asc - damping * new_state_a[...], desc - damping * new_state_d[...])
        basis[0], basis[1] = new
        return new

    backward_forward(
        chunks, (meta_a.at[0], meta_d.at[0]), z_ref, (phi_a, phi_d),
        Finish(state_a.shape[0], finish), send, value_ref,
    )


def final_kernel(scalars, state_a, basis_0, basis_1, basis_2, desc, out_a, out_d):
    y = solve(scalars)
    out_a[...] = state_a[...] + combine(y, [basis_0[0], basis_1[0], basis_2[0]])
    out_d[...] = desc[0] + combine(y, [desc[1], desc[2], desc[3]])


def body(coef_asc, coef_desc, cross_asc, cross_desc, time_asc, time_desc, height, block_fill):
    owned_asc, terms = coef_asc.shape
    owned_desc = coef_desc.shape[0]
    blocks, width = cross_asc.shape
    na = lax.axis_size("asc")
    nd = lax.axis_size("desc")
    fold = na // nd
    rows = blocks * width // na // LANES
    all_rows = na * rows
    steps = all_rows // STEP_ROWS
    step_width = STEP_ROWS * LANES
    shape = jax.ShapeDtypeStruct

    def call(kernel, outs, scratch, *args):
        return pl.pallas_call(
            kernel,
            out_shape=outs,
            in_specs=whole(len(args)),
            out_specs=jax.tree.map(lambda _: pl.BlockSpec(memory_space=pltpu.VMEM), outs),
            scratch_shapes=scratch,
            compiler_params=params(),
        )(*args)

    to_role = []
    for p in range(na):
        for q in range(nd):
            to_role.append((p * nd + q, (q * fold + p // nd) * nd + p % nd))
    to_native = [(b, a) for a, b in to_role]
    role_desc = lax.ppermute(coef_desc, ("asc", "desc"), to_role)

    packed = call(
        functools.partial(pack_kernel, na, nd, owned_asc, owned_desc),
        shape((nd, fold, FIELDS, rows, LANES), F32),
        [pltpu.VMEM((FIELDS, blocks, width), F32)],
        cross_asc, cross_desc, time_asc, time_desc, height, block_fill.reshape(1, blocks),
    )
    at_asc = lax.all_to_all(packed, "desc", split_axis=0, concat_axis=0, tiled=True)
    at_asc = at_asc.reshape(na, FIELDS, rows, LANES)
    at_desc = lax.all_to_all(at_asc, "asc", split_axis=0, concat_axis=0, tiled=True)

    phi_shape = shape((steps, 2 * terms, step_width), BF16)
    meta_shape = shape((3, all_rows, LANES), F32)
    send_shape = shape((na, 2, rows, LANES), F32)
    pair_shape = shape((2, all_rows, LANES), F32)
    field_shape = shape((2, owned_asc, terms), F32)
    flat_scratch = pltpu.VMEM((all_rows, LANES), F32)
    pass_scratch = [
        pltpu.VMEM((4, all_rows, LANES), F32),
        pltpu.VMEM((2, all_rows, LANES), F32),
    ]
    phi_a, value_asc, meta_a = call(
        functools.partial(setup_asc_kernel, na),
        [phi_shape, shape((all_rows, LANES), F32), meta_shape],
        [flat_scratch],
        at_asc, coef_asc,
    )
    phi_d, meta_d, sent = call(
        functools.partial(setup_desc_kernel, na),
        [phi_shape, meta_shape, send_shape],
        [flat_scratch, flat_scratch],
        at_desc, role_desc, value_asc,
    )

    def exchange(x):
        return lax.all_to_all(x, "asc", split_axis=0, concat_axis=0, tiled=True)

    def share(x):
        return lax.all_to_all(x, ("asc", "desc"), split_axis=0, concat_axis=0, tiled=True)

    fixed = (meta_a, meta_d, phi_a, phi_d)
    state_a, state_d = coef_asc, role_desc
    for outer in range(GN_STEPS):
        if outer == 0:
            got = exchange(sent)
            model, weights, basis_0, sent = call(
                functools.partial(first_kernel, na),
                [pair_shape, pair_shape, field_shape, send_shape],
                pass_scratch,
                got, sent, *fixed, state_a, state_d,
            )
        else:
            state_a, state_d, model, weights, basis_0, sent = call(
                functools.partial(next_kernel, na),
                [
                    shape(state_a.shape, F32), shape(state_d.shape, F32),
                    pair_shape, pair_shape, field_shape, send_shape,
                ],
                pass_scratch,
                scalars, *fixed, state_a, state_d, model,
                *crossed, *bases,
            )
        bases, crossed = [basis_0], []
        for inner in range(2):
            got = exchange(sent)
            crossed_now, basis_now, sent = call(
                functools.partial(image_kernel, na),
                [pair_shape, field_shape, send_shape],
                pass_scratch,
                got, sent, *fixed, weights, bases[-1],
            )
            crossed.append(crossed_now)
            bases.append(basis_now)
        if outer + 1 == GN_STEPS:
            leaving = jnp.stack([state_d, bases[0][1], bases[1][1], bases[2][1]])
            native = lax.ppermute(leaving, ("asc", "desc"), to_native)
        got = exchange(sent)
        crossed_now, scalars = call(
            functools.partial(gram_kernel, na),
            [pair_shape, shape((na * nd, 8, LANES), F32)],
            [],
            got, sent, weights, *crossed, *bases,
        )
        crossed.append(crossed_now)
        scalars = share(scalars)
    return tuple(
        call(
            final_kernel,
            [shape(coef_asc.shape, F32), shape(coef_desc.shape, F32)],
            [],
            scalars, state_a, *bases, native,
        )
    )


def solution(mesh):
    split_rows = P(("asc", "desc"), None)
    return jax.shard_map(
        body,
        mesh=mesh,
        in_specs=(split_rows,) * 7 + (P(("asc", "desc")),),
        out_specs=(split_rows, split_rows),
        check_vma=False,
    )
```

```python
import functools
import math

import jax
import jax.numpy as jnp
from jax import lax
from jax.experimental import pallas as pl
from jax.experimental.pallas import tpu as pltpu
from jax.sharding import PartitionSpec as P

GN_STEPS = 2
damping = 2.0
cauchy_square = 2.25

LANES = 128
STEP_ROWS = 2
UNROLL = 4
SETUP_UNROLL = 2
DUMMY_ROWS = 8
SCALE = 1.0 / 128.0
FIELDS = 5
PIVOT_FLOOR = 1e-6
F32 = jnp.float32
BF16 = jnp.bfloat16

COS_TERMS = [(-1.0) ** i * math.pi ** (2 * i) / math.factorial(2 * i) for i in range(8)]
SIN_TERMS = [(-1.0) ** i * math.pi ** (2 * i + 1) / math.factorial(2 * i + 1) for i in range(7)]


def in_smem(x):
    return x.dtype == jnp.int32 and len(x.shape) == 1


def params(mebibytes):
    return pltpu.CompilerParams(vmem_limit_bytes=mebibytes * 1024 * 1024)


def place(x):
    return pl.BlockSpec(memory_space=pltpu.SMEM if in_smem(x) else pltpu.VMEM)


def split(x):
    high = x.astype(BF16)
    low = (x - high.astype(F32)).astype(BF16)
    return high, low


def flat(ref, field, chunks):
    return jnp.concatenate([ref[j, field] for j in range(chunks)], axis=0)


def local_id(ids, owned):
    if owned & (owned - 1) == 0:
        return ids & (owned - 1)
    return lax.rem(ids, owned)


def pack_kernel(
    na, nd, owned_asc, owned_desc, ca_in, cd_in, ta_in, td_in, height_in, fill_in, out,
    ca, cd, ta, td, height, fill, turned, sems,
):
    copies = [
        pltpu.make_async_copy(source, target, sems.at[i])
        for i, (source, target) in enumerate(
            [
                (fill_in, fill), (ca_in, ca), (ta_in, ta),
                (cd_in, cd), (td_in, td), (height_in, height),
            ]
        )
    ]
    for copy in copies:
        copy.start()
    for copy in copies:
        copy.wait()
    blocks, width = ca.shape
    group = width // na
    rows = blocks // na
    fill_row = fill[...]
    row_id = lax.broadcasted_iota(jnp.int32, (blocks, blocks), 0)
    col_id = lax.broadcasted_iota(jnp.int32, (blocks, blocks), 1)
    fill_col = jnp.sum(
        jnp.where(row_id == col_id, fill_row, 0).astype(F32), axis=1, keepdims=True
    )
    lane = lax.broadcasted_iota(jnp.int32, (blocks, width), 1)
    live = lane.astype(F32) < fill_col
    fields = [
        jnp.where(live, local_id(ca[...], owned_asc).astype(F32), -1.0),
        ta[...],
        jnp.where(live, local_id(cd[...], owned_desc).astype(F32), -1.0),
        td[...],
        height[...],
    ]
    source = lax.broadcasted_iota(jnp.int32, (width, width), 0)
    target = lax.broadcasted_iota(jnp.int32, (width, width), 1)
    owner = target // group
    place = target - owner * group
    order = (source == place * na + owner).astype(F32).astype(BF16)
    for f, x in enumerate(fields):
        high = x.astype(BF16)
        rest = x - high.astype(F32)
        middle = rest.astype(BF16)
        low = (rest - middle.astype(F32)).astype(BF16)
        turned[f] = (
            jnp.dot(high, order, preferred_element_type=F32)
            + jnp.dot(middle, order, preferred_element_type=F32)
        ) + jnp.dot(low, order, preferred_element_type=F32)
    lane_group = lax.broadcasted_iota(jnp.int32, (rows, width), 1) // group
    for f in range(FIELDS):
        parts = [None] * na
        for k in range(na):
            piece = turned[f, pl.ds(k, rows, stride=na), :]
            for r in range(na):
                amount = ((k - r) * group) % width
                moved = pltpu.roll(piece, amount, 1) if amount else piece
                parts[r] = moved if k == 0 else jnp.where(lane_group == k, moved, parts[r])
        for r in range(na):
            out[r % nd, r // nd, f] = parts[r]


def cos_sin_pi(x):
    turns = jnp.floor(x + 0.5)
    f = x - turns
    sign = 1.0 - 2.0 * (turns - 2.0 * jnp.floor(turns * 0.5))
    u = f * f
    c = COS_TERMS[-1]
    for term in COS_TERMS[-2::-1]:
        c = c * u + term
    s = SIN_TERMS[-1]
    for term in SIN_TERMS[-2::-1]:
        s = s * u + term
    return c * sign, s * (f * sign)


def rows_pair(ref, rows):
    return jnp.concatenate([ref[pl.ds(r, 1), :] for r in rows], axis=1)


def used_rows(ids_ref, chunks, rows, table):
    count = jnp.int32(0)
    level = lax.broadcasted_iota(jnp.int32, (rows, LANES), 0).astype(F32) + 1.0
    for j in range(chunks):
        ids = ids_ref[j * rows : (j + 1) * rows, :]
        used = jnp.max(jnp.where(ids >= 0.0, level, 0.0)).astype(jnp.int32)
        for i in range(rows):
            table[count + i] = j * rows + i
        count = count + used
    group = STEP_ROWS * UNROLL
    for i in range(group):
        table[count + i] = chunks * rows
    table[table.shape[0] - 1] = lax.div(count + (group - 1), group)


def step_rows(table, n):
    return [table[n * STEP_ROWS + i] for i in range(STEP_ROWS)]


def stacked(field):
    high, low = split(field)
    top = jnp.concatenate([high, high], axis=1)
    bottom = jnp.concatenate([low, jnp.zeros_like(low)], axis=1)
    return jnp.concatenate([top, bottom], axis=0)


def forward_step(stack, phi, ids_row, row_iota, owned):
    both = jnp.dot(stack, phi, preferred_element_type=F32)
    value = both[:owned] + both[owned:]
    return jnp.sum(jnp.where(row_iota == ids_row, value, 0.0), axis=0, keepdims=True)


def store_rows(ref, rows, value):
    for i, r in enumerate(rows):
        ref[pl.ds(r, 1), :] = value[:, i * LANES : (i + 1) * LANES]


def basis_loop(table, ids_ref, time_ref, coef, phi_ref, value_ref):
    owned, terms = coef.shape
    half = terms // 2
    value_ref[...] = jnp.zeros(value_ref.shape, F32)
    width = phi_ref.shape[2]
    stack = stacked(coef)
    row_iota = lax.broadcasted_iota(jnp.int32, (owned, width), 0).astype(F32)
    fine = (lax.broadcasted_iota(jnp.int32, (8, width), 0) + 1).astype(F32)
    coarse = (lax.broadcasted_iota(jnp.int32, (half // 8, width), 0) * 8).astype(F32)

    def step(n):
        rows = step_rows(table, n)
        times = rows_pair(time_ref, rows)
        cos_fine, sin_fine = cos_sin_pi(fine * times)
        cos_coarse, sin_coarse = cos_sin_pi(coarse * times)
        cos_parts, sin_parts = [], []
        for j in range(half // 8):
            cj = cos_coarse[j : j + 1]
            sj = sin_coarse[j : j + 1]
            cos_parts.append(cj * cos_fine - sj * sin_fine)
            sin_parts.append(sj * cos_fine + cj * sin_fine)
        high, low = split(jnp.concatenate(cos_parts + sin_parts, axis=0))
        phi = jnp.concatenate([high, low], axis=0)
        phi_ref[n] = phi
        value = forward_step(stack, phi, rows_pair(ids_ref, rows), row_iota, owned)
        store_rows(value_ref, rows, value)

    def block(i, carry):
        for u in range(SETUP_UNROLL):
            step(i * SETUP_UNROLL + u)
        return carry

    blocks = table[table.shape[0] - 1] * (UNROLL // SETUP_UNROLL)
    lax.fori_loop(0, blocks, block, 0)


def unpack(packed, chunks, first, meta, times):
    rows = packed.shape[2]
    count = chunks * rows
    meta[0, :count] = flat(packed, first, chunks)
    meta[0, count:] = jnp.full((DUMMY_ROWS, LANES), -1.0, F32)
    meta[1, :count] = flat(packed, 4, chunks)
    meta[1, count:] = jnp.zeros((DUMMY_ROWS, LANES), F32)
    times[:count] = flat(packed, first + 1, chunks)
    times[count:] = jnp.zeros((DUMMY_ROWS, LANES), F32)


def setup_asc_kernel(chunks, packed, coef, phi, value, meta, table, times):
    unpack(packed, chunks, 0, meta, times)
    used_rows(meta.at[0], chunks, packed.shape[2], table)
    basis_loop(table, meta.at[0], times, coef[...], phi, value)


def setup_desc_kernel(chunks, packed, coef, value_asc, phi, meta, send, table, times, value):
    rows = send.shape[2]
    unpack(packed, chunks, 2, meta, times)
    used_rows(meta.at[0], chunks, rows, table)
    basis_loop(table, meta.at[0], times, coef[...], phi, value)
    for j in range(chunks):
        send[j, 0] = value_asc[j * rows : (j + 1) * rows, :]
        send[j, 1] = value[j * rows : (j + 1) * rows, :]


def backward_forward(chunks, tables, ids, z_ref, phis, finish, send, value_ref):
    owned = finish.owned
    steps, double, width = phis[0].shape
    terms = double // 2
    row_iota = lax.broadcasted_iota(jnp.int32, (owned, width), 0).astype(F32)

    def back(role):
        def gather(n):
            rows = step_rows(tables[role], n)
            hit = row_iota == rows_pair(ids[role], rows)
            high = jnp.where(hit, rows_pair(z_ref.at[2 * role], rows), 0.0).astype(BF16)
            low = jnp.where(hit, rows_pair(z_ref.at[2 * role + 1], rows), 0.0).astype(BF16)
            return lax.dot_general(
                jnp.concatenate([high, low], axis=0),
                phis[role][n],
                (((1,), (1,)), ((), ())),
                preferred_element_type=F32,
            )

        def block(i, carry):
            parts = [gather(i * UNROLL + u) for u in range(UNROLL)]
            while len(parts) > 1:
                parts = [sum(parts[k : k + 2]) for k in range(0, len(parts), 2)]
            return carry + parts[0]

        table = tables[role]
        g = lax.fori_loop(
            0, table[table.shape[0] - 1], block, jnp.zeros((2 * owned, double), F32)
        )
        return g[:owned, :terms] + (g[:owned, terms:] + g[owned:, :terms])

    fields = finish(back(0), -back(1))
    value_ref[...] = jnp.zeros(value_ref.shape, F32)
    for role in range(2):
        stack = stacked(fields[role])
        table = tables[role]

        def block(i, carry):
            for u in range(UNROLL):
                n = i * UNROLL + u
                rows = step_rows(table, n)
                value = forward_step(
                    stack, phis[role][n], rows_pair(ids[role], rows), row_iota, owned
                )
                store_rows(value_ref.at[role], rows, value)
            return carry

        lax.fori_loop(0, table[table.shape[0] - 1], block, 0)
    rows = send.shape[2]
    for j in range(chunks):
        for role in range(2):
            send[j, role] = value_ref[role, j * rows : (j + 1) * rows, :]


class Finish:
    def __init__(self, owned, call):
        self.owned = owned
        self.call = call

    def __call__(self, asc, desc):
        return self.call(asc, desc)


def store_split(z_ref, role, z):
    count = z.shape[0]
    high = z.astype(BF16).astype(F32)
    z_ref[2 * role, :count] = high
    z_ref[2 * role + 1, :count] = z - high
    z_ref[2 * role : 2 * role + 2, count:] = jnp.zeros((2, DUMMY_ROWS, LANES), F32)


def cross_values(chunks, got, sent, role):
    if role == 0:
        return flat(sent, 0, chunks) - flat(got, 1, chunks)
    return flat(got, 0, chunks) - flat(sent, 1, chunks)


def weigh(model, meta, role, weights, z_ref):
    count = model.shape[0]
    live = meta[0, :count] >= 0.0
    misfit = jnp.where(live, meta[1, :count] - model, 0.0)
    weight = jnp.where(live, 1.0 / (1.0 + misfit * misfit / cauchy_square), 0.0)
    weights[role] = weight
    store_split(z_ref, role, weight * misfit)


def first_kernel(
    chunks, got, sent, meta_a, meta_d, phi_a, phi_d, table_a, table_d, state_a, state_d,
    model, weights, basis, send, z_ref, value_ref,
):
    for role, meta in enumerate((meta_a, meta_d)):
        values = cross_values(chunks, got, sent, role)
        model[role] = values
        weigh(values, meta, role, weights, z_ref)

    def finish(asc, desc):
        new = (asc - damping * state_a[...], desc - damping * state_d[...])
        basis[0], basis[1] = new
        return new

    backward_forward(
        chunks, (table_a, table_d), (meta_a.at[0], meta_d.at[0]), z_ref, (phi_a, phi_d),
        Finish(state_a.shape[0], finish), send, value_ref,
    )


def image_kernel(
    chunks, got, sent, meta_a, meta_d, phi_a, phi_d, table_a, table_d, weights, before,
    crossed, basis, send, z_ref, value_ref,
):
    for role, meta in enumerate((meta_a, meta_d)):
        values = cross_values(chunks, got, sent, role)
        crossed[role] = values
        store_split(z_ref, role, weights[role] * values)

    def finish(asc, desc):
        new = (
            SCALE * (asc + damping * before[0]),
            SCALE * (desc + damping * before[1]),
        )
        basis[0], basis[1] = new
        return new

    backward_forward(
        chunks, (table_a, table_d), (meta_a.at[0], meta_d.at[0]), z_ref, (phi_a, phi_d),
        Finish(before.shape[1], finish), send, value_ref,
    )


def total(x):
    return jnp.sum(jnp.sum(x, axis=0, keepdims=True), axis=1, keepdims=True)


PAIRS = [(0, 0), (0, 1), (0, 2), (1, 1), (1, 2), (2, 2)]


def gram_kernel(
    chunks, got, sent, weights, crossed_0, crossed_1, basis_0, basis_1, basis_2,
    crossed_2, scalars,
):
    for role in range(2):
        crossed_2[role] = cross_values(chunks, got, sent, role)
    weight = weights[0]
    values = [crossed_0[0], crossed_1[0], crossed_2[0]]
    bases = [basis_0, basis_1, basis_2]
    lane = lax.broadcasted_iota(jnp.int32, (1, LANES), 1)
    line = jnp.zeros((1, LANES), F32)
    for place, (i, j) in enumerate(PAIRS):
        dots = total(bases[i][0] * bases[j][0] + bases[i][1] * bases[j][1])
        curve = total(weight * values[i] * values[j]) + damping * dots
        line = jnp.where(lane == place, curve, line)
        if i == 0:
            line = jnp.where(lane == len(PAIRS) + j, dots, line)
    for d in range(scalars.shape[0]):
        scalars[d] = jnp.broadcast_to(line, scalars.shape[1:])


def solve(scalars):
    summed = scalars[0]
    for d in range(1, scalars.shape[0]):
        summed = summed + scalars[d]
    line = summed[0:1]
    lane = lax.broadcasted_iota(jnp.int32, (1, LANES), 1)

    def pick(place):
        return jnp.sum(jnp.where(lane == place, line, 0.0), axis=1, keepdims=True)

    g = {pair: pick(place) for place, pair in enumerate(PAIRS)}
    right = [pick(len(PAIRS) + i) for i in range(3)]
    s = [
        jnp.where(g[i, i] > 0.0, lax.rsqrt(jnp.maximum(g[i, i], 1e-37)), 0.0) for i in range(3)
    ]
    l10 = g[0, 1] * s[0] * s[1]
    l20 = g[0, 2] * s[0] * s[2]
    g21 = g[1, 2] * s[1] * s[2]
    c = [right[i] * s[i] for i in range(3)]

    def inverse(pivot):
        good = pivot > PIVOT_FLOOR
        return jnp.where(good, 1.0 / jnp.where(good, pivot, 1.0), 0.0)

    inv1 = inverse(1.0 - l10 * l10)
    t21 = g21 - l20 * l10
    l21 = t21 * inv1
    inv2 = inverse(1.0 - l20 * l20 - l21 * t21)
    u1 = c[1] - l10 * c[0]
    u2 = c[2] - l20 * c[0] - l21 * u1
    x2 = u2 * inv2
    x1 = u1 * inv1 - l21 * x2
    x0 = c[0] - l10 * x1 - l20 * x2
    return [x0 * s[0], x1 * s[1], x2 * s[2]]


def combine(y, parts):
    return y[0] * parts[0] + (y[1] * parts[1] + y[2] * parts[2])


def next_kernel(
    chunks, scalars, meta_a, meta_d, phi_a, phi_d, table_a, table_d, state_a, state_d, model,
    crossed_0, crossed_1, crossed_2, basis_0, basis_1, basis_2,
    new_state_a, new_state_d, new_model, weights, basis, send, z_ref, value_ref,
):
    y = solve(scalars)
    for role, meta in enumerate((meta_a, meta_d)):
        values = model[role] + combine(y, [crossed_0[role], crossed_1[role], crossed_2[role]])
        new_model[role] = values
        weigh(values, meta, role, weights, z_ref)
    new_state_a[...] = state_a[...] + combine(y, [basis_0[0], basis_1[0], basis_2[0]])
    new_state_d[...] = state_d[...] + combine(y, [basis_0[1], basis_1[1], basis_2[1]])

    def finish(asc, desc):
        new = (asc - damping * new_state_a[...], desc - damping * new_state_d[...])
        basis[0], basis[1] = new
        return new

    backward_forward(
        chunks, (table_a, table_d), (meta_a.at[0], meta_d.at[0]), z_ref, (phi_a, phi_d),
        Finish(state_a.shape[0], finish), send, value_ref,
    )


def final_kernel(scalars, state_a, basis_0, basis_1, basis_2, desc, out_a, out_d):
    y = solve(scalars)
    out_a[...] = state_a[...] + combine(y, [basis_0[0], basis_1[0], basis_2[0]])
    out_d[...] = desc[0] + combine(y, [desc[1], desc[2], desc[3]])


def body(coef_asc, coef_desc, cross_asc, cross_desc, time_asc, time_desc, height, block_fill):
    owned_asc, terms = coef_asc.shape
    owned_desc = coef_desc.shape[0]
    blocks, width = cross_asc.shape
    na = lax.axis_size("asc")
    nd = lax.axis_size("desc")
    fold = na // nd
    rows = blocks * width // na // LANES
    all_rows = na * rows
    group = STEP_ROWS * UNROLL
    steps = -(-all_rows // group) * UNROLL
    step_width = STEP_ROWS * LANES
    shape = jax.ShapeDtypeStruct

    def call(kernel, outs, scratch, *args, in_specs=None, mebibytes=16):
        return pl.pallas_call(
            kernel,
            out_shape=outs,
            in_specs=[place(x) for x in args] if in_specs is None else in_specs,
            out_specs=jax.tree.map(place, outs),
            scratch_shapes=scratch,
            compiler_params=params(mebibytes),
        )(*args)

    to_role = []
    for p in range(na):
        for q in range(nd):
            to_role.append((p * nd + q, (q * fold + p // nd) * nd + p % nd))
    to_native = [(b, a) for a, b in to_role]
    role_desc = lax.ppermute(coef_desc, ("asc", "desc"), to_role)

    slots = (cross_asc, cross_desc, time_asc, time_desc, height)
    packed = call(
        functools.partial(pack_kernel, na, nd, owned_asc, owned_desc),
        shape((nd, fold, FIELDS, rows, LANES), F32),
        [pltpu.VMEM((blocks, width), x.dtype) for x in slots]
        + [
            pltpu.VMEM((1, blocks), jnp.int32),
            pltpu.VMEM((FIELDS, blocks, width), F32),
            pltpu.SemaphoreType.DMA((len(slots) + 1,)),
        ],
        *slots, block_fill.reshape(1, blocks),
        in_specs=[pl.BlockSpec(memory_space=pltpu.HBM)] * (len(slots) + 1),
        mebibytes=60,
    )
    at_asc = lax.all_to_all(packed, "desc", split_axis=0, concat_axis=0, tiled=True)
    at_asc = at_asc.reshape(na, FIELDS, rows, LANES)
    at_desc = lax.all_to_all(at_asc, "asc", split_axis=0, concat_axis=0, tiled=True)

    phi_shape = shape((steps, 2 * terms, step_width), BF16)
    meta_shape = shape((2, all_rows + DUMMY_ROWS, LANES), F32)
    table_shape = shape((all_rows + rows + STEP_ROWS * UNROLL + 1,), jnp.int32)
    send_shape = shape((na, 2, rows, LANES), F32)
    pair_shape = shape((2, all_rows, LANES), F32)
    field_shape = shape((2, owned_asc, terms), F32)
    flat_scratch = pltpu.VMEM((all_rows + DUMMY_ROWS, LANES), F32)
    pass_scratch = [
        pltpu.VMEM((4, all_rows + DUMMY_ROWS, LANES), F32),
        pltpu.VMEM((2, all_rows + DUMMY_ROWS, LANES), F32),
    ]
    phi_a, value_asc, meta_a, table_a = call(
        functools.partial(setup_asc_kernel, na),
        [phi_shape, shape((all_rows + DUMMY_ROWS, LANES), F32), meta_shape, table_shape],
        [flat_scratch],
        at_asc, coef_asc,
    )
    phi_d, meta_d, sent, table_d = call(
        functools.partial(setup_desc_kernel, na),
        [phi_shape, meta_shape, send_shape, table_shape],
        [flat_scratch, flat_scratch],
        at_desc, role_desc, value_asc,
    )

    def exchange(x):
        return lax.all_to_all(x, "asc", split_axis=0, concat_axis=0, tiled=True)

    def share(x):
        return lax.all_to_all(x, ("asc", "desc"), split_axis=0, concat_axis=0, tiled=True)

    fixed = (meta_a, meta_d, phi_a, phi_d, table_a, table_d)
    state_a, state_d = coef_asc, role_desc
    for outer in range(GN_STEPS):
        if outer == 0:
            got = exchange(sent)
            model, weights, basis_0, sent = call(
                functools.partial(first_kernel, na),
                [pair_shape, pair_shape, field_shape, send_shape],
                pass_scratch,
                got, sent, *fixed, state_a, state_d,
            )
        else:
            state_a, state_d, model, weights, basis_0, sent = call(
                functools.partial(next_kernel, na),
                [
                    shape(state_a.shape, F32), shape(state_d.shape, F32),
                    pair_shape, pair_shape, field_shape, send_shape,
                ],
                pass_scratch,
                scalars, *fixed, state_a, state_d, model,
                *crossed, *bases,
            )
        bases, crossed = [basis_0], []
        for inner in range(2):
            got = exchange(sent)
            crossed_now, basis_now, sent = call(
                functools.partial(image_kernel, na),
                [pair_shape, field_shape, send_shape],
                pass_scratch,
                got, sent, *fixed, weights, bases[-1],
            )
            crossed.append(crossed_now)
            bases.append(basis_now)
        if outer + 1 == GN_STEPS:
            leaving = jnp.stack([state_d, bases[0][1], bases[1][1], bases[2][1]])
            native = lax.ppermute(leaving, ("asc", "desc"), to_native)
        got = exchange(sent)
        crossed_now, scalars = call(
            functools.partial(gram_kernel, na),
            [pair_shape, shape((na * nd, 8, LANES), F32)],
            [],
            got, sent, weights, *crossed, *bases,
        )
        crossed.append(crossed_now)
        scalars = share(scalars)
    return tuple(
        call(
            final_kernel,
            [shape(coef_asc.shape, F32), shape(coef_desc.shape, F32)],
            [],
            scalars, state_a, *bases, native,
        )
    )


def solution(mesh):
    split_rows = P(("asc", "desc"), None)
    return jax.shard_map(
        body,
        mesh=mesh,
        in_specs=(split_rows,) * 7 + (P(("asc", "desc")),),
        out_specs=(split_rows, split_rows),
        check_vma=False,
    )
```

```python
import functools
import math

import jax
import jax.numpy as jnp
from jax import lax
from jax.experimental import pallas as pl
from jax.experimental.pallas import tpu as pltpu
from jax.sharding import PartitionSpec as P

GN_STEPS = 2
damping = 2.0
cauchy_square = 2.25

LANES = 128
STEP_ROWS = 2
UNROLL = 4
SETUP_UNROLL = 2
DUMMY_ROWS = 8
SCALE = 1.0 / 128.0
FIELDS = 5
PIVOT_FLOOR = 1e-6
F32 = jnp.float32
BF16 = jnp.bfloat16

COS_TERMS = [(-1.0) ** i * math.pi ** (2 * i) / math.factorial(2 * i) for i in range(8)]
SIN_TERMS = [(-1.0) ** i * math.pi ** (2 * i + 1) / math.factorial(2 * i + 1) for i in range(7)]


def in_smem(x):
    return x.dtype == jnp.int32 and len(x.shape) == 1


def params(mebibytes):
    return pltpu.CompilerParams(vmem_limit_bytes=mebibytes * 1024 * 1024)


def place(x):
    return pl.BlockSpec(memory_space=pltpu.SMEM if in_smem(x) else pltpu.VMEM)


def split(x):
    high = x.astype(BF16)
    low = (x - high.astype(F32)).astype(BF16)
    return high, low


def flat(ref, field, chunks):
    return jnp.concatenate([ref[j, field] for j in range(chunks)], axis=0)


def local_id(ids, owned):
    if owned & (owned - 1) == 0:
        return ids & (owned - 1)
    return lax.rem(ids, owned)


def pack_kernel(
    na, nd, owned_asc, owned_desc, ca_in, cd_in, ta_in, td_in, height_in, fill_in, out,
    ca, cd, ta, td, height, fill, turned, sems,
):
    copies = [
        pltpu.make_async_copy(source, target, sems.at[i])
        for i, (source, target) in enumerate(
            [
                (fill_in, fill), (ca_in, ca), (ta_in, ta),
                (cd_in, cd), (td_in, td), (height_in, height),
            ]
        )
    ]
    for copy in copies:
        copy.start()
    for copy in copies:
        copy.wait()
    blocks, width = ca.shape
    group = width // na
    rows = blocks // na
    fill_row = fill[...]
    row_id = lax.broadcasted_iota(jnp.int32, (blocks, blocks), 0)
    col_id = lax.broadcasted_iota(jnp.int32, (blocks, blocks), 1)
    fill_col = jnp.sum(
        jnp.where(row_id == col_id, fill_row, 0).astype(F32), axis=1, keepdims=True
    )
    lane = lax.broadcasted_iota(jnp.int32, (blocks, width), 1)
    live = lane.astype(F32) < fill_col
    fields = [
        jnp.where(live, local_id(ca[...], owned_asc).astype(F32), -1.0),
        ta[...],
        jnp.where(live, local_id(cd[...], owned_desc).astype(F32), -1.0),
        td[...],
        height[...],
    ]
    source = lax.broadcasted_iota(jnp.int32, (width, width), 0)
    target = lax.broadcasted_iota(jnp.int32, (width, width), 1)
    owner = target // group
    place = target - owner * group
    order = (source == place * na + owner).astype(F32).astype(BF16)
    for f, x in enumerate(fields):
        high = x.astype(BF16)
        rest = x - high.astype(F32)
        middle = rest.astype(BF16)
        low = (rest - middle.astype(F32)).astype(BF16)
        turned[f] = (
            jnp.dot(high, order, preferred_element_type=F32)
            + jnp.dot(middle, order, preferred_element_type=F32)
        ) + jnp.dot(low, order, preferred_element_type=F32)
    lane_group = lax.broadcasted_iota(jnp.int32, (rows, width), 1) // group
    for f in range(FIELDS):
        parts = [None] * na
        for k in range(na):
            piece = turned[f, pl.ds(k, rows, stride=na), :]
            for r in range(na):
                amount = ((k - r) * group) % width
                moved = pltpu.roll(piece, amount, 1) if amount else piece
                parts[r] = moved if k == 0 else jnp.where(lane_group == k, moved, parts[r])
        for r in range(na):
            out[r % nd, r // nd, f] = parts[r]


def cos_sin_pi(x):
    turns = jnp.floor(x + 0.5)
    f = x - turns
    sign = 1.0 - 2.0 * (turns - 2.0 * jnp.floor(turns * 0.5))
    u = f * f
    c = COS_TERMS[-1]
    for term in COS_TERMS[-2::-1]:
        c = c * u + term
    s = SIN_TERMS[-1]
    for term in SIN_TERMS[-2::-1]:
        s = s * u + term
    return c * sign, s * (f * sign)


def rows_pair(ref, rows):
    return jnp.concatenate([ref[pl.ds(r, 1), :] for r in rows], axis=1)


def used_rows(ids_ref, chunks, rows, table):
    count = jnp.int32(0)
    level = lax.broadcasted_iota(jnp.int32, (rows, LANES), 0).astype(F32) + 1.0
    for j in range(chunks):
        ids = ids_ref[j * rows : (j + 1) * rows, :]
        used = jnp.max(jnp.where(ids >= 0.0, level, 0.0)).astype(jnp.int32)
        for i in range(rows):
            table[count + i] = j * rows + i
        count = count + used
    group = STEP_ROWS * UNROLL
    for i in range(group):
        table[count + i] = chunks * rows
    table[table.shape[0] - 1] = lax.div(count + (group - 1), group)


def step_rows(table, n):
    return [table[n * STEP_ROWS + i] for i in range(STEP_ROWS)]


def stacked(field):
    high, low = split(field)
    top = jnp.concatenate([high, high], axis=1)
    bottom = jnp.concatenate([low, jnp.zeros_like(low)], axis=1)
    return jnp.concatenate([top, bottom], axis=0)


def forward_step(stack, phi, ids_row, row_iota, owned):
    both = jnp.dot(stack, phi, preferred_element_type=F32)
    value = both[:owned] + both[owned:]
    return jnp.sum(jnp.where(row_iota == ids_row, value, 0.0), axis=0, keepdims=True)


def store_rows(ref, rows, value):
    for i, r in enumerate(rows):
        ref[pl.ds(r, 1), :] = value[:, i * LANES : (i + 1) * LANES]


def basis_loop(table, ids_ref, time_ref, coef, phi_ref, value_ref):
    owned, terms = coef.shape
    half = terms // 2
    value_ref[...] = jnp.zeros(value_ref.shape, F32)
    width = phi_ref.shape[2]
    stack = stacked(coef)
    row_iota = lax.broadcasted_iota(jnp.int32, (owned, width), 0).astype(F32)
    fine = (lax.broadcasted_iota(jnp.int32, (8, width), 0) + 1).astype(F32)
    coarse = (lax.broadcasted_iota(jnp.int32, (half // 8, width), 0) * 8).astype(F32)

    def step(n):
        rows = step_rows(table, n)
        times = rows_pair(time_ref, rows)
        cos_fine, sin_fine = cos_sin_pi(fine * times)
        cos_coarse, sin_coarse = cos_sin_pi(coarse * times)
        cos_parts, sin_parts = [], []
        for j in range(half // 8):
            cj = cos_coarse[j : j + 1]
            sj = sin_coarse[j : j + 1]
            cos_parts.append(cj * cos_fine - sj * sin_fine)
            sin_parts.append(sj * cos_fine + cj * sin_fine)
        high, low = split(jnp.concatenate(cos_parts + sin_parts, axis=0))
        phi = jnp.concatenate([high, low], axis=0)
        phi_ref[n] = phi
        value = forward_step(stack, phi, rows_pair(ids_ref, rows), row_iota, owned)
        store_rows(value_ref, rows, value)

    def block(i, carry):
        for u in range(SETUP_UNROLL):
            step(i * SETUP_UNROLL + u)
        return carry

    blocks = table[table.shape[0] - 1] * (UNROLL // SETUP_UNROLL)
    lax.fori_loop(0, blocks, block, 0)


def unpack(packed, chunks, first, meta, times):
    rows = packed.shape[2]
    count = chunks * rows
    meta[0, :count] = flat(packed, first, chunks)
    meta[0, count:] = jnp.full((DUMMY_ROWS, LANES), -1.0, F32)
    meta[1, :count] = flat(packed, 4, chunks)
    meta[1, count:] = jnp.zeros((DUMMY_ROWS, LANES), F32)
    times[:count] = flat(packed, first + 1, chunks)
    times[count:] = jnp.zeros((DUMMY_ROWS, LANES), F32)


def setup_kernel(
    chunks, at_asc, at_desc, coef_a, coef_d,
    meta_a, meta_d, phi_a, phi_d, table_a, table_d, value, *rest,
):
    sends, (times,) = rest[:chunks], rest[chunks:]
    rows = at_asc.shape[2]
    unpack(at_asc, chunks, 0, meta_a, times)
    used_rows(meta_a.at[0], chunks, rows, table_a)
    basis_loop(table_a, meta_a.at[0], times, coef_a[...], phi_a, value.at[0])
    unpack(at_desc, chunks, 2, meta_d, times)
    used_rows(meta_d.at[0], chunks, rows, table_d)
    basis_loop(table_d, meta_d.at[0], times, coef_d[...], phi_d, value.at[1])
    hand_out(value, sends)


def partner(index, offset, count, back):
    if count & (count - 1) == 0:
        return index ^ offset
    return (index - offset if back else index + offset) % count


def hand_out(value, sends):
    chunks, rows = len(sends), sends[0].shape[1]
    me = lax.axis_index("asc")
    for d, send in enumerate(sends):
        start = pl.multiple_of(partner(me, d, chunks, False) * rows, rows)
        for role in range(2):
            send[role] = value[role, pl.ds(start, rows), :]


def take_in(gots, own, flat_got):
    chunks, rows = len(gots) + 1, own.shape[1]
    me = lax.axis_index("asc")
    for d, got in enumerate([own] + list(gots)):
        start = pl.multiple_of(partner(me, d, chunks, True) * rows, rows)
        for role in range(2):
            flat_got[role, pl.ds(start, rows), :] = got[role]


def backward_forward(tables, ids, z_ref, phis, finish, value_ref, sends):
    owned = finish.owned
    steps, double, width = phis[0].shape
    terms = double // 2
    row_iota = lax.broadcasted_iota(jnp.int32, (owned, width), 0).astype(F32)

    def back(role):
        def gather(n):
            rows = step_rows(tables[role], n)
            hit = row_iota == rows_pair(ids[role], rows)
            high = jnp.where(hit, rows_pair(z_ref.at[2 * role], rows), 0.0).astype(BF16)
            low = jnp.where(hit, rows_pair(z_ref.at[2 * role + 1], rows), 0.0).astype(BF16)
            return lax.dot_general(
                jnp.concatenate([high, low], axis=0),
                phis[role][n],
                (((1,), (1,)), ((), ())),
                preferred_element_type=F32,
            )

        def block(i, carry):
            parts = [gather(i * UNROLL + u) for u in range(UNROLL)]
            while len(parts) > 1:
                parts = [sum(parts[k : k + 2]) for k in range(0, len(parts), 2)]
            return carry + parts[0]

        table = tables[role]
        g = lax.fori_loop(
            0, table[table.shape[0] - 1], block, jnp.zeros((2 * owned, double), F32)
        )
        return g[:owned, :terms] + (g[:owned, terms:] + g[owned:, :terms])

    fields = finish(back(0), -back(1))
    value_ref[...] = jnp.zeros(value_ref.shape, F32)
    for role in range(2):
        stack = stacked(fields[role])
        table = tables[role]

        def block(i, carry):
            for u in range(UNROLL):
                n = i * UNROLL + u
                rows = step_rows(table, n)
                value = forward_step(
                    stack, phis[role][n], rows_pair(ids[role], rows), row_iota, owned
                )
                store_rows(value_ref.at[role], rows, value)
            return carry

        lax.fori_loop(0, table[table.shape[0] - 1], block, 0)
    hand_out(value_ref, sends)


class Finish:
    def __init__(self, owned, call):
        self.owned = owned
        self.call = call

    def __call__(self, asc, desc):
        return self.call(asc, desc)


def store_split(z_ref, role, z):
    count = z.shape[0]
    high = z.astype(BF16).astype(F32)
    z_ref[2 * role, :count] = high
    z_ref[2 * role + 1, :count] = z - high
    z_ref[2 * role : 2 * role + 2, count:] = jnp.zeros((2, DUMMY_ROWS, LANES), F32)


def cross_values(flat_got, mine, role):
    count = flat_got.shape[1]
    if role == 0:
        return mine[0, :count] - flat_got[1]
    return flat_got[0] - mine[1, :count]


def weigh(model, meta, role, weights, z_ref):
    count = model.shape[0]
    live = meta[0, :count] >= 0.0
    misfit = jnp.where(live, meta[1, :count] - model, 0.0)
    weight = jnp.where(live, 1.0 / (1.0 + misfit * misfit / cauchy_square), 0.0)
    weights[role] = weight
    store_split(z_ref, role, weight * misfit)


def first_kernel(
    chunks, own, mine, meta_a, meta_d, phi_a, phi_d, table_a, table_d, state_a, state_d, *rest,
):
    gots, rest = rest[: chunks - 1], rest[chunks - 1 :]
    model, weights, basis, value_ref = rest[:4]
    sends, (z_ref, flat_got) = rest[4 : 4 + chunks], rest[4 + chunks :]
    take_in(gots, own, flat_got)
    for role, meta in enumerate((meta_a, meta_d)):
        values = cross_values(flat_got, mine, role)
        model[role] = values
        weigh(values, meta, role, weights, z_ref)

    def finish(asc, desc):
        new = (asc - damping * state_a[...], desc - damping * state_d[...])
        basis[0], basis[1] = new
        return new

    backward_forward(
        (table_a, table_d), (meta_a.at[0], meta_d.at[0]), z_ref, (phi_a, phi_d),
        Finish(state_a.shape[0], finish), value_ref, sends,
    )


def image_kernel(
    chunks, own, mine, meta_a, meta_d, phi_a, phi_d, table_a, table_d, weights, before, *rest,
):
    gots, rest = rest[: chunks - 1], rest[chunks - 1 :]
    crossed, basis, value_ref = rest[:3]
    sends, (z_ref, flat_got) = rest[3 : 3 + chunks], rest[3 + chunks :]
    take_in(gots, own, flat_got)
    for role in range(2):
        values = cross_values(flat_got, mine, role)
        crossed[role] = values
        store_split(z_ref, role, weights[role] * values)

    def finish(asc, desc):
        new = (
            SCALE * (asc + damping * before[0]),
            SCALE * (desc + damping * before[1]),
        )
        basis[0], basis[1] = new
        return new

    backward_forward(
        (table_a, table_d), (meta_a.at[0], meta_d.at[0]), z_ref, (phi_a, phi_d),
        Finish(before.shape[1], finish), value_ref, sends,
    )


def total(x):
    return jnp.sum(jnp.sum(x, axis=0, keepdims=True), axis=1, keepdims=True)


PAIRS = [(0, 0), (0, 1), (0, 2), (1, 1), (1, 2), (2, 2)]


def gram_kernel(
    chunks, own, mine, weights, crossed_0, crossed_1, basis_0, basis_1, basis_2, *rest,
):
    gots, (crossed_2, scalars, flat_got) = rest[: chunks - 1], rest[chunks - 1 :]
    take_in(gots, own, flat_got)
    for role in range(2):
        crossed_2[role] = cross_values(flat_got, mine, role)
    weight = weights[0]
    values = [crossed_0[0], crossed_1[0], crossed_2[0]]
    bases = [basis_0, basis_1, basis_2]
    lane = lax.broadcasted_iota(jnp.int32, (1, LANES), 1)
    line = jnp.zeros((1, LANES), F32)
    for place, (i, j) in enumerate(PAIRS):
        dots = total(bases[i][0] * bases[j][0] + bases[i][1] * bases[j][1])
        curve = total(weight * values[i] * values[j]) + damping * dots
        line = jnp.where(lane == place, curve, line)
        if i == 0:
            line = jnp.where(lane == len(PAIRS) + j, dots, line)
    for d in range(scalars.shape[0]):
        scalars[d] = jnp.broadcast_to(line, scalars.shape[1:])


def solve(scalars):
    summed = scalars[0]
    for d in range(1, scalars.shape[0]):
        summed = summed + scalars[d]
    line = summed[0:1]
    lane = lax.broadcasted_iota(jnp.int32, (1, LANES), 1)

    def pick(place):
        return jnp.sum(jnp.where(lane == place, line, 0.0), axis=1, keepdims=True)

    g = {pair: pick(place) for place, pair in enumerate(PAIRS)}
    right = [pick(len(PAIRS) + i) for i in range(3)]
    s = [
        jnp.where(g[i, i] > 0.0, lax.rsqrt(jnp.maximum(g[i, i], 1e-37)), 0.0) for i in range(3)
    ]
    l10 = g[0, 1] * s[0] * s[1]
    l20 = g[0, 2] * s[0] * s[2]
    g21 = g[1, 2] * s[1] * s[2]
    c = [right[i] * s[i] for i in range(3)]

    def inverse(pivot):
        good = pivot > PIVOT_FLOOR
        return jnp.where(good, 1.0 / jnp.where(good, pivot, 1.0), 0.0)

    inv1 = inverse(1.0 - l10 * l10)
    t21 = g21 - l20 * l10
    l21 = t21 * inv1
    inv2 = inverse(1.0 - l20 * l20 - l21 * t21)
    u1 = c[1] - l10 * c[0]
    u2 = c[2] - l20 * c[0] - l21 * u1
    x2 = u2 * inv2
    x1 = u1 * inv1 - l21 * x2
    x0 = c[0] - l10 * x1 - l20 * x2
    return [x0 * s[0], x1 * s[1], x2 * s[2]]


def combine(y, parts):
    return y[0] * parts[0] + (y[1] * parts[1] + y[2] * parts[2])


def next_kernel(
    chunks, scalars, meta_a, meta_d, phi_a, phi_d, table_a, table_d, state_a, state_d, model,
    crossed_0, crossed_1, crossed_2, basis_0, basis_1, basis_2,
    new_state_a, new_state_d, new_model, weights, basis, value_ref, *rest,
):
    sends, (z_ref,) = rest[:chunks], rest[chunks:]
    y = solve(scalars)
    for role, meta in enumerate((meta_a, meta_d)):
        values = model[role] + combine(y, [crossed_0[role], crossed_1[role], crossed_2[role]])
        new_model[role] = values
        weigh(values, meta, role, weights, z_ref)
    new_state_a[...] = state_a[...] + combine(y, [basis_0[0], basis_1[0], basis_2[0]])
    new_state_d[...] = state_d[...] + combine(y, [basis_0[1], basis_1[1], basis_2[1]])

    def finish(asc, desc):
        new = (asc - damping * new_state_a[...], desc - damping * new_state_d[...])
        basis[0], basis[1] = new
        return new

    backward_forward(
        (table_a, table_d), (meta_a.at[0], meta_d.at[0]), z_ref, (phi_a, phi_d),
        Finish(state_a.shape[0], finish), value_ref, sends,
    )


def final_kernel(scalars, state_a, basis_0, basis_1, basis_2, desc, out_a, out_d):
    y = solve(scalars)
    out_a[...] = state_a[...] + combine(y, [basis_0[0], basis_1[0], basis_2[0]])
    out_d[...] = desc[0] + combine(y, [desc[1], desc[2], desc[3]])


def body(coef_asc, coef_desc, cross_asc, cross_desc, time_asc, time_desc, height, block_fill):
    owned_asc, terms = coef_asc.shape
    owned_desc = coef_desc.shape[0]
    blocks, width = cross_asc.shape
    na = lax.axis_size("asc")
    nd = lax.axis_size("desc")
    fold = na // nd
    rows = blocks * width // na // LANES
    all_rows = na * rows
    group = STEP_ROWS * UNROLL
    steps = -(-all_rows // group) * UNROLL
    step_width = STEP_ROWS * LANES
    shape = jax.ShapeDtypeStruct

    def call(kernel, outs, scratch, *args, in_specs=None, mebibytes=16):
        return pl.pallas_call(
            kernel,
            out_shape=outs,
            in_specs=[place(x) for x in args] if in_specs is None else in_specs,
            out_specs=jax.tree.map(place, outs),
            scratch_shapes=scratch,
            compiler_params=params(mebibytes),
        )(*args)

    to_role = []
    for p in range(na):
        for q in range(nd):
            to_role.append((p * nd + q, (q * fold + p // nd) * nd + p % nd))
    to_native = [(b, a) for a, b in to_role]
    role_desc = lax.ppermute(coef_desc, ("asc", "desc"), to_role)

    slots = (cross_asc, cross_desc, time_asc, time_desc, height)
    packed = call(
        functools.partial(pack_kernel, na, nd, owned_asc, owned_desc),
        shape((nd, fold, FIELDS, rows, LANES), F32),
        [pltpu.VMEM((blocks, width), x.dtype) for x in slots]
        + [
            pltpu.VMEM((1, blocks), jnp.int32),
            pltpu.VMEM((FIELDS, blocks, width), F32),
            pltpu.SemaphoreType.DMA((len(slots) + 1,)),
        ],
        *slots, block_fill.reshape(1, blocks),
        in_specs=[pl.BlockSpec(memory_space=pltpu.HBM)] * (len(slots) + 1),
        mebibytes=60,
    )
    at_asc = lax.all_to_all(packed, "desc", split_axis=0, concat_axis=0, tiled=True)
    at_asc = at_asc.reshape(na, FIELDS, rows, LANES)
    at_desc = lax.all_to_all(at_asc, "asc", split_axis=0, concat_axis=0, tiled=True)

    padded = all_rows + DUMMY_ROWS
    phi_shape = shape((steps, 2 * terms, step_width), BF16)
    meta_shape = shape((2, padded, LANES), F32)
    table_shape = shape((all_rows + rows + group + 1,), jnp.int32)
    value_shape = shape((2, padded, LANES), F32)
    send_shapes = [shape((2, rows, LANES), F32)] * na
    pair_shape = shape((2, all_rows, LANES), F32)
    field_shape = shape((2, owned_asc, terms), F32)
    z_scratch = pltpu.VMEM((4, padded, LANES), F32)
    got_scratch = pltpu.VMEM((2, all_rows, LANES), F32)
    outs = call(
        functools.partial(setup_kernel, na),
        [meta_shape] * 2 + [phi_shape] * 2 + [table_shape] * 2 + [value_shape] + send_shapes,
        [pltpu.VMEM((padded, LANES), F32)],
        at_asc, at_desc, coef_asc, role_desc,
    )
    fixed, mine, sends = outs[:6], outs[6], outs[7:]

    def exchange(chunks):
        return [
            lax.ppermute(
                chunks[d], "asc", [(i, partner(i, d, na, False)) for i in range(na)]
            )
            for d in range(1, na)
        ]

    def share(x):
        return lax.all_to_all(x, ("asc", "desc"), split_axis=0, concat_axis=0, tiled=True)

    state_a, state_d = coef_asc, role_desc
    for outer in range(GN_STEPS):
        if outer == 0:
            gots = exchange(sends)
            outs = call(
                functools.partial(first_kernel, na),
                [pair_shape, pair_shape, field_shape, value_shape] + send_shapes,
                [z_scratch, got_scratch],
                sends[0], mine, *fixed, state_a, state_d, *gots,
            )
            model, weights, basis_0, mine = outs[:4]
            sends = outs[4:]
        else:
            outs = call(
                functools.partial(next_kernel, na),
                [
                    shape(state_a.shape, F32), shape(state_d.shape, F32),
                    pair_shape, pair_shape, field_shape, value_shape,
                ] + send_shapes,
                [z_scratch],
                scalars, *fixed, state_a, state_d, model,
                *crossed, *bases,
            )
            state_a, state_d, model, weights, basis_0, mine = outs[:6]
            sends = outs[6:]
        bases, crossed = [basis_0], []
        for inner in range(2):
            gots = exchange(sends)
            outs = call(
                functools.partial(image_kernel, na),
                [pair_shape, field_shape, value_shape] + send_shapes,
                [z_scratch, got_scratch],
                sends[0], mine, *fixed, weights, bases[-1], *gots,
            )
            crossed.append(outs[0])
            bases.append(outs[1])
            mine, sends = outs[2], outs[3:]
        if outer + 1 == GN_STEPS:
            leaving = jnp.stack([state_d, bases[0][1], bases[1][1], bases[2][1]])
            native = lax.ppermute(leaving, ("asc", "desc"), to_native)
        gots = exchange(sends)
        crossed_now, scalars = call(
            functools.partial(gram_kernel, na),
            [pair_shape, shape((na * nd, 8, LANES), F32)],
            [got_scratch],
            sends[0], mine, weights, *crossed, *bases, *gots,
        )
        crossed.append(crossed_now)
        scalars = share(scalars)
    return tuple(
        call(
            final_kernel,
            [shape(coef_asc.shape, F32), shape(coef_desc.shape, F32)],
            [],
            scalars, state_a, *bases, native,
        )
    )


def solution(mesh):
    split_rows = P(("asc", "desc"), None)
    return jax.shard_map(
        body,
        mesh=mesh,
        in_specs=(split_rows,) * 7 + (P(("asc", "desc")),),
        out_specs=(split_rows, split_rows),
        check_vma=False,
    )
```

```python
import functools
import math

import jax
import jax.numpy as jnp
from jax import lax
from jax.experimental import pallas as pl
from jax.experimental.pallas import tpu as pltpu
from jax.sharding import PartitionSpec as P

GN_STEPS = 2
damping = 2.0
cauchy_square = 2.25

LANES = 128
STEP_ROWS = 2
UNROLL = 4
SETUP_UNROLL = 2
DUMMY_ROWS = 8
SCALE = 1.0 / 128.0
FIELDS = 5
PIVOT_FLOOR = 1e-6
F32 = jnp.float32
BF16 = jnp.bfloat16

COS_TERMS = [(-1.0) ** i * math.pi ** (2 * i) / math.factorial(2 * i) for i in range(8)]
SIN_TERMS = [(-1.0) ** i * math.pi ** (2 * i + 1) / math.factorial(2 * i + 1) for i in range(7)]


def in_smem(x):
    return x.dtype == jnp.int32 and len(x.shape) == 1


def params(mebibytes):
    return pltpu.CompilerParams(vmem_limit_bytes=mebibytes * 1024 * 1024)


def place(x):
    return pl.BlockSpec(memory_space=pltpu.SMEM if in_smem(x) else pltpu.VMEM)


def split(x):
    high = x.astype(BF16)
    low = (x - high.astype(F32)).astype(BF16)
    return high, low


def flat(ref, field, chunks):
    return jnp.concatenate([ref[j, field] for j in range(chunks)], axis=0)


def local_id(ids, owned):
    if owned & (owned - 1) == 0:
        return ids & (owned - 1)
    return lax.rem(ids, owned)


def pack_kernel(
    na, nd, owned_asc, owned_desc, ca_in, cd_in, ta_in, td_in, height_in, fill_in, out,
    ca, cd, ta, td, height, fill, turned, sems,
):
    copies = [
        pltpu.make_async_copy(source, target, sems.at[i])
        for i, (source, target) in enumerate(
            [
                (fill_in, fill), (ca_in, ca), (ta_in, ta),
                (cd_in, cd), (td_in, td), (height_in, height),
            ]
        )
    ]
    for copy in copies:
        copy.start()
    for copy in copies:
        copy.wait()
    blocks, width = ca.shape
    group = width // na
    rows = blocks // na
    fill_row = fill[...]
    row_id = lax.broadcasted_iota(jnp.int32, (blocks, blocks), 0)
    col_id = lax.broadcasted_iota(jnp.int32, (blocks, blocks), 1)
    fill_col = jnp.sum(
        jnp.where(row_id == col_id, fill_row, 0).astype(F32), axis=1, keepdims=True
    )
    lane = lax.broadcasted_iota(jnp.int32, (blocks, width), 1)
    live = lane.astype(F32) < fill_col
    fields = [
        jnp.where(live, local_id(ca[...], owned_asc).astype(F32), -1.0),
        ta[...],
        jnp.where(live, local_id(cd[...], owned_desc).astype(F32), -1.0),
        td[...],
        height[...],
    ]
    source = lax.broadcasted_iota(jnp.int32, (width, width), 0)
    target = lax.broadcasted_iota(jnp.int32, (width, width), 1)
    owner = target // group
    place = target - owner * group
    order = (source == place * na + owner).astype(F32).astype(BF16)
    for f, x in enumerate(fields):
        high = x.astype(BF16)
        rest = x - high.astype(F32)
        middle = rest.astype(BF16)
        low = (rest - middle.astype(F32)).astype(BF16)
        turned[f] = (
            jnp.dot(high, order, preferred_element_type=F32)
            + jnp.dot(middle, order, preferred_element_type=F32)
        ) + jnp.dot(low, order, preferred_element_type=F32)
    lane_group = lax.broadcasted_iota(jnp.int32, (rows, width), 1) // group
    for f in range(FIELDS):
        parts = [None] * na
        for k in range(na):
            piece = turned[f, pl.ds(k, rows, stride=na), :]
            for r in range(na):
                amount = ((k - r) * group) % width
                moved = pltpu.roll(piece, amount, 1) if amount else piece
                parts[r] = moved if k == 0 else jnp.where(lane_group == k, moved, parts[r])
        for r in range(na):
            out[r % nd, r // nd, f] = parts[r]


def cos_sin_pi(x):
    turns = jnp.floor(x + 0.5)
    f = x - turns
    sign = 1.0 - 2.0 * (turns - 2.0 * jnp.floor(turns * 0.5))
    u = f * f
    c = COS_TERMS[-1]
    for term in COS_TERMS[-2::-1]:
        c = c * u + term
    s = SIN_TERMS[-1]
    for term in SIN_TERMS[-2::-1]:
        s = s * u + term
    return c * sign, s * (f * sign)


def rows_pair(ref, rows):
    return jnp.concatenate([ref[pl.ds(r, 1), :] for r in rows], axis=1)


def used_rows(ids_ref, chunks, rows, table):
    count = jnp.int32(0)
    level = lax.broadcasted_iota(jnp.int32, (rows, LANES), 0).astype(F32) + 1.0
    for j in range(chunks):
        ids = ids_ref[j * rows : (j + 1) * rows, :]
        used = jnp.max(jnp.where(ids >= 0.0, level, 0.0)).astype(jnp.int32)
        for i in range(rows):
            table[count + i] = j * rows + i
        count = count + used
    group = STEP_ROWS * UNROLL
    for i in range(group):
        table[count + i] = chunks * rows
    table[table.shape[0] - 1] = lax.div(count + (group - 1), group)


def step_rows(table, n):
    return [table[n * STEP_ROWS + i] for i in range(STEP_ROWS)]


def stacked(field):
    high, low = split(field)
    top = jnp.concatenate([high, high], axis=1)
    bottom = jnp.concatenate([low, jnp.zeros_like(low)], axis=1)
    return jnp.concatenate([top, bottom], axis=0)


def forward_step(stack, phi, ids_row, row_iota, owned):
    both = jnp.dot(stack, phi, preferred_element_type=F32)
    value = both[:owned] + both[owned:]
    return jnp.sum(jnp.where(row_iota == ids_row, value, 0.0), axis=0, keepdims=True)


def store_rows(ref, rows, value):
    for i, r in enumerate(rows):
        ref[pl.ds(r, 1), :] = value[:, i * LANES : (i + 1) * LANES]


def basis_loop(table, ids_ref, time_ref, coef, phi_ref, value_ref):
    owned, terms = coef.shape
    half = terms // 2
    value_ref[...] = jnp.zeros(value_ref.shape, F32)
    width = phi_ref.shape[2]
    stack = stacked(coef)
    row_iota = lax.broadcasted_iota(jnp.int32, (owned, width), 0).astype(F32)
    fine = (lax.broadcasted_iota(jnp.int32, (8, width), 0) + 1).astype(F32)
    coarse = (lax.broadcasted_iota(jnp.int32, (half // 8, width), 0) * 8).astype(F32)

    def step(n):
        rows = step_rows(table, n)
        times = rows_pair(time_ref, rows)
        cos_fine, sin_fine = cos_sin_pi(fine * times)
        cos_coarse, sin_coarse = cos_sin_pi(coarse * times)
        cos_parts, sin_parts = [], []
        for j in range(half // 8):
            cj = cos_coarse[j : j + 1]
            sj = sin_coarse[j : j + 1]
            cos_parts.append(cj * cos_fine - sj * sin_fine)
            sin_parts.append(sj * cos_fine + cj * sin_fine)
        high, low = split(jnp.concatenate(cos_parts + sin_parts, axis=0))
        phi = jnp.concatenate([high, low], axis=0)
        phi_ref[n] = phi
        value = forward_step(stack, phi, rows_pair(ids_ref, rows), row_iota, owned)
        store_rows(value_ref, rows, value)

    def block(i, carry):
        for u in range(SETUP_UNROLL):
            step(i * SETUP_UNROLL + u)
        return carry

    blocks = table[table.shape[0] - 1] * (UNROLL // SETUP_UNROLL)
    lax.fori_loop(0, blocks, block, 0)


class Role:
    def __init__(self, sign, table, meta, phi, z_ref, value_ref):
        self.sign = sign
        self.table = table
        self.ids = meta.at[0]
        self.meta = meta
        self.phi = phi
        self.z_ref = z_ref
        self.value_ref = value_ref
        self.count = meta.shape[1] - DUMMY_ROWS

    def cross(self, mine, other):
        return mine - other if self.sign > 0 else other - mine

    def backward(self, z, owned):
        high = z.astype(BF16).astype(F32)
        self.z_ref[0, : self.count] = high
        self.z_ref[1, : self.count] = z - high
        self.z_ref[:, self.count :] = jnp.zeros((2, DUMMY_ROWS, LANES), F32)
        steps, double, width = self.phi.shape
        terms = double // 2
        row_iota = lax.broadcasted_iota(jnp.int32, (owned, width), 0).astype(F32)

        def gather(n):
            rows = step_rows(self.table, n)
            hit = row_iota == rows_pair(self.ids, rows)
            parts = [
                jnp.where(hit, rows_pair(self.z_ref.at[k], rows), 0.0).astype(BF16)
                for k in range(2)
            ]
            return lax.dot_general(
                jnp.concatenate(parts, axis=0),
                self.phi[n],
                (((1,), (1,)), ((), ())),
                preferred_element_type=F32,
            )

        def block(i, carry):
            parts = [gather(i * UNROLL + u) for u in range(UNROLL)]
            while len(parts) > 1:
                parts = [sum(parts[k : k + 2]) for k in range(0, len(parts), 2)]
            return carry + parts[0]

        blocks = self.table[self.table.shape[0] - 1]
        g = lax.fori_loop(0, blocks, block, jnp.zeros((2 * owned, double), F32))
        return self.sign * (g[:owned, :terms] + (g[:owned, terms:] + g[owned:, :terms]))

    def forward(self, field):
        owned = field.shape[0]
        stack = stacked(field)
        width = self.phi.shape[2]
        row_iota = lax.broadcasted_iota(jnp.int32, (owned, width), 0).astype(F32)
        self.value_ref[...] = jnp.zeros(self.value_ref.shape, F32)

        def block(i, carry):
            for u in range(UNROLL):
                n = i * UNROLL + u
                rows = step_rows(self.table, n)
                value = forward_step(
                    stack, self.phi[n], rows_pair(self.ids, rows), row_iota, owned
                )
                store_rows(self.value_ref, rows, value)
            return carry

        lax.fori_loop(0, self.table[self.table.shape[0] - 1], block, 0)
        return self.value_ref[: self.count]

    def weigh(self, model):
        live = self.meta[0, : self.count] >= 0.0
        misfit = jnp.where(live, self.meta[1, : self.count] - model, 0.0)
        weight = jnp.where(live, 1.0 / (1.0 + misfit * misfit / cauchy_square), 0.0)
        return weight, weight * misfit

    def gradient(self, z, state):
        return self.backward(z, state.shape[0]) - damping * state

    def image(self, z, before):
        return SCALE * (self.backward(z, before.shape[0]) + damping * before)


def write_chunks(send, first, values):
    chunks, rows = send.shape[0], send.shape[2]
    for j in range(chunks):
        send[j, first] = values[j * rows : (j + 1) * rows, :]


def fill_padded(ref, values):
    count = values.shape[0]
    ref[:count] = values
    ref[count:] = jnp.zeros((ref.shape[0] - count,) + values.shape[1:], F32)


def setup_asc_kernel(
    chunks, packed, coef, role_desc, meta, phi, table, value, onward, times, value_ref
):
    rows = packed.shape[2]
    count = chunks * rows
    meta[0, :count] = flat(packed, 0, chunks)
    meta[0, count:] = jnp.full((DUMMY_ROWS, LANES), -1.0, F32)
    fill_padded(meta.at[1], flat(packed, 4, chunks))
    fill_padded(times, flat(packed, 1, chunks))
    used_rows(meta.at[0], chunks, rows, table)
    basis_loop(table, meta.at[0], times, coef[...], phi, value_ref)
    value[...] = value_ref[:count]
    for j in range(chunks):
        onward[j, 0] = packed[j, 2]
        onward[j, 1] = packed[j, 3]
        onward[j, 2] = packed[j, 4]
    write_chunks(onward, 3, value_ref[:count])


def setup_desc_kernel(
    chunks, packed, state, meta, phi, table, model, weights, basis_0, value_0, send,
    times, z_ref, value_ref,
):
    rows = packed.shape[2]
    count = chunks * rows
    meta[0, :count] = flat(packed, 0, chunks)
    meta[0, count:] = jnp.full((DUMMY_ROWS, LANES), -1.0, F32)
    fill_padded(meta.at[1], flat(packed, 2, chunks))
    fill_padded(times, flat(packed, 1, chunks))
    used_rows(meta.at[0], chunks, rows, table)
    basis_loop(table, meta.at[0], times, state[...], phi, value_ref)
    role = Role(-1.0, table, meta, phi, z_ref, value_ref)
    own = value_ref[:count]
    write_chunks(send, 0, own)
    modelled = role.cross(own, flat(packed, 3, chunks))
    model[...] = modelled
    weights[...], z = role.weigh(modelled)
    basis_0[...] = role.gradient(z, state[...])
    own = role.forward(basis_0[...])
    value_0[...] = own
    write_chunks(send, 1, own)


def first_asc_kernel(
    chunks, got, value, meta, phi, table, state,
    model, weights, crossed_0, basis_0, basis_1, value_1, send, z_ref, value_ref,
):
    role = Role(1.0, table, meta, phi, z_ref, value_ref)
    modelled = role.cross(value[...], flat(got, 0, chunks))
    model[...] = modelled
    weights[...], z = role.weigh(modelled)
    basis_0[...] = role.gradient(z, state[...])
    own = role.forward(basis_0[...])
    write_chunks(send, 0, own)
    crossed = role.cross(own, flat(got, 1, chunks))
    crossed_0[...] = crossed
    basis_1[...] = role.image(weights[...] * crossed, basis_0[...])
    own = role.forward(basis_1[...])
    value_1[...] = own
    write_chunks(send, 1, own)


def images_kernel(
    sign, chunks, got, value_0, meta, phi, table, weights, basis_0,
    crossed_0, crossed_1, basis_1, basis_2, value_2, send, z_ref, value_ref,
):
    role = Role(sign, table, meta, phi, z_ref, value_ref)
    crossed = role.cross(value_0[...], flat(got, 0, chunks))
    crossed_0[...] = crossed
    basis_1[...] = role.image(weights[...] * crossed, basis_0[...])
    own = role.forward(basis_1[...])
    write_chunks(send, 0, own)
    crossed = role.cross(own, flat(got, 1, chunks))
    crossed_1[...] = crossed
    basis_2[...] = role.image(weights[...] * crossed, basis_1[...])
    own = role.forward(basis_2[...])
    value_2[...] = own
    write_chunks(send, 1, own)


def total(x):
    return jnp.sum(jnp.sum(x, axis=0, keepdims=True), axis=1, keepdims=True)


PAIRS = [(0, 0), (0, 1), (0, 2), (1, 1), (1, 2), (2, 2)]


def gram_kernel(
    sign, chunks, got, value_1, meta, phi, table, weights, crossed_0, basis_0, basis_1,
    other_0, other_1, other_2,
    crossed_1, crossed_2, basis_2, value_2, scalars, z_ref, value_ref,
):
    role = Role(sign, table, meta, phi, z_ref, value_ref)
    weight = weights[...]
    crossed = role.cross(value_1[...], flat(got, 0, chunks))
    crossed_1[...] = crossed
    basis_2[...] = role.image(weight * crossed, basis_1[...])
    own = role.forward(basis_2[...])
    value_2[...] = own
    last = role.cross(own, flat(got, 1, chunks))
    crossed_2[...] = last
    values = [crossed_0[...], crossed, last]
    mine = [basis_0[...], basis_1[...], basis_2[...]]
    others = [other_0[...], other_1[...], other_2[...]]
    lane = lax.broadcasted_iota(jnp.int32, (1, LANES), 1)
    line = jnp.zeros((1, LANES), F32)
    for place_in_line, (i, j) in enumerate(PAIRS):
        dots = total(mine[i] * mine[j] + others[i] * others[j])
        curve = total(weight * values[i] * values[j]) + damping * dots
        line = jnp.where(lane == place_in_line, curve, line)
        if i == 0:
            line = jnp.where(lane == len(PAIRS) + j, dots, line)
    for d in range(scalars.shape[0]):
        scalars[d] = line


def solve(scalars):
    summed = scalars[0]
    for d in range(1, scalars.shape[0]):
        summed = summed + scalars[d]
    line = summed
    lane = lax.broadcasted_iota(jnp.int32, (1, LANES), 1)

    def pick(place):
        return jnp.sum(jnp.where(lane == place, line, 0.0), axis=1, keepdims=True)

    g = {pair: pick(place) for place, pair in enumerate(PAIRS)}
    right = [pick(len(PAIRS) + i) for i in range(3)]
    s = [
        jnp.where(g[i, i] > 0.0, lax.rsqrt(jnp.maximum(g[i, i], 1e-37)), 0.0) for i in range(3)
    ]
    l10 = g[0, 1] * s[0] * s[1]
    l20 = g[0, 2] * s[0] * s[2]
    g21 = g[1, 2] * s[1] * s[2]
    c = [right[i] * s[i] for i in range(3)]

    def inverse(pivot):
        good = pivot > PIVOT_FLOOR
        return jnp.where(good, 1.0 / jnp.where(good, pivot, 1.0), 0.0)

    inv1 = inverse(1.0 - l10 * l10)
    t21 = g21 - l20 * l10
    l21 = t21 * inv1
    inv2 = inverse(1.0 - l20 * l20 - l21 * t21)
    u1 = c[1] - l10 * c[0]
    u2 = c[2] - l20 * c[0] - l21 * u1
    x2 = u2 * inv2
    x1 = u1 * inv1 - l21 * x2
    x0 = c[0] - l10 * x1 - l20 * x2
    return [x0 * s[0], x1 * s[1], x2 * s[2]]


def combine(y, parts):
    return y[0] * parts[0] + (y[1] * parts[1] + y[2] * parts[2])


def next_asc_kernel(
    chunks, scalars, meta, phi, table, model, crossed_0, crossed_1, crossed_2,
    basis_a0, basis_a1, basis_a2, basis_d0, basis_d1, basis_d2, state_a, state_d, value_2,
    new_a, new_d, shares, weights, basis_0, value_0, send, z_ref, value_ref,
):
    role = Role(1.0, table, meta, phi, z_ref, value_ref)
    write_chunks(send, 0, value_2[...])
    y = solve(scalars)
    for i in range(3):
        shares[i : i + 1] = jnp.broadcast_to(y[i], (1, LANES))
    modelled = model[...] + combine(y, [crossed_0[...], crossed_1[...], crossed_2[...]])
    new_a[...] = state_a[...] + combine(y, [basis_a0[...], basis_a1[...], basis_a2[...]])
    new_d[...] = state_d[...] + combine(y, [basis_d0[...], basis_d1[...], basis_d2[...]])
    weights[...], z = role.weigh(modelled)
    basis_0[...] = role.gradient(z, new_a[...])
    own = role.forward(basis_0[...])
    value_0[...] = own
    write_chunks(send, 1, own)


def next_desc_kernel(
    chunks, got, shares, meta, phi, table, model, crossed_0, crossed_1, value_2, state,
    weights, new_crossed_0, basis_0, basis_1, value_1, send, z_ref, value_ref,
):
    role = Role(-1.0, table, meta, phi, z_ref, value_ref)
    y = [shares[i : i + 1] for i in range(3)]
    crossed_2 = role.cross(value_2[...], flat(got, 0, chunks))
    modelled = model[...] + combine(y, [crossed_0[...], crossed_1[...], crossed_2])
    weights[...], z = role.weigh(modelled)
    basis_0[...] = role.gradient(z, state[...])
    own = role.forward(basis_0[...])
    write_chunks(send, 0, own)
    crossed = role.cross(own, flat(got, 1, chunks))
    new_crossed_0[...] = crossed
    basis_1[...] = role.image(weights[...] * crossed, basis_0[...])
    own = role.forward(basis_1[...])
    value_1[...] = own
    write_chunks(send, 1, own)


def final_kernel(scalars, state_a, basis_0, basis_1, basis_2, desc, out_a, out_d):
    y = solve(scalars)
    out_a[...] = state_a[...] + combine(y, [basis_0[...], basis_1[...], basis_2[...]])
    out_d[...] = desc[0] + combine(y, [desc[1], desc[2], desc[3]])


def body(coef_asc, coef_desc, cross_asc, cross_desc, time_asc, time_desc, height, block_fill):
    owned_asc, terms = coef_asc.shape
    owned_desc = coef_desc.shape[0]
    blocks, width = cross_asc.shape
    na = lax.axis_size("asc")
    nd = lax.axis_size("desc")
    fold = na // nd
    rows = blocks * width // na // LANES
    all_rows = na * rows
    group = STEP_ROWS * UNROLL
    steps = -(-all_rows // group) * UNROLL
    step_width = STEP_ROWS * LANES
    shape = jax.ShapeDtypeStruct

    def call(kernel, outs, scratch, *args, in_specs=None, mebibytes=16):
        return pl.pallas_call(
            kernel,
            out_shape=outs,
            in_specs=[place(x) for x in args] if in_specs is None else in_specs,
            out_specs=jax.tree.map(place, outs),
            scratch_shapes=scratch,
            compiler_params=params(mebibytes),
        )(*args)

    to_role = []
    for p in range(na):
        for q in range(nd):
            to_role.append((p * nd + q, (q * fold + p // nd) * nd + p % nd))
    to_native = [(b, a) for a, b in to_role]
    role_desc = lax.ppermute(coef_desc, ("asc", "desc"), to_role)

    slots = (cross_asc, cross_desc, time_asc, time_desc, height)
    packed = call(
        functools.partial(pack_kernel, na, nd, owned_asc, owned_desc),
        shape((nd, fold, FIELDS, rows, LANES), F32),
        [pltpu.VMEM((blocks, width), x.dtype) for x in slots]
        + [
            pltpu.VMEM((1, blocks), jnp.int32),
            pltpu.VMEM((FIELDS, blocks, width), F32),
            pltpu.SemaphoreType.DMA((len(slots) + 1,)),
        ],
        *slots, block_fill.reshape(1, blocks),
        in_specs=[pl.BlockSpec(memory_space=pltpu.HBM)] * (len(slots) + 1),
        mebibytes=60,
    )
    at_asc = lax.all_to_all(packed, "desc", split_axis=0, concat_axis=0, tiled=True)
    at_asc = at_asc.reshape(na, FIELDS, rows, LANES)

    padded = all_rows + DUMMY_ROWS
    meta_shape = shape((2, padded, LANES), F32)
    phi_shape = shape((steps, 2 * terms, step_width), BF16)
    table_shape = shape((all_rows + rows + group + 1,), jnp.int32)
    role_shapes = [meta_shape, phi_shape, table_shape]
    slot_shape = shape((all_rows, LANES), F32)
    send_shape = shape((na, 2, rows, LANES), F32)
    field_a = shape(coef_asc.shape, F32)
    field_d = shape(coef_desc.shape, F32)
    line_shape = shape((na * nd, 1, LANES), F32)
    times_scratch = pltpu.VMEM((padded, LANES), F32)
    scratch = [pltpu.VMEM((2, padded, LANES), F32), pltpu.VMEM((padded, LANES), F32)]

    def exchange(x):
        return lax.all_to_all(x, "asc", split_axis=0, concat_axis=0, tiled=True)

    def share(x):
        return lax.all_to_all(x, ("asc", "desc"), split_axis=0, concat_axis=0, tiled=True)

    *asc, value, onward = call(
        functools.partial(setup_asc_kernel, na),
        role_shapes + [slot_shape, shape((na, 4, rows, LANES), F32)],
        [times_scratch, scratch[1]],
        at_asc, coef_asc, role_desc,
    )
    *desc, model_d, weights_d, d0, own_d, send = call(
        functools.partial(setup_desc_kernel, na),
        role_shapes + [slot_shape, slot_shape, field_d, slot_shape, send_shape],
        [times_scratch] + scratch,
        exchange(onward), role_desc,
    )
    model_a, weights_a, crossed_a0, a0, a1, own_a, send = call(
        functools.partial(first_asc_kernel, na),
        [slot_shape, slot_shape, slot_shape, field_a, field_a, slot_shape, send_shape],
        scratch,
        exchange(send), value, *asc, coef_asc,
    )
    crossed_d0, crossed_d1, d1, d2, own_d, send = call(
        functools.partial(images_kernel, -1.0, na),
        [slot_shape, slot_shape, field_d, field_d, slot_shape, send_shape],
        scratch,
        exchange(send), own_d, *desc, weights_d, d0,
    )
    crossed_a1, crossed_a2, a2, own_a, scalars = call(
        functools.partial(gram_kernel, 1.0, na),
        [slot_shape, slot_shape, field_a, slot_shape, line_shape],
        scratch,
        exchange(send), own_a, *asc, weights_a, crossed_a0, a0, a1, d0, d1, d2,
    )
    state_a, state_d, shares, weights_a, a0, own_a, send = call(
        functools.partial(next_asc_kernel, na),
        [
            field_a, field_d, shape((8, LANES), F32),
            slot_shape, field_a, slot_shape, send_shape,
        ],
        scratch,
        share(scalars), *asc, model_a, crossed_a0, crossed_a1, crossed_a2,
        a0, a1, a2, d0, d1, d2, coef_asc, role_desc, own_a,
    )
    weights_d, crossed_d0, d0, d1, own_d, send = call(
        functools.partial(next_desc_kernel, na),
        [slot_shape, slot_shape, field_d, field_d, slot_shape, send_shape],
        scratch,
        exchange(send), shares, *desc, model_d, crossed_d0, crossed_d1, own_d, state_d,
    )
    _, _, a1, a2, _, send = call(
        functools.partial(images_kernel, 1.0, na),
        [slot_shape, slot_shape, field_a, field_a, slot_shape, send_shape],
        scratch,
        exchange(send), own_a, *asc, weights_a, a0,
    )
    _, _, d2, _, scalars = call(
        functools.partial(gram_kernel, -1.0, na),
        [slot_shape, slot_shape, field_d, slot_shape, line_shape],
        scratch,
        exchange(send), own_d, *desc, weights_d, crossed_d0, d0, d1, a0, a1, a2,
    )
    leaving = jnp.stack([state_d, d0, d1, d2])
    native = lax.ppermute(leaving, ("asc", "desc"), to_native)
    return tuple(
        call(
            final_kernel,
            [field_a, field_d],
            [],
            share(scalars), state_a, a0, a1, a2, native,
        )
    )


def solution(mesh):
    split_rows = P(("asc", "desc"), None)
    return jax.shard_map(
        body,
        mesh=mesh,
        in_specs=(split_rows,) * 7 + (P(("asc", "desc")),),
        out_specs=(split_rows, split_rows),
        check_vma=False,
    )
```

```python
import functools
import math

import jax
import jax.numpy as jnp
from jax import lax
from jax.experimental import pallas as pl
from jax.experimental.pallas import tpu as pltpu
from jax.sharding import PartitionSpec as P

GN_STEPS = 2
damping = 2.0
cauchy_square = 2.25

LANES = 128
STEP_ROWS = 2
UNROLL = 4
BLOCK_ROWS = STEP_ROWS * UNROLL
STEP_LANES = STEP_ROWS * LANES
DUMMY_ROWS = 8
TURN = 2
SCALE = 1.0 / 128.0
FIELDS = 5
PIVOT_FLOOR = 1e-6
F32 = jnp.float32
BF16 = jnp.bfloat16

COS_TERMS = [(-1.0) ** i * math.pi ** (2 * i) / math.factorial(2 * i) for i in range(8)]
SIN_TERMS = [(-1.0) ** i * math.pi ** (2 * i + 1) / math.factorial(2 * i + 1) for i in range(7)]


def in_smem(x):
    return x.dtype == jnp.int32 and len(x.shape) == 1


def params(mebibytes):
    return pltpu.CompilerParams(vmem_limit_bytes=mebibytes * 1024 * 1024)


def place(x):
    return pl.BlockSpec(memory_space=pltpu.SMEM if in_smem(x) else pltpu.VMEM)


def split(x):
    high = x.astype(BF16)
    low = (x - high.astype(F32)).astype(BF16)
    return high, low


def flat(ref, field, chunks):
    return jnp.concatenate([ref[j, field] for j in range(chunks)], axis=0)


def local_id(ids, owned):
    if owned & (owned - 1) == 0:
        return ids & (owned - 1)
    return lax.rem(ids, owned)


def pack_kernel(
    na, nd, owned_asc, owned_desc, ca_in, cd_in, ta_in, td_in, height_in, fill_in, out,
    ca, cd, ta, td, height, fill, turned, sems,
):
    copies = [
        pltpu.make_async_copy(source, target, sems.at[i])
        for i, (source, target) in enumerate(
            [
                (fill_in, fill), (ca_in, ca), (ta_in, ta),
                (cd_in, cd), (td_in, td), (height_in, height),
            ]
        )
    ]
    for copy in copies:
        copy.start()
    for copy in copies:
        copy.wait()
    blocks, width = ca.shape
    group = width // na
    rows = blocks // na
    fill_row = fill[...]
    row_id = lax.broadcasted_iota(jnp.int32, (blocks, blocks), 0)
    col_id = lax.broadcasted_iota(jnp.int32, (blocks, blocks), 1)
    fill_col = jnp.sum(
        jnp.where(row_id == col_id, fill_row, 0).astype(F32), axis=1, keepdims=True
    )
    lane = lax.broadcasted_iota(jnp.int32, (blocks, width), 1)
    live = lane.astype(F32) < fill_col
    fields = [
        jnp.where(live, local_id(ca[...], owned_asc).astype(F32), -1.0),
        ta[...],
        jnp.where(live, local_id(cd[...], owned_desc).astype(F32), -1.0),
        td[...],
        height[...],
    ]
    source = lax.broadcasted_iota(jnp.int32, (width, width), 0)
    target = lax.broadcasted_iota(jnp.int32, (width, width), 1)
    owner = target // group
    place = target - owner * group
    order = (source == place * na + owner).astype(F32).astype(BF16)
    for f, x in enumerate(fields):
        high = x.astype(BF16)
        rest = x - high.astype(F32)
        middle = rest.astype(BF16)
        low = (rest - middle.astype(F32)).astype(BF16)
        turned[f] = (
            jnp.dot(high, order, preferred_element_type=F32)
            + jnp.dot(middle, order, preferred_element_type=F32)
        ) + jnp.dot(low, order, preferred_element_type=F32)
    lane_group = lax.broadcasted_iota(jnp.int32, (rows, width), 1) // group
    for f in range(FIELDS):
        parts = [None] * na
        for k in range(na):
            piece = turned[f, pl.ds(k, rows, stride=na), :]
            for r in range(na):
                amount = ((k - r) * group) % width
                moved = pltpu.roll(piece, amount, 1) if amount else piece
                parts[r] = moved if k == 0 else jnp.where(lane_group == k, moved, parts[r])
        for r in range(na):
            out[r % nd, r // nd, f] = parts[r]


def cos_sin_pi(x):
    turns = jnp.floor(x + 0.5)
    f = x - turns
    sign = 1.0 - 2.0 * (turns - 2.0 * jnp.floor(turns * 0.5))
    u = f * f
    c = COS_TERMS[-1]
    for term in COS_TERMS[-2::-1]:
        c = c * u + term
    s = SIN_TERMS[-1]
    for term in SIN_TERMS[-2::-1]:
        s = s * u + term
    return c * sign, s * (f * sign)


def rows_pair(ref, rows):
    return jnp.concatenate([ref[pl.ds(r, 1), :] for r in rows], axis=1)


def used_rows(ids_ref, chunks, rows, table):
    count = jnp.int32(0)
    level = lax.broadcasted_iota(jnp.int32, (rows, LANES), 0).astype(F32) + 1.0
    for j in range(chunks):
        ids = ids_ref[j * rows : (j + 1) * rows, :]
        used = jnp.max(jnp.where(ids >= 0.0, level, 0.0)).astype(jnp.int32)
        for i in range(rows):
            table[count + i] = j * rows + i
        count = count + used
    for i in range(BLOCK_ROWS):
        table[count + i] = chunks * rows
    table[table.shape[0] - 1] = lax.div(count + (BLOCK_ROWS - 1), BLOCK_ROWS)


def listed_rows(table, first, count):
    return [table[first + i] for i in range(count)]


def over_blocks(table, step, carry):
    blocks = table[table.shape[0] - 1]
    turns = lax.div(blocks, TURN)

    def turn(i, carry):
        for u in range(TURN):
            carry = step(i * TURN + u, carry)
        return carry

    carry = lax.fori_loop(0, turns, turn, carry)
    return lax.fori_loop(turns * TURN, blocks, step, carry)


def stacked(field):
    high, low = split(field)
    top = jnp.concatenate([high, high], axis=1)
    bottom = jnp.concatenate([low, jnp.zeros_like(low)], axis=1)
    return jnp.concatenate([top, bottom], axis=0)


def forward_step(stack, phi, ids_row, row_iota, owned):
    both = jnp.dot(stack, phi, preferred_element_type=F32)
    value = both[:owned] + both[owned:]
    return jnp.sum(jnp.where(row_iota == ids_row, value, 0.0), axis=0, keepdims=True)


def store_rows(ref, rows, value):
    for i, r in enumerate(rows):
        ref[pl.ds(r, 1), :] = value[:, i * LANES : (i + 1) * LANES]


def basis_loop(table, ids_ref, time_ref, coef, phi_ref, value_ref):
    owned, terms = coef.shape
    half = terms // 2
    value_ref[...] = jnp.zeros(value_ref.shape, F32)
    width = STEP_LANES
    stack = stacked(coef)
    row_iota = lax.broadcasted_iota(jnp.int32, (owned, width), 0).astype(F32)
    fine = (lax.broadcasted_iota(jnp.int32, (8, width), 0) + 1).astype(F32)
    coarse = (lax.broadcasted_iota(jnp.int32, (half // 8, width), 0) * 8).astype(F32)

    def step(block, u):
        rows = listed_rows(table, block * BLOCK_ROWS + u * STEP_ROWS, STEP_ROWS)
        times = rows_pair(time_ref, rows)
        cos_fine, sin_fine = cos_sin_pi(fine * times)
        cos_coarse, sin_coarse = cos_sin_pi(coarse * times)
        cos_parts, sin_parts = [], []
        for j in range(half // 8):
            cj = cos_coarse[j : j + 1]
            sj = sin_coarse[j : j + 1]
            cos_parts.append(cj * cos_fine - sj * sin_fine)
            sin_parts.append(sj * cos_fine + cj * sin_fine)
        high, low = split(jnp.concatenate(cos_parts + sin_parts, axis=0))
        phi = jnp.concatenate([high, low], axis=0)
        phi_ref[block, :, u * width : (u + 1) * width] = phi
        value = forward_step(stack, phi, rows_pair(ids_ref, rows), row_iota, owned)
        store_rows(value_ref, rows, value)

    def whole_block(block, carry):
        for u in range(UNROLL):
            step(block, u)
        return carry

    lax.fori_loop(0, table[table.shape[0] - 1], whole_block, 0)


class Role:
    def __init__(self, sign, table, meta, phi, z_ref, value_ref):
        self.sign = sign
        self.table = table
        self.ids = meta.at[0]
        self.meta = meta
        self.phi = phi
        self.z_ref = z_ref
        self.value_ref = value_ref
        self.count = meta.shape[1] - DUMMY_ROWS

    def cross(self, mine, other):
        return mine - other if self.sign > 0 else other - mine

    def backward(self, z, owned):
        high = z.astype(BF16).astype(F32)
        self.z_ref[0, : self.count] = high
        self.z_ref[1, : self.count] = z - high
        self.z_ref[:, self.count :] = jnp.zeros((2, DUMMY_ROWS, LANES), F32)
        blocks, double, width = self.phi.shape
        terms = double // 2
        row_iota = lax.broadcasted_iota(jnp.int32, (owned, width), 0).astype(F32)

        def gather(block, carry):
            rows = listed_rows(self.table, block * BLOCK_ROWS, BLOCK_ROWS)
            hit = row_iota == rows_pair(self.ids, rows)
            parts = [
                jnp.where(hit, rows_pair(self.z_ref.at[k], rows), 0.0).astype(BF16)
                for k in range(2)
            ]
            return carry + lax.dot_general(
                jnp.concatenate(parts, axis=0),
                self.phi[block],
                (((1,), (1,)), ((), ())),
                preferred_element_type=F32,
            )

        g = over_blocks(self.table, gather, jnp.zeros((2 * owned, double), F32))
        return self.sign * (g[:owned, :terms] + (g[:owned, terms:] + g[owned:, :terms]))

    def forward(self, field):
        owned = field.shape[0]
        stack = stacked(field)
        row_iota = lax.broadcasted_iota(jnp.int32, (owned, STEP_LANES), 0).astype(F32)
        self.value_ref[...] = jnp.zeros(self.value_ref.shape, F32)

        def ahead(block, carry):
            for u in range(UNROLL):
                rows = listed_rows(self.table, block * BLOCK_ROWS + u * STEP_ROWS, STEP_ROWS)
                phi = self.phi[block, :, u * STEP_LANES : (u + 1) * STEP_LANES]
                value = forward_step(stack, phi, rows_pair(self.ids, rows), row_iota, owned)
                store_rows(self.value_ref, rows, value)
            return carry

        over_blocks(self.table, ahead, 0)
        return self.value_ref[: self.count]

    def weigh(self, model):
        live = self.meta[0, : self.count] >= 0.0
        misfit = jnp.where(live, self.meta[1, : self.count] - model, 0.0)
        weight = jnp.where(live, 1.0 / (1.0 + misfit * misfit / cauchy_square), 0.0)
        return weight, weight * misfit

    def gradient(self, z, state):
        return self.backward(z, state.shape[0]) - damping * state

    def image(self, z, before):
        return SCALE * (self.backward(z, before.shape[0]) + damping * before)


def write_chunks(send, first, values):
    chunks, rows = send.shape[0], send.shape[2]
    for j in range(chunks):
        send[j, first] = values[j * rows : (j + 1) * rows, :]


def fill_padded(ref, values):
    count = values.shape[0]
    ref[:count] = values
    ref[count:] = jnp.zeros((ref.shape[0] - count,) + values.shape[1:], F32)


def setup_asc_kernel(
    chunks, packed, coef, role_desc, meta, phi, table, state, value, onward, times, value_ref
):
    state[...] = coef[...]
    rows = packed.shape[2]
    count = chunks * rows
    meta[0, :count] = flat(packed, 0, chunks)
    meta[0, count:] = jnp.full((DUMMY_ROWS, LANES), -1.0, F32)
    fill_padded(meta.at[1], flat(packed, 4, chunks))
    fill_padded(times, flat(packed, 1, chunks))
    used_rows(meta.at[0], chunks, rows, table)
    basis_loop(table, meta.at[0], times, coef[...], phi, value_ref)
    value[...] = value_ref[:count]
    for j in range(chunks):
        onward[j, 0] = packed[j, 2]
        onward[j, 1] = packed[j, 3]
        onward[j, 2] = packed[j, 4]
    write_chunks(onward, 3, value_ref[:count])


def setup_desc_kernel(
    chunks, packed, state, meta, phi, table, model, weights, basis_0, value_0, send,
    times, z_ref, value_ref,
):
    rows = packed.shape[2]
    count = chunks * rows
    meta[0, :count] = flat(packed, 0, chunks)
    meta[0, count:] = jnp.full((DUMMY_ROWS, LANES), -1.0, F32)
    fill_padded(meta.at[1], flat(packed, 2, chunks))
    fill_padded(times, flat(packed, 1, chunks))
    used_rows(meta.at[0], chunks, rows, table)
    basis_loop(table, meta.at[0], times, state[...], phi, value_ref)
    role = Role(-1.0, table, meta, phi, z_ref, value_ref)
    own = value_ref[:count]
    write_chunks(send, 0, own)
    modelled = role.cross(own, flat(packed, 3, chunks))
    model[...] = modelled
    weights[...], z = role.weigh(modelled)
    basis_0[...] = role.gradient(z, state[...])
    own = role.forward(basis_0[...])
    value_0[...] = own
    write_chunks(send, 1, own)


def first_asc_kernel(
    chunks, got, value, meta, phi, table, state,
    model, weights, crossed_0, basis_0, basis_1, value_1, send, z_ref, value_ref,
):
    role = Role(1.0, table, meta, phi, z_ref, value_ref)
    modelled = role.cross(value[...], flat(got, 0, chunks))
    model[...] = modelled
    weights[...], z = role.weigh(modelled)
    basis_0[...] = role.gradient(z, state[...])
    own = role.forward(basis_0[...])
    write_chunks(send, 0, own)
    crossed = role.cross(own, flat(got, 1, chunks))
    crossed_0[...] = crossed
    basis_1[...] = role.image(weights[...] * crossed, basis_0[...])
    own = role.forward(basis_1[...])
    value_1[...] = own
    write_chunks(send, 1, own)


def images_kernel(
    sign, chunks, got, value_0, meta, phi, table, weights, basis_0,
    crossed_0, crossed_1, basis_1, basis_2, value_2, send, z_ref, value_ref,
):
    role = Role(sign, table, meta, phi, z_ref, value_ref)
    crossed = role.cross(value_0[...], flat(got, 0, chunks))
    crossed_0[...] = crossed
    basis_1[...] = role.image(weights[...] * crossed, basis_0[...])
    own = role.forward(basis_1[...])
    write_chunks(send, 0, own)
    crossed = role.cross(own, flat(got, 1, chunks))
    crossed_1[...] = crossed
    basis_2[...] = role.image(weights[...] * crossed, basis_1[...])
    own = role.forward(basis_2[...])
    value_2[...] = own
    write_chunks(send, 1, own)


def total(x):
    return jnp.sum(jnp.sum(x, axis=0, keepdims=True), axis=1, keepdims=True)


PAIRS = [(0, 0), (0, 1), (0, 2), (1, 1), (1, 2), (2, 2)]


def gram_kernel(
    sign, chunks, got, value_1, meta, phi, table, weights, crossed_0, basis_0, basis_1,
    other_0, other_1, other_2,
    crossed_1, crossed_2, basis_2, value_2, scalars, z_ref, value_ref,
):
    role = Role(sign, table, meta, phi, z_ref, value_ref)
    weight = weights[...]
    crossed = role.cross(value_1[...], flat(got, 0, chunks))
    crossed_1[...] = crossed
    basis_2[...] = role.image(weight * crossed, basis_1[...])
    own = role.forward(basis_2[...])
    value_2[...] = own
    last = role.cross(own, flat(got, 1, chunks))
    crossed_2[...] = last
    values = [crossed_0[...], crossed, last]
    mine = [basis_0[...], basis_1[...], basis_2[...]]
    others = [other_0[...], other_1[...], other_2[...]]
    lane = lax.broadcasted_iota(jnp.int32, (1, LANES), 1)
    line = jnp.zeros((1, LANES), F32)
    for place_in_line, (i, j) in enumerate(PAIRS):
        dots = total(mine[i] * mine[j] + others[i] * others[j])
        curve = total(weight * values[i] * values[j]) + damping * dots
        line = jnp.where(lane == place_in_line, curve, line)
        if i == 0:
            line = jnp.where(lane == len(PAIRS) + j, dots, line)
    for d in range(scalars.shape[0]):
        scalars[d] = line


def solve(scalars):
    summed = scalars[0]
    for d in range(1, scalars.shape[0]):
        summed = summed + scalars[d]
    line = summed
    lane = lax.broadcasted_iota(jnp.int32, (1, LANES), 1)

    def pick(place):
        return jnp.sum(jnp.where(lane == place, line, 0.0), axis=1, keepdims=True)

    g = {pair: pick(place) for place, pair in enumerate(PAIRS)}
    right = [pick(len(PAIRS) + i) for i in range(3)]
    s = [
        jnp.where(g[i, i] > 0.0, lax.rsqrt(jnp.maximum(g[i, i], 1e-37)), 0.0) for i in range(3)
    ]
    l10 = g[0, 1] * s[0] * s[1]
    l20 = g[0, 2] * s[0] * s[2]
    g21 = g[1, 2] * s[1] * s[2]
    c = [right[i] * s[i] for i in range(3)]

    def inverse(pivot):
        good = pivot > PIVOT_FLOOR
        return jnp.where(good, 1.0 / jnp.where(good, pivot, 1.0), 0.0)

    inv1 = inverse(1.0 - l10 * l10)
    t21 = g21 - l20 * l10
    l21 = t21 * inv1
    inv2 = inverse(1.0 - l20 * l20 - l21 * t21)
    u1 = c[1] - l10 * c[0]
    u2 = c[2] - l20 * c[0] - l21 * u1
    x2 = u2 * inv2
    x1 = u1 * inv1 - l21 * x2
    x0 = c[0] - l10 * x1 - l20 * x2
    return [x0 * s[0], x1 * s[1], x2 * s[2]]


def combine(y, parts):
    return y[0] * parts[0] + (y[1] * parts[1] + y[2] * parts[2])


def next_asc_kernel(
    chunks, scalars, meta, phi, table, model, crossed_0, crossed_1, crossed_2,
    basis_a0, basis_a1, basis_a2, basis_d0, basis_d1, basis_d2, state_a, state_d, value_2,
    new_a, new_d, shares, weights, basis_0, value_0, send, z_ref, value_ref,
):
    role = Role(1.0, table, meta, phi, z_ref, value_ref)
    write_chunks(send, 0, value_2[...])
    y = solve(scalars)
    for i in range(3):
        shares[i : i + 1] = jnp.broadcast_to(y[i], (1, LANES))
    modelled = model[...] + combine(y, [crossed_0[...], crossed_1[...], crossed_2[...]])
    new_a[...] = state_a[...] + combine(y, [basis_a0[...], basis_a1[...], basis_a2[...]])
    new_d[...] = state_d[...] + combine(y, [basis_d0[...], basis_d1[...], basis_d2[...]])
    weights[...], z = role.weigh(modelled)
    basis_0[...] = role.gradient(z, new_a[...])
    own = role.forward(basis_0[...])
    value_0[...] = own
    write_chunks(send, 1, own)


def next_desc_kernel(
    chunks, got, shares, meta, phi, table, model, crossed_0, crossed_1, value_2, state,
    weights, new_crossed_0, basis_0, basis_1, value_1, send, z_ref, value_ref,
):
    role = Role(-1.0, table, meta, phi, z_ref, value_ref)
    y = [shares[i : i + 1] for i in range(3)]
    crossed_2 = role.cross(value_2[...], flat(got, 0, chunks))
    modelled = model[...] + combine(y, [crossed_0[...], crossed_1[...], crossed_2])
    weights[...], z = role.weigh(modelled)
    basis_0[...] = role.gradient(z, state[...])
    own = role.forward(basis_0[...])
    write_chunks(send, 0, own)
    crossed = role.cross(own, flat(got, 1, chunks))
    new_crossed_0[...] = crossed
    basis_1[...] = role.image(weights[...] * crossed, basis_0[...])
    own = role.forward(basis_1[...])
    value_1[...] = own
    write_chunks(send, 1, own)


def final_kernel(scalars, state_a, basis_0, basis_1, basis_2, desc, out_a, out_d):
    y = solve(scalars)
    out_a[...] = state_a[...] + combine(y, [basis_0[...], basis_1[...], basis_2[...]])
    out_d[...] = desc[0] + combine(y, [desc[1], desc[2], desc[3]])


def body(coef_asc, coef_desc, cross_asc, cross_desc, time_asc, time_desc, height, block_fill):
    owned_asc, terms = coef_asc.shape
    owned_desc = coef_desc.shape[0]
    blocks, width = cross_asc.shape
    na = lax.axis_size("asc")
    nd = lax.axis_size("desc")
    fold = na // nd
    rows = blocks * width // na // LANES
    all_rows = na * rows
    all_blocks = -(-all_rows // BLOCK_ROWS)
    shape = jax.ShapeDtypeStruct

    def call(kernel, outs, scratch, *args, in_specs=None, mebibytes=16):
        return pl.pallas_call(
            kernel,
            out_shape=outs,
            in_specs=[place(x) for x in args] if in_specs is None else in_specs,
            out_specs=jax.tree.map(place, outs),
            scratch_shapes=scratch,
            compiler_params=params(mebibytes),
        )(*args)

    to_role = []
    for p in range(na):
        for q in range(nd):
            to_role.append((p * nd + q, (q * fold + p // nd) * nd + p % nd))
    to_native = [(b, a) for a, b in to_role]
    role_desc = lax.ppermute(coef_desc, ("asc", "desc"), to_role)

    slots = (cross_asc, cross_desc, time_asc, time_desc, height)
    packed = call(
        functools.partial(pack_kernel, na, nd, owned_asc, owned_desc),
        shape((nd, fold, FIELDS, rows, LANES), F32),
        [pltpu.VMEM((blocks, width), x.dtype) for x in slots]
        + [
            pltpu.VMEM((1, blocks), jnp.int32),
            pltpu.VMEM((FIELDS, blocks, width), F32),
            pltpu.SemaphoreType.DMA((len(slots) + 1,)),
        ],
        *slots, block_fill.reshape(1, blocks),
        in_specs=[pl.BlockSpec(memory_space=pltpu.HBM)] * (len(slots) + 1),
        mebibytes=60,
    )
    at_asc = lax.all_to_all(packed, "desc", split_axis=0, concat_axis=0, tiled=True)
    at_asc = at_asc.reshape(na, FIELDS, rows, LANES)

    padded = all_rows + DUMMY_ROWS
    meta_shape = shape((2, padded, LANES), F32)
    phi_shape = shape((all_blocks, 2 * terms, BLOCK_ROWS * LANES), BF16)
    table_shape = shape((all_rows + rows + BLOCK_ROWS + 1,), jnp.int32)
    role_shapes = [meta_shape, phi_shape, table_shape]
    slot_shape = shape((all_rows, LANES), F32)
    send_shape = shape((na, 2, rows, LANES), F32)
    field_a = shape(coef_asc.shape, F32)
    field_d = shape(coef_desc.shape, F32)
    line_shape = shape((na * nd, 1, LANES), F32)
    times_scratch = pltpu.VMEM((padded, LANES), F32)
    scratch = [pltpu.VMEM((2, padded, LANES), F32), pltpu.VMEM((padded, LANES), F32)]

    def exchange(x):
        return lax.all_to_all(x, "asc", split_axis=0, concat_axis=0, tiled=True)

    def share(x):
        return lax.all_to_all(x, ("asc", "desc"), split_axis=0, concat_axis=0, tiled=True)

    *asc, state_a, value, onward = call(
        functools.partial(setup_asc_kernel, na),
        role_shapes + [field_a, slot_shape, shape((na, 4, rows, LANES), F32)],
        [times_scratch, scratch[1]],
        at_asc, coef_asc, role_desc,
    )
    *desc, model_d, weights_d, d0, own_d, send = call(
        functools.partial(setup_desc_kernel, na),
        role_shapes + [slot_shape, slot_shape, field_d, slot_shape, send_shape],
        [times_scratch] + scratch,
        exchange(onward), role_desc,
    )
    model_a, weights_a, crossed_a0, a0, a1, own_a, send = call(
        functools.partial(first_asc_kernel, na),
        [slot_shape, slot_shape, slot_shape, field_a, field_a, slot_shape, send_shape],
        scratch,
        exchange(send), value, *asc, state_a,
    )
    crossed_d0, crossed_d1, d1, d2, own_d, send = call(
        functools.partial(images_kernel, -1.0, na),
        [slot_shape, slot_shape, field_d, field_d, slot_shape, send_shape],
        scratch,
        exchange(send), own_d, *desc, weights_d, d0,
    )
    crossed_a1, crossed_a2, a2, own_a, scalars = call(
        functools.partial(gram_kernel, 1.0, na),
        [slot_shape, slot_shape, field_a, slot_shape, line_shape],
        scratch,
        exchange(send), own_a, *asc, weights_a, crossed_a0, a0, a1, d0, d1, d2,
    )
    state_a, state_d, shares, weights_a, a0, own_a, send = call(
        functools.partial(next_asc_kernel, na),
        [
            field_a, field_d, shape((8, LANES), F32),
            slot_shape, field_a, slot_shape, send_shape,
        ],
        scratch,
        share(scalars), *asc, model_a, crossed_a0, crossed_a1, crossed_a2,
        a0, a1, a2, d0, d1, d2, state_a, role_desc, own_a,
    )
    weights_d, crossed_d0, d0, d1, own_d, send = call(
        functools.partial(next_desc_kernel, na),
        [slot_shape, slot_shape, field_d, field_d, slot_shape, send_shape],
        scratch,
        exchange(send), shares, *desc, model_d, crossed_d0, crossed_d1, own_d, state_d,
    )
    _, _, a1, a2, _, send = call(
        functools.partial(images_kernel, 1.0, na),
        [slot_shape, slot_shape, field_a, field_a, slot_shape, send_shape],
        scratch,
        exchange(send), own_a, *asc, weights_a, a0,
    )
    _, _, d2, _, scalars = call(
        functools.partial(gram_kernel, -1.0, na),
        [slot_shape, slot_shape, field_d, slot_shape, line_shape],
        scratch,
        exchange(send), own_d, *desc, weights_d, crossed_d0, d0, d1, a0, a1, a2,
    )
    leaving = jnp.stack([state_d, d0, d1, d2])
    native = lax.ppermute(leaving, ("asc", "desc"), to_native)
    return tuple(
        call(
            final_kernel,
            [field_a, field_d],
            [],
            share(scalars), state_a, a0, a1, a2, native,
        )
    )


def solution(mesh):
    split_rows = P(("asc", "desc"), None)
    return jax.shard_map(
        body,
        mesh=mesh,
        in_specs=(split_rows,) * 7 + (P(("asc", "desc")),),
        out_specs=(split_rows, split_rows),
        check_vma=False,
    )
```

```python
import functools
import math

import jax
import jax.numpy as jnp
from jax import lax
from jax.experimental import pallas as pl
from jax.experimental.pallas import tpu as pltpu
from jax.sharding import PartitionSpec as P

GN_STEPS = 2
damping = 2.0
cauchy_square = 2.25

LANES = 128
STEP_ROWS = 2
UNROLL = 4
BLOCK_ROWS = STEP_ROWS * UNROLL
STEP_LANES = STEP_ROWS * LANES
DUMMY_ROWS = 8
TURNS = (4, 2, 1)
SCALE = 1.0 / 128.0
FIELDS = 5
PIVOT_FLOOR = 1e-6
F32 = jnp.float32
BF16 = jnp.bfloat16

COS_TERMS = [(-1.0) ** i * math.pi ** (2 * i) / math.factorial(2 * i) for i in range(8)]
SIN_TERMS = [(-1.0) ** i * math.pi ** (2 * i + 1) / math.factorial(2 * i + 1) for i in range(7)]


def in_smem(x):
    return x.dtype == jnp.int32 and len(x.shape) == 1


def params(mebibytes):
    return pltpu.CompilerParams(vmem_limit_bytes=mebibytes * 1024 * 1024)


def place(x):
    return pl.BlockSpec(memory_space=pltpu.SMEM if in_smem(x) else pltpu.VMEM)


def split(x):
    high = x.astype(BF16)
    low = (x - high.astype(F32)).astype(BF16)
    return high, low


def flat_first(ref, field, fold, rows):
    parts = []
    for j in range(ref.shape[0] * fold):
        start = (j % fold * FIELDS + field) * rows
        parts.append(ref[j // fold, start : start + rows])
    return jnp.concatenate(parts, axis=0)


def flat_second(ref, field, rows):
    start = field * rows
    return jnp.concatenate([ref[j, start : start + rows] for j in range(ref.shape[0])], axis=0)


def flat(ref, field, chunks):
    return jnp.concatenate([ref[j, field] for j in range(chunks)], axis=0)


def local_id(ids, owned):
    if owned & (owned - 1) == 0:
        return ids & (owned - 1)
    return lax.rem(ids, owned)


def pack_kernel(
    na, nd, owned_asc, coef_in, ca_in, cd_in, ta_in, td_in, height_in, fill_in, out,
    coef, ca, cd, ta, td, height, fill, turned, sems,
):
    copies = [
        pltpu.make_async_copy(source, target, sems.at[i])
        for i, (source, target) in enumerate(
            [
                (fill_in, fill), (ca_in, ca), (ta_in, ta),
                (cd_in, cd), (td_in, td), (height_in, height), (coef_in, coef),
            ]
        )
    ]
    for copy in copies:
        copy.start()
    for copy in copies:
        copy.wait()
    owned_desc = coef.shape[0]
    blocks, width = ca.shape
    group = width // na
    rows = blocks // na
    fill_row = fill[...]
    row_id = lax.broadcasted_iota(jnp.int32, (blocks, blocks), 0)
    col_id = lax.broadcasted_iota(jnp.int32, (blocks, blocks), 1)
    fill_col = jnp.sum(
        jnp.where(row_id == col_id, fill_row, 0).astype(F32), axis=1, keepdims=True
    )
    lane = lax.broadcasted_iota(jnp.int32, (blocks, width), 1)
    live = lane.astype(F32) < fill_col
    fields = [
        jnp.where(live, local_id(ca[...], owned_asc).astype(F32), -1.0),
        ta[...],
        jnp.where(live, local_id(cd[...], owned_desc).astype(F32), -1.0),
        td[...],
        height[...],
    ]
    source = lax.broadcasted_iota(jnp.int32, (width, width), 0)
    target = lax.broadcasted_iota(jnp.int32, (width, width), 1)
    owner = target // group
    place = target - owner * group
    order = (source == place * na + owner).astype(F32).astype(BF16)
    for f, x in enumerate(fields):
        high = x.astype(BF16)
        rest = x - high.astype(F32)
        middle = rest.astype(BF16)
        low = (rest - middle.astype(F32)).astype(BF16)
        turned[f] = (
            jnp.dot(high, order, preferred_element_type=F32)
            + jnp.dot(middle, order, preferred_element_type=F32)
        ) + jnp.dot(low, order, preferred_element_type=F32)
    lane_group = lax.broadcasted_iota(jnp.int32, (rows, width), 1) // group
    for f in range(FIELDS):
        parts = [None] * na
        for k in range(na):
            piece = turned[f, pl.ds(k, rows, stride=na), :]
            for r in range(na):
                amount = ((k - r) * group) % width
                moved = pltpu.roll(piece, amount, 1) if amount else piece
                parts[r] = moved if k == 0 else jnp.where(lane_group == k, moved, parts[r])
        for r in range(na):
            start = (r // nd * FIELDS + f) * rows
            out[r % nd, start : start + rows] = parts[r]
    for q in range(nd):
        out[q, out.shape[1] - owned_desc :] = coef[...]


def cos_sin_pi(x):
    turns = jnp.floor(x + 0.5)
    f = x - turns
    sign = 1.0 - 2.0 * (turns - 2.0 * jnp.floor(turns * 0.5))
    u = f * f
    c = COS_TERMS[-1]
    for term in COS_TERMS[-2::-1]:
        c = c * u + term
    s = SIN_TERMS[-1]
    for term in SIN_TERMS[-2::-1]:
        s = s * u + term
    return c * sign, s * (f * sign)


def rows_pair(ref, rows):
    return jnp.concatenate([ref[pl.ds(r, 1), :] for r in rows], axis=1)


def used_rows(ids_ref, chunks, rows, table):
    count = jnp.int32(0)
    level = lax.broadcasted_iota(jnp.int32, (rows, LANES), 0).astype(F32) + 1.0
    for j in range(chunks):
        ids = ids_ref[j * rows : (j + 1) * rows, :]
        used = jnp.max(jnp.where(ids >= 0.0, level, 0.0)).astype(jnp.int32)
        for i in range(rows):
            table[count + i] = j * rows + i
        count = count + used
    for i in range(BLOCK_ROWS):
        table[count + i] = chunks * rows
    table[table.shape[0] - 1] = lax.div(count + (BLOCK_ROWS - 1), BLOCK_ROWS)


def listed_rows(table, first, count):
    return [table[first + i] for i in range(count)]


def over_blocks(table, step, carry):
    blocks = table[table.shape[0] - 1]
    done = jnp.int32(0)
    for size in TURNS:
        turns = lax.div(blocks - done, size)

        def turn(i, carry, done=done, size=size):
            for u in range(size):
                carry = step(done + i * size + u, carry)
            return carry

        carry = lax.fori_loop(0, turns, turn, carry)
        done = done + turns * size
    return carry


def stacked(field):
    high, low = split(field)
    top = jnp.concatenate([high, high], axis=1)
    bottom = jnp.concatenate([low, jnp.zeros_like(low)], axis=1)
    return jnp.concatenate([top, bottom], axis=0)


def forward_step(stack, phi, ids_row, row_iota, owned):
    both = jnp.dot(stack, phi, preferred_element_type=F32)
    value = both[:owned] + both[owned:]
    return jnp.sum(jnp.where(row_iota == ids_row, value, 0.0), axis=0, keepdims=True)


def store_rows(ref, rows, value):
    for i, r in enumerate(rows):
        ref[pl.ds(r, 1), :] = value[:, i * LANES : (i + 1) * LANES]


def basis_loop(table, ids_ref, time_ref, coef, phi_ref, value_ref):
    owned, terms = coef.shape
    half = terms // 2
    value_ref[...] = jnp.zeros(value_ref.shape, F32)
    width = STEP_LANES
    stack = stacked(coef)
    row_iota = lax.broadcasted_iota(jnp.int32, (owned, width), 0).astype(F32)
    fine = (lax.broadcasted_iota(jnp.int32, (8, width), 0) + 1).astype(F32)
    coarse = (lax.broadcasted_iota(jnp.int32, (half // 8, width), 0) * 8).astype(F32)

    def step(block, u):
        rows = listed_rows(table, block * BLOCK_ROWS + u * STEP_ROWS, STEP_ROWS)
        times = rows_pair(time_ref, rows)
        cos_fine, sin_fine = cos_sin_pi(fine * times)
        cos_coarse, sin_coarse = cos_sin_pi(coarse * times)
        cos_parts, sin_parts = [], []
        for j in range(half // 8):
            cj = cos_coarse[j : j + 1]
            sj = sin_coarse[j : j + 1]
            cos_parts.append(cj * cos_fine - sj * sin_fine)
            sin_parts.append(sj * cos_fine + cj * sin_fine)
        high, low = split(jnp.concatenate(cos_parts + sin_parts, axis=0))
        phi = jnp.concatenate([high, low], axis=0)
        phi_ref[block, :, u * width : (u + 1) * width] = phi
        value = forward_step(stack, phi, rows_pair(ids_ref, rows), row_iota, owned)
        store_rows(value_ref, rows, value)

    def whole_block(block, carry):
        for u in range(UNROLL):
            step(block, u)
        return carry

    lax.fori_loop(0, table[table.shape[0] - 1], whole_block, 0)


class Role:
    def __init__(self, sign, table, meta, phi, z_ref, value_ref):
        self.sign = sign
        self.table = table
        self.ids = meta.at[0]
        self.meta = meta
        self.phi = phi
        self.z_ref = z_ref
        self.value_ref = value_ref
        self.count = meta.shape[1] - DUMMY_ROWS

    def cross(self, mine, other):
        return mine - other if self.sign > 0 else other - mine

    def backward(self, z, owned):
        high = z.astype(BF16).astype(F32)
        self.z_ref[0, : self.count] = high
        self.z_ref[1, : self.count] = z - high
        self.z_ref[:, self.count :] = jnp.zeros((2, DUMMY_ROWS, LANES), F32)
        blocks, double, width = self.phi.shape
        terms = double // 2
        row_iota = lax.broadcasted_iota(jnp.int32, (owned, width), 0).astype(F32)

        def gather(block, carry):
            rows = listed_rows(self.table, block * BLOCK_ROWS, BLOCK_ROWS)
            hit = row_iota == rows_pair(self.ids, rows)
            parts = [
                jnp.where(hit, rows_pair(self.z_ref.at[k], rows), 0.0).astype(BF16)
                for k in range(2)
            ]
            return carry + lax.dot_general(
                jnp.concatenate(parts, axis=0),
                self.phi[block],
                (((1,), (1,)), ((), ())),
                preferred_element_type=F32,
            )

        g = over_blocks(self.table, gather, jnp.zeros((2 * owned, double), F32))
        return self.sign * (g[:owned, :terms] + (g[:owned, terms:] + g[owned:, :terms]))

    def forward(self, field):
        owned = field.shape[0]
        stack = stacked(field)
        row_iota = lax.broadcasted_iota(jnp.int32, (owned, STEP_LANES), 0).astype(F32)
        self.value_ref[...] = jnp.zeros(self.value_ref.shape, F32)

        def ahead(block, carry):
            for u in range(UNROLL):
                rows = listed_rows(self.table, block * BLOCK_ROWS + u * STEP_ROWS, STEP_ROWS)
                phi = self.phi[block, :, u * STEP_LANES : (u + 1) * STEP_LANES]
                value = forward_step(stack, phi, rows_pair(self.ids, rows), row_iota, owned)
                store_rows(self.value_ref, rows, value)
            return carry

        over_blocks(self.table, ahead, 0)
        return self.value_ref[: self.count]

    def weigh(self, model):
        live = self.meta[0, : self.count] >= 0.0
        misfit = jnp.where(live, self.meta[1, : self.count] - model, 0.0)
        weight = jnp.where(live, 1.0 / (1.0 + misfit * misfit / cauchy_square), 0.0)
        return weight, weight * misfit

    def gradient(self, z, state):
        return self.backward(z, state.shape[0]) - damping * state

    def image(self, z, before):
        return SCALE * (self.backward(z, before.shape[0]) + damping * before)


def write_chunks(send, first, values):
    chunks, rows = send.shape[0], send.shape[2]
    for j in range(chunks):
        send[j, first] = values[j * rows : (j + 1) * rows, :]


def fill_padded(ref, values):
    count = values.shape[0]
    ref[:count] = values
    ref[count:] = jnp.zeros((ref.shape[0] - count,) + values.shape[1:], F32)


def setup_asc_kernel(
    fold, rows, packed, coef, meta, phi, table, state, value, onward, times, value_ref
):
    state[...] = coef[...]
    chunks = packed.shape[0] * fold
    count = chunks * rows
    meta[0, :count] = flat_first(packed, 0, fold, rows)
    meta[0, count:] = jnp.full((DUMMY_ROWS, LANES), -1.0, F32)
    fill_padded(meta.at[1], flat_first(packed, 4, fold, rows))
    fill_padded(times, flat_first(packed, 1, fold, rows))
    used_rows(meta.at[0], chunks, rows, table)
    basis_loop(table, meta.at[0], times, coef[...], phi, value_ref)
    value[...] = value_ref[:count]
    for j in range(chunks):
        base = j % fold * FIELDS
        for f in range(3):
            start = (base + f + 2) * rows
            onward[j, f * rows : (f + 1) * rows] = packed[j // fold, start : start + rows]
        onward[j, 3 * rows : 4 * rows] = value_ref[j * rows : (j + 1) * rows]
        onward[j, 4 * rows :] = packed[j // fold, fold * FIELDS * rows :]


def setup_desc_kernel(
    fold, rows, packed, meta, phi, table, state, model, weights, basis_0, value_0, send,
    times, z_ref, value_ref,
):
    chunks = packed.shape[0]
    count = chunks * rows
    home = lax.rem(lax.axis_index("asc"), fold) * (chunks // fold) + lax.axis_index("desc")
    state[...] = packed[home, 4 * rows :]
    meta[0, :count] = flat_second(packed, 0, rows)
    meta[0, count:] = jnp.full((DUMMY_ROWS, LANES), -1.0, F32)
    fill_padded(meta.at[1], flat_second(packed, 2, rows))
    fill_padded(times, flat_second(packed, 1, rows))
    used_rows(meta.at[0], chunks, rows, table)
    basis_loop(table, meta.at[0], times, state[...], phi, value_ref)
    role = Role(-1.0, table, meta, phi, z_ref, value_ref)
    own = value_ref[:count]
    write_chunks(send, 0, own)
    modelled = role.cross(own, flat_second(packed, 3, rows))
    model[...] = modelled
    weights[...], z = role.weigh(modelled)
    basis_0[...] = role.gradient(z, state[...])
    own = role.forward(basis_0[...])
    value_0[...] = own
    write_chunks(send, 1, own)


def first_asc_kernel(
    chunks, got, value, meta, phi, table, state,
    model, weights, crossed_0, basis_0, basis_1, value_1, send, z_ref, value_ref,
):
    role = Role(1.0, table, meta, phi, z_ref, value_ref)
    modelled = role.cross(value[...], flat(got, 0, chunks))
    model[...] = modelled
    weights[...], z = role.weigh(modelled)
    basis_0[...] = role.gradient(z, state[...])
    own = role.forward(basis_0[...])
    write_chunks(send, 0, own)
    crossed = role.cross(own, flat(got, 1, chunks))
    crossed_0[...] = crossed
    basis_1[...] = role.image(weights[...] * crossed, basis_0[...])
    own = role.forward(basis_1[...])
    value_1[...] = own
    write_chunks(send, 1, own)


def images_kernel(
    sign, chunks, got, value_0, meta, phi, table, weights, basis_0,
    crossed_0, crossed_1, basis_1, basis_2, value_2, send, z_ref, value_ref,
):
    role = Role(sign, table, meta, phi, z_ref, value_ref)
    crossed = role.cross(value_0[...], flat(got, 0, chunks))
    crossed_0[...] = crossed
    basis_1[...] = role.image(weights[...] * crossed, basis_0[...])
    own = role.forward(basis_1[...])
    write_chunks(send, 0, own)
    crossed = role.cross(own, flat(got, 1, chunks))
    crossed_1[...] = crossed
    basis_2[...] = role.image(weights[...] * crossed, basis_1[...])
    own = role.forward(basis_2[...])
    value_2[...] = own
    write_chunks(send, 1, own)


def total(x):
    return jnp.sum(jnp.sum(x, axis=0, keepdims=True), axis=1, keepdims=True)


PAIRS = [(0, 0), (0, 1), (0, 2), (1, 1), (1, 2), (2, 2)]


def gram_kernel(
    sign, chunks, got, value_1, meta, phi, table, weights, crossed_0, basis_0, basis_1,
    other_0, other_1, other_2,
    crossed_1, crossed_2, basis_2, value_2, scalars, z_ref, value_ref,
):
    role = Role(sign, table, meta, phi, z_ref, value_ref)
    weight = weights[...]
    crossed = role.cross(value_1[...], flat(got, 0, chunks))
    crossed_1[...] = crossed
    basis_2[...] = role.image(weight * crossed, basis_1[...])
    own = role.forward(basis_2[...])
    value_2[...] = own
    last = role.cross(own, flat(got, 1, chunks))
    crossed_2[...] = last
    values = [crossed_0[...], crossed, last]
    mine = [basis_0[...], basis_1[...], basis_2[...]]
    others = [other_0[...], other_1[...], other_2[...]]
    lane = lax.broadcasted_iota(jnp.int32, (1, LANES), 1)
    line = jnp.zeros((1, LANES), F32)
    for place_in_line, (i, j) in enumerate(PAIRS):
        dots = total(mine[i] * mine[j] + others[i] * others[j])
        curve = total(weight * values[i] * values[j]) + damping * dots
        line = jnp.where(lane == place_in_line, curve, line)
        if i == 0:
            line = jnp.where(lane == len(PAIRS) + j, dots, line)
    for d in range(scalars.shape[0]):
        scalars[d] = line


def solve(scalars):
    summed = scalars[0]
    for d in range(1, scalars.shape[0]):
        summed = summed + scalars[d]
    line = summed
    lane = lax.broadcasted_iota(jnp.int32, (1, LANES), 1)

    def pick(place):
        return jnp.sum(jnp.where(lane == place, line, 0.0), axis=1, keepdims=True)

    g = {pair: pick(place) for place, pair in enumerate(PAIRS)}
    right = [pick(len(PAIRS) + i) for i in range(3)]
    s = [
        jnp.where(g[i, i] > 0.0, lax.rsqrt(jnp.maximum(g[i, i], 1e-37)), 0.0) for i in range(3)
    ]
    l10 = g[0, 1] * s[0] * s[1]
    l20 = g[0, 2] * s[0] * s[2]
    g21 = g[1, 2] * s[1] * s[2]
    c = [right[i] * s[i] for i in range(3)]

    def inverse(pivot):
        good = pivot > PIVOT_FLOOR
        return jnp.where(good, 1.0 / jnp.where(good, pivot, 1.0), 0.0)

    inv1 = inverse(1.0 - l10 * l10)
    t21 = g21 - l20 * l10
    l21 = t21 * inv1
    inv2 = inverse(1.0 - l20 * l20 - l21 * t21)
    u1 = c[1] - l10 * c[0]
    u2 = c[2] - l20 * c[0] - l21 * u1
    x2 = u2 * inv2
    x1 = u1 * inv1 - l21 * x2
    x0 = c[0] - l10 * x1 - l20 * x2
    return [x0 * s[0], x1 * s[1], x2 * s[2]]


def combine(y, parts):
    return y[0] * parts[0] + (y[1] * parts[1] + y[2] * parts[2])


def next_asc_kernel(
    chunks, scalars, meta, phi, table, model, crossed_0, crossed_1, crossed_2,
    basis_a0, basis_a1, basis_a2, basis_d0, basis_d1, basis_d2, state_a, state_d, value_2,
    new_a, new_d, shares, weights, basis_0, value_0, send, z_ref, value_ref,
):
    role = Role(1.0, table, meta, phi, z_ref, value_ref)
    write_chunks(send, 0, value_2[...])
    y = solve(scalars)
    for i in range(3):
        shares[i : i + 1] = jnp.broadcast_to(y[i], (1, LANES))
    modelled = model[...] + combine(y, [crossed_0[...], crossed_1[...], crossed_2[...]])
    new_a[...] = state_a[...] + combine(y, [basis_a0[...], basis_a1[...], basis_a2[...]])
    new_d[...] = state_d[...] + combine(y, [basis_d0[...], basis_d1[...], basis_d2[...]])
    weights[...], z = role.weigh(modelled)
    basis_0[...] = role.gradient(z, new_a[...])
    own = role.forward(basis_0[...])
    value_0[...] = own
    write_chunks(send, 1, own)


def next_desc_kernel(
    chunks, got, shares, meta, phi, table, model, crossed_0, crossed_1, value_2, state,
    weights, new_crossed_0, basis_0, basis_1, value_1, send, z_ref, value_ref,
):
    role = Role(-1.0, table, meta, phi, z_ref, value_ref)
    y = [shares[i : i + 1] for i in range(3)]
    crossed_2 = role.cross(value_2[...], flat(got, 0, chunks))
    modelled = model[...] + combine(y, [crossed_0[...], crossed_1[...], crossed_2])
    weights[...], z = role.weigh(modelled)
    basis_0[...] = role.gradient(z, state[...])
    own = role.forward(basis_0[...])
    write_chunks(send, 0, own)
    crossed = role.cross(own, flat(got, 1, chunks))
    new_crossed_0[...] = crossed
    basis_1[...] = role.image(weights[...] * crossed, basis_0[...])
    own = role.forward(basis_1[...])
    value_1[...] = own
    write_chunks(send, 1, own)


def final_kernel(scalars, state_a, basis_0, basis_1, basis_2, desc, out_a, out_d):
    y = solve(scalars)
    out_a[...] = state_a[...] + combine(y, [basis_0[...], basis_1[...], basis_2[...]])
    out_d[...] = desc[0] + combine(y, [desc[1], desc[2], desc[3]])


def body(coef_asc, coef_desc, cross_asc, cross_desc, time_asc, time_desc, height, block_fill):
    owned_asc, terms = coef_asc.shape
    owned_desc = coef_desc.shape[0]
    blocks, width = cross_asc.shape
    na = lax.axis_size("asc")
    nd = lax.axis_size("desc")
    fold = na // nd
    rows = blocks * width // na // LANES
    all_rows = na * rows
    all_blocks = -(-all_rows // BLOCK_ROWS)
    shape = jax.ShapeDtypeStruct

    def call(kernel, outs, scratch, *args, in_specs=None, mebibytes=16):
        return pl.pallas_call(
            kernel,
            out_shape=outs,
            in_specs=[place(x) for x in args] if in_specs is None else in_specs,
            out_specs=jax.tree.map(place, outs),
            scratch_shapes=scratch,
            compiler_params=params(mebibytes),
        )(*args)

    to_role = []
    for p in range(na):
        for q in range(nd):
            to_role.append((p * nd + q, (q * fold + p // nd) * nd + p % nd))
    to_native = [(b, a) for a, b in to_role]
    slots = (cross_asc, cross_desc, time_asc, time_desc, height)
    packed = call(
        functools.partial(pack_kernel, na, nd, owned_asc),
        shape((nd, fold * FIELDS * rows + owned_desc, LANES), F32),
        [pltpu.VMEM(coef_desc.shape, F32)]
        + [pltpu.VMEM((blocks, width), x.dtype) for x in slots]
        + [
            pltpu.VMEM((1, blocks), jnp.int32),
            pltpu.VMEM((FIELDS, blocks, width), F32),
            pltpu.SemaphoreType.DMA((len(slots) + 2,)),
        ],
        coef_desc, *slots, block_fill.reshape(1, blocks),
        in_specs=[pl.BlockSpec(memory_space=pltpu.HBM)] * (len(slots) + 2),
        mebibytes=60,
    )
    at_asc = lax.all_to_all(packed, "desc", split_axis=0, concat_axis=0, tiled=True)

    padded = all_rows + DUMMY_ROWS
    meta_shape = shape((2, padded, LANES), F32)
    phi_shape = shape((all_blocks, 2 * terms, BLOCK_ROWS * LANES), BF16)
    table_shape = shape((all_rows + rows + BLOCK_ROWS + 1,), jnp.int32)
    role_shapes = [meta_shape, phi_shape, table_shape]
    slot_shape = shape((all_rows, LANES), F32)
    send_shape = shape((na, 2, rows, LANES), F32)
    field_a = shape(coef_asc.shape, F32)
    field_d = shape(coef_desc.shape, F32)
    line_shape = shape((na * nd, 1, LANES), F32)
    times_scratch = pltpu.VMEM((padded, LANES), F32)
    scratch = [pltpu.VMEM((2, padded, LANES), F32), pltpu.VMEM((padded, LANES), F32)]

    def exchange(x):
        return lax.all_to_all(x, "asc", split_axis=0, concat_axis=0, tiled=True)

    def share(x):
        return lax.all_to_all(x, ("asc", "desc"), split_axis=0, concat_axis=0, tiled=True)

    *asc, state_a, value, onward = call(
        functools.partial(setup_asc_kernel, fold, rows),
        role_shapes + [field_a, slot_shape, shape((na, 4 * rows + owned_desc, LANES), F32)],
        [times_scratch, scratch[1]],
        at_asc, coef_asc,
    )
    *desc, state_d, model_d, weights_d, d0, own_d, send = call(
        functools.partial(setup_desc_kernel, fold, rows),
        role_shapes + [field_d, slot_shape, slot_shape, field_d, slot_shape, send_shape],
        [times_scratch] + scratch,
        exchange(onward),
    )
    model_a, weights_a, crossed_a0, a0, a1, own_a, send = call(
        functools.partial(first_asc_kernel, na),
        [slot_shape, slot_shape, slot_shape, field_a, field_a, slot_shape, send_shape],
        scratch,
        exchange(send), value, *asc, state_a,
    )
    crossed_d0, crossed_d1, d1, d2, own_d, send = call(
        functools.partial(images_kernel, -1.0, na),
        [slot_shape, slot_shape, field_d, field_d, slot_shape, send_shape],
        scratch,
        exchange(send), own_d, *desc, weights_d, d0,
    )
    crossed_a1, crossed_a2, a2, own_a, scalars = call(
        functools.partial(gram_kernel, 1.0, na),
        [slot_shape, slot_shape, field_a, slot_shape, line_shape],
        scratch,
        exchange(send), own_a, *asc, weights_a, crossed_a0, a0, a1, d0, d1, d2,
    )
    state_a, state_d, shares, weights_a, a0, own_a, send = call(
        functools.partial(next_asc_kernel, na),
        [
            field_a, field_d, shape((8, LANES), F32),
            slot_shape, field_a, slot_shape, send_shape,
        ],
        scratch,
        share(scalars), *asc, model_a, crossed_a0, crossed_a1, crossed_a2,
        a0, a1, a2, d0, d1, d2, state_a, state_d, own_a,
    )
    weights_d, crossed_d0, d0, d1, own_d, send = call(
        functools.partial(next_desc_kernel, na),
        [slot_shape, slot_shape, field_d, field_d, slot_shape, send_shape],
        scratch,
        exchange(send), shares, *desc, model_d, crossed_d0, crossed_d1, own_d, state_d,
    )
    _, _, a1, a2, _, send = call(
        functools.partial(images_kernel, 1.0, na),
        [slot_shape, slot_shape, field_a, field_a, slot_shape, send_shape],
        scratch,
        exchange(send), own_a, *asc, weights_a, a0,
    )
    _, _, d2, _, scalars = call(
        functools.partial(gram_kernel, -1.0, na),
        [slot_shape, slot_shape, field_d, slot_shape, line_shape],
        scratch,
        exchange(send), own_d, *desc, weights_d, crossed_d0, d0, d1, a0, a1, a2,
    )
    leaving = jnp.stack([state_d, d0, d1, d2])
    native = lax.ppermute(leaving, ("asc", "desc"), to_native)
    return tuple(
        call(
            final_kernel,
            [field_a, field_d],
            [],
            share(scalars), state_a, a0, a1, a2, native,
        )
    )


def solution(mesh):
    split_rows = P(("asc", "desc"), None)
    return jax.shard_map(
        body,
        mesh=mesh,
        in_specs=(split_rows,) * 7 + (P(("asc", "desc")),),
        out_specs=(split_rows, split_rows),
        check_vma=False,
    )
```

```python
import functools
import math

import jax
import jax.numpy as jnp
from jax import lax
from jax.experimental import pallas as pl
from jax.experimental.pallas import tpu as pltpu
from jax.sharding import PartitionSpec as P

GN_STEPS = 2
damping = 2.0
cauchy_square = 2.25

LANES = 128
STEP_ROWS = 2
UNROLL = 4
BLOCK_ROWS = STEP_ROWS * UNROLL
STEP_LANES = STEP_ROWS * LANES
DUMMY_ROWS = 8
TURNS = (4, 2, 1)
SCALE = 1.0 / 128.0
FIELDS = 5
PIVOT_FLOOR = 1e-6
F32 = jnp.float32
BF16 = jnp.bfloat16

COS_TERMS = [(-1.0) ** i * math.pi ** (2 * i) / math.factorial(2 * i) for i in range(8)]
SIN_TERMS = [(-1.0) ** i * math.pi ** (2 * i + 1) / math.factorial(2 * i + 1) for i in range(7)]


def in_smem(x):
    return x.dtype == jnp.int32 and len(x.shape) == 1


def params(mebibytes):
    return pltpu.CompilerParams(vmem_limit_bytes=mebibytes * 1024 * 1024)


def place(x):
    return pl.BlockSpec(memory_space=pltpu.SMEM if in_smem(x) else pltpu.VMEM)


def split(x):
    high = x.astype(BF16)
    low = (x - high.astype(F32)).astype(BF16)
    return high, low


def flat_first(ref, field, fold, rows):
    parts = []
    for j in range(ref.shape[0] * fold):
        start = (j % fold * FIELDS + field) * rows
        parts.append(ref[j // fold, start : start + rows])
    return jnp.concatenate(parts, axis=0)


def flat_second(ref, field, rows):
    start = field * rows
    return jnp.concatenate([ref[j, start : start + rows] for j in range(ref.shape[0])], axis=0)


def flat(ref, field, chunks):
    return jnp.concatenate([ref[j, field] for j in range(chunks)], axis=0)


def local_id(ids, owned):
    if owned & (owned - 1) == 0:
        return ids & (owned - 1)
    return lax.rem(ids, owned)


def pack_kernel(
    na, nd, owned_asc, coef_in, ca_in, cd_in, ta_in, td_in, height_in, fill_in, out,
    coef, ca, cd, ta, td, height, fill, turned, sems,
):
    copies = [
        pltpu.make_async_copy(source, target, sems.at[i])
        for i, (source, target) in enumerate(
            [
                (fill_in, fill), (ca_in, ca), (ta_in, ta),
                (cd_in, cd), (td_in, td), (height_in, height), (coef_in, coef),
            ]
        )
    ]
    for copy in copies:
        copy.start()
    for copy in copies:
        copy.wait()
    owned_desc = coef.shape[0]
    blocks, width = ca.shape
    group = width // na
    rows = blocks // na
    fill_row = fill[...]
    row_id = lax.broadcasted_iota(jnp.int32, (blocks, blocks), 0)
    col_id = lax.broadcasted_iota(jnp.int32, (blocks, blocks), 1)
    fill_col = jnp.sum(
        jnp.where(row_id == col_id, fill_row, 0).astype(F32), axis=1, keepdims=True
    )
    lane = lax.broadcasted_iota(jnp.int32, (blocks, width), 1)
    live = lane.astype(F32) < fill_col
    fields = [
        jnp.where(live, local_id(ca[...], owned_asc).astype(F32), -1.0),
        ta[...],
        jnp.where(live, local_id(cd[...], owned_desc).astype(F32), -1.0),
        td[...],
        height[...],
    ]
    source = lax.broadcasted_iota(jnp.int32, (width, width), 0)
    target = lax.broadcasted_iota(jnp.int32, (width, width), 1)
    owner = target // group
    place = target - owner * group
    order = (source == place * na + owner).astype(F32).astype(BF16)
    for f, x in enumerate(fields):
        high = x.astype(BF16)
        rest = x - high.astype(F32)
        middle = rest.astype(BF16)
        low = (rest - middle.astype(F32)).astype(BF16)
        turned[f] = (
            jnp.dot(high, order, preferred_element_type=F32)
            + jnp.dot(middle, order, preferred_element_type=F32)
        ) + jnp.dot(low, order, preferred_element_type=F32)
    lane_group = lax.broadcasted_iota(jnp.int32, (rows, width), 1) // group
    for f in range(FIELDS):
        parts = [None] * na
        for k in range(na):
            piece = turned[f, pl.ds(k, rows, stride=na), :]
            for r in range(na):
                amount = ((k - r) * group) % width
                moved = pltpu.roll(piece, amount, 1) if amount else piece
                parts[r] = moved if k == 0 else jnp.where(lane_group == k, moved, parts[r])
        for r in range(na):
            start = (r // nd * FIELDS + f) * rows
            out[r % nd, start : start + rows] = parts[r]
    for q in range(nd):
        out[q, out.shape[1] - owned_desc :] = coef[...]


def cos_sin_pi(x):
    turns = jnp.floor(x + 0.5)
    f = x - turns
    sign = 1.0 - 2.0 * (turns - 2.0 * jnp.floor(turns * 0.5))
    u = f * f
    c = COS_TERMS[-1]
    for term in COS_TERMS[-2::-1]:
        c = c * u + term
    s = SIN_TERMS[-1]
    for term in SIN_TERMS[-2::-1]:
        s = s * u + term
    return c * sign, s * (f * sign)


def rows_pair(ref, rows):
    return jnp.concatenate([ref[pl.ds(r, 1), :] for r in rows], axis=1)


def used_rows(ids_ref, chunks, rows, table):
    count = jnp.int32(0)
    level = lax.broadcasted_iota(jnp.int32, (rows, LANES), 0).astype(F32) + 1.0
    for j in range(chunks):
        ids = ids_ref[j * rows : (j + 1) * rows, :]
        used = jnp.max(jnp.where(ids >= 0.0, level, 0.0)).astype(jnp.int32)
        for i in range(rows):
            table[count + i] = j * rows + i
        count = count + used
    for i in range(BLOCK_ROWS):
        table[count + i] = chunks * rows
    table[table.shape[0] - 1] = lax.div(count + (BLOCK_ROWS - 1), BLOCK_ROWS)


def listed_rows(table, first, count):
    return [table[first + i] for i in range(count)]


def over_blocks(table, step, carry):
    blocks = table[table.shape[0] - 1]
    done = jnp.int32(0)
    for size in TURNS:
        turns = lax.div(blocks - done, size)

        def turn(i, carry, done=done, size=size):
            for u in range(size):
                carry = step(done + i * size + u, carry)
            return carry

        carry = lax.fori_loop(0, turns, turn, carry)
        done = done + turns * size
    return carry


def stacked(field):
    high, low = split(field)
    top = jnp.concatenate([high, high], axis=1)
    bottom = jnp.concatenate([low, jnp.zeros_like(low)], axis=1)
    return jnp.concatenate([top, bottom], axis=0)


def forward_step(stack, phi, ids_row, row_iota, owned):
    both = jnp.dot(stack, phi, preferred_element_type=F32)
    value = both[:owned] + both[owned:]
    return jnp.sum(jnp.where(row_iota == ids_row, value, 0.0), axis=0, keepdims=True)


def store_rows(ref, rows, value):
    for i, r in enumerate(rows):
        ref[pl.ds(r, 1), :] = value[:, i * LANES : (i + 1) * LANES]


def basis_loop(table, ids_ref, time_ref, coef, phi_ref, value_ref):
    owned, terms = coef.shape
    half = terms // 2
    value_ref[...] = jnp.zeros(value_ref.shape, F32)
    width = STEP_LANES
    stack = stacked(coef)
    row_iota = lax.broadcasted_iota(jnp.int32, (owned, width), 0).astype(F32)
    fine = (lax.broadcasted_iota(jnp.int32, (8, width), 0) + 1).astype(F32)
    coarse = (lax.broadcasted_iota(jnp.int32, (half // 8, width), 0) * 8).astype(F32)

    def step(block, u):
        rows = listed_rows(table, block * BLOCK_ROWS + u * STEP_ROWS, STEP_ROWS)
        times = rows_pair(time_ref, rows)
        cos_fine, sin_fine = cos_sin_pi(fine * times)
        cos_coarse, sin_coarse = cos_sin_pi(coarse * times)
        cos_parts, sin_parts = [], []
        for j in range(half // 8):
            cj = cos_coarse[j : j + 1]
            sj = sin_coarse[j : j + 1]
            cos_parts.append(cj * cos_fine - sj * sin_fine)
            sin_parts.append(sj * cos_fine + cj * sin_fine)
        high, low = split(jnp.concatenate(cos_parts + sin_parts, axis=0))
        phi = jnp.concatenate([high, low], axis=0)
        phi_ref[block, :, u * width : (u + 1) * width] = phi
        value = forward_step(stack, phi, rows_pair(ids_ref, rows), row_iota, owned)
        store_rows(value_ref, rows, value)

    def whole_block(block, carry):
        for u in range(UNROLL):
            step(block, u)
        return carry

    lax.fori_loop(0, table[table.shape[0] - 1], whole_block, 0)


class Role:
    def __init__(self, sign, table, meta, phi, z_ref, value_ref):
        self.sign = sign
        self.table = table
        self.ids = meta
        self.phi = phi
        self.z_ref = z_ref
        self.value_ref = value_ref
        self.count = meta.shape[0] - DUMMY_ROWS

    def cross(self, mine, other):
        return mine - other if self.sign > 0 else other - mine

    def backward(self, z, owned):
        high = z.astype(BF16).astype(F32)
        self.z_ref[0, : self.count] = high
        self.z_ref[1, : self.count] = z - high
        self.z_ref[:, self.count :] = jnp.zeros((2, DUMMY_ROWS, LANES), F32)
        blocks, double, width = self.phi.shape
        terms = double // 2
        row_iota = lax.broadcasted_iota(jnp.int32, (owned, width), 0).astype(F32)

        def gather(block, carry):
            rows = listed_rows(self.table, block * BLOCK_ROWS, BLOCK_ROWS)
            hit = row_iota == rows_pair(self.ids, rows)
            parts = [
                jnp.where(hit, rows_pair(self.z_ref.at[k], rows), 0.0).astype(BF16)
                for k in range(2)
            ]
            return carry + lax.dot_general(
                jnp.concatenate(parts, axis=0),
                self.phi[block],
                (((1,), (1,)), ((), ())),
                preferred_element_type=F32,
            )

        g = over_blocks(self.table, gather, jnp.zeros((2 * owned, double), F32))
        return self.sign * (g[:owned, :terms] + (g[:owned, terms:] + g[owned:, :terms]))

    def forward(self, field):
        owned = field.shape[0]
        stack = stacked(field)
        row_iota = lax.broadcasted_iota(jnp.int32, (owned, STEP_LANES), 0).astype(F32)
        self.value_ref[...] = jnp.zeros(self.value_ref.shape, F32)

        def ahead(block, carry):
            for u in range(UNROLL):
                rows = listed_rows(self.table, block * BLOCK_ROWS + u * STEP_ROWS, STEP_ROWS)
                phi = self.phi[block, :, u * STEP_LANES : (u + 1) * STEP_LANES]
                value = forward_step(stack, phi, rows_pair(self.ids, rows), row_iota, owned)
                store_rows(self.value_ref, rows, value)
            return carry

        over_blocks(self.table, ahead, 0)
        return self.value_ref[: self.count]

    def weigh(self, residual):
        live = self.ids[: self.count] >= 0.0
        misfit = jnp.where(live, residual, 0.0)
        weight = jnp.where(live, 1.0 / (1.0 + misfit * misfit / cauchy_square), 0.0)
        return weight, weight * misfit

    def gradient(self, z, state):
        return self.backward(z, state.shape[0]) - damping * state

    def image(self, z, before):
        return SCALE * (self.backward(z, before.shape[0]) + damping * before)


def write_chunks(send, first, values):
    chunks, rows = send.shape[0], send.shape[2]
    for j in range(chunks):
        send[j, first] = values[j * rows : (j + 1) * rows, :]


def fill_padded(ref, values):
    count = values.shape[0]
    ref[:count] = values
    ref[count:] = jnp.zeros((ref.shape[0] - count,) + values.shape[1:], F32)


def setup_asc_kernel(
    fold, rows, packed, coef, meta, phi, table, state, short, onward, times, value_ref
):
    state[...] = coef[...]
    chunks = packed.shape[0] * fold
    count = chunks * rows
    meta[:count] = flat_first(packed, 0, fold, rows)
    meta[count:] = jnp.full((DUMMY_ROWS, LANES), -1.0, F32)
    fill_padded(times, flat_first(packed, 1, fold, rows))
    used_rows(meta, chunks, rows, table)
    basis_loop(table, meta, times, coef[...], phi, value_ref)
    short[...] = flat_first(packed, 4, fold, rows) - value_ref[:count]
    for j in range(chunks):
        base = j % fold * FIELDS
        for f in range(2):
            start = (base + f + 2) * rows
            onward[j, f * rows : (f + 1) * rows] = packed[j // fold, start : start + rows]
        onward[j, 2 * rows : 3 * rows] = short[j * rows : (j + 1) * rows]
        onward[j, 3 * rows :] = packed[j // fold, fold * FIELDS * rows :]


def setup_desc_kernel(
    fold, rows, packed, meta, phi, table, state, residual, weights, basis_0, value_0, send,
    times, z_ref, value_ref,
):
    chunks = packed.shape[0]
    count = chunks * rows
    home = lax.rem(lax.axis_index("asc"), fold) * (chunks // fold) + lax.axis_index("desc")
    state[...] = packed[home, 3 * rows :]
    meta[:count] = flat_second(packed, 0, rows)
    meta[count:] = jnp.full((DUMMY_ROWS, LANES), -1.0, F32)
    fill_padded(times, flat_second(packed, 1, rows))
    used_rows(meta, chunks, rows, table)
    basis_loop(table, meta, times, state[...], phi, value_ref)
    role = Role(-1.0, table, meta, phi, z_ref, value_ref)
    own = value_ref[:count]
    write_chunks(send, 0, own)
    left = flat_second(packed, 2, rows) + own
    residual[...] = left
    weights[...], z = role.weigh(left)
    basis_0[...] = role.gradient(z, state[...])
    own = role.forward(basis_0[...])
    value_0[...] = own
    write_chunks(send, 1, own)


def first_asc_kernel(
    chunks, got, short, meta, phi, table, state,
    residual, weights, crossed_0, basis_0, basis_1, value_1, send, z_ref, value_ref,
):
    role = Role(1.0, table, meta, phi, z_ref, value_ref)
    left = short[...] + flat(got, 0, chunks)
    residual[...] = left
    weights[...], z = role.weigh(left)
    basis_0[...] = role.gradient(z, state[...])
    own = role.forward(basis_0[...])
    write_chunks(send, 0, own)
    crossed = role.cross(own, flat(got, 1, chunks))
    crossed_0[...] = crossed
    basis_1[...] = role.image(weights[...] * crossed, basis_0[...])
    own = role.forward(basis_1[...])
    value_1[...] = own
    write_chunks(send, 1, own)


def images_kernel(
    sign, chunks, got, value_0, meta, phi, table, weights, basis_0,
    crossed_0, crossed_1, basis_1, basis_2, value_2, send, z_ref, value_ref,
):
    role = Role(sign, table, meta, phi, z_ref, value_ref)
    crossed = role.cross(value_0[...], flat(got, 0, chunks))
    crossed_0[...] = crossed
    basis_1[...] = role.image(weights[...] * crossed, basis_0[...])
    own = role.forward(basis_1[...])
    write_chunks(send, 0, own)
    crossed = role.cross(own, flat(got, 1, chunks))
    crossed_1[...] = crossed
    basis_2[...] = role.image(weights[...] * crossed, basis_1[...])
    own = role.forward(basis_2[...])
    value_2[...] = own
    write_chunks(send, 1, own)


def total(x):
    return jnp.sum(jnp.sum(x, axis=0, keepdims=True), axis=1, keepdims=True)


PAIRS = [(0, 0), (0, 1), (0, 2), (1, 1), (1, 2), (2, 2)]


def gram_kernel(
    sign, chunks, got, value_1, meta, phi, table, weights, crossed_0, basis_0, basis_1,
    other_0, other_1, other_2,
    crossed_1, crossed_2, basis_2, value_2, scalars, z_ref, value_ref,
):
    role = Role(sign, table, meta, phi, z_ref, value_ref)
    weight = weights[...]
    crossed = role.cross(value_1[...], flat(got, 0, chunks))
    crossed_1[...] = crossed
    basis_2[...] = role.image(weight * crossed, basis_1[...])
    own = role.forward(basis_2[...])
    value_2[...] = own
    last = role.cross(own, flat(got, 1, chunks))
    crossed_2[...] = last
    values = [crossed_0[...], crossed, last]
    mine = [basis_0[...], basis_1[...], basis_2[...]]
    others = [other_0[...], other_1[...], other_2[...]]
    lane = lax.broadcasted_iota(jnp.int32, (1, LANES), 1)
    line = jnp.zeros((1, LANES), F32)
    for place_in_line, (i, j) in enumerate(PAIRS):
        dots = total(mine[i] * mine[j] + others[i] * others[j])
        curve = total(weight * values[i] * values[j]) + damping * dots
        line = jnp.where(lane == place_in_line, curve, line)
        if i == 0:
            line = jnp.where(lane == len(PAIRS) + j, dots, line)
    scalars[0] = line


def solve(scalars):
    summed = scalars[0]
    for d in range(1, scalars.shape[0]):
        summed = summed + scalars[d]
    line = summed
    lane = lax.broadcasted_iota(jnp.int32, (1, LANES), 1)

    def pick(place):
        return jnp.sum(jnp.where(lane == place, line, 0.0), axis=1, keepdims=True)

    g = {pair: pick(place) for place, pair in enumerate(PAIRS)}
    right = [pick(len(PAIRS) + i) for i in range(3)]
    s = [
        jnp.where(g[i, i] > 0.0, lax.rsqrt(jnp.maximum(g[i, i], 1e-37)), 0.0) for i in range(3)
    ]
    l10 = g[0, 1] * s[0] * s[1]
    l20 = g[0, 2] * s[0] * s[2]
    g21 = g[1, 2] * s[1] * s[2]
    c = [right[i] * s[i] for i in range(3)]

    def inverse(pivot):
        good = pivot > PIVOT_FLOOR
        return jnp.where(good, 1.0 / jnp.where(good, pivot, 1.0), 0.0)

    inv1 = inverse(1.0 - l10 * l10)
    t21 = g21 - l20 * l10
    l21 = t21 * inv1
    inv2 = inverse(1.0 - l20 * l20 - l21 * t21)
    u1 = c[1] - l10 * c[0]
    u2 = c[2] - l20 * c[0] - l21 * u1
    x2 = u2 * inv2
    x1 = u1 * inv1 - l21 * x2
    x0 = c[0] - l10 * x1 - l20 * x2
    return [x0 * s[0], x1 * s[1], x2 * s[2]]


def combine(y, parts):
    return y[0] * parts[0] + (y[1] * parts[1] + y[2] * parts[2])


def next_asc_kernel(
    chunks, scalars, meta, phi, table, residual, crossed_0, crossed_1, crossed_2,
    basis_a0, basis_a1, basis_a2, basis_d0, basis_d1, basis_d2, state_a, state_d, value_2,
    new_a, new_d, shares, weights, basis_0, value_0, send, z_ref, value_ref,
):
    role = Role(1.0, table, meta, phi, z_ref, value_ref)
    write_chunks(send, 0, value_2[...])
    y = solve(scalars)
    for i in range(3):
        shares[i : i + 1] = jnp.broadcast_to(y[i], (1, LANES))
    left = residual[...] - combine(y, [crossed_0[...], crossed_1[...], crossed_2[...]])
    new_a[...] = state_a[...] + combine(y, [basis_a0[...], basis_a1[...], basis_a2[...]])
    new_d[...] = state_d[...] + combine(y, [basis_d0[...], basis_d1[...], basis_d2[...]])
    weights[...], z = role.weigh(left)
    basis_0[...] = role.gradient(z, new_a[...])
    own = role.forward(basis_0[...])
    value_0[...] = own
    write_chunks(send, 1, own)


def next_desc_kernel(
    chunks, got, shares, meta, phi, table, residual, crossed_0, crossed_1, value_2, state,
    weights, new_crossed_0, basis_0, basis_1, value_1, send, z_ref, value_ref,
):
    role = Role(-1.0, table, meta, phi, z_ref, value_ref)
    y = [shares[i : i + 1] for i in range(3)]
    crossed_2 = role.cross(value_2[...], flat(got, 0, chunks))
    left = residual[...] - combine(y, [crossed_0[...], crossed_1[...], crossed_2])
    weights[...], z = role.weigh(left)
    basis_0[...] = role.gradient(z, state[...])
    own = role.forward(basis_0[...])
    write_chunks(send, 0, own)
    crossed = role.cross(own, flat(got, 1, chunks))
    new_crossed_0[...] = crossed
    basis_1[...] = role.image(weights[...] * crossed, basis_0[...])
    own = role.forward(basis_1[...])
    value_1[...] = own
    write_chunks(send, 1, own)


def final_kernel(scalars, state_a, basis_0, basis_1, basis_2, desc, out_a, out_d):
    y = solve(scalars)
    out_a[...] = state_a[...] + combine(y, [basis_0[...], basis_1[...], basis_2[...]])
    out_d[...] = desc[0] + combine(y, [desc[1], desc[2], desc[3]])


def body(coef_asc, coef_desc, cross_asc, cross_desc, time_asc, time_desc, height, block_fill):
    owned_asc, terms = coef_asc.shape
    owned_desc = coef_desc.shape[0]
    blocks, width = cross_asc.shape
    na = lax.axis_size("asc")
    nd = lax.axis_size("desc")
    fold = na // nd
    rows = blocks * width // na // LANES
    all_rows = na * rows
    all_blocks = -(-all_rows // BLOCK_ROWS)
    shape = jax.ShapeDtypeStruct

    def call(kernel, outs, scratch, *args, in_specs=None, mebibytes=16):
        return pl.pallas_call(
            kernel,
            out_shape=outs,
            in_specs=[place(x) for x in args] if in_specs is None else in_specs,
            out_specs=jax.tree.map(place, outs),
            scratch_shapes=scratch,
            compiler_params=params(mebibytes),
        )(*args)

    to_role = []
    for p in range(na):
        for q in range(nd):
            to_role.append((p * nd + q, (q * fold + p // nd) * nd + p % nd))
    to_native = [(b, a) for a, b in to_role]
    slots = (cross_asc, cross_desc, time_asc, time_desc, height)
    packed = call(
        functools.partial(pack_kernel, na, nd, owned_asc),
        shape((nd, fold * FIELDS * rows + owned_desc, LANES), F32),
        [pltpu.VMEM(coef_desc.shape, F32)]
        + [pltpu.VMEM((blocks, width), x.dtype) for x in slots]
        + [
            pltpu.VMEM((1, blocks), jnp.int32),
            pltpu.VMEM((FIELDS, blocks, width), F32),
            pltpu.SemaphoreType.DMA((len(slots) + 2,)),
        ],
        coef_desc, *slots, block_fill.reshape(1, blocks),
        in_specs=[pl.BlockSpec(memory_space=pltpu.HBM)] * (len(slots) + 2),
        mebibytes=60,
    )
    at_asc = lax.all_to_all(packed, "desc", split_axis=0, concat_axis=0, tiled=True)

    padded = all_rows + DUMMY_ROWS
    meta_shape = shape((padded, LANES), F32)
    phi_shape = shape((all_blocks, 2 * terms, BLOCK_ROWS * LANES), BF16)
    table_shape = shape((all_rows + rows + BLOCK_ROWS + 1,), jnp.int32)
    role_shapes = [meta_shape, phi_shape, table_shape]
    slot_shape = shape((all_rows, LANES), F32)
    send_shape = shape((na, 2, rows, LANES), F32)
    field_a = shape(coef_asc.shape, F32)
    field_d = shape(coef_desc.shape, F32)
    line_shape = shape((1, 1, LANES), F32)
    times_scratch = pltpu.VMEM((padded, LANES), F32)
    scratch = [pltpu.VMEM((2, padded, LANES), F32), pltpu.VMEM((padded, LANES), F32)]

    def exchange(x):
        return lax.all_to_all(x, "asc", split_axis=0, concat_axis=0, tiled=True)

    def share(x):
        return lax.all_gather(x, ("asc", "desc"), axis=0, tiled=True)

    *asc, state_a, short, onward = call(
        functools.partial(setup_asc_kernel, fold, rows),
        role_shapes + [field_a, slot_shape, shape((na, 3 * rows + owned_desc, LANES), F32)],
        [times_scratch, scratch[1]],
        at_asc, coef_asc,
    )
    *desc, state_d, residual_d, weights_d, d0, own_d, send = call(
        functools.partial(setup_desc_kernel, fold, rows),
        role_shapes + [field_d, slot_shape, slot_shape, field_d, slot_shape, send_shape],
        [times_scratch] + scratch,
        exchange(onward),
    )
    residual_a, weights_a, crossed_a0, a0, a1, own_a, send = call(
        functools.partial(first_asc_kernel, na),
        [slot_shape, slot_shape, slot_shape, field_a, field_a, slot_shape, send_shape],
        scratch,
        exchange(send), short, *asc, state_a,
    )
    crossed_d0, crossed_d1, d1, d2, own_d, send = call(
        functools.partial(images_kernel, -1.0, na),
        [slot_shape, slot_shape, field_d, field_d, slot_shape, send_shape],
        scratch,
        exchange(send), own_d, *desc, weights_d, d0,
    )
    crossed_a1, crossed_a2, a2, own_a, scalars = call(
        functools.partial(gram_kernel, 1.0, na),
        [slot_shape, slot_shape, field_a, slot_shape, line_shape],
        scratch,
        exchange(send), own_a, *asc, weights_a, crossed_a0, a0, a1, d0, d1, d2,
    )
    state_a, state_d, shares, weights_a, a0, own_a, send = call(
        functools.partial(next_asc_kernel, na),
        [
            field_a, field_d, shape((8, LANES), F32),
            slot_shape, field_a, slot_shape, send_shape,
        ],
        scratch,
        share(scalars), *asc, residual_a, crossed_a0, crossed_a1, crossed_a2,
        a0, a1, a2, d0, d1, d2, state_a, state_d, own_a,
    )
    weights_d, crossed_d0, d0, d1, own_d, send = call(
        functools.partial(next_desc_kernel, na),
        [slot_shape, slot_shape, field_d, field_d, slot_shape, send_shape],
        scratch,
        exchange(send), shares, *desc, residual_d, crossed_d0, crossed_d1, own_d, state_d,
    )
    _, _, a1, a2, _, send = call(
        functools.partial(images_kernel, 1.0, na),
        [slot_shape, slot_shape, field_a, field_a, slot_shape, send_shape],
        scratch,
        exchange(send), own_a, *asc, weights_a, a0,
    )
    _, _, d2, _, scalars = call(
        functools.partial(gram_kernel, -1.0, na),
        [slot_shape, slot_shape, field_d, slot_shape, line_shape],
        scratch,
        exchange(send), own_d, *desc, weights_d, crossed_d0, d0, d1, a0, a1, a2,
    )
    leaving = jnp.stack([state_d, d0, d1, d2])
    native = lax.ppermute(leaving, ("asc", "desc"), to_native)
    return tuple(
        call(
            final_kernel,
            [field_a, field_d],
            [],
            share(scalars), state_a, a0, a1, a2, native,
        )
    )


def solution(mesh):
    split_rows = P(("asc", "desc"), None)
    return jax.shard_map(
        body,
        mesh=mesh,
        in_specs=(split_rows,) * 7 + (P(("asc", "desc")),),
        out_specs=(split_rows, split_rows),
        check_vma=False,
    )
```

```python
import functools
import math

import jax
import jax.numpy as jnp
from jax import lax
from jax.experimental import pallas as pl
from jax.experimental.pallas import tpu as pltpu
from jax.sharding import PartitionSpec as P

GN_STEPS = 2
damping = 2.0
cauchy_square = 2.25

LANES = 128
STEP_ROWS = 2
UNROLL = 4
BLOCK_ROWS = STEP_ROWS * UNROLL
STEP_LANES = STEP_ROWS * LANES
DUMMY_ROWS = 8
TURNS = (4, 2, 1)
SCALE = 1.0 / 128.0
FIELDS = 5
PIVOT_FLOOR = 1e-6
F32 = jnp.float32
BF16 = jnp.bfloat16

COS_TERMS = [(-1.0) ** i * math.pi ** (2 * i) / math.factorial(2 * i) for i in range(8)]
SIN_TERMS = [(-1.0) ** i * math.pi ** (2 * i + 1) / math.factorial(2 * i + 1) for i in range(7)]


def params(mebibytes):
    return pltpu.CompilerParams(vmem_limit_bytes=mebibytes * 1024 * 1024)


def place(x):
    return pl.BlockSpec(memory_space=pltpu.VMEM)


def split(x):
    high = x.astype(BF16)
    low = (x - high.astype(F32)).astype(BF16)
    return high, low


def flat_first(ref, field, fold, rows):
    parts = []
    for j in range(ref.shape[0] * fold):
        start = (j % fold * FIELDS + field) * rows
        parts.append(ref[j // fold, start : start + rows])
    return jnp.concatenate(parts, axis=0)


def flat_second(ref, field, rows):
    start = field * rows
    return jnp.concatenate([ref[j, start : start + rows] for j in range(ref.shape[0])], axis=0)


def flat(ref, field, chunks):
    return jnp.concatenate([ref[j, field] for j in range(chunks)], axis=0)


def local_id(ids, owned):
    if owned & (owned - 1) == 0:
        return ids & (owned - 1)
    return lax.rem(ids, owned)


def pack_kernel(
    na, nd, owned_asc, coef_in, ca_in, cd_in, ta_in, td_in, height_in, fill_in, out,
    coef, ca, cd, ta, td, height, fill, turned, sems,
):
    copies = [
        pltpu.make_async_copy(source, target, sems.at[i])
        for i, (source, target) in enumerate(
            [
                (fill_in, fill), (ca_in, ca), (ta_in, ta),
                (cd_in, cd), (td_in, td), (height_in, height), (coef_in, coef),
            ]
        )
    ]
    for copy in copies:
        copy.start()
    copies[0].wait()
    owned_desc = coef.shape[0]
    blocks, width = ca.shape
    group = width // na
    rows = blocks // na
    fill_row = fill[...]
    row_id = lax.broadcasted_iota(jnp.int32, (blocks, blocks), 0)
    col_id = lax.broadcasted_iota(jnp.int32, (blocks, blocks), 1)
    fill_col = jnp.sum(
        jnp.where(row_id == col_id, fill_row, 0).astype(F32), axis=1, keepdims=True
    )
    lane = lax.broadcasted_iota(jnp.int32, (blocks, width), 1)
    live = lane.astype(F32) < fill_col
    fields = [
        lambda: jnp.where(live, local_id(ca[...], owned_asc).astype(F32), -1.0),
        lambda: ta[...],
        lambda: jnp.where(live, local_id(cd[...], owned_desc).astype(F32), -1.0),
        lambda: td[...],
        lambda: height[...],
    ]
    source = lax.broadcasted_iota(jnp.int32, (width, width), 0)
    target = lax.broadcasted_iota(jnp.int32, (width, width), 1)
    owner = target // group
    place = target - owner * group
    order = (source == place * na + owner).astype(F32).astype(BF16)
    for f, field in enumerate(fields):
        copies[1 + f].wait()
        x = field()
        high = x.astype(BF16)
        rest = x - high.astype(F32)
        middle = rest.astype(BF16)
        low = (rest - middle.astype(F32)).astype(BF16)
        turned[f] = (
            jnp.dot(high, order, preferred_element_type=F32)
            + jnp.dot(middle, order, preferred_element_type=F32)
        ) + jnp.dot(low, order, preferred_element_type=F32)
    lane_group = lax.broadcasted_iota(jnp.int32, (rows, width), 1) // group
    for f in range(FIELDS):
        parts = [None] * na
        for k in range(na):
            piece = turned[f, pl.ds(k, rows, stride=na), :]
            for r in range(na):
                amount = ((k - r) * group) % width
                moved = pltpu.roll(piece, amount, 1) if amount else piece
                parts[r] = moved if k == 0 else jnp.where(lane_group == k, moved, parts[r])
        for r in range(na):
            start = (r // nd * FIELDS + f) * rows
            out[r % nd, start : start + rows] = parts[r]
    copies[-1].wait()
    for q in range(nd):
        out[q, out.shape[1] - owned_desc :] = coef[...]


def cos_sin_pi(x):
    turns = jnp.floor(x + 0.5)
    f = x - turns
    sign = 1.0 - 2.0 * (turns - 2.0 * jnp.floor(turns * 0.5))
    u = f * f
    c = COS_TERMS[-1]
    for term in COS_TERMS[-2::-1]:
        c = c * u + term
    s = SIN_TERMS[-1]
    for term in SIN_TERMS[-2::-1]:
        s = s * u + term
    return c * sign, s * (f * sign)


def rows_pair(ref, rows):
    return jnp.concatenate([ref[pl.ds(r, 1), :] for r in rows], axis=1)


def used_rows(ids_ref, chunks, rows, table):
    count = jnp.int32(0)
    level = lax.broadcasted_iota(jnp.int32, (rows, LANES), 0).astype(F32) + 1.0
    for j in range(chunks):
        ids = ids_ref[j * rows : (j + 1) * rows, :]
        used = jnp.max(jnp.where(ids >= 0.0, level, 0.0)).astype(jnp.int32)
        for i in range(rows):
            table[count + i] = j * rows + i
        count = count + used
    for i in range(BLOCK_ROWS):
        table[count + i] = chunks * rows
    table[table.shape[0] - 1] = lax.div(count + (BLOCK_ROWS - 1), BLOCK_ROWS)


def listed_rows(table, first, count):
    return [table[first + i] for i in range(count)]


def over_blocks(table, step, carry):
    blocks = table[table.shape[0] - 1]
    done = jnp.int32(0)
    for size in TURNS:
        turns = lax.div(blocks - done, size)

        def turn(i, carry, done=done, size=size):
            for u in range(size):
                carry = step(done + i * size + u, carry)
            return carry

        carry = lax.fori_loop(0, turns, turn, carry)
        done = done + turns * size
    return carry


def stacked(field):
    high, low = split(field)
    top = jnp.concatenate([high, high], axis=1)
    bottom = jnp.concatenate([low, jnp.zeros_like(low)], axis=1)
    return jnp.concatenate([top, bottom], axis=0)


def forward_step(stack, phi, ids_row, row_iota, owned):
    both = jnp.dot(stack, phi, preferred_element_type=F32)
    value = both[:owned] + both[owned:]
    return jnp.sum(jnp.where(row_iota == ids_row, value, 0.0), axis=0, keepdims=True)


def store_rows(ref, rows, value):
    for i, r in enumerate(rows):
        ref[pl.ds(r, 1), :] = value[:, i * LANES : (i + 1) * LANES]


def basis_loop(table, ids_ref, time_ref, coef, phi_ref, value_ref):
    owned, terms = coef.shape
    half = terms // 2
    value_ref[...] = jnp.zeros(value_ref.shape, F32)
    width = STEP_LANES
    stack = stacked(coef)
    row_iota = lax.broadcasted_iota(jnp.int32, (owned, width), 0).astype(F32)
    fine = (lax.broadcasted_iota(jnp.int32, (8, width), 0) + 1).astype(F32)
    coarse = (lax.broadcasted_iota(jnp.int32, (half // 8, width), 0) * 8).astype(F32)

    def step(block, u):
        rows = listed_rows(table, block * BLOCK_ROWS + u * STEP_ROWS, STEP_ROWS)
        times = rows_pair(time_ref, rows)
        cos_fine, sin_fine = cos_sin_pi(fine * times)
        cos_coarse, sin_coarse = cos_sin_pi(coarse * times)
        cos_parts, sin_parts = [], []
        for j in range(half // 8):
            cj = cos_coarse[j : j + 1]
            sj = sin_coarse[j : j + 1]
            cos_parts.append(cj * cos_fine - sj * sin_fine)
            sin_parts.append(sj * cos_fine + cj * sin_fine)
        high, low = split(jnp.concatenate(cos_parts + sin_parts, axis=0))
        phi = jnp.concatenate([high, low], axis=0)
        phi_ref[block, :, u * width : (u + 1) * width] = phi
        value = forward_step(stack, phi, rows_pair(ids_ref, rows), row_iota, owned)
        store_rows(value_ref, rows, value)

    def whole_block(block, carry):
        for u in range(UNROLL):
            step(block, u)
        return carry

    lax.fori_loop(0, table[table.shape[0] - 1], whole_block, 0)


class Role:
    def __init__(self, sign, send, meta, phi, table, z_ref, value_ref, listed=False):
        if not listed:
            rows = (meta.shape[0] - DUMMY_ROWS) // send.shape[0]
            used_rows(meta, send.shape[0], rows, table)
        self.sign = sign
        self.table = table
        self.ids = meta
        self.phi = phi
        self.z_ref = z_ref
        self.value_ref = value_ref
        self.count = meta.shape[0] - DUMMY_ROWS

    def cross(self, mine, other):
        return mine - other if self.sign > 0 else other - mine

    def backward(self, z, owned):
        high = z.astype(BF16).astype(F32)
        self.z_ref[0, : self.count] = high
        self.z_ref[1, : self.count] = z - high
        self.z_ref[:, self.count :] = jnp.zeros((2, DUMMY_ROWS, LANES), F32)
        blocks, double, width = self.phi.shape
        row_iota = lax.broadcasted_iota(jnp.int32, (owned, width), 0).astype(F32)

        def gather(block, carry):
            rows = listed_rows(self.table, block * BLOCK_ROWS, BLOCK_ROWS)
            hit = row_iota == rows_pair(self.ids, rows)
            parts = [
                jnp.where(hit, rows_pair(self.z_ref.at[k], rows), 0.0).astype(BF16)
                for k in range(2)
            ]
            return carry + lax.dot_general(
                jnp.concatenate(parts, axis=0),
                self.phi[block],
                (((1,), (1,)), ((), ())),
                preferred_element_type=F32,
            )

        return self.gathered(over_blocks(self.table, gather, jnp.zeros((2 * owned, double), F32)))

    def gathered(self, g):
        owned, terms = g.shape[0] // 2, g.shape[1] // 2
        return self.sign * (g[:owned, :terms] + (g[:owned, terms:] + g[owned:, :terms]))

    def forward(self, field):
        owned = field.shape[0]
        stack = stacked(field)
        row_iota = lax.broadcasted_iota(jnp.int32, (owned, STEP_LANES), 0).astype(F32)
        self.value_ref[...] = jnp.zeros(self.value_ref.shape, F32)

        def ahead(block, carry):
            for u in range(UNROLL):
                rows = listed_rows(self.table, block * BLOCK_ROWS + u * STEP_ROWS, STEP_ROWS)
                phi = self.phi[block, :, u * STEP_LANES : (u + 1) * STEP_LANES]
                value = forward_step(stack, phi, rows_pair(self.ids, rows), row_iota, owned)
                store_rows(self.value_ref, rows, value)
            return carry

        over_blocks(self.table, ahead, 0)
        return self.value_ref[: self.count]

    def forward_image(self, field, other, weight):
        owned = field.shape[0]
        stack = stacked(field)
        blocks, double, width = self.phi.shape
        row_iota = lax.broadcasted_iota(jnp.int32, (owned, width), 0).astype(F32)
        fill_padded(self.z_ref.at[0], other)
        fill_padded(self.z_ref.at[1], weight)
        self.value_ref[...] = jnp.zeros(self.value_ref.shape, F32)

        def both(block, carry):
            rows = listed_rows(self.table, block * BLOCK_ROWS, BLOCK_ROWS)
            phi = self.phi[block]
            hit = row_iota == rows_pair(self.ids, rows)
            values = []
            for u in range(UNROLL):
                part = slice(u * STEP_LANES, (u + 1) * STEP_LANES)
                product = jnp.dot(stack, phi[:, part], preferred_element_type=F32)
                value = product[:owned] + product[owned:]
                values.append(
                    jnp.sum(jnp.where(hit[:, part], value, 0.0), axis=0, keepdims=True)
                )
            value = jnp.concatenate(values, axis=1)
            store_rows(self.value_ref, rows, value)
            z = rows_pair(self.z_ref.at[1], rows) * self.cross(
                value, rows_pair(self.z_ref.at[0], rows)
            )
            high = z.astype(BF16).astype(F32)
            parts = [jnp.where(hit, x, 0.0).astype(BF16) for x in (high, z - high)]
            return carry + lax.dot_general(
                jnp.concatenate(parts, axis=0),
                phi,
                (((1,), (1,)), ((), ())),
                preferred_element_type=F32,
            )

        image = self.gathered(
            over_blocks(self.table, both, jnp.zeros((2 * owned, double), F32))
        )
        return self.value_ref[: self.count], SCALE * (image + damping * field)

    def weigh(self, residual):
        live = self.ids[: self.count] >= 0.0
        misfit = jnp.where(live, residual, 0.0)
        weight = jnp.where(live, 1.0 / (1.0 + misfit * misfit / cauchy_square), 0.0)
        return weight, weight * misfit

    def gradient(self, z, state):
        return self.backward(z, state.shape[0]) - damping * state

    def image(self, z, before):
        return SCALE * (self.backward(z, before.shape[0]) + damping * before)


def write_chunks(send, first, values):
    chunks, rows = send.shape[0], send.shape[2]
    for j in range(chunks):
        send[j, first] = values[j * rows : (j + 1) * rows, :]


def fill_padded(ref, values):
    count = values.shape[0]
    ref[:count] = values
    ref[count:] = jnp.zeros((ref.shape[0] - count,) + values.shape[1:], F32)


def setup_asc_kernel(
    fold, rows, packed, coef, meta, phi, state, short, onward, times, table, value_ref
):
    state[...] = coef[...]
    chunks = packed.shape[0] * fold
    count = chunks * rows
    meta[:count] = flat_first(packed, 0, fold, rows)
    meta[count:] = jnp.full((DUMMY_ROWS, LANES), -1.0, F32)
    fill_padded(times, flat_first(packed, 1, fold, rows))
    used_rows(meta, chunks, rows, table)
    basis_loop(table, meta, times, coef[...], phi, value_ref)
    short[...] = flat_first(packed, 4, fold, rows) - value_ref[:count]
    for j in range(chunks):
        base = j % fold * FIELDS
        for f in range(2):
            start = (base + f + 2) * rows
            onward[j, f * rows : (f + 1) * rows] = packed[j // fold, start : start + rows]
        onward[j, 2 * rows : 3 * rows] = short[j * rows : (j + 1) * rows]
        onward[j, 3 * rows :] = packed[j // fold, fold * FIELDS * rows :]


def setup_desc_kernel(
    fold, rows, packed, meta, phi, state, residual, weights, basis_0, value_0, send,
    times, table, z_ref, value_ref,
):
    chunks = packed.shape[0]
    count = chunks * rows
    home = lax.rem(lax.axis_index("asc"), fold) * (chunks // fold) + lax.axis_index("desc")
    state[...] = packed[home, 3 * rows :]
    meta[:count] = flat_second(packed, 0, rows)
    meta[count:] = jnp.full((DUMMY_ROWS, LANES), -1.0, F32)
    fill_padded(times, flat_second(packed, 1, rows))
    used_rows(meta, chunks, rows, table)
    basis_loop(table, meta, times, state[...], phi, value_ref)
    role = Role(-1.0, send, meta, phi, table, z_ref, value_ref, listed=True)
    own = value_ref[:count]
    write_chunks(send, 0, own)
    left = flat_second(packed, 2, rows) + own
    residual[...] = left
    weights[...], z = role.weigh(left)
    basis_0[...] = role.gradient(z, state[...])
    own = role.forward(basis_0[...])
    value_0[...] = own
    write_chunks(send, 1, own)


def first_asc_kernel(
    chunks, got, short, meta, phi, state,
    residual, weights, crossed_0, basis_0, basis_1, value_1, send, table, z_ref, value_ref,
):
    role = Role(1.0, send, meta, phi, table, z_ref, value_ref)
    left = short[...] + flat(got, 0, chunks)
    residual[...] = left
    weights[...], z = role.weigh(left)
    basis_0[...] = role.gradient(z, state[...])
    other = flat(got, 1, chunks)
    own, basis_1[...] = role.forward_image(basis_0[...], other, weights[...])
    write_chunks(send, 0, own)
    crossed_0[...] = role.cross(own, other)
    own = role.forward(basis_1[...])
    value_1[...] = own
    write_chunks(send, 1, own)


def images_kernel(
    sign, chunks, got, value_0, meta, phi, weights, basis_0,
    crossed_0, crossed_1, basis_1, basis_2, value_2, send, table, z_ref, value_ref,
):
    role = Role(sign, send, meta, phi, table, z_ref, value_ref)
    crossed = role.cross(value_0[...], flat(got, 0, chunks))
    crossed_0[...] = crossed
    basis_1[...] = role.image(weights[...] * crossed, basis_0[...])
    other = flat(got, 1, chunks)
    own, basis_2[...] = role.forward_image(basis_1[...], other, weights[...])
    write_chunks(send, 0, own)
    crossed_1[...] = role.cross(own, other)
    own = role.forward(basis_2[...])
    value_2[...] = own
    write_chunks(send, 1, own)


def total(x):
    return jnp.sum(jnp.sum(x, axis=0, keepdims=True), axis=1, keepdims=True)


PAIRS = [(0, 0), (0, 1), (0, 2), (1, 1), (1, 2), (2, 2)]


def gram_kernel(
    sign, chunks, got, value_1, meta, phi, weights, crossed_0, basis_0, basis_1,
    other_0, other_1, other_2,
    crossed_1, crossed_2, basis_2, value_2, scalars, table, z_ref, value_ref,
):
    role = Role(sign, got, meta, phi, table, z_ref, value_ref)
    weight = weights[...]
    crossed = role.cross(value_1[...], flat(got, 0, chunks))
    crossed_1[...] = crossed
    basis_2[...] = role.image(weight * crossed, basis_1[...])
    own = role.forward(basis_2[...])
    value_2[...] = own
    last = role.cross(own, flat(got, 1, chunks))
    crossed_2[...] = last
    values = [crossed_0[...], crossed, last]
    mine = [basis_0[...], basis_1[...], basis_2[...]]
    others = [other_0[...], other_1[...], other_2[...]]
    lane = lax.broadcasted_iota(jnp.int32, (1, LANES), 1)
    line = jnp.zeros((1, LANES), F32)
    for place_in_line, (i, j) in enumerate(PAIRS):
        dots = total(mine[i] * mine[j] + others[i] * others[j])
        curve = total(weight * values[i] * values[j]) + damping * dots
        line = jnp.where(lane == place_in_line, curve, line)
        if i == 0:
            line = jnp.where(lane == len(PAIRS) + j, dots, line)
    for d in range(scalars.shape[0]):
        scalars[d] = line


def solve(scalars):
    summed = scalars[0]
    for d in range(1, scalars.shape[0]):
        summed = summed + scalars[d]
    line = summed
    lane = lax.broadcasted_iota(jnp.int32, (1, LANES), 1)

    def pick(place):
        return jnp.sum(jnp.where(lane == place, line, 0.0), axis=1, keepdims=True)

    g = {pair: pick(place) for place, pair in enumerate(PAIRS)}
    right = [pick(len(PAIRS) + i) for i in range(3)]
    s = [
        jnp.where(g[i, i] > 0.0, lax.rsqrt(jnp.maximum(g[i, i], 1e-37)), 0.0) for i in range(3)
    ]
    l10 = g[0, 1] * s[0] * s[1]
    l20 = g[0, 2] * s[0] * s[2]
    g21 = g[1, 2] * s[1] * s[2]
    c = [right[i] * s[i] for i in range(3)]

    def inverse(pivot):
        good = pivot > PIVOT_FLOOR
        return jnp.where(good, 1.0 / jnp.where(good, pivot, 1.0), 0.0)

    inv1 = inverse(1.0 - l10 * l10)
    t21 = g21 - l20 * l10
    l21 = t21 * inv1
    inv2 = inverse(1.0 - l20 * l20 - l21 * t21)
    u1 = c[1] - l10 * c[0]
    u2 = c[2] - l20 * c[0] - l21 * u1
    x2 = u2 * inv2
    x1 = u1 * inv1 - l21 * x2
    x0 = c[0] - l10 * x1 - l20 * x2
    return [x0 * s[0], x1 * s[1], x2 * s[2]]


def combine(y, parts):
    return y[0] * parts[0] + (y[1] * parts[1] + y[2] * parts[2])


def next_asc_kernel(
    chunks, scalars, meta, phi, residual, crossed_0, crossed_1, crossed_2,
    basis_a0, basis_a1, basis_a2, basis_d0, basis_d1, basis_d2, state_a, state_d, value_2,
    new_a, new_d, shares, weights, basis_0, value_0, send, table, z_ref, value_ref,
):
    role = Role(1.0, send, meta, phi, table, z_ref, value_ref)
    write_chunks(send, 0, value_2[...])
    y = solve(scalars)
    for i in range(3):
        shares[i : i + 1] = jnp.broadcast_to(y[i], (1, LANES))
    left = residual[...] - combine(y, [crossed_0[...], crossed_1[...], crossed_2[...]])
    new_a[...] = state_a[...] + combine(y, [basis_a0[...], basis_a1[...], basis_a2[...]])
    new_d[...] = state_d[...] + combine(y, [basis_d0[...], basis_d1[...], basis_d2[...]])
    weights[...], z = role.weigh(left)
    basis_0[...] = role.gradient(z, new_a[...])
    own = role.forward(basis_0[...])
    value_0[...] = own
    write_chunks(send, 1, own)


def next_desc_kernel(
    chunks, got, shares, meta, phi, residual, crossed_0, crossed_1, value_2, state,
    weights, new_crossed_0, basis_0, basis_1, value_1, send, table, z_ref, value_ref,
):
    role = Role(-1.0, send, meta, phi, table, z_ref, value_ref)
    y = [shares[i : i + 1] for i in range(3)]
    crossed_2 = role.cross(value_2[...], flat(got, 0, chunks))
    left = residual[...] - combine(y, [crossed_0[...], crossed_1[...], crossed_2])
    weights[...], z = role.weigh(left)
    basis_0[...] = role.gradient(z, state[...])
    other = flat(got, 1, chunks)
    own, basis_1[...] = role.forward_image(basis_0[...], other, weights[...])
    write_chunks(send, 0, own)
    new_crossed_0[...] = role.cross(own, other)
    own = role.forward(basis_1[...])
    value_1[...] = own
    write_chunks(send, 1, own)


def final_kernel(scalars, state_a, basis_0, basis_1, basis_2, desc, out_a, out_d):
    y = solve(scalars)
    out_a[...] = state_a[...] + combine(y, [basis_0[...], basis_1[...], basis_2[...]])
    out_d[...] = desc[0] + combine(y, [desc[1], desc[2], desc[3]])


def body(coef_asc, coef_desc, cross_asc, cross_desc, time_asc, time_desc, height, block_fill):
    owned_asc, terms = coef_asc.shape
    owned_desc = coef_desc.shape[0]
    blocks, width = cross_asc.shape
    na = lax.axis_size("asc")
    nd = lax.axis_size("desc")
    fold = na // nd
    rows = blocks * width // na // LANES
    all_rows = na * rows
    all_blocks = -(-all_rows // BLOCK_ROWS)
    shape = jax.ShapeDtypeStruct

    def call(kernel, outs, scratch, *args, in_specs=None, mebibytes=16):
        return pl.pallas_call(
            kernel,
            out_shape=outs,
            in_specs=[place(x) for x in args] if in_specs is None else in_specs,
            out_specs=jax.tree.map(place, outs),
            scratch_shapes=scratch,
            compiler_params=params(mebibytes),
        )(*args)

    to_role = []
    for p in range(na):
        for q in range(nd):
            to_role.append((p * nd + q, (q * fold + p // nd) * nd + p % nd))
    to_native = [(b, a) for a, b in to_role]
    slots = (cross_asc, cross_desc, time_asc, time_desc, height)
    packed = call(
        functools.partial(pack_kernel, na, nd, owned_asc),
        shape((nd, fold * FIELDS * rows + owned_desc, LANES), F32),
        [pltpu.VMEM(coef_desc.shape, F32)]
        + [pltpu.VMEM((blocks, width), x.dtype) for x in slots]
        + [
            pltpu.VMEM((1, blocks), jnp.int32),
            pltpu.VMEM((FIELDS, blocks, width), F32),
            pltpu.SemaphoreType.DMA((len(slots) + 2,)),
        ],
        coef_desc, *slots, block_fill.reshape(1, blocks),
        in_specs=[pl.BlockSpec(memory_space=pltpu.HBM)] * (len(slots) + 2),
        mebibytes=60,
    )
    at_asc = lax.all_to_all(packed, "desc", split_axis=0, concat_axis=0, tiled=True)

    padded = all_rows + DUMMY_ROWS
    meta_shape = shape((padded, LANES), F32)
    phi_shape = shape((all_blocks, 2 * terms, BLOCK_ROWS * LANES), BF16)
    role_shapes = [meta_shape, phi_shape]
    table = pltpu.SMEM((all_rows + rows + BLOCK_ROWS + 1,), jnp.int32)
    slot_shape = shape((all_rows, LANES), F32)
    send_shape = shape((na, 2, rows, LANES), F32)
    field_a = shape(coef_asc.shape, F32)
    field_d = shape(coef_desc.shape, F32)
    line_shape = shape((na * nd, 1, LANES), F32)
    times_scratch = pltpu.VMEM((padded, LANES), F32)
    scratch = [
        table, pltpu.VMEM((2, padded, LANES), F32), pltpu.VMEM((padded, LANES), F32),
    ]

    def exchange(x):
        return lax.all_to_all(x, "asc", split_axis=0, concat_axis=0, tiled=True)

    def share(x):
        return lax.all_to_all(x, ("asc", "desc"), split_axis=0, concat_axis=0, tiled=True)

    *asc, state_a, short, onward = call(
        functools.partial(setup_asc_kernel, fold, rows),
        role_shapes + [field_a, slot_shape, shape((na, 3 * rows + owned_desc, LANES), F32)],
        [times_scratch, table, scratch[2]],
        at_asc, coef_asc,
    )
    *desc, state_d, residual_d, weights_d, d0, own_d, send = call(
        functools.partial(setup_desc_kernel, fold, rows),
        role_shapes + [field_d, slot_shape, slot_shape, field_d, slot_shape, send_shape],
        [times_scratch] + scratch,
        exchange(onward),
    )
    residual_a, weights_a, crossed_a0, a0, a1, own_a, send = call(
        functools.partial(first_asc_kernel, na),
        [slot_shape, slot_shape, slot_shape, field_a, field_a, slot_shape, send_shape],
        scratch,
        exchange(send), short, *asc, state_a,
    )
    crossed_d0, crossed_d1, d1, d2, own_d, send = call(
        functools.partial(images_kernel, -1.0, na),
        [slot_shape, slot_shape, field_d, field_d, slot_shape, send_shape],
        scratch,
        exchange(send), own_d, *desc, weights_d, d0,
    )
    crossed_a1, crossed_a2, a2, own_a, scalars = call(
        functools.partial(gram_kernel, 1.0, na),
        [slot_shape, slot_shape, field_a, slot_shape, line_shape],
        scratch,
        exchange(send), own_a, *asc, weights_a, crossed_a0, a0, a1, d0, d1, d2,
    )
    state_a, state_d, shares, weights_a, a0, own_a, send = call(
        functools.partial(next_asc_kernel, na),
        [
            field_a, field_d, shape((8, LANES), F32),
            slot_shape, field_a, slot_shape, send_shape,
        ],
        scratch,
        share(scalars), *asc, residual_a, crossed_a0, crossed_a1, crossed_a2,
        a0, a1, a2, d0, d1, d2, state_a, state_d, own_a,
    )
    weights_d, crossed_d0, d0, d1, own_d, send = call(
        functools.partial(next_desc_kernel, na),
        [slot_shape, slot_shape, field_d, field_d, slot_shape, send_shape],
        scratch,
        exchange(send), shares, *desc, residual_d, crossed_d0, crossed_d1, own_d, state_d,
    )
    _, _, a1, a2, _, send = call(
        functools.partial(images_kernel, 1.0, na),
        [slot_shape, slot_shape, field_a, field_a, slot_shape, send_shape],
        scratch,
        exchange(send), own_a, *asc, weights_a, a0,
    )
    _, _, d2, _, scalars = call(
        functools.partial(gram_kernel, -1.0, na),
        [slot_shape, slot_shape, field_d, slot_shape, line_shape],
        scratch,
        exchange(send), own_d, *desc, weights_d, crossed_d0, d0, d1, a0, a1, a2,
    )
    leaving = jnp.stack([state_d, d0, d1, d2])
    native = lax.ppermute(leaving, ("asc", "desc"), to_native)
    return tuple(
        call(
            final_kernel,
            [field_a, field_d],
            [],
            share(scalars), state_a, a0, a1, a2, native,
        )
    )


def solution(mesh):
    split_rows = P(("asc", "desc"), None)
    return jax.shard_map(
        body,
        mesh=mesh,
        in_specs=(split_rows,) * 7 + (P(("asc", "desc")),),
        out_specs=(split_rows, split_rows),
        check_vma=False,
    )
```

```python
import functools
import math

import jax
import jax.numpy as jnp
from jax import lax
from jax.experimental import pallas as pl
from jax.experimental.pallas import tpu as pltpu
from jax.sharding import PartitionSpec as P

GN_STEPS = 2
damping = 2.0
cauchy_square = 2.25

LANES = 128
STEP_ROWS = 2
UNROLL = 4
BLOCK_ROWS = STEP_ROWS * UNROLL
STEP_LANES = STEP_ROWS * LANES
DUMMY_ROWS = 8
TURNS = (5, 4, 3, 2, 1)
SCALE = 1.0 / 128.0
FIELDS = 5
PIVOT_FLOOR = 1e-6
F32 = jnp.float32
BF16 = jnp.bfloat16

COS_TERMS = [(-1.0) ** i * math.pi ** (2 * i) / math.factorial(2 * i) for i in range(8)]
SIN_TERMS = [(-1.0) ** i * math.pi ** (2 * i + 1) / math.factorial(2 * i + 1) for i in range(7)]


def params(mebibytes):
    return pltpu.CompilerParams(vmem_limit_bytes=mebibytes * 1024 * 1024)


def place(x):
    return pl.BlockSpec(memory_space=pltpu.VMEM)


def split(x):
    high = x.astype(BF16)
    low = (x - high.astype(F32)).astype(BF16)
    return high, low


def flat_first(ref, field, fold, rows):
    parts = []
    for j in range(ref.shape[0] * fold):
        start = (j % fold * FIELDS + field) * rows
        parts.append(ref[j // fold, start : start + rows])
    return jnp.concatenate(parts, axis=0)


def flat_second(ref, field, rows):
    start = field * rows
    return jnp.concatenate([ref[j, start : start + rows] for j in range(ref.shape[0])], axis=0)


def flat(ref, field, chunks):
    return jnp.concatenate([ref[j, field] for j in range(chunks)], axis=0)


def local_id(ids, owned):
    if owned & (owned - 1) == 0:
        return ids & (owned - 1)
    return lax.rem(ids, owned)


def pack_kernel(
    na, nd, owned_asc, coef_in, ca_in, cd_in, ta_in, td_in, height_in, fill_in, out,
    coef, ca, cd, ta, td, height, fill, turned, sems,
):
    copies = [
        pltpu.make_async_copy(source, target, sems.at[i])
        for i, (source, target) in enumerate(
            [
                (fill_in, fill), (ca_in, ca), (ta_in, ta),
                (cd_in, cd), (td_in, td), (height_in, height), (coef_in, coef),
            ]
        )
    ]
    for copy in copies:
        copy.start()
    for copy in copies:
        copy.wait()
    owned_desc = coef.shape[0]
    blocks, width = ca.shape
    group = width // na
    rows = blocks // na
    fill_row = fill[...]
    row_id = lax.broadcasted_iota(jnp.int32, (blocks, blocks), 0)
    col_id = lax.broadcasted_iota(jnp.int32, (blocks, blocks), 1)
    fill_col = jnp.sum(
        jnp.where(row_id == col_id, fill_row, 0).astype(F32), axis=1, keepdims=True
    )
    lane = lax.broadcasted_iota(jnp.int32, (blocks, width), 1)
    live = lane.astype(F32) < fill_col
    fields = [
        lambda: jnp.where(live, local_id(ca[...], owned_asc).astype(F32), -1.0),
        lambda: ta[...],
        lambda: jnp.where(live, local_id(cd[...], owned_desc).astype(F32), -1.0),
        lambda: td[...],
        lambda: height[...],
    ]
    source = lax.broadcasted_iota(jnp.int32, (width, width), 0)
    target = lax.broadcasted_iota(jnp.int32, (width, width), 1)
    owner = target // group
    place = target - owner * group
    order = (source == place * na + owner).astype(F32).astype(BF16)
    for f, field in enumerate(fields):
        x = field()
        high = x.astype(BF16)
        rest = x - high.astype(F32)
        middle = rest.astype(BF16)
        low = (rest - middle.astype(F32)).astype(BF16)
        turned[f] = (
            jnp.dot(high, order, preferred_element_type=F32)
            + jnp.dot(middle, order, preferred_element_type=F32)
        ) + jnp.dot(low, order, preferred_element_type=F32)
    lane_group = lax.broadcasted_iota(jnp.int32, (rows, width), 1) // group
    for f in range(FIELDS):
        parts = [None] * na
        for k in range(na):
            piece = turned[f, pl.ds(k, rows, stride=na), :]
            for r in range(na):
                amount = ((k - r) * group) % width
                moved = pltpu.roll(piece, amount, 1) if amount else piece
                parts[r] = moved if k == 0 else jnp.where(lane_group == k, moved, parts[r])
        for r in range(na):
            start = (r // nd * FIELDS + f) * rows
            out[r % nd, start : start + rows] = parts[r]
    for q in range(nd):
        out[q, out.shape[1] - owned_desc :] = coef[...]


def cos_sin_pi(x):
    turns = jnp.floor(x + 0.5)
    f = x - turns
    sign = 1.0 - 2.0 * (turns - 2.0 * jnp.floor(turns * 0.5))
    u = f * f
    c = COS_TERMS[-1]
    for term in COS_TERMS[-2::-1]:
        c = c * u + term
    s = SIN_TERMS[-1]
    for term in SIN_TERMS[-2::-1]:
        s = s * u + term
    return c * sign, s * (f * sign)


def rows_pair(ref, rows):
    return jnp.concatenate([ref[pl.ds(r, 1), :] for r in rows], axis=1)


def used_rows(ids_ref, chunks, rows, table):
    count = jnp.int32(0)
    level = lax.broadcasted_iota(jnp.int32, (rows, LANES), 0).astype(F32) + 1.0
    for j in range(chunks):
        ids = ids_ref[j * rows : (j + 1) * rows, :]
        used = jnp.max(jnp.where(ids >= 0.0, level, 0.0)).astype(jnp.int32)
        for i in range(rows):
            table[count + i] = j * rows + i
        count = count + used
    for i in range(BLOCK_ROWS):
        table[count + i] = chunks * rows
    table[table.shape[0] - 1] = lax.div(count + (BLOCK_ROWS - 1), BLOCK_ROWS)


def listed_rows(table, first, count):
    return [table[first + i] for i in range(count)]


def over_blocks(table, step, carry):
    blocks = table[table.shape[0] - 1]
    done = jnp.int32(0)
    for size in TURNS:
        turns = lax.div(blocks - done, size)

        def turn(i, carry, done=done, size=size):
            for u in range(size):
                carry = step(done + i * size + u, carry)
            return carry

        carry = lax.fori_loop(0, turns, turn, carry)
        done = done + turns * size
    return carry


def stacked(field):
    high, low = split(field)
    top = jnp.concatenate([high, high], axis=1)
    bottom = jnp.concatenate([low, jnp.zeros_like(low)], axis=1)
    return jnp.concatenate([top, bottom], axis=0)


def forward_step(stack, phi, ids_row, row_iota, owned):
    both = jnp.dot(stack, phi, preferred_element_type=F32)
    value = both[:owned] + both[owned:]
    return jnp.sum(jnp.where(row_iota == ids_row, value, 0.0), axis=0, keepdims=True)


def store_rows(ref, rows, value):
    for i, r in enumerate(rows):
        ref[pl.ds(r, 1), :] = value[:, i * LANES : (i + 1) * LANES]


def basis_loop(table, ids_ref, time_ref, coef, phi_ref, value_ref):
    owned, terms = coef.shape
    half = terms // 2
    value_ref[...] = jnp.zeros(value_ref.shape, F32)
    width = STEP_LANES
    stack = stacked(coef)
    row_iota = lax.broadcasted_iota(jnp.int32, (owned, width), 0).astype(F32)
    fine = (lax.broadcasted_iota(jnp.int32, (8, width), 0) + 1).astype(F32)
    coarse = (lax.broadcasted_iota(jnp.int32, (half // 8, width), 0) * 8).astype(F32)

    def step(block, u):
        rows = listed_rows(table, block * BLOCK_ROWS + u * STEP_ROWS, STEP_ROWS)
        times = rows_pair(time_ref, rows)
        cos_fine, sin_fine = cos_sin_pi(fine * times)
        cos_coarse, sin_coarse = cos_sin_pi(coarse * times)
        cos_parts, sin_parts = [], []
        for j in range(half // 8):
            cj = cos_coarse[j : j + 1]
            sj = sin_coarse[j : j + 1]
            cos_parts.append(cj * cos_fine - sj * sin_fine)
            sin_parts.append(sj * cos_fine + cj * sin_fine)
        high, low = split(jnp.concatenate(cos_parts + sin_parts, axis=0))
        phi = jnp.concatenate([high, low], axis=0)
        phi_ref[block, :, u * width : (u + 1) * width] = phi
        value = forward_step(stack, phi, rows_pair(ids_ref, rows), row_iota, owned)
        store_rows(value_ref, rows, value)

    def whole_block(block, carry):
        for u in range(UNROLL):
            step(block, u)
        return carry

    lax.fori_loop(0, table[table.shape[0] - 1], whole_block, 0)


class Role:
    def __init__(self, sign, send, meta, phi, table, z_ref, value_ref, listed=False):
        if not listed:
            rows = (meta.shape[0] - DUMMY_ROWS) // send.shape[0]
            used_rows(meta, send.shape[0], rows, table)
        self.sign = sign
        self.table = table
        self.ids = meta
        self.phi = phi
        self.z_ref = z_ref
        self.value_ref = value_ref
        self.count = meta.shape[0] - DUMMY_ROWS

    def cross(self, mine, other):
        return mine - other if self.sign > 0 else other - mine

    def backward(self, z, owned):
        high = z.astype(BF16).astype(F32)
        self.z_ref[0, : self.count] = high
        self.z_ref[1, : self.count] = z - high
        self.z_ref[:, self.count :] = jnp.zeros((2, DUMMY_ROWS, LANES), F32)
        blocks, double, width = self.phi.shape
        row_iota = lax.broadcasted_iota(jnp.int32, (owned, width), 0).astype(F32)

        def gather(block, carry):
            rows = listed_rows(self.table, block * BLOCK_ROWS, BLOCK_ROWS)
            hit = row_iota == rows_pair(self.ids, rows)
            parts = [
                jnp.where(hit, rows_pair(self.z_ref.at[k], rows), 0.0).astype(BF16)
                for k in range(2)
            ]
            return carry + lax.dot_general(
                jnp.concatenate(parts, axis=0),
                self.phi[block],
                (((1,), (1,)), ((), ())),
                preferred_element_type=F32,
            )

        return self.gathered(over_blocks(self.table, gather, jnp.zeros((2 * owned, double), F32)))

    def gathered(self, g):
        owned, terms = g.shape[0] // 2, g.shape[1] // 2
        return self.sign * (g[:owned, :terms] + (g[:owned, terms:] + g[owned:, :terms]))

    def forward(self, field):
        owned = field.shape[0]
        stack = stacked(field)
        row_iota = lax.broadcasted_iota(jnp.int32, (owned, STEP_LANES), 0).astype(F32)
        self.value_ref[...] = jnp.zeros(self.value_ref.shape, F32)

        def ahead(block, carry):
            for u in range(UNROLL):
                rows = listed_rows(self.table, block * BLOCK_ROWS + u * STEP_ROWS, STEP_ROWS)
                phi = self.phi[block, :, u * STEP_LANES : (u + 1) * STEP_LANES]
                value = forward_step(stack, phi, rows_pair(self.ids, rows), row_iota, owned)
                store_rows(self.value_ref, rows, value)
            return carry

        over_blocks(self.table, ahead, 0)
        return self.value_ref[: self.count]

    def forward_image(self, field, other, weight):
        owned = field.shape[0]
        stack = stacked(field)
        blocks, double, width = self.phi.shape
        row_iota = lax.broadcasted_iota(jnp.int32, (owned, width), 0).astype(F32)
        fill_padded(self.z_ref.at[0], other)
        fill_padded(self.z_ref.at[1], weight)
        self.value_ref[...] = jnp.zeros(self.value_ref.shape, F32)

        def both(block, carry):
            rows = listed_rows(self.table, block * BLOCK_ROWS, BLOCK_ROWS)
            phi = self.phi[block]
            hit = row_iota == rows_pair(self.ids, rows)
            values = []
            for u in range(UNROLL):
                part = slice(u * STEP_LANES, (u + 1) * STEP_LANES)
                product = jnp.dot(stack, phi[:, part], preferred_element_type=F32)
                value = product[:owned] + product[owned:]
                values.append(
                    jnp.sum(jnp.where(hit[:, part], value, 0.0), axis=0, keepdims=True)
                )
            value = jnp.concatenate(values, axis=1)
            store_rows(self.value_ref, rows, value)
            z = rows_pair(self.z_ref.at[1], rows) * self.cross(
                value, rows_pair(self.z_ref.at[0], rows)
            )
            high = z.astype(BF16).astype(F32)
            parts = [jnp.where(hit, x, 0.0).astype(BF16) for x in (high, z - high)]
            return carry + lax.dot_general(
                jnp.concatenate(parts, axis=0),
                phi,
                (((1,), (1,)), ((), ())),
                preferred_element_type=F32,
            )

        image = self.gathered(
            over_blocks(self.table, both, jnp.zeros((2 * owned, double), F32))
        )
        return self.value_ref[: self.count], SCALE * (image + damping * field)

    def weigh(self, residual):
        live = self.ids[: self.count] >= 0.0
        misfit = jnp.where(live, residual, 0.0)
        weight = jnp.where(live, 1.0 / (1.0 + misfit * misfit / cauchy_square), 0.0)
        return weight, weight * misfit

    def gradient(self, z, state):
        return self.backward(z, state.shape[0]) - damping * state

    def image(self, z, before):
        return SCALE * (self.backward(z, before.shape[0]) + damping * before)


def write_chunks(send, first, values):
    chunks, rows = send.shape[0], send.shape[2]
    for j in range(chunks):
        send[j, first] = values[j * rows : (j + 1) * rows, :]


def fill_padded(ref, values):
    count = values.shape[0]
    ref[:count] = values
    ref[count:] = jnp.zeros((ref.shape[0] - count,) + values.shape[1:], F32)


def setup_asc_kernel(
    fold, rows, packed, coef, meta, phi, state, short, onward, times, table, value_ref
):
    state[...] = coef[...]
    chunks = packed.shape[0] * fold
    count = chunks * rows
    meta[:count] = flat_first(packed, 0, fold, rows)
    meta[count:] = jnp.full((DUMMY_ROWS, LANES), -1.0, F32)
    fill_padded(times, flat_first(packed, 1, fold, rows))
    used_rows(meta, chunks, rows, table)
    basis_loop(table, meta, times, coef[...], phi, value_ref)
    short[...] = flat_first(packed, 4, fold, rows) - value_ref[:count]
    for j in range(chunks):
        base = j % fold * FIELDS
        for f in range(2):
            start = (base + f + 2) * rows
            onward[j, f * rows : (f + 1) * rows] = packed[j // fold, start : start + rows]
        onward[j, 2 * rows : 3 * rows] = short[j * rows : (j + 1) * rows]
        onward[j, 3 * rows :] = packed[j // fold, fold * FIELDS * rows :]


def setup_desc_kernel(
    fold, rows, packed, meta, phi, state, residual, weights, basis_0, value_0, send,
    times, table, z_ref, value_ref,
):
    chunks = packed.shape[0]
    count = chunks * rows
    home = lax.rem(lax.axis_index("asc"), fold) * (chunks // fold) + lax.axis_index("desc")
    state[...] = packed[home, 3 * rows :]
    meta[:count] = flat_second(packed, 0, rows)
    meta[count:] = jnp.full((DUMMY_ROWS, LANES), -1.0, F32)
    fill_padded(times, flat_second(packed, 1, rows))
    used_rows(meta, chunks, rows, table)
    basis_loop(table, meta, times, state[...], phi, value_ref)
    role = Role(-1.0, send, meta, phi, table, z_ref, value_ref, listed=True)
    own = value_ref[:count]
    write_chunks(send, 0, own)
    left = flat_second(packed, 2, rows) + own
    residual[...] = left
    weights[...], z = role.weigh(left)
    basis_0[...] = role.gradient(z, state[...])
    own = role.forward(basis_0[...])
    value_0[...] = own
    write_chunks(send, 1, own)


def first_asc_kernel(
    chunks, got, short, meta, phi, state,
    residual, weights, crossed_0, basis_0, basis_1, value_1, send, table, z_ref, value_ref,
):
    role = Role(1.0, send, meta, phi, table, z_ref, value_ref)
    left = short[...] + flat(got, 0, chunks)
    residual[...] = left
    weights[...], z = role.weigh(left)
    basis_0[...] = role.gradient(z, state[...])
    other = flat(got, 1, chunks)
    own, basis_1[...] = role.forward_image(basis_0[...], other, weights[...])
    write_chunks(send, 0, own)
    crossed_0[...] = role.cross(own, other)
    own = role.forward(basis_1[...])
    value_1[...] = own
    write_chunks(send, 1, own)


def images_kernel(sign, chunks, keep, got, value_0, meta, phi, weights, basis_0, *rest):
    basis_1, basis_2, send, *kept = rest[:-3]
    role = Role(sign, send, meta, phi, *rest[-3:])
    first = role.cross(value_0[...], flat(got, 0, chunks))
    basis_1[...] = role.image(weights[...] * first, basis_0[...])
    other = flat(got, 1, chunks)
    own, basis_2[...] = role.forward_image(basis_1[...], other, weights[...])
    write_chunks(send, 0, own)
    second = role.cross(own, other)
    own = role.forward(basis_2[...])
    write_chunks(send, 1, own)
    if keep:
        crossed_0, crossed_1, value_2 = kept
        crossed_0[...] = first
        crossed_1[...] = second
        value_2[...] = own


def total(x):
    return jnp.sum(jnp.sum(x, axis=0, keepdims=True), axis=1, keepdims=True)


PAIRS = [(0, 0), (0, 1), (0, 2), (1, 1), (1, 2), (2, 2)]


def gram_kernel(
    sign, chunks, keep, got, value_1, meta, phi, weights, crossed_0, basis_0, basis_1,
    other_0, other_1, other_2, *rest,
):
    basis_2, scalars, *kept = rest[:-3]
    role = Role(sign, got, meta, phi, *rest[-3:])
    weight = weights[...]
    crossed = role.cross(value_1[...], flat(got, 0, chunks))
    basis_2[...] = role.image(weight * crossed, basis_1[...])
    own = role.forward(basis_2[...])
    last = role.cross(own, flat(got, 1, chunks))
    if keep:
        crossed_1, crossed_2, value_2 = kept
        crossed_1[...] = crossed
        crossed_2[...] = last
        value_2[...] = own
    values = [crossed_0[...], crossed, last]
    mine = [basis_0[...], basis_1[...], basis_2[...]]
    others = [other_0[...], other_1[...], other_2[...]]
    lane = lax.broadcasted_iota(jnp.int32, (1, LANES), 1)
    line = jnp.zeros((1, LANES), F32)
    for place_in_line, (i, j) in enumerate(PAIRS):
        dots = total(mine[i] * mine[j] + others[i] * others[j])
        curve = total(weight * values[i] * values[j]) + damping * dots
        line = jnp.where(lane == place_in_line, curve, line)
        if i == 0:
            line = jnp.where(lane == len(PAIRS) + j, dots, line)
    for d in range(scalars.shape[0]):
        scalars[d] = line


def solve(scalars):
    summed = scalars[0]
    for d in range(1, scalars.shape[0]):
        summed = summed + scalars[d]
    line = summed
    lane = lax.broadcasted_iota(jnp.int32, (1, LANES), 1)

    def pick(place):
        return jnp.sum(jnp.where(lane == place, line, 0.0), axis=1, keepdims=True)

    g = {pair: pick(place) for place, pair in enumerate(PAIRS)}
    right = [pick(len(PAIRS) + i) for i in range(3)]
    s = [
        jnp.where(g[i, i] > 0.0, lax.rsqrt(jnp.maximum(g[i, i], 1e-37)), 0.0) for i in range(3)
    ]
    l10 = g[0, 1] * s[0] * s[1]
    l20 = g[0, 2] * s[0] * s[2]
    g21 = g[1, 2] * s[1] * s[2]
    c = [right[i] * s[i] for i in range(3)]

    def inverse(pivot):
        good = pivot > PIVOT_FLOOR
        return jnp.where(good, 1.0 / jnp.where(good, pivot, 1.0), 0.0)

    inv1 = inverse(1.0 - l10 * l10)
    t21 = g21 - l20 * l10
    l21 = t21 * inv1
    inv2 = inverse(1.0 - l20 * l20 - l21 * t21)
    u1 = c[1] - l10 * c[0]
    u2 = c[2] - l20 * c[0] - l21 * u1
    x2 = u2 * inv2
    x1 = u1 * inv1 - l21 * x2
    x0 = c[0] - l10 * x1 - l20 * x2
    return [x0 * s[0], x1 * s[1], x2 * s[2]]


def combine(y, parts):
    return y[0] * parts[0] + (y[1] * parts[1] + y[2] * parts[2])


def next_asc_kernel(
    chunks, scalars, meta, phi, residual, crossed_0, crossed_1, crossed_2,
    basis_a0, basis_a1, basis_a2, basis_d0, basis_d1, basis_d2, state_a, state_d, value_2,
    new_a, new_d, shares, weights, basis_0, value_0, send, table, z_ref, value_ref,
):
    role = Role(1.0, send, meta, phi, table, z_ref, value_ref)
    write_chunks(send, 0, value_2[...])
    y = solve(scalars)
    for i in range(3):
        shares[i : i + 1] = jnp.broadcast_to(y[i], (1, LANES))
    left = residual[...] - combine(y, [crossed_0[...], crossed_1[...], crossed_2[...]])
    new_a[...] = state_a[...] + combine(y, [basis_a0[...], basis_a1[...], basis_a2[...]])
    new_d[...] = state_d[...] + combine(y, [basis_d0[...], basis_d1[...], basis_d2[...]])
    weights[...], z = role.weigh(left)
    basis_0[...] = role.gradient(z, new_a[...])
    own = role.forward(basis_0[...])
    value_0[...] = own
    write_chunks(send, 1, own)


def next_desc_kernel(
    chunks, got, shares, meta, phi, residual, crossed_0, crossed_1, value_2, state,
    weights, new_crossed_0, basis_0, basis_1, value_1, send, table, z_ref, value_ref,
):
    role = Role(-1.0, send, meta, phi, table, z_ref, value_ref)
    y = [shares[i : i + 1] for i in range(3)]
    crossed_2 = role.cross(value_2[...], flat(got, 0, chunks))
    left = residual[...] - combine(y, [crossed_0[...], crossed_1[...], crossed_2])
    weights[...], z = role.weigh(left)
    basis_0[...] = role.gradient(z, state[...])
    other = flat(got, 1, chunks)
    own, basis_1[...] = role.forward_image(basis_0[...], other, weights[...])
    write_chunks(send, 0, own)
    new_crossed_0[...] = role.cross(own, other)
    own = role.forward(basis_1[...])
    value_1[...] = own
    write_chunks(send, 1, own)


def final_kernel(scalars, state_a, basis_0, basis_1, basis_2, desc, out_a, out_d):
    y = solve(scalars)
    out_a[...] = state_a[...] + combine(y, [basis_0[...], basis_1[...], basis_2[...]])
    out_d[...] = desc[0] + combine(y, [desc[1], desc[2], desc[3]])


def body(coef_asc, coef_desc, cross_asc, cross_desc, time_asc, time_desc, height, block_fill):
    owned_asc, terms = coef_asc.shape
    owned_desc = coef_desc.shape[0]
    blocks, width = cross_asc.shape
    na = lax.axis_size("asc")
    nd = lax.axis_size("desc")
    fold = na // nd
    rows = blocks * width // na // LANES
    all_rows = na * rows
    all_blocks = -(-all_rows // BLOCK_ROWS)
    shape = jax.ShapeDtypeStruct

    def call(kernel, outs, scratch, *args, in_specs=None, mebibytes=16):
        return pl.pallas_call(
            kernel,
            out_shape=outs,
            in_specs=[place(x) for x in args] if in_specs is None else in_specs,
            out_specs=jax.tree.map(place, outs),
            scratch_shapes=scratch,
            compiler_params=params(mebibytes),
        )(*args)

    to_role = []
    for p in range(na):
        for q in range(nd):
            to_role.append((p * nd + q, (q * fold + p // nd) * nd + p % nd))
    to_native = [(b, a) for a, b in to_role]
    slots = (cross_asc, cross_desc, time_asc, time_desc, height)
    packed = call(
        functools.partial(pack_kernel, na, nd, owned_asc),
        shape((nd, fold * FIELDS * rows + owned_desc, LANES), F32),
        [pltpu.VMEM(coef_desc.shape, F32)]
        + [pltpu.VMEM((blocks, width), x.dtype) for x in slots]
        + [
            pltpu.VMEM((1, blocks), jnp.int32),
            pltpu.VMEM((FIELDS, blocks, width), F32),
            pltpu.SemaphoreType.DMA((len(slots) + 2,)),
        ],
        coef_desc, *slots, block_fill.reshape(1, blocks),
        in_specs=[pl.BlockSpec(memory_space=pltpu.HBM)] * (len(slots) + 2),
        mebibytes=60,
    )
    at_asc = lax.all_to_all(packed, "desc", split_axis=0, concat_axis=0, tiled=True)

    padded = all_rows + DUMMY_ROWS
    meta_shape = shape((padded, LANES), F32)
    phi_shape = shape((all_blocks, 2 * terms, BLOCK_ROWS * LANES), BF16)
    role_shapes = [meta_shape, phi_shape]
    table = pltpu.SMEM((all_rows + rows + BLOCK_ROWS + 1,), jnp.int32)
    slot_shape = shape((all_rows, LANES), F32)
    send_shape = shape((na, 2, rows, LANES), F32)
    field_a = shape(coef_asc.shape, F32)
    field_d = shape(coef_desc.shape, F32)
    line_shape = shape((na * nd, 1, LANES), F32)
    times_scratch = pltpu.VMEM((padded, LANES), F32)
    scratch = [
        table, pltpu.VMEM((2, padded, LANES), F32), pltpu.VMEM((padded, LANES), F32),
    ]

    def exchange(x):
        return lax.all_to_all(x, "asc", split_axis=0, concat_axis=0, tiled=True)

    def share(x):
        return lax.all_to_all(x, ("asc", "desc"), split_axis=0, concat_axis=0, tiled=True)

    *asc, state_a, short, onward = call(
        functools.partial(setup_asc_kernel, fold, rows),
        role_shapes + [field_a, slot_shape, shape((na, 3 * rows + owned_desc, LANES), F32)],
        [times_scratch, table, scratch[2]],
        at_asc, coef_asc,
    )
    *desc, state_d, residual_d, weights_d, d0, own_d, send = call(
        functools.partial(setup_desc_kernel, fold, rows),
        role_shapes + [field_d, slot_shape, slot_shape, field_d, slot_shape, send_shape],
        [times_scratch] + scratch,
        exchange(onward),
    )
    residual_a, weights_a, crossed_a0, a0, a1, own_a, send = call(
        functools.partial(first_asc_kernel, na),
        [slot_shape, slot_shape, slot_shape, field_a, field_a, slot_shape, send_shape],
        scratch,
        exchange(send), short, *asc, state_a,
    )
    kept = [slot_shape] * 3
    d1, d2, send, crossed_d0, crossed_d1, own_d = call(
        functools.partial(images_kernel, -1.0, na, True),
        [field_d, field_d, send_shape] + kept,
        scratch,
        exchange(send), own_d, *desc, weights_d, d0,
    )
    a2, scalars, crossed_a1, crossed_a2, own_a = call(
        functools.partial(gram_kernel, 1.0, na, True),
        [field_a, line_shape] + kept,
        scratch,
        exchange(send), own_a, *asc, weights_a, crossed_a0, a0, a1, d0, d1, d2,
    )
    state_a, state_d, shares, weights_a, a0, own_a, send = call(
        functools.partial(next_asc_kernel, na),
        [
            field_a, field_d, shape((8, LANES), F32),
            slot_shape, field_a, slot_shape, send_shape,
        ],
        scratch,
        share(scalars), *asc, residual_a, crossed_a0, crossed_a1, crossed_a2,
        a0, a1, a2, d0, d1, d2, state_a, state_d, own_a,
    )
    weights_d, crossed_d0, d0, d1, own_d, send = call(
        functools.partial(next_desc_kernel, na),
        [slot_shape, slot_shape, field_d, field_d, slot_shape, send_shape],
        scratch,
        exchange(send), shares, *desc, residual_d, crossed_d0, crossed_d1, own_d, state_d,
    )
    a1, a2, send = call(
        functools.partial(images_kernel, 1.0, na, False),
        [field_a, field_a, send_shape],
        scratch,
        exchange(send), own_a, *asc, weights_a, a0,
    )
    d2, scalars = call(
        functools.partial(gram_kernel, -1.0, na, False),
        [field_d, line_shape],
        scratch,
        exchange(send), own_d, *desc, weights_d, crossed_d0, d0, d1, a0, a1, a2,
    )
    leaving = jnp.stack([state_d, d0, d1, d2])
    native = lax.ppermute(leaving, ("asc", "desc"), to_native)
    return tuple(
        call(
            final_kernel,
            [field_a, field_d],
            [],
            share(scalars), state_a, a0, a1, a2, native,
        )
    )


def solution(mesh):
    split_rows = P(("asc", "desc"), None)
    return jax.shard_map(
        body,
        mesh=mesh,
        in_specs=(split_rows,) * 7 + (P(("asc", "desc")),),
        out_specs=(split_rows, split_rows),
        check_vma=False,
    )
```

```python
import functools
import math

import jax
import jax.numpy as jnp
from jax import lax
from jax.experimental import pallas as pl
from jax.experimental.pallas import tpu as pltpu
from jax.sharding import PartitionSpec as P

GN_STEPS = 2
damping = 2.0
cauchy_square = 2.25

LANES = 128
STEP_ROWS = 2
UNROLL = 4
BLOCK_ROWS = STEP_ROWS * UNROLL
STEP_LANES = STEP_ROWS * LANES
DUMMY_ROWS = 8
TURNS = (4, 1)
SCALE = 1.0 / 128.0
FIELDS = 5
PIVOT_FLOOR = 1e-6
F32 = jnp.float32
BF16 = jnp.bfloat16

COS_TERMS = [(-1.0) ** i * math.pi ** (2 * i) / math.factorial(2 * i) for i in range(8)]
SIN_TERMS = [(-1.0) ** i * math.pi ** (2 * i + 1) / math.factorial(2 * i + 1) for i in range(7)]


def params(mebibytes):
    return pltpu.CompilerParams(vmem_limit_bytes=mebibytes * 1024 * 1024)


def place(x):
    return pl.BlockSpec(memory_space=pltpu.VMEM)


def split(x):
    high = x.astype(BF16)
    low = (x - high.astype(F32)).astype(BF16)
    return high, low


def flat_first(ref, field, fold, rows):
    parts = []
    for j in range(ref.shape[0] * fold):
        start = (j % fold * FIELDS + field) * rows
        parts.append(ref[j // fold, start : start + rows])
    return jnp.concatenate(parts, axis=0)


def flat_second(ref, field, rows):
    start = field * rows
    return jnp.concatenate([ref[j, start : start + rows] for j in range(ref.shape[0])], axis=0)


def flat(ref, field, chunks):
    return jnp.concatenate([ref[j, field] for j in range(chunks)], axis=0)


def local_id(ids, owned):
    if owned & (owned - 1) == 0:
        return ids & (owned - 1)
    return lax.rem(ids, owned)


def pack_kernel(
    na, nd, owned_asc, coef_in, ca_in, cd_in, ta_in, td_in, height_in, fill_in, out,
    coef, ca, cd, ta, td, height, fill, turned, sems,
):
    copies = [
        pltpu.make_async_copy(source, target, sems.at[i])
        for i, (source, target) in enumerate(
            [
                (fill_in, fill), (ca_in, ca), (ta_in, ta),
                (cd_in, cd), (td_in, td), (height_in, height), (coef_in, coef),
            ]
        )
    ]
    for copy in copies:
        copy.start()
    for copy in copies:
        copy.wait()
    owned_desc = coef.shape[0]
    blocks, width = ca.shape
    group = width // na
    rows = blocks // na
    fill_row = fill[...]
    row_id = lax.broadcasted_iota(jnp.int32, (blocks, blocks), 0)
    col_id = lax.broadcasted_iota(jnp.int32, (blocks, blocks), 1)
    fill_col = jnp.sum(
        jnp.where(row_id == col_id, fill_row, 0).astype(F32), axis=1, keepdims=True
    )
    lane = lax.broadcasted_iota(jnp.int32, (blocks, width), 1)
    live = lane.astype(F32) < fill_col
    fields = [
        lambda: jnp.where(live, local_id(ca[...], owned_asc).astype(F32), -1.0),
        lambda: ta[...],
        lambda: jnp.where(live, local_id(cd[...], owned_desc).astype(F32), -1.0),
        lambda: td[...],
        lambda: height[...],
    ]
    source = lax.broadcasted_iota(jnp.int32, (width, width), 0)
    target = lax.broadcasted_iota(jnp.int32, (width, width), 1)
    owner = target // group
    place = target - owner * group
    order = (source == place * na + owner).astype(F32).astype(BF16)
    for f, field in enumerate(fields):
        x = field()
        high = x.astype(BF16)
        rest = x - high.astype(F32)
        middle = rest.astype(BF16)
        low = (rest - middle.astype(F32)).astype(BF16)
        turned[f] = (
            jnp.dot(high, order, preferred_element_type=F32)
            + jnp.dot(middle, order, preferred_element_type=F32)
        ) + jnp.dot(low, order, preferred_element_type=F32)
    lane_group = lax.broadcasted_iota(jnp.int32, (rows, width), 1) // group
    for f in range(FIELDS):
        parts = [None] * na
        for k in range(na):
            piece = turned[f, pl.ds(k, rows, stride=na), :]
            for r in range(na):
                amount = ((k - r) * group) % width
                moved = pltpu.roll(piece, amount, 1) if amount else piece
                parts[r] = moved if k == 0 else jnp.where(lane_group == k, moved, parts[r])
        for r in range(na):
            start = (r // nd * FIELDS + f) * rows
            out[r % nd, start : start + rows] = parts[r]
    for q in range(nd):
        out[q, out.shape[1] - owned_desc :] = coef[...]


def cos_sin_pi(x):
    turns = jnp.floor(x + 0.5)
    f = x - turns
    sign = 1.0 - 2.0 * (turns - 2.0 * jnp.floor(turns * 0.5))
    u = f * f
    c = COS_TERMS[-1]
    for term in COS_TERMS[-2::-1]:
        c = c * u + term
    s = SIN_TERMS[-1]
    for term in SIN_TERMS[-2::-1]:
        s = s * u + term
    return c * sign, s * (f * sign)


def rows_pair(ref, rows):
    return jnp.concatenate([ref[pl.ds(r, 1), :] for r in rows], axis=1)


def used_rows(ids_ref, chunks, rows, table):
    count = jnp.int32(0)
    level = lax.broadcasted_iota(jnp.int32, (rows, LANES), 0).astype(F32) + 1.0
    for j in range(chunks):
        ids = ids_ref[j * rows : (j + 1) * rows, :]
        used = jnp.max(jnp.where(ids >= 0.0, level, 0.0)).astype(jnp.int32)
        for i in range(rows):
            table[count + i] = j * rows + i
        count = count + used
    for i in range(BLOCK_ROWS):
        table[count + i] = chunks * rows
    table[table.shape[0] - 1] = lax.div(count + (BLOCK_ROWS - 1), BLOCK_ROWS)


def listed_rows(table, first, count):
    return [table[first + i] for i in range(count)]


def over_blocks(table, step):
    blocks = table[table.shape[0] - 1]
    done = jnp.int32(0)
    for size in TURNS:
        turns = lax.div(blocks - done, size)

        def turn(i, carry, done=done, size=size):
            step([done + i * size + u for u in range(size)])
            return carry

        lax.fori_loop(0, turns, turn, 0)
        done = done + turns * size


def stacked(field):
    high, low = split(field)
    top = jnp.concatenate([high, high], axis=1)
    bottom = jnp.concatenate([low, jnp.zeros_like(low)], axis=1)
    return jnp.concatenate([top, bottom], axis=0)


def forward_step(stack, phi, ids_row, row_iota, owned):
    both = jnp.dot(stack, phi, preferred_element_type=F32)
    value = both[:owned] + both[owned:]
    return jnp.sum(jnp.where(row_iota == ids_row, value, 0.0), axis=0, keepdims=True)


def store_rows(ref, rows, value):
    for i, r in enumerate(rows):
        ref[pl.ds(r, 1), :] = value[:, i * LANES : (i + 1) * LANES]


def basis_loop(table, ids_ref, time_ref, coef, phi_ref, value_ref):
    owned, terms = coef.shape
    half = terms // 2
    value_ref[...] = jnp.zeros(value_ref.shape, F32)
    width = STEP_LANES
    stack = stacked(coef)
    row_iota = lax.broadcasted_iota(jnp.int32, (owned, width), 0).astype(F32)
    fine = (lax.broadcasted_iota(jnp.int32, (8, width), 0) + 1).astype(F32)
    coarse = (lax.broadcasted_iota(jnp.int32, (half // 8, width), 0) * 8).astype(F32)

    def step(block, u):
        rows = listed_rows(table, block * BLOCK_ROWS + u * STEP_ROWS, STEP_ROWS)
        times = rows_pair(time_ref, rows)
        cos_fine, sin_fine = cos_sin_pi(fine * times)
        cos_coarse, sin_coarse = cos_sin_pi(coarse * times)
        cos_parts, sin_parts = [], []
        for j in range(half // 8):
            cj = cos_coarse[j : j + 1]
            sj = sin_coarse[j : j + 1]
            cos_parts.append(cj * cos_fine - sj * sin_fine)
            sin_parts.append(sj * cos_fine + cj * sin_fine)
        high, low = split(jnp.concatenate(cos_parts + sin_parts, axis=0))
        phi = jnp.concatenate([high, low], axis=0)
        phi_ref[block, :, u * width : (u + 1) * width] = phi
        value = forward_step(stack, phi, rows_pair(ids_ref, rows), row_iota, owned)
        store_rows(value_ref, rows, value)

    def whole_block(block, carry):
        for u in range(UNROLL):
            step(block, u)
        return carry

    lax.fori_loop(0, table[table.shape[0] - 1], whole_block, 0)


class Role:
    def __init__(self, sign, send, meta, phi, table, z_ref, value_ref, sum_ref, listed=False):
        if not listed:
            rows = (meta.shape[0] - DUMMY_ROWS) // send.shape[0]
            used_rows(meta, send.shape[0], rows, table)
        self.sign = sign
        self.table = table
        self.ids = meta
        self.phi = phi
        self.z_ref = z_ref
        self.value_ref = value_ref
        self.sum_ref = sum_ref
        self.count = meta.shape[0] - DUMMY_ROWS

    def cross(self, mine, other):
        return mine - other if self.sign > 0 else other - mine

    def backward(self, z, owned):
        high = z.astype(BF16).astype(F32)
        self.z_ref[0, : self.count] = high
        self.z_ref[1, : self.count] = z - high
        self.z_ref[:, self.count :] = jnp.zeros((2, DUMMY_ROWS, LANES), F32)
        blocks, double, width = self.phi.shape
        row_iota = lax.broadcasted_iota(jnp.int32, (owned, width), 0).astype(F32)

        def gather(block):
            rows = listed_rows(self.table, block * BLOCK_ROWS, BLOCK_ROWS)
            hit = row_iota == rows_pair(self.ids, rows)
            parts = [
                jnp.where(hit, rows_pair(self.z_ref.at[k], rows), 0.0).astype(BF16)
                for k in range(2)
            ]
            return lax.dot_general(
                jnp.concatenate(parts, axis=0),
                self.phi[block],
                (((1,), (1,)), ((), ())),
                preferred_element_type=F32,
            )

        return self.gathered(gather)

    def gathered(self, gather):
        self.sum_ref[...] = jnp.zeros(self.sum_ref.shape, F32)

        def step(blocks):
            self.sum_ref[...] += sum(gather(block) for block in blocks)

        over_blocks(self.table, step)
        g = self.sum_ref[...]
        owned, terms = g.shape[0] // 2, g.shape[1] // 2
        return self.sign * (g[:owned, :terms] + (g[:owned, terms:] + g[owned:, :terms]))

    def forward(self, field):
        owned = field.shape[0]
        stack = stacked(field)
        row_iota = lax.broadcasted_iota(jnp.int32, (owned, STEP_LANES), 0).astype(F32)
        self.value_ref[...] = jnp.zeros(self.value_ref.shape, F32)

        def ahead(block):
            for u in range(UNROLL):
                rows = listed_rows(self.table, block * BLOCK_ROWS + u * STEP_ROWS, STEP_ROWS)
                phi = self.phi[block, :, u * STEP_LANES : (u + 1) * STEP_LANES]
                value = forward_step(stack, phi, rows_pair(self.ids, rows), row_iota, owned)
                store_rows(self.value_ref, rows, value)

        def step(blocks):
            for block in blocks:
                ahead(block)

        over_blocks(self.table, step)
        return self.value_ref[: self.count]

    def forward_image(self, field, other, weight):
        owned = field.shape[0]
        stack = stacked(field)
        blocks, double, width = self.phi.shape
        row_iota = lax.broadcasted_iota(jnp.int32, (owned, width), 0).astype(F32)
        fill_padded(self.z_ref.at[0], other)
        fill_padded(self.z_ref.at[1], weight)
        self.value_ref[...] = jnp.zeros(self.value_ref.shape, F32)

        def both(block):
            rows = listed_rows(self.table, block * BLOCK_ROWS, BLOCK_ROWS)
            phi = self.phi[block]
            hit = row_iota == rows_pair(self.ids, rows)
            values = []
            for u in range(UNROLL):
                part = slice(u * STEP_LANES, (u + 1) * STEP_LANES)
                product = jnp.dot(stack, phi[:, part], preferred_element_type=F32)
                value = product[:owned] + product[owned:]
                values.append(
                    jnp.sum(jnp.where(hit[:, part], value, 0.0), axis=0, keepdims=True)
                )
            value = jnp.concatenate(values, axis=1)
            store_rows(self.value_ref, rows, value)
            z = rows_pair(self.z_ref.at[1], rows) * self.cross(
                value, rows_pair(self.z_ref.at[0], rows)
            )
            high = z.astype(BF16).astype(F32)
            parts = [jnp.where(hit, x, 0.0).astype(BF16) for x in (high, z - high)]
            return lax.dot_general(
                jnp.concatenate(parts, axis=0),
                phi,
                (((1,), (1,)), ((), ())),
                preferred_element_type=F32,
            )

        image = self.gathered(both)
        return self.value_ref[: self.count], SCALE * (image + damping * field)

    def weigh(self, residual):
        live = self.ids[: self.count] >= 0.0
        misfit = jnp.where(live, residual, 0.0)
        weight = jnp.where(live, 1.0 / (1.0 + misfit * misfit / cauchy_square), 0.0)
        return weight, weight * misfit

    def gradient(self, z, state):
        return self.backward(z, state.shape[0]) - damping * state

    def image(self, z, before):
        return SCALE * (self.backward(z, before.shape[0]) + damping * before)


def write_chunks(send, first, values):
    chunks, rows = send.shape[0], send.shape[2]
    for j in range(chunks):
        send[j, first] = values[j * rows : (j + 1) * rows, :]


def fill_padded(ref, values):
    count = values.shape[0]
    ref[:count] = values
    ref[count:] = jnp.zeros((ref.shape[0] - count,) + values.shape[1:], F32)


def setup_asc_kernel(
    fold, rows, packed, coef, meta, phi, state, short, onward, times, table, value_ref
):
    state[...] = coef[...]
    chunks = packed.shape[0] * fold
    count = chunks * rows
    meta[:count] = flat_first(packed, 0, fold, rows)
    meta[count:] = jnp.full((DUMMY_ROWS, LANES), -1.0, F32)
    fill_padded(times, flat_first(packed, 1, fold, rows))
    used_rows(meta, chunks, rows, table)
    basis_loop(table, meta, times, coef[...], phi, value_ref)
    short[...] = flat_first(packed, 4, fold, rows) - value_ref[:count]
    for j in range(chunks):
        base = j % fold * FIELDS
        for f in range(2):
            start = (base + f + 2) * rows
            onward[j, f * rows : (f + 1) * rows] = packed[j // fold, start : start + rows]
        onward[j, 2 * rows : 3 * rows] = short[j * rows : (j + 1) * rows]
        onward[j, 3 * rows :] = packed[j // fold, fold * FIELDS * rows :]


def setup_desc_kernel(
    fold, rows, packed, meta, phi, state, residual, weights, basis_0, value_0, send,
    times, table, z_ref, value_ref, sum_ref,
):
    chunks = packed.shape[0]
    count = chunks * rows
    home = lax.rem(lax.axis_index("asc"), fold) * (chunks // fold) + lax.axis_index("desc")
    state[...] = packed[home, 3 * rows :]
    meta[:count] = flat_second(packed, 0, rows)
    meta[count:] = jnp.full((DUMMY_ROWS, LANES), -1.0, F32)
    fill_padded(times, flat_second(packed, 1, rows))
    used_rows(meta, chunks, rows, table)
    basis_loop(table, meta, times, state[...], phi, value_ref)
    role = Role(-1.0, send, meta, phi, table, z_ref, value_ref, sum_ref, listed=True)
    own = value_ref[:count]
    write_chunks(send, 0, own)
    left = flat_second(packed, 2, rows) + own
    residual[...] = left
    weights[...], z = role.weigh(left)
    basis_0[...] = role.gradient(z, state[...])
    own = role.forward(basis_0[...])
    value_0[...] = own
    write_chunks(send, 1, own)


def first_asc_kernel(
    chunks, got, short, meta, phi, state,
    residual, weights, crossed_0, basis_0, basis_1, value_1, send, table, z_ref, value_ref, sum_ref,
):
    role = Role(1.0, send, meta, phi, table, z_ref, value_ref, sum_ref)
    left = short[...] + flat(got, 0, chunks)
    residual[...] = left
    weights[...], z = role.weigh(left)
    basis_0[...] = role.gradient(z, state[...])
    other = flat(got, 1, chunks)
    own, basis_1[...] = role.forward_image(basis_0[...], other, weights[...])
    write_chunks(send, 0, own)
    crossed_0[...] = role.cross(own, other)
    own = role.forward(basis_1[...])
    value_1[...] = own
    write_chunks(send, 1, own)


def images_kernel(sign, chunks, keep, got, value_0, meta, phi, weights, basis_0, *rest):
    basis_1, basis_2, send, *kept = rest[:-4]
    role = Role(sign, send, meta, phi, *rest[-4:])
    first = role.cross(value_0[...], flat(got, 0, chunks))
    basis_1[...] = role.image(weights[...] * first, basis_0[...])
    other = flat(got, 1, chunks)
    own, basis_2[...] = role.forward_image(basis_1[...], other, weights[...])
    write_chunks(send, 0, own)
    second = role.cross(own, other)
    own = role.forward(basis_2[...])
    write_chunks(send, 1, own)
    if keep:
        crossed_0, crossed_1, value_2 = kept
        crossed_0[...] = first
        crossed_1[...] = second
        value_2[...] = own


def total(x):
    return jnp.sum(jnp.sum(x, axis=0, keepdims=True), axis=1, keepdims=True)


PAIRS = [(0, 0), (0, 1), (0, 2), (1, 1), (1, 2), (2, 2)]


def gram_kernel(
    sign, chunks, keep, got, value_1, meta, phi, weights, crossed_0, basis_0, basis_1,
    other_0, other_1, other_2, *rest,
):
    basis_2, scalars, *kept = rest[:-4]
    role = Role(sign, got, meta, phi, *rest[-4:])
    weight = weights[...]
    crossed = role.cross(value_1[...], flat(got, 0, chunks))
    basis_2[...] = role.image(weight * crossed, basis_1[...])
    own = role.forward(basis_2[...])
    last = role.cross(own, flat(got, 1, chunks))
    if keep:
        crossed_1, crossed_2, value_2 = kept
        crossed_1[...] = crossed
        crossed_2[...] = last
        value_2[...] = own
    values = [crossed_0[...], crossed, last]
    mine = [basis_0[...], basis_1[...], basis_2[...]]
    others = [other_0[...], other_1[...], other_2[...]]
    lane = lax.broadcasted_iota(jnp.int32, (1, LANES), 1)
    line = jnp.zeros((1, LANES), F32)
    for place_in_line, (i, j) in enumerate(PAIRS):
        dots = total(mine[i] * mine[j] + others[i] * others[j])
        curve = total(weight * values[i] * values[j]) + damping * dots
        line = jnp.where(lane == place_in_line, curve, line)
        if i == 0:
            line = jnp.where(lane == len(PAIRS) + j, dots, line)
    for d in range(scalars.shape[0]):
        scalars[d] = line


def solve(scalars):
    summed = scalars[0]
    for d in range(1, scalars.shape[0]):
        summed = summed + scalars[d]
    line = summed
    lane = lax.broadcasted_iota(jnp.int32, (1, LANES), 1)

    def pick(place):
        return jnp.sum(jnp.where(lane == place, line, 0.0), axis=1, keepdims=True)

    g = {pair: pick(place) for place, pair in enumerate(PAIRS)}
    right = [pick(len(PAIRS) + i) for i in range(3)]
    s = [
        jnp.where(g[i, i] > 0.0, lax.rsqrt(jnp.maximum(g[i, i], 1e-37)), 0.0) for i in range(3)
    ]
    l10 = g[0, 1] * s[0] * s[1]
    l20 = g[0, 2] * s[0] * s[2]
    g21 = g[1, 2] * s[1] * s[2]
    c = [right[i] * s[i] for i in range(3)]

    def inverse(pivot):
        good = pivot > PIVOT_FLOOR
        return jnp.where(good, 1.0 / jnp.where(good, pivot, 1.0), 0.0)

    inv1 = inverse(1.0 - l10 * l10)
    t21 = g21 - l20 * l10
    l21 = t21 * inv1
    inv2 = inverse(1.0 - l20 * l20 - l21 * t21)
    u1 = c[1] - l10 * c[0]
    u2 = c[2] - l20 * c[0] - l21 * u1
    x2 = u2 * inv2
    x1 = u1 * inv1 - l21 * x2
    x0 = c[0] - l10 * x1 - l20 * x2
    return [x0 * s[0], x1 * s[1], x2 * s[2]]


def combine(y, parts):
    return y[0] * parts[0] + (y[1] * parts[1] + y[2] * parts[2])


def next_asc_kernel(
    chunks, scalars, meta, phi, residual, crossed_0, crossed_1, crossed_2,
    basis_a0, basis_a1, basis_a2, basis_d0, basis_d1, basis_d2, state_a, state_d, value_2,
    new_a, new_d, shares, weights, basis_0, value_0, send, table, z_ref, value_ref, sum_ref,
):
    role = Role(1.0, send, meta, phi, table, z_ref, value_ref, sum_ref)
    write_chunks(send, 0, value_2[...])
    y = solve(scalars)
    for i in range(3):
        shares[i : i + 1] = jnp.broadcast_to(y[i], (1, LANES))
    left = residual[...] - combine(y, [crossed_0[...], crossed_1[...], crossed_2[...]])
    new_a[...] = state_a[...] + combine(y, [basis_a0[...], basis_a1[...], basis_a2[...]])
    new_d[...] = state_d[...] + combine(y, [basis_d0[...], basis_d1[...], basis_d2[...]])
    weights[...], z = role.weigh(left)
    basis_0[...] = role.gradient(z, new_a[...])
    own = role.forward(basis_0[...])
    value_0[...] = own
    write_chunks(send, 1, own)


def next_desc_kernel(
    chunks, got, shares, meta, phi, residual, crossed_0, crossed_1, value_2, state,
    weights, new_crossed_0, basis_0, basis_1, value_1, send, table, z_ref, value_ref, sum_ref,
):
    role = Role(-1.0, send, meta, phi, table, z_ref, value_ref, sum_ref)
    y = [shares[i : i + 1] for i in range(3)]
    crossed_2 = role.cross(value_2[...], flat(got, 0, chunks))
    left = residual[...] - combine(y, [crossed_0[...], crossed_1[...], crossed_2])
    weights[...], z = role.weigh(left)
    basis_0[...] = role.gradient(z, state[...])
    other = flat(got, 1, chunks)
    own, basis_1[...] = role.forward_image(basis_0[...], other, weights[...])
    write_chunks(send, 0, own)
    new_crossed_0[...] = role.cross(own, other)
    own = role.forward(basis_1[...])
    value_1[...] = own
    write_chunks(send, 1, own)


def final_kernel(scalars, state_a, basis_0, basis_1, basis_2, desc, out_a, out_d):
    y = solve(scalars)
    out_a[...] = state_a[...] + combine(y, [basis_0[...], basis_1[...], basis_2[...]])
    out_d[...] = desc[0] + combine(y, [desc[1], desc[2], desc[3]])


def body(coef_asc, coef_desc, cross_asc, cross_desc, time_asc, time_desc, height, block_fill):
    owned_asc, terms = coef_asc.shape
    owned_desc = coef_desc.shape[0]
    blocks, width = cross_asc.shape
    na = lax.axis_size("asc")
    nd = lax.axis_size("desc")
    fold = na // nd
    rows = blocks * width // na // LANES
    all_rows = na * rows
    all_blocks = -(-all_rows // BLOCK_ROWS)
    shape = jax.ShapeDtypeStruct

    def call(kernel, outs, scratch, *args, in_specs=None, mebibytes=16):
        return pl.pallas_call(
            kernel,
            out_shape=outs,
            in_specs=[place(x) for x in args] if in_specs is None else in_specs,
            out_specs=jax.tree.map(place, outs),
            scratch_shapes=scratch,
            compiler_params=params(mebibytes),
        )(*args)

    to_role = []
    for p in range(na):
        for q in range(nd):
            to_role.append((p * nd + q, (q * fold + p // nd) * nd + p % nd))
    to_native = [(b, a) for a, b in to_role]
    slots = (cross_asc, cross_desc, time_asc, time_desc, height)
    packed = call(
        functools.partial(pack_kernel, na, nd, owned_asc),
        shape((nd, fold * FIELDS * rows + owned_desc, LANES), F32),
        [pltpu.VMEM(coef_desc.shape, F32)]
        + [pltpu.VMEM((blocks, width), x.dtype) for x in slots]
        + [
            pltpu.VMEM((1, blocks), jnp.int32),
            pltpu.VMEM((FIELDS, blocks, width), F32),
            pltpu.SemaphoreType.DMA((len(slots) + 2,)),
        ],
        coef_desc, *slots, block_fill.reshape(1, blocks),
        in_specs=[pl.BlockSpec(memory_space=pltpu.HBM)] * (len(slots) + 2),
        mebibytes=60,
    )
    at_asc = lax.all_to_all(packed, "desc", split_axis=0, concat_axis=0, tiled=True)

    padded = all_rows + DUMMY_ROWS
    meta_shape = shape((padded, LANES), F32)
    phi_shape = shape((all_blocks, 2 * terms, BLOCK_ROWS * LANES), BF16)
    role_shapes = [meta_shape, phi_shape]
    table = pltpu.SMEM((all_rows + rows + BLOCK_ROWS + 1,), jnp.int32)
    slot_shape = shape((all_rows, LANES), F32)
    send_shape = shape((na, 2, rows, LANES), F32)
    field_a = shape(coef_asc.shape, F32)
    field_d = shape(coef_desc.shape, F32)
    line_shape = shape((na * nd, 1, LANES), F32)
    times_scratch = pltpu.VMEM((padded, LANES), F32)
    scratch = [
        table, pltpu.VMEM((2, padded, LANES), F32), pltpu.VMEM((padded, LANES), F32),
        pltpu.VMEM((2 * owned_asc, 2 * terms), F32),
    ]

    def exchange(x):
        return lax.all_to_all(x, "asc", split_axis=0, concat_axis=0, tiled=True)

    def share(x):
        return lax.all_to_all(x, ("asc", "desc"), split_axis=0, concat_axis=0, tiled=True)

    *asc, state_a, short, onward = call(
        functools.partial(setup_asc_kernel, fold, rows),
        role_shapes + [field_a, slot_shape, shape((na, 3 * rows + owned_desc, LANES), F32)],
        [times_scratch, table, scratch[2]],
        at_asc, coef_asc,
    )
    *desc, state_d, residual_d, weights_d, d0, own_d, send = call(
        functools.partial(setup_desc_kernel, fold, rows),
        role_shapes + [field_d, slot_shape, slot_shape, field_d, slot_shape, send_shape],
        [times_scratch] + scratch,
        exchange(onward),
    )
    residual_a, weights_a, crossed_a0, a0, a1, own_a, send = call(
        functools.partial(first_asc_kernel, na),
        [slot_shape, slot_shape, slot_shape, field_a, field_a, slot_shape, send_shape],
        scratch,
        exchange(send), short, *asc, state_a,
    )
    kept = [slot_shape] * 3
    d1, d2, send, crossed_d0, crossed_d1, own_d = call(
        functools.partial(images_kernel, -1.0, na, True),
        [field_d, field_d, send_shape] + kept,
        scratch,
        exchange(send), own_d, *desc, weights_d, d0,
    )
    a2, scalars, crossed_a1, crossed_a2, own_a = call(
        functools.partial(gram_kernel, 1.0, na, True),
        [field_a, line_shape] + kept,
        scratch,
        exchange(send), own_a, *asc, weights_a, crossed_a0, a0, a1, d0, d1, d2,
    )
    state_a, state_d, shares, weights_a, a0, own_a, send = call(
        functools.partial(next_asc_kernel, na),
        [
            field_a, field_d, shape((8, LANES), F32),
            slot_shape, field_a, slot_shape, send_shape,
        ],
        scratch,
        share(scalars), *asc, residual_a, crossed_a0, crossed_a1, crossed_a2,
        a0, a1, a2, d0, d1, d2, state_a, state_d, own_a,
    )
    weights_d, crossed_d0, d0, d1, own_d, send = call(
        functools.partial(next_desc_kernel, na),
        [slot_shape, slot_shape, field_d, field_d, slot_shape, send_shape],
        scratch,
        exchange(send), shares, *desc, residual_d, crossed_d0, crossed_d1, own_d, state_d,
    )
    a1, a2, send = call(
        functools.partial(images_kernel, 1.0, na, False),
        [field_a, field_a, send_shape],
        scratch,
        exchange(send), own_a, *asc, weights_a, a0,
    )
    d2, scalars = call(
        functools.partial(gram_kernel, -1.0, na, False),
        [field_d, line_shape],
        scratch,
        exchange(send), own_d, *desc, weights_d, crossed_d0, d0, d1, a0, a1, a2,
    )
    leaving = jnp.stack([state_d, d0, d1, d2])
    native = lax.ppermute(leaving, ("asc", "desc"), to_native)
    return tuple(
        call(
            final_kernel,
            [field_a, field_d],
            [],
            share(scalars), state_a, a0, a1, a2, native,
        )
    )


def solution(mesh):
    split_rows = P(("asc", "desc"), None)
    return jax.shard_map(
        body,
        mesh=mesh,
        in_specs=(split_rows,) * 7 + (P(("asc", "desc")),),
        out_specs=(split_rows, split_rows),
        check_vma=False,
    )
```

```python
import functools
import math

import jax
import jax.numpy as jnp
from jax import lax
from jax.experimental import pallas as pl
from jax.experimental.pallas import tpu as pltpu
from jax.sharding import PartitionSpec as P

GN_STEPS = 2
damping = 2.0
cauchy_square = 2.25

LANES = 128
STEP_ROWS = 2
UNROLL = 4
BLOCK_ROWS = STEP_ROWS * UNROLL
STEP_LANES = STEP_ROWS * LANES
DUMMY_ROWS = 8
TURNS = (4, 1)
SCALE = 1.0 / 128.0
FIELDS = 5
PIVOT_FLOOR = 1e-6
F32 = jnp.float32
BF16 = jnp.bfloat16

COS_TERMS = [(-1.0) ** i * math.pi ** (2 * i) / math.factorial(2 * i) for i in range(8)]
SIN_TERMS = [(-1.0) ** i * math.pi ** (2 * i + 1) / math.factorial(2 * i + 1) for i in range(7)]


def params(mebibytes):
    return pltpu.CompilerParams(vmem_limit_bytes=mebibytes * 1024 * 1024)


def place(x):
    return pl.BlockSpec(memory_space=pltpu.VMEM)


def split(x):
    high = x.astype(BF16)
    low = (x - high.astype(F32)).astype(BF16)
    return high, low


def flat_first(ref, field, fold, rows):
    parts = []
    nd = ref.shape[0]
    for j in range(nd * fold):
        start = (j // nd * FIELDS + field) * rows
        parts.append(ref[j % nd, start : start + rows])
    return jnp.concatenate(parts, axis=0)


def flat_second(ref, field, rows):
    start = field * rows
    return jnp.concatenate([ref[j, start : start + rows] for j in range(ref.shape[0])], axis=0)


def flat(ref, field, chunks):
    return jnp.concatenate([ref[j, field] for j in range(chunks)], axis=0)


def local_id(ids, owned):
    if owned & (owned - 1) == 0:
        return ids & (owned - 1)
    return lax.rem(ids, owned)


def pack_kernel(
    na, nd, owned_asc, coef_in, ca_in, cd_in, ta_in, td_in, height_in, fill_in, out,
    coef, ca, cd, ta, td, height, fill, turned, sems,
):
    copies = [
        pltpu.make_async_copy(source, target, sems.at[i])
        for i, (source, target) in enumerate(
            [
                (fill_in, fill), (ca_in, ca), (ta_in, ta),
                (cd_in, cd), (td_in, td), (height_in, height), (coef_in, coef),
            ]
        )
    ]
    for copy in copies:
        copy.start()
    for copy in copies:
        copy.wait()
    owned_desc = coef.shape[0]
    blocks, width = ca.shape
    group = width // na
    rows = blocks // na
    fill_row = fill[...]
    row_id = lax.broadcasted_iota(jnp.int32, (blocks, blocks), 0)
    col_id = lax.broadcasted_iota(jnp.int32, (blocks, blocks), 1)
    fill_col = jnp.sum(
        jnp.where(row_id == col_id, fill_row, 0).astype(F32), axis=1, keepdims=True
    )
    lane = lax.broadcasted_iota(jnp.int32, (blocks, width), 1)
    live = lane.astype(F32) < fill_col
    fields = [
        lambda: jnp.where(live, local_id(ca[...], owned_asc).astype(F32), -1.0),
        lambda: ta[...],
        lambda: jnp.where(live, local_id(cd[...], owned_desc).astype(F32), -1.0),
        lambda: td[...],
        lambda: height[...],
    ]
    source = lax.broadcasted_iota(jnp.int32, (width, width), 0)
    target = lax.broadcasted_iota(jnp.int32, (width, width), 1)
    owner = target // group
    place = target - owner * group
    order = (source == place * na + owner).astype(F32).astype(BF16)
    for f, field in enumerate(fields):
        x = field()
        high = x.astype(BF16)
        rest = x - high.astype(F32)
        middle = rest.astype(BF16)
        low = (rest - middle.astype(F32)).astype(BF16)
        turned[f] = (
            jnp.dot(high, order, preferred_element_type=F32)
            + jnp.dot(middle, order, preferred_element_type=F32)
        ) + jnp.dot(low, order, preferred_element_type=F32)
    lane_group = lax.broadcasted_iota(jnp.int32, (rows, width), 1) // group
    for f in range(FIELDS):
        parts = [None] * na
        for k in range(na):
            piece = turned[f, pl.ds(k, rows, stride=na), :]
            for r in range(na):
                amount = ((k - r) * group) % width
                moved = pltpu.roll(piece, amount, 1) if amount else piece
                parts[r] = moved if k == 0 else jnp.where(lane_group == k, moved, parts[r])
        for r in range(na):
            start = (r // nd * FIELDS + f) * rows
            out[r % nd, start : start + rows] = parts[r]
    for q in range(nd):
        out[q, out.shape[1] - owned_desc :] = coef[...]


def cos_sin_pi(x):
    turns = jnp.floor(x + 0.5)
    f = x - turns
    sign = 1.0 - 2.0 * (turns - 2.0 * jnp.floor(turns * 0.5))
    u = f * f
    c = COS_TERMS[-1]
    for term in COS_TERMS[-2::-1]:
        c = c * u + term
    s = SIN_TERMS[-1]
    for term in SIN_TERMS[-2::-1]:
        s = s * u + term
    return c * sign, s * (f * sign)


def rows_pair(ref, rows):
    return jnp.concatenate([ref[pl.ds(r, 1), :] for r in rows], axis=1)


def used_rows(ids_ref, chunks, rows, table):
    count = jnp.int32(0)
    level = lax.broadcasted_iota(jnp.int32, (rows, LANES), 0).astype(F32) + 1.0
    for j in range(chunks):
        ids = ids_ref[j * rows : (j + 1) * rows, :]
        used = jnp.max(jnp.where(ids >= 0.0, level, 0.0)).astype(jnp.int32)
        for i in range(rows):
            table[count + i] = j * rows + i
        count = count + used
    for i in range(BLOCK_ROWS):
        table[count + i] = chunks * rows
    table[table.shape[0] - 1] = lax.div(count + (BLOCK_ROWS - 1), BLOCK_ROWS)


def listed_rows(table, first, count):
    return [table[first + i] for i in range(count)]


def over_blocks(table, step):
    blocks = table[table.shape[0] - 1]
    done = jnp.int32(0)
    for size in TURNS:
        turns = lax.div(blocks - done, size)

        def turn(i, carry, done=done, size=size):
            step([done + i * size + u for u in range(size)])
            return carry

        lax.fori_loop(0, turns, turn, 0)
        done = done + turns * size


def stacked(field):
    high, low = split(field)
    top = jnp.concatenate([high, high], axis=1)
    bottom = jnp.concatenate([low, jnp.zeros_like(low)], axis=1)
    return jnp.concatenate([top, bottom], axis=0)


def forward_step(stack, phi, ids_row, row_iota, owned):
    both = jnp.dot(stack, phi, preferred_element_type=F32)
    value = both[:owned] + both[owned:]
    return jnp.sum(jnp.where(row_iota == ids_row, value, 0.0), axis=0, keepdims=True)


def store_rows(ref, rows, value):
    for i, r in enumerate(rows):
        ref[pl.ds(r, 1), :] = value[:, i * LANES : (i + 1) * LANES]


def basis_loop(table, ids_ref, time_ref, coef, phi_ref, value_ref):
    owned, terms = coef.shape
    half = terms // 2
    value_ref[...] = jnp.zeros(value_ref.shape, F32)
    width = STEP_LANES
    stack = stacked(coef)
    row_iota = lax.broadcasted_iota(jnp.int32, (owned, width), 0).astype(F32)
    fine = (lax.broadcasted_iota(jnp.int32, (8, width), 0) + 1).astype(F32)
    coarse = (lax.broadcasted_iota(jnp.int32, (half // 8, width), 0) * 8).astype(F32)

    def step(block, u):
        rows = listed_rows(table, block * BLOCK_ROWS + u * STEP_ROWS, STEP_ROWS)
        times = rows_pair(time_ref, rows)
        cos_fine, sin_fine = cos_sin_pi(fine * times)
        cos_coarse, sin_coarse = cos_sin_pi(coarse * times)
        cos_parts, sin_parts = [], []
        for j in range(half // 8):
            cj = cos_coarse[j : j + 1]
            sj = sin_coarse[j : j + 1]
            cos_parts.append(cj * cos_fine - sj * sin_fine)
            sin_parts.append(sj * cos_fine + cj * sin_fine)
        high, low = split(jnp.concatenate(cos_parts + sin_parts, axis=0))
        phi = jnp.concatenate([high, low], axis=0)
        phi_ref[block, :, u * width : (u + 1) * width] = phi
        value = forward_step(stack, phi, rows_pair(ids_ref, rows), row_iota, owned)
        store_rows(value_ref, rows, value)

    def whole_block(block, carry):
        for u in range(UNROLL):
            step(block, u)
        return carry

    lax.fori_loop(0, table[table.shape[0] - 1], whole_block, 0)


class Role:
    def __init__(self, sign, send, meta, phi, table, z_ref, value_ref, sum_ref, listed=False):
        if not listed:
            rows = (meta.shape[0] - DUMMY_ROWS) // send.shape[0]
            used_rows(meta, send.shape[0], rows, table)
        self.sign = sign
        self.table = table
        self.ids = meta
        self.phi = phi
        self.z_ref = z_ref
        self.value_ref = value_ref
        self.sum_ref = sum_ref
        self.count = meta.shape[0] - DUMMY_ROWS

    def cross(self, mine, other):
        return mine - other if self.sign > 0 else other - mine

    def backward(self, z, owned):
        high = z.astype(BF16).astype(F32)
        self.z_ref[0, : self.count] = high
        self.z_ref[1, : self.count] = z - high
        self.z_ref[:, self.count :] = jnp.zeros((2, DUMMY_ROWS, LANES), F32)
        blocks, double, width = self.phi.shape
        row_iota = lax.broadcasted_iota(jnp.int32, (owned, width), 0).astype(F32)

        def gather(block):
            rows = listed_rows(self.table, block * BLOCK_ROWS, BLOCK_ROWS)
            hit = row_iota == rows_pair(self.ids, rows)
            parts = [
                jnp.where(hit, rows_pair(self.z_ref.at[k], rows), 0.0).astype(BF16)
                for k in range(2)
            ]
            return lax.dot_general(
                self.phi[block],
                jnp.concatenate(parts, axis=0),
                (((1,), (1,)), ((), ())),
                preferred_element_type=F32,
            )

        return self.gathered(gather)

    def gathered(self, gather):
        self.sum_ref[...] = jnp.zeros(self.sum_ref.shape, F32)

        def step(blocks):
            self.sum_ref[...] += sum(gather(block) for block in blocks)

        over_blocks(self.table, step)
        terms, owned = self.sum_ref.shape[0] // 2, self.sum_ref.shape[1] // 2
        high, low = self.sum_ref[:terms], self.sum_ref[terms:]
        turned = high[:, :owned] + (high[:, owned:] + low[:, :owned])
        wide = jnp.concatenate([turned, jnp.zeros((terms, LANES - owned), F32)], axis=1)
        return self.sign * wide.T[:owned]

    def forward(self, field):
        owned = field.shape[0]
        stack = stacked(field)
        row_iota = lax.broadcasted_iota(jnp.int32, (owned, STEP_LANES), 0).astype(F32)
        self.value_ref[...] = jnp.zeros(self.value_ref.shape, F32)

        def ahead(block):
            for u in range(UNROLL):
                rows = listed_rows(self.table, block * BLOCK_ROWS + u * STEP_ROWS, STEP_ROWS)
                phi = self.phi[block, :, u * STEP_LANES : (u + 1) * STEP_LANES]
                value = forward_step(stack, phi, rows_pair(self.ids, rows), row_iota, owned)
                store_rows(self.value_ref, rows, value)

        def step(blocks):
            for block in blocks:
                ahead(block)

        over_blocks(self.table, step)
        return self.value_ref[: self.count]

    def forward_image(self, field, other, weight):
        owned = field.shape[0]
        stack = stacked(field)
        blocks, double, width = self.phi.shape
        row_iota = lax.broadcasted_iota(jnp.int32, (owned, width), 0).astype(F32)
        fill_padded(self.z_ref.at[0], other)
        fill_padded(self.z_ref.at[1], weight)
        self.value_ref[...] = jnp.zeros(self.value_ref.shape, F32)

        def both(block):
            rows = listed_rows(self.table, block * BLOCK_ROWS, BLOCK_ROWS)
            phi = self.phi[block]
            hit = row_iota == rows_pair(self.ids, rows)
            values = []
            for u in range(UNROLL):
                part = slice(u * STEP_LANES, (u + 1) * STEP_LANES)
                product = jnp.dot(stack, phi[:, part], preferred_element_type=F32)
                value = product[:owned] + product[owned:]
                values.append(
                    jnp.sum(jnp.where(hit[:, part], value, 0.0), axis=0, keepdims=True)
                )
            value = jnp.concatenate(values, axis=1)
            store_rows(self.value_ref, rows, value)
            z = rows_pair(self.z_ref.at[1], rows) * self.cross(
                value, rows_pair(self.z_ref.at[0], rows)
            )
            high = z.astype(BF16).astype(F32)
            parts = [jnp.where(hit, x, 0.0).astype(BF16) for x in (high, z - high)]
            return lax.dot_general(
                phi,
                jnp.concatenate(parts, axis=0),
                (((1,), (1,)), ((), ())),
                preferred_element_type=F32,
            )

        image = self.gathered(both)
        return self.value_ref[: self.count], SCALE * (image + damping * field)

    def weigh(self, residual):
        live = self.ids[: self.count] >= 0.0
        misfit = jnp.where(live, residual, 0.0)
        weight = jnp.where(live, 1.0 / (1.0 + misfit * misfit / cauchy_square), 0.0)
        return weight, weight * misfit

    def gradient(self, z, state):
        return self.backward(z, state.shape[0]) - damping * state

    def image(self, z, before):
        return SCALE * (self.backward(z, before.shape[0]) + damping * before)


def write_chunks(send, first, values):
    chunks, rows = send.shape[0], send.shape[2]
    for j in range(chunks):
        send[j, first] = values[j * rows : (j + 1) * rows, :]


def fill_padded(ref, values):
    count = values.shape[0]
    ref[:count] = values
    ref[count:] = jnp.zeros((ref.shape[0] - count,) + values.shape[1:], F32)


def setup_asc_kernel(
    fold, rows, packed, coef, meta, phi, state, short, onward, times, table, value_ref
):
    state[...] = coef[...]
    nd = packed.shape[0]
    chunks = nd * fold
    count = chunks * rows
    meta[:count] = flat_first(packed, 0, fold, rows)
    meta[count:] = jnp.full((DUMMY_ROWS, LANES), -1.0, F32)
    fill_padded(times, flat_first(packed, 1, fold, rows))
    used_rows(meta, chunks, rows, table)
    basis_loop(table, meta, times, coef[...], phi, value_ref)
    short[...] = flat_first(packed, 4, fold, rows) - value_ref[:count]
    for j in range(chunks):
        base = j // nd * FIELDS
        for f in range(2):
            start = (base + f + 2) * rows
            onward[j, f * rows : (f + 1) * rows] = packed[j % nd, start : start + rows]
        onward[j, 2 * rows : 3 * rows] = short[j * rows : (j + 1) * rows]
        onward[j, 3 * rows :] = packed[j % nd, fold * FIELDS * rows :]


def setup_desc_kernel(
    fold, rows, packed, meta, phi, state, residual, weights, basis_0, value_0, send,
    times, table, z_ref, value_ref, sum_ref,
):
    chunks = packed.shape[0]
    count = chunks * rows
    nd = chunks // fold
    home = lax.div(lax.axis_index("asc"), nd) * nd + lax.axis_index("desc")
    state[...] = packed[home, 3 * rows :]
    meta[:count] = flat_second(packed, 0, rows)
    meta[count:] = jnp.full((DUMMY_ROWS, LANES), -1.0, F32)
    fill_padded(times, flat_second(packed, 1, rows))
    used_rows(meta, chunks, rows, table)
    basis_loop(table, meta, times, state[...], phi, value_ref)
    role = Role(-1.0, send, meta, phi, table, z_ref, value_ref, sum_ref, listed=True)
    own = value_ref[:count]
    write_chunks(send, 0, own)
    left = flat_second(packed, 2, rows) + own
    residual[...] = left
    weights[...], z = role.weigh(left)
    basis_0[...] = role.gradient(z, state[...])
    own = role.forward(basis_0[...])
    value_0[...] = own
    write_chunks(send, 1, own)


def first_asc_kernel(
    chunks, got, short, meta, phi, state,
    residual, weights, crossed_0, basis_0, basis_1, value_1, send, table, z_ref, value_ref, sum_ref,
):
    role = Role(1.0, send, meta, phi, table, z_ref, value_ref, sum_ref)
    left = short[...] + flat(got, 0, chunks)
    residual[...] = left
    weights[...], z = role.weigh(left)
    basis_0[...] = role.gradient(z, state[...])
    other = flat(got, 1, chunks)
    own, basis_1[...] = role.forward_image(basis_0[...], other, weights[...])
    write_chunks(send, 0, own)
    crossed_0[...] = role.cross(own, other)
    own = role.forward(basis_1[...])
    value_1[...] = own
    write_chunks(send, 1, own)


def images_kernel(sign, chunks, keep, got, value_0, meta, phi, weights, basis_0, *rest):
    basis_1, basis_2, send, *kept = rest[:-4]
    role = Role(sign, send, meta, phi, *rest[-4:])
    first = role.cross(value_0[...], flat(got, 0, chunks))
    basis_1[...] = role.image(weights[...] * first, basis_0[...])
    other = flat(got, 1, chunks)
    own, basis_2[...] = role.forward_image(basis_1[...], other, weights[...])
    write_chunks(send, 0, own)
    second = role.cross(own, other)
    own = role.forward(basis_2[...])
    write_chunks(send, 1, own)
    if keep:
        crossed_0, crossed_1, value_2 = kept
        crossed_0[...] = first
        crossed_1[...] = second
        value_2[...] = own


def total(x):
    return jnp.sum(jnp.sum(x, axis=0, keepdims=True), axis=1, keepdims=True)


PAIRS = [(0, 0), (0, 1), (0, 2), (1, 1), (1, 2), (2, 2)]


def gram_kernel(
    sign, chunks, keep, got, value_1, meta, phi, weights, crossed_0, basis_0, basis_1,
    other_0, other_1, other_2, *rest,
):
    basis_2, scalars, *kept = rest[:-4]
    role = Role(sign, got, meta, phi, *rest[-4:])
    weight = weights[...]
    crossed = role.cross(value_1[...], flat(got, 0, chunks))
    basis_2[...] = role.image(weight * crossed, basis_1[...])
    own = role.forward(basis_2[...])
    last = role.cross(own, flat(got, 1, chunks))
    if keep:
        crossed_1, crossed_2, value_2 = kept
        crossed_1[...] = crossed
        crossed_2[...] = last
        value_2[...] = own
    values = [crossed_0[...], crossed, last]
    mine = [basis_0[...], basis_1[...], basis_2[...]]
    others = [other_0[...], other_1[...], other_2[...]]
    lane = lax.broadcasted_iota(jnp.int32, (1, LANES), 1)
    line = jnp.zeros((1, LANES), F32)
    for place_in_line, (i, j) in enumerate(PAIRS):
        dots = total(mine[i] * mine[j] + others[i] * others[j])
        curve = total(weight * values[i] * values[j]) + damping * dots
        line = jnp.where(lane == place_in_line, curve, line)
        if i == 0:
            line = jnp.where(lane == len(PAIRS) + j, dots, line)
    for d in range(scalars.shape[0]):
        scalars[d] = line


def solve(scalars):
    summed = scalars[0]
    for d in range(1, scalars.shape[0]):
        summed = summed + scalars[d]
    line = summed
    lane = lax.broadcasted_iota(jnp.int32, (1, LANES), 1)

    def pick(place):
        return jnp.sum(jnp.where(lane == place, line, 0.0), axis=1, keepdims=True)

    g = {pair: pick(place) for place, pair in enumerate(PAIRS)}
    right = [pick(len(PAIRS) + i) for i in range(3)]
    s = [
        jnp.where(g[i, i] > 0.0, lax.rsqrt(jnp.maximum(g[i, i], 1e-37)), 0.0) for i in range(3)
    ]
    l10 = g[0, 1] * s[0] * s[1]
    l20 = g[0, 2] * s[0] * s[2]
    g21 = g[1, 2] * s[1] * s[2]
    c = [right[i] * s[i] for i in range(3)]

    def inverse(pivot):
        good = pivot > PIVOT_FLOOR
        return jnp.where(good, 1.0 / jnp.where(good, pivot, 1.0), 0.0)

    inv1 = inverse(1.0 - l10 * l10)
    t21 = g21 - l20 * l10
    l21 = t21 * inv1
    inv2 = inverse(1.0 - l20 * l20 - l21 * t21)
    u1 = c[1] - l10 * c[0]
    u2 = c[2] - l20 * c[0] - l21 * u1
    x2 = u2 * inv2
    x1 = u1 * inv1 - l21 * x2
    x0 = c[0] - l10 * x1 - l20 * x2
    return [x0 * s[0], x1 * s[1], x2 * s[2]]


def combine(y, parts):
    return y[0] * parts[0] + (y[1] * parts[1] + y[2] * parts[2])


def next_asc_kernel(
    chunks, scalars, meta, phi, residual, crossed_0, crossed_1, crossed_2,
    basis_a0, basis_a1, basis_a2, basis_d0, basis_d1, basis_d2, state_a, state_d, value_2,
    new_a, new_d, shares, weights, basis_0, value_0, send, table, z_ref, value_ref, sum_ref,
):
    role = Role(1.0, send, meta, phi, table, z_ref, value_ref, sum_ref)
    write_chunks(send, 0, value_2[...])
    y = solve(scalars)
    for i in range(3):
        shares[i : i + 1] = jnp.broadcast_to(y[i], (1, LANES))
    left = residual[...] - combine(y, [crossed_0[...], crossed_1[...], crossed_2[...]])
    new_a[...] = state_a[...] + combine(y, [basis_a0[...], basis_a1[...], basis_a2[...]])
    new_d[...] = state_d[...] + combine(y, [basis_d0[...], basis_d1[...], basis_d2[...]])
    weights[...], z = role.weigh(left)
    basis_0[...] = role.gradient(z, new_a[...])
    own = role.forward(basis_0[...])
    value_0[...] = own
    write_chunks(send, 1, own)


def next_desc_kernel(
    chunks, got, shares, meta, phi, residual, crossed_0, crossed_1, value_2, state,
    weights, new_crossed_0, basis_0, basis_1, value_1, send, table, z_ref, value_ref, sum_ref,
):
    role = Role(-1.0, send, meta, phi, table, z_ref, value_ref, sum_ref)
    y = [shares[i : i + 1] for i in range(3)]
    crossed_2 = role.cross(value_2[...], flat(got, 0, chunks))
    left = residual[...] - combine(y, [crossed_0[...], crossed_1[...], crossed_2])
    weights[...], z = role.weigh(left)
    basis_0[...] = role.gradient(z, state[...])
    other = flat(got, 1, chunks)
    own, basis_1[...] = role.forward_image(basis_0[...], other, weights[...])
    write_chunks(send, 0, own)
    new_crossed_0[...] = role.cross(own, other)
    own = role.forward(basis_1[...])
    value_1[...] = own
    write_chunks(send, 1, own)


def final_kernel(scalars, state_a, basis_0, basis_1, basis_2, desc, out_a, out_d):
    y = solve(scalars)
    out_a[...] = state_a[...] + combine(y, [basis_0[...], basis_1[...], basis_2[...]])
    out_d[...] = desc[0] + combine(y, [desc[1], desc[2], desc[3]])


def body(coef_asc, coef_desc, cross_asc, cross_desc, time_asc, time_desc, height, block_fill):
    owned_asc, terms = coef_asc.shape
    owned_desc = coef_desc.shape[0]
    blocks, width = cross_asc.shape
    na = lax.axis_size("asc")
    nd = lax.axis_size("desc")
    fold = na // nd
    rows = blocks * width // na // LANES
    all_rows = na * rows
    all_blocks = -(-all_rows // BLOCK_ROWS)
    shape = jax.ShapeDtypeStruct

    def call(kernel, outs, scratch, *args, in_specs=None, mebibytes=16):
        return pl.pallas_call(
            kernel,
            out_shape=outs,
            in_specs=[place(x) for x in args] if in_specs is None else in_specs,
            out_specs=jax.tree.map(place, outs),
            scratch_shapes=scratch,
            compiler_params=params(mebibytes),
        )(*args)

    swap = []
    for p in range(na):
        for q in range(nd):
            swap.append((p * nd + q, (p // nd * nd + q) * nd + p % nd))
    slots = (cross_asc, cross_desc, time_asc, time_desc, height)
    packed = call(
        functools.partial(pack_kernel, na, nd, owned_asc),
        shape((nd, fold * FIELDS * rows + owned_desc, LANES), F32),
        [pltpu.VMEM(coef_desc.shape, F32)]
        + [pltpu.VMEM((blocks, width), x.dtype) for x in slots]
        + [
            pltpu.VMEM((1, blocks), jnp.int32),
            pltpu.VMEM((FIELDS, blocks, width), F32),
            pltpu.SemaphoreType.DMA((len(slots) + 2,)),
        ],
        coef_desc, *slots, block_fill.reshape(1, blocks),
        in_specs=[pl.BlockSpec(memory_space=pltpu.HBM)] * (len(slots) + 2),
        mebibytes=60,
    )
    at_asc = lax.all_to_all(packed, "desc", split_axis=0, concat_axis=0, tiled=True)

    padded = all_rows + DUMMY_ROWS
    meta_shape = shape((padded, LANES), F32)
    phi_shape = shape((all_blocks, 2 * terms, BLOCK_ROWS * LANES), BF16)
    role_shapes = [meta_shape, phi_shape]
    table = pltpu.SMEM((all_rows + rows + BLOCK_ROWS + 1,), jnp.int32)
    slot_shape = shape((all_rows, LANES), F32)
    send_shape = shape((na, 2, rows, LANES), F32)
    field_a = shape(coef_asc.shape, F32)
    field_d = shape(coef_desc.shape, F32)
    line_shape = shape((na * nd, 1, LANES), F32)
    times_scratch = pltpu.VMEM((padded, LANES), F32)
    scratch = [
        table, pltpu.VMEM((2, padded, LANES), F32), pltpu.VMEM((padded, LANES), F32),
        pltpu.VMEM((2 * terms, 2 * owned_asc), F32),
    ]

    def exchange(x):
        return lax.all_to_all(x, "asc", split_axis=0, concat_axis=0, tiled=True)

    def share(x):
        return lax.all_to_all(x, ("asc", "desc"), split_axis=0, concat_axis=0, tiled=True)

    *asc, state_a, short, onward = call(
        functools.partial(setup_asc_kernel, fold, rows),
        role_shapes + [field_a, slot_shape, shape((na, 3 * rows + owned_desc, LANES), F32)],
        [times_scratch, table, scratch[2]],
        at_asc, coef_asc,
    )
    *desc, state_d, residual_d, weights_d, d0, own_d, send = call(
        functools.partial(setup_desc_kernel, fold, rows),
        role_shapes + [field_d, slot_shape, slot_shape, field_d, slot_shape, send_shape],
        [times_scratch] + scratch,
        exchange(onward),
    )
    residual_a, weights_a, crossed_a0, a0, a1, own_a, send = call(
        functools.partial(first_asc_kernel, na),
        [slot_shape, slot_shape, slot_shape, field_a, field_a, slot_shape, send_shape],
        scratch,
        exchange(send), short, *asc, state_a,
    )
    kept = [slot_shape] * 3
    d1, d2, send, crossed_d0, crossed_d1, own_d = call(
        functools.partial(images_kernel, -1.0, na, True),
        [field_d, field_d, send_shape] + kept,
        scratch,
        exchange(send), own_d, *desc, weights_d, d0,
    )
    a2, scalars, crossed_a1, crossed_a2, own_a = call(
        functools.partial(gram_kernel, 1.0, na, True),
        [field_a, line_shape] + kept,
        scratch,
        exchange(send), own_a, *asc, weights_a, crossed_a0, a0, a1, d0, d1, d2,
    )
    state_a, state_d, shares, weights_a, a0, own_a, send = call(
        functools.partial(next_asc_kernel, na),
        [
            field_a, field_d, shape((8, LANES), F32),
            slot_shape, field_a, slot_shape, send_shape,
        ],
        scratch,
        share(scalars), *asc, residual_a, crossed_a0, crossed_a1, crossed_a2,
        a0, a1, a2, d0, d1, d2, state_a, state_d, own_a,
    )
    weights_d, crossed_d0, d0, d1, own_d, send = call(
        functools.partial(next_desc_kernel, na),
        [slot_shape, slot_shape, field_d, field_d, slot_shape, send_shape],
        scratch,
        exchange(send), shares, *desc, residual_d, crossed_d0, crossed_d1, own_d, state_d,
    )
    a1, a2, send = call(
        functools.partial(images_kernel, 1.0, na, False),
        [field_a, field_a, send_shape],
        scratch,
        exchange(send), own_a, *asc, weights_a, a0,
    )
    d2, scalars = call(
        functools.partial(gram_kernel, -1.0, na, False),
        [field_d, line_shape],
        scratch,
        exchange(send), own_d, *desc, weights_d, crossed_d0, d0, d1, a0, a1, a2,
    )
    leaving = jnp.stack([state_d, d0, d1, d2])
    native = lax.ppermute(leaving, ("asc", "desc"), swap)
    return tuple(
        call(
            final_kernel,
            [field_a, field_d],
            [],
            share(scalars), state_a, a0, a1, a2, native,
        )
    )


def solution(mesh):
    split_rows = P(("asc", "desc"), None)
    return jax.shard_map(
        body,
        mesh=mesh,
        in_specs=(split_rows,) * 7 + (P(("asc", "desc")),),
        out_specs=(split_rows, split_rows),
        check_vma=False,
    )
```

```python
import functools
import math

import jax
import jax.numpy as jnp
from jax import lax
from jax.experimental import pallas as pl
from jax.experimental.pallas import tpu as pltpu
from jax.sharding import PartitionSpec as P

GN_STEPS = 2
damping = 2.0
cauchy_square = 2.25

LANES = 128
STEP_ROWS = 2
UNROLL = 4
BLOCK_ROWS = STEP_ROWS * UNROLL
STEP_LANES = STEP_ROWS * LANES
DUMMY_ROWS = 8
TURN = 5
SCALE = 1.0 / 128.0
FIELDS = 5
PIVOT_FLOOR = 1e-6
F32 = jnp.float32
BF16 = jnp.bfloat16

COS_TERMS = [(-1.0) ** i * math.pi ** (2 * i) / math.factorial(2 * i) for i in range(8)]
SIN_TERMS = [(-1.0) ** i * math.pi ** (2 * i + 1) / math.factorial(2 * i + 1) for i in range(7)]


def params(mebibytes):
    return pltpu.CompilerParams(vmem_limit_bytes=mebibytes * 1024 * 1024)


def place(x):
    return pl.BlockSpec(memory_space=pltpu.VMEM)


def split(x):
    high = x.astype(BF16)
    low = (x - high.astype(F32)).astype(BF16)
    return high, low


def flat_first(ref, field, fold, rows):
    parts = []
    for j in range(ref.shape[0] * fold):
        start = (j % fold * FIELDS + field) * rows
        parts.append(ref[j // fold, start : start + rows])
    return jnp.concatenate(parts, axis=0)


def flat_second(ref, field, rows):
    start = field * rows
    return jnp.concatenate([ref[j, start : start + rows] for j in range(ref.shape[0])], axis=0)


def flat(ref, field, chunks):
    return jnp.concatenate([ref[j, field] for j in range(chunks)], axis=0)


def local_id(ids, owned):
    if owned & (owned - 1) == 0:
        return ids & (owned - 1)
    return lax.rem(ids, owned)


def pack_kernel(
    na, nd, owned_asc, coef_in, ca_in, cd_in, ta_in, td_in, height_in, fill_in, out,
    coef, ca, cd, ta, td, height, fill, turned, sems,
):
    copies = [
        pltpu.make_async_copy(source, target, sems.at[i])
        for i, (source, target) in enumerate(
            [
                (fill_in, fill), (ca_in, ca), (ta_in, ta),
                (cd_in, cd), (td_in, td), (height_in, height), (coef_in, coef),
            ]
        )
    ]
    for copy in copies:
        copy.start()
    for copy in copies:
        copy.wait()
    owned_desc = coef.shape[0]
    blocks, width = ca.shape
    group = width // na
    rows = blocks // na
    fill_row = fill[...]
    row_id = lax.broadcasted_iota(jnp.int32, (blocks, blocks), 0)
    col_id = lax.broadcasted_iota(jnp.int32, (blocks, blocks), 1)
    fill_col = jnp.sum(
        jnp.where(row_id == col_id, fill_row, 0).astype(F32), axis=1, keepdims=True
    )
    lane = lax.broadcasted_iota(jnp.int32, (blocks, width), 1)
    live = lane.astype(F32) < fill_col
    fields = [
        lambda: jnp.where(live, local_id(ca[...], owned_asc).astype(F32), -1.0),
        lambda: ta[...],
        lambda: jnp.where(live, local_id(cd[...], owned_desc).astype(F32), -1.0),
        lambda: td[...],
        lambda: height[...],
    ]
    source = lax.broadcasted_iota(jnp.int32, (width, width), 0)
    target = lax.broadcasted_iota(jnp.int32, (width, width), 1)
    owner = target // group
    place = target - owner * group
    order = (source == place * na + owner).astype(F32).astype(BF16)
    for f, field in enumerate(fields):
        x = field()
        high = x.astype(BF16)
        rest = x - high.astype(F32)
        middle = rest.astype(BF16)
        low = (rest - middle.astype(F32)).astype(BF16)
        turned[f] = (
            jnp.dot(high, order, preferred_element_type=F32)
            + jnp.dot(middle, order, preferred_element_type=F32)
        ) + jnp.dot(low, order, preferred_element_type=F32)
    lane_group = lax.broadcasted_iota(jnp.int32, (rows, width), 1) // group
    for f in range(FIELDS):
        parts = [None] * na
        for k in range(na):
            piece = turned[f, pl.ds(k, rows, stride=na), :]
            for r in range(na):
                amount = ((k - r) * group) % width
                moved = pltpu.roll(piece, amount, 1) if amount else piece
                parts[r] = moved if k == 0 else jnp.where(lane_group == k, moved, parts[r])
        for r in range(na):
            start = (r // nd * FIELDS + f) * rows
            out[r % nd, start : start + rows] = parts[r]
    for q in range(nd):
        out[q, out.shape[1] - owned_desc :] = coef[...]


def cos_sin_pi(x):
    turns = jnp.floor(x + 0.5)
    f = x - turns
    sign = 1.0 - 2.0 * (turns - 2.0 * jnp.floor(turns * 0.5))
    u = f * f
    c = COS_TERMS[-1]
    for term in COS_TERMS[-2::-1]:
        c = c * u + term
    s = SIN_TERMS[-1]
    for term in SIN_TERMS[-2::-1]:
        s = s * u + term
    return c * sign, s * (f * sign)


def rows_pair(ref, rows):
    return jnp.concatenate([ref[pl.ds(r, 1), :] for r in rows], axis=1)


def used_rows(ids_ref, chunks, rows, table):
    count = jnp.int32(0)
    level = lax.broadcasted_iota(jnp.int32, (rows, LANES), 0).astype(F32) + 1.0
    for j in range(chunks):
        ids = ids_ref[j * rows : (j + 1) * rows, :]
        used = jnp.max(jnp.where(ids >= 0.0, level, 0.0)).astype(jnp.int32)
        for i in range(rows):
            table[count + i] = j * rows + i
        count = count + used
    for i in range(TURN * BLOCK_ROWS):
        table[count + i] = chunks * rows
    table[table.shape[0] - 1] = lax.div(count + (BLOCK_ROWS - 1), BLOCK_ROWS)


def listed_rows(table, first, count):
    return [table[first + i] for i in range(count)]


def over_blocks(table, step):
    blocks = table[table.shape[0] - 1]

    def turn(i, carry):
        step([(i * TURN + u, jnp.minimum(i * TURN + u, blocks - 1)) for u in range(TURN)])
        return carry

    lax.fori_loop(0, lax.div(blocks + (TURN - 1), TURN), turn, 0)


def stacked(field):
    high, low = split(field)
    top = jnp.concatenate([high, high], axis=1)
    bottom = jnp.concatenate([low, jnp.zeros_like(low)], axis=1)
    return jnp.concatenate([top, bottom], axis=0)


def forward_step(stack, phi, ids_row, row_iota, owned):
    both = jnp.dot(stack, phi, preferred_element_type=F32)
    value = both[:owned] + both[owned:]
    return jnp.sum(jnp.where(row_iota == ids_row, value, 0.0), axis=0, keepdims=True)


def store_rows(ref, rows, value):
    for i, r in enumerate(rows):
        ref[pl.ds(r, 1), :] = value[:, i * LANES : (i + 1) * LANES]


def basis_loop(table, ids_ref, time_ref, coef, phi_ref, value_ref):
    owned, terms = coef.shape
    half = terms // 2
    value_ref[...] = jnp.zeros(value_ref.shape, F32)
    width = STEP_LANES
    stack = stacked(coef)
    row_iota = lax.broadcasted_iota(jnp.int32, (owned, width), 0).astype(F32)
    fine = (lax.broadcasted_iota(jnp.int32, (8, width), 0) + 1).astype(F32)
    coarse = (lax.broadcasted_iota(jnp.int32, (half // 8, width), 0) * 8).astype(F32)

    def step(block, u):
        rows = listed_rows(table, block * BLOCK_ROWS + u * STEP_ROWS, STEP_ROWS)
        times = rows_pair(time_ref, rows)
        cos_fine, sin_fine = cos_sin_pi(fine * times)
        cos_coarse, sin_coarse = cos_sin_pi(coarse * times)
        cos_parts, sin_parts = [], []
        for j in range(half // 8):
            cj = cos_coarse[j : j + 1]
            sj = sin_coarse[j : j + 1]
            cos_parts.append(cj * cos_fine - sj * sin_fine)
            sin_parts.append(sj * cos_fine + cj * sin_fine)
        high, low = split(jnp.concatenate(cos_parts + sin_parts, axis=0))
        phi = jnp.concatenate([high, low], axis=0)
        phi_ref[block, :, u * width : (u + 1) * width] = phi
        value = forward_step(stack, phi, rows_pair(ids_ref, rows), row_iota, owned)
        store_rows(value_ref, rows, value)

    def whole_block(block, carry):
        for u in range(UNROLL):
            step(block, u)
        return carry

    lax.fori_loop(0, table[table.shape[0] - 1], whole_block, 0)


class Role:
    def __init__(self, sign, send, meta, phi, table, z_ref, value_ref, sum_ref, listed=False):
        if not listed:
            rows = (meta.shape[0] - DUMMY_ROWS) // send.shape[0]
            used_rows(meta, send.shape[0], rows, table)
        self.sign = sign
        self.table = table
        self.ids = meta
        self.phi = phi
        self.z_ref = z_ref
        self.value_ref = value_ref
        self.sum_ref = sum_ref
        self.count = meta.shape[0] - DUMMY_ROWS

    def cross(self, mine, other):
        return mine - other if self.sign > 0 else other - mine

    def backward(self, z, owned):
        high = z.astype(BF16).astype(F32)
        self.z_ref[0, : self.count] = high
        self.z_ref[1, : self.count] = z - high
        self.z_ref[:, self.count :] = jnp.zeros((2, DUMMY_ROWS, LANES), F32)
        blocks, double, width = self.phi.shape
        row_iota = lax.broadcasted_iota(jnp.int32, (owned, width), 0).astype(F32)

        def gather(block, stored):
            rows = listed_rows(self.table, block * BLOCK_ROWS, BLOCK_ROWS)
            hit = row_iota == rows_pair(self.ids, rows)
            parts = [
                jnp.where(hit, rows_pair(self.z_ref.at[k], rows), 0.0).astype(BF16)
                for k in range(2)
            ]
            return lax.dot_general(
                jnp.concatenate(parts, axis=0),
                self.phi[stored],
                (((1,), (1,)), ((), ())),
                preferred_element_type=F32,
            )

        return self.gathered(gather)

    def gathered(self, gather):
        self.sum_ref[...] = jnp.zeros(self.sum_ref.shape, F32)

        def step(blocks):
            self.sum_ref[...] += sum(gather(*block) for block in blocks)

        over_blocks(self.table, step)
        g = self.sum_ref[...]
        owned, terms = g.shape[0] // 2, g.shape[1] // 2
        return self.sign * (g[:owned, :terms] + (g[:owned, terms:] + g[owned:, :terms]))

    def forward(self, field):
        owned = field.shape[0]
        stack = stacked(field)
        row_iota = lax.broadcasted_iota(jnp.int32, (owned, STEP_LANES), 0).astype(F32)
        self.value_ref[...] = jnp.zeros(self.value_ref.shape, F32)

        def ahead(block, stored):
            for u in range(UNROLL):
                rows = listed_rows(self.table, block * BLOCK_ROWS + u * STEP_ROWS, STEP_ROWS)
                phi = self.phi[stored, :, u * STEP_LANES : (u + 1) * STEP_LANES]
                value = forward_step(stack, phi, rows_pair(self.ids, rows), row_iota, owned)
                store_rows(self.value_ref, rows, value)

        def step(blocks):
            for block in blocks:
                ahead(*block)

        over_blocks(self.table, step)
        return self.value_ref[: self.count]

    def forward_image(self, field, other, weight):
        owned = field.shape[0]
        stack = stacked(field)
        blocks, double, width = self.phi.shape
        row_iota = lax.broadcasted_iota(jnp.int32, (owned, width), 0).astype(F32)
        fill_padded(self.z_ref.at[0], other)
        fill_padded(self.z_ref.at[1], weight)
        self.value_ref[...] = jnp.zeros(self.value_ref.shape, F32)

        def both(block, stored):
            rows = listed_rows(self.table, block * BLOCK_ROWS, BLOCK_ROWS)
            phi = self.phi[stored]
            hit = row_iota == rows_pair(self.ids, rows)
            values = []
            for u in range(UNROLL):
                part = slice(u * STEP_LANES, (u + 1) * STEP_LANES)
                product = jnp.dot(stack, phi[:, part], preferred_element_type=F32)
                value = product[:owned] + product[owned:]
                values.append(
                    jnp.sum(jnp.where(hit[:, part], value, 0.0), axis=0, keepdims=True)
                )
            value = jnp.concatenate(values, axis=1)
            store_rows(self.value_ref, rows, value)
            z = rows_pair(self.z_ref.at[1], rows) * self.cross(
                value, rows_pair(self.z_ref.at[0], rows)
            )
            high = z.astype(BF16).astype(F32)
            parts = [jnp.where(hit, x, 0.0).astype(BF16) for x in (high, z - high)]
            return lax.dot_general(
                jnp.concatenate(parts, axis=0),
                phi,
                (((1,), (1,)), ((), ())),
                preferred_element_type=F32,
            )

        image = self.gathered(both)
        return self.value_ref[: self.count], SCALE * (image + damping * field)

    def weigh(self, residual):
        live = self.ids[: self.count] >= 0.0
        misfit = jnp.where(live, residual, 0.0)
        weight = jnp.where(live, 1.0 / (1.0 + misfit * misfit / cauchy_square), 0.0)
        return weight, weight * misfit

    def gradient(self, z, state):
        return self.backward(z, state.shape[0]) - damping * state

    def image(self, z, before):
        return SCALE * (self.backward(z, before.shape[0]) + damping * before)


def write_chunks(send, first, values):
    chunks, rows = send.shape[0], send.shape[2]
    for j in range(chunks):
        send[j, first] = values[j * rows : (j + 1) * rows, :]


def fill_padded(ref, values):
    count = values.shape[0]
    ref[:count] = values
    ref[count:] = jnp.zeros((ref.shape[0] - count,) + values.shape[1:], F32)


def setup_asc_kernel(
    fold, rows, packed, coef, meta, phi, state, short, onward, times, table, value_ref
):
    state[...] = coef[...]
    chunks = packed.shape[0] * fold
    count = chunks * rows
    meta[:count] = flat_first(packed, 0, fold, rows)
    meta[count:] = jnp.full((DUMMY_ROWS, LANES), -1.0, F32)
    fill_padded(times, flat_first(packed, 1, fold, rows))
    used_rows(meta, chunks, rows, table)
    basis_loop(table, meta, times, coef[...], phi, value_ref)
    short[...] = flat_first(packed, 4, fold, rows) - value_ref[:count]
    for j in range(chunks):
        base = j % fold * FIELDS
        for f in range(2):
            start = (base + f + 2) * rows
            onward[j, f * rows : (f + 1) * rows] = packed[j // fold, start : start + rows]
        onward[j, 2 * rows : 3 * rows] = short[j * rows : (j + 1) * rows]
        onward[j, 3 * rows :] = packed[j // fold, fold * FIELDS * rows :]


def setup_desc_kernel(
    fold, rows, packed, meta, phi, state, residual, weights, basis_0, value_0, send,
    times, table, z_ref, value_ref, sum_ref,
):
    chunks = packed.shape[0]
    count = chunks * rows
    home = lax.rem(lax.axis_index("asc"), fold) * (chunks // fold) + lax.axis_index("desc")
    state[...] = packed[home, 3 * rows :]
    meta[:count] = flat_second(packed, 0, rows)
    meta[count:] = jnp.full((DUMMY_ROWS, LANES), -1.0, F32)
    fill_padded(times, flat_second(packed, 1, rows))
    used_rows(meta, chunks, rows, table)
    basis_loop(table, meta, times, state[...], phi, value_ref)
    role = Role(-1.0, send, meta, phi, table, z_ref, value_ref, sum_ref, listed=True)
    own = value_ref[:count]
    write_chunks(send, 0, own)
    left = flat_second(packed, 2, rows) + own
    residual[...] = left
    weights[...], z = role.weigh(left)
    basis_0[...] = role.gradient(z, state[...])
    own = role.forward(basis_0[...])
    value_0[...] = own
    write_chunks(send, 1, own)


def first_asc_kernel(
    chunks, got, short, meta, phi, state,
    residual, weights, crossed_0, basis_0, basis_1, value_1, send, table, z_ref, value_ref, sum_ref,
):
    role = Role(1.0, send, meta, phi, table, z_ref, value_ref, sum_ref)
    left = short[...] + flat(got, 0, chunks)
    residual[...] = left
    weights[...], z = role.weigh(left)
    basis_0[...] = role.gradient(z, state[...])
    other = flat(got, 1, chunks)
    own, basis_1[...] = role.forward_image(basis_0[...], other, weights[...])
    write_chunks(send, 0, own)
    crossed_0[...] = role.cross(own, other)
    own = role.forward(basis_1[...])
    value_1[...] = own
    write_chunks(send, 1, own)


def images_kernel(sign, chunks, keep, got, value_0, meta, phi, weights, basis_0, *rest):
    basis_1, basis_2, send, *kept = rest[:-4]
    role = Role(sign, send, meta, phi, *rest[-4:])
    first = role.cross(value_0[...], flat(got, 0, chunks))
    basis_1[...] = role.image(weights[...] * first, basis_0[...])
    other = flat(got, 1, chunks)
    own, basis_2[...] = role.forward_image(basis_1[...], other, weights[...])
    write_chunks(send, 0, own)
    second = role.cross(own, other)
    own = role.forward(basis_2[...])
    write_chunks(send, 1, own)
    if keep:
        crossed_0, crossed_1, value_2 = kept
        crossed_0[...] = first
        crossed_1[...] = second
        value_2[...] = own


def total(x):
    return jnp.sum(jnp.sum(x, axis=0, keepdims=True), axis=1, keepdims=True)


PAIRS = [(0, 0), (0, 1), (0, 2), (1, 1), (1, 2), (2, 2)]


def gram_kernel(
    sign, chunks, keep, got, value_1, meta, phi, weights, crossed_0, basis_0, basis_1,
    other_0, other_1, other_2, *rest,
):
    basis_2, scalars, *kept = rest[:-4]
    role = Role(sign, got, meta, phi, *rest[-4:])
    weight = weights[...]
    crossed = role.cross(value_1[...], flat(got, 0, chunks))
    basis_2[...] = role.image(weight * crossed, basis_1[...])
    own = role.forward(basis_2[...])
    last = role.cross(own, flat(got, 1, chunks))
    if keep:
        crossed_1, crossed_2, value_2 = kept
        crossed_1[...] = crossed
        crossed_2[...] = last
        value_2[...] = own
    values = [crossed_0[...], crossed, last]
    mine = [basis_0[...], basis_1[...], basis_2[...]]
    others = [other_0[...], other_1[...], other_2[...]]
    lane = lax.broadcasted_iota(jnp.int32, (1, LANES), 1)
    line = jnp.zeros((1, LANES), F32)
    for place_in_line, (i, j) in enumerate(PAIRS):
        dots = total(mine[i] * mine[j] + others[i] * others[j])
        curve = total(weight * values[i] * values[j]) + damping * dots
        line = jnp.where(lane == place_in_line, curve, line)
        if i == 0:
            line = jnp.where(lane == len(PAIRS) + j, dots, line)
    for d in range(scalars.shape[0]):
        scalars[d] = line


def solve(scalars):
    summed = scalars[0]
    for d in range(1, scalars.shape[0]):
        summed = summed + scalars[d]
    line = summed
    lane = lax.broadcasted_iota(jnp.int32, (1, LANES), 1)

    def pick(place):
        return jnp.sum(jnp.where(lane == place, line, 0.0), axis=1, keepdims=True)

    g = {pair: pick(place) for place, pair in enumerate(PAIRS)}
    right = [pick(len(PAIRS) + i) for i in range(3)]
    s = [
        jnp.where(g[i, i] > 0.0, lax.rsqrt(jnp.maximum(g[i, i], 1e-37)), 0.0) for i in range(3)
    ]
    l10 = g[0, 1] * s[0] * s[1]
    l20 = g[0, 2] * s[0] * s[2]
    g21 = g[1, 2] * s[1] * s[2]
    c = [right[i] * s[i] for i in range(3)]

    def inverse(pivot):
        good = pivot > PIVOT_FLOOR
        return jnp.where(good, 1.0 / jnp.where(good, pivot, 1.0), 0.0)

    inv1 = inverse(1.0 - l10 * l10)
    t21 = g21 - l20 * l10
    l21 = t21 * inv1
    inv2 = inverse(1.0 - l20 * l20 - l21 * t21)
    u1 = c[1] - l10 * c[0]
    u2 = c[2] - l20 * c[0] - l21 * u1
    x2 = u2 * inv2
    x1 = u1 * inv1 - l21 * x2
    x0 = c[0] - l10 * x1 - l20 * x2
    return [x0 * s[0], x1 * s[1], x2 * s[2]]


def combine(y, parts):
    return y[0] * parts[0] + (y[1] * parts[1] + y[2] * parts[2])


def next_asc_kernel(
    chunks, scalars, meta, phi, residual, crossed_0, crossed_1, crossed_2,
    basis_a0, basis_a1, basis_a2, basis_d0, basis_d1, basis_d2, state_a, state_d, value_2,
    new_a, new_d, shares, weights, basis_0, value_0, send, table, z_ref, value_ref, sum_ref,
):
    role = Role(1.0, send, meta, phi, table, z_ref, value_ref, sum_ref)
    write_chunks(send, 0, value_2[...])
    y = solve(scalars)
    for i in range(3):
        shares[i : i + 1] = jnp.broadcast_to(y[i], (1, LANES))
    left = residual[...] - combine(y, [crossed_0[...], crossed_1[...], crossed_2[...]])
    new_a[...] = state_a[...] + combine(y, [basis_a0[...], basis_a1[...], basis_a2[...]])
    new_d[...] = state_d[...] + combine(y, [basis_d0[...], basis_d1[...], basis_d2[...]])
    weights[...], z = role.weigh(left)
    basis_0[...] = role.gradient(z, new_a[...])
    own = role.forward(basis_0[...])
    value_0[...] = own
    write_chunks(send, 1, own)


def next_desc_kernel(
    chunks, got, shares, meta, phi, residual, crossed_0, crossed_1, value_2, state,
    weights, new_crossed_0, basis_0, basis_1, value_1, send, table, z_ref, value_ref, sum_ref,
):
    role = Role(-1.0, send, meta, phi, table, z_ref, value_ref, sum_ref)
    y = [shares[i : i + 1] for i in range(3)]
    crossed_2 = role.cross(value_2[...], flat(got, 0, chunks))
    left = residual[...] - combine(y, [crossed_0[...], crossed_1[...], crossed_2])
    weights[...], z = role.weigh(left)
    basis_0[...] = role.gradient(z, state[...])
    other = flat(got, 1, chunks)
    own, basis_1[...] = role.forward_image(basis_0[...], other, weights[...])
    write_chunks(send, 0, own)
    new_crossed_0[...] = role.cross(own, other)
    own = role.forward(basis_1[...])
    value_1[...] = own
    write_chunks(send, 1, own)


def final_kernel(scalars, state_a, basis_0, basis_1, basis_2, desc, out_a, out_d):
    y = solve(scalars)
    out_a[...] = state_a[...] + combine(y, [basis_0[...], basis_1[...], basis_2[...]])
    out_d[...] = desc[0] + combine(y, [desc[1], desc[2], desc[3]])


def body(coef_asc, coef_desc, cross_asc, cross_desc, time_asc, time_desc, height, block_fill):
    owned_asc, terms = coef_asc.shape
    owned_desc = coef_desc.shape[0]
    blocks, width = cross_asc.shape
    na = lax.axis_size("asc")
    nd = lax.axis_size("desc")
    fold = na // nd
    rows = blocks * width // na // LANES
    all_rows = na * rows
    all_blocks = -(-all_rows // BLOCK_ROWS)
    shape = jax.ShapeDtypeStruct

    def call(kernel, outs, scratch, *args, in_specs=None, mebibytes=16):
        return pl.pallas_call(
            kernel,
            out_shape=outs,
            in_specs=[place(x) for x in args] if in_specs is None else in_specs,
            out_specs=jax.tree.map(place, outs),
            scratch_shapes=scratch,
            compiler_params=params(mebibytes),
        )(*args)

    to_role = []
    for p in range(na):
        for q in range(nd):
            to_role.append((p * nd + q, (q * fold + p // nd) * nd + p % nd))
    to_native = [(b, a) for a, b in to_role]
    slots = (cross_asc, cross_desc, time_asc, time_desc, height)
    packed = call(
        functools.partial(pack_kernel, na, nd, owned_asc),
        shape((nd, fold * FIELDS * rows + owned_desc, LANES), F32),
        [pltpu.VMEM(coef_desc.shape, F32)]
        + [pltpu.VMEM((blocks, width), x.dtype) for x in slots]
        + [
            pltpu.VMEM((1, blocks), jnp.int32),
            pltpu.VMEM((FIELDS, blocks, width), F32),
            pltpu.SemaphoreType.DMA((len(slots) + 2,)),
        ],
        coef_desc, *slots, block_fill.reshape(1, blocks),
        in_specs=[pl.BlockSpec(memory_space=pltpu.HBM)] * (len(slots) + 2),
        mebibytes=60,
    )
    at_asc = lax.all_to_all(packed, "desc", split_axis=0, concat_axis=0, tiled=True)

    padded = all_rows + DUMMY_ROWS
    meta_shape = shape((padded, LANES), F32)
    phi_shape = shape((all_blocks, 2 * terms, BLOCK_ROWS * LANES), BF16)
    role_shapes = [meta_shape, phi_shape]
    table = pltpu.SMEM((all_rows + rows + TURN * BLOCK_ROWS + 1,), jnp.int32)
    slot_shape = shape((all_rows, LANES), F32)
    send_shape = shape((na, 2, rows, LANES), F32)
    field_a = shape(coef_asc.shape, F32)
    field_d = shape(coef_desc.shape, F32)
    line_shape = shape((na * nd, 1, LANES), F32)
    times_scratch = pltpu.VMEM((padded, LANES), F32)
    scratch = [
        table, pltpu.VMEM((2, padded, LANES), F32), pltpu.VMEM((padded, LANES), F32),
        pltpu.VMEM((2 * owned_asc, 2 * terms), F32),
    ]

    def exchange(x):
        return lax.all_to_all(x, "asc", split_axis=0, concat_axis=0, tiled=True)

    def share(x):
        return lax.all_to_all(x, ("asc", "desc"), split_axis=0, concat_axis=0, tiled=True)

    *asc, state_a, short, onward = call(
        functools.partial(setup_asc_kernel, fold, rows),
        role_shapes + [field_a, slot_shape, shape((na, 3 * rows + owned_desc, LANES), F32)],
        [times_scratch, table, scratch[2]],
        at_asc, coef_asc,
    )
    *desc, state_d, residual_d, weights_d, d0, own_d, send = call(
        functools.partial(setup_desc_kernel, fold, rows),
        role_shapes + [field_d, slot_shape, slot_shape, field_d, slot_shape, send_shape],
        [times_scratch] + scratch,
        exchange(onward),
    )
    residual_a, weights_a, crossed_a0, a0, a1, own_a, send = call(
        functools.partial(first_asc_kernel, na),
        [slot_shape, slot_shape, slot_shape, field_a, field_a, slot_shape, send_shape],
        scratch,
        exchange(send), short, *asc, state_a,
    )
    kept = [slot_shape] * 3
    d1, d2, send, crossed_d0, crossed_d1, own_d = call(
        functools.partial(images_kernel, -1.0, na, True),
        [field_d, field_d, send_shape] + kept,
        scratch,
        exchange(send), own_d, *desc, weights_d, d0,
    )
    a2, scalars, crossed_a1, crossed_a2, own_a = call(
        functools.partial(gram_kernel, 1.0, na, True),
        [field_a, line_shape] + kept,
        scratch,
        exchange(send), own_a, *asc, weights_a, crossed_a0, a0, a1, d0, d1, d2,
    )
    state_a, state_d, shares, weights_a, a0, own_a, send = call(
        functools.partial(next_asc_kernel, na),
        [
            field_a, field_d, shape((8, LANES), F32),
            slot_shape, field_a, slot_shape, send_shape,
        ],
        scratch,
        share(scalars), *asc, residual_a, crossed_a0, crossed_a1, crossed_a2,
        a0, a1, a2, d0, d1, d2, state_a, state_d, own_a,
    )
    weights_d, crossed_d0, d0, d1, own_d, send = call(
        functools.partial(next_desc_kernel, na),
        [slot_shape, slot_shape, field_d, field_d, slot_shape, send_shape],
        scratch,
        exchange(send), shares, *desc, residual_d, crossed_d0, crossed_d1, own_d, state_d,
    )
    a1, a2, send = call(
        functools.partial(images_kernel, 1.0, na, False),
        [field_a, field_a, send_shape],
        scratch,
        exchange(send), own_a, *asc, weights_a, a0,
    )
    d2, scalars = call(
        functools.partial(gram_kernel, -1.0, na, False),
        [field_d, line_shape],
        scratch,
        exchange(send), own_d, *desc, weights_d, crossed_d0, d0, d1, a0, a1, a2,
    )
    leaving = jnp.stack([state_d, d0, d1, d2])
    native = lax.ppermute(leaving, ("asc", "desc"), to_native)
    return tuple(
        call(
            final_kernel,
            [field_a, field_d],
            [],
            share(scalars), state_a, a0, a1, a2, native,
        )
    )


def solution(mesh):
    split_rows = P(("asc", "desc"), None)
    return jax.shard_map(
        body,
        mesh=mesh,
        in_specs=(split_rows,) * 7 + (P(("asc", "desc")),),
        out_specs=(split_rows, split_rows),
        check_vma=False,
    )
```

```python
import functools
import math

import jax
import jax.numpy as jnp
from jax import lax
from jax.experimental import pallas as pl
from jax.experimental.pallas import tpu as pltpu
from jax.sharding import PartitionSpec as P

GN_STEPS = 2
damping = 2.0
cauchy_square = 2.25

LANES = 128
STEP_ROWS = 2
UNROLL = 4
BLOCK_ROWS = STEP_ROWS * UNROLL
STEP_LANES = STEP_ROWS * LANES
DUMMY_ROWS = 8
TURNS = (4, 1)
SCALE = 1.0 / 128.0
FIELDS = 5
PIVOT_FLOOR = 1e-6
F32 = jnp.float32
BF16 = jnp.bfloat16

COS_TERMS = [(-1.0) ** i * math.pi ** (2 * i) / math.factorial(2 * i) for i in range(8)]
SIN_TERMS = [(-1.0) ** i * math.pi ** (2 * i + 1) / math.factorial(2 * i + 1) for i in range(7)]


def params(mebibytes):
    return pltpu.CompilerParams(vmem_limit_bytes=mebibytes * 1024 * 1024)


def place(x):
    return pl.BlockSpec(memory_space=pltpu.VMEM)


def split(x):
    high = x.astype(BF16)
    low = (x - high.astype(F32)).astype(BF16)
    return high, low


def flat_first(ref, field, fold, rows):
    parts = []
    for j in range(ref.shape[0] * fold):
        start = (j % fold * FIELDS + field) * rows
        parts.append(ref[j // fold, start : start + rows])
    return jnp.concatenate(parts, axis=0)


def flat_second(ref, field, rows):
    start = field * rows
    return jnp.concatenate([ref[j, start : start + rows] for j in range(ref.shape[0])], axis=0)


def flat(ref, field, chunks):
    return jnp.concatenate([ref[j, field] for j in range(chunks)], axis=0)


def local_id(ids, owned):
    if owned & (owned - 1) == 0:
        return ids & (owned - 1)
    return lax.rem(ids, owned)


def pack_kernel(
    na, nd, owned_asc, owned_desc, ca_in, cd_in, ta_in, td_in, height_in, fill_in, out,
    ca, cd, ta, td, height, fill, turned, sems,
):
    copies = [
        pltpu.make_async_copy(source, target, sems.at[i])
        for i, (source, target) in enumerate(
            [
                (fill_in, fill), (ca_in, ca), (ta_in, ta),
                (cd_in, cd), (td_in, td), (height_in, height),
            ]
        )
    ]
    for copy in copies:
        copy.start()
    for copy in copies:
        copy.wait()
    blocks, width = ca.shape
    group = width // na
    rows = blocks // na
    fill_row = fill[...]
    row_id = lax.broadcasted_iota(jnp.int32, (blocks, blocks), 0)
    col_id = lax.broadcasted_iota(jnp.int32, (blocks, blocks), 1)
    fill_col = jnp.sum(
        jnp.where(row_id == col_id, fill_row, 0).astype(F32), axis=1, keepdims=True
    )
    lane = lax.broadcasted_iota(jnp.int32, (blocks, width), 1)
    live = lane.astype(F32) < fill_col
    fields = [
        lambda: jnp.where(live, local_id(ca[...], owned_asc).astype(F32), -1.0),
        lambda: ta[...],
        lambda: jnp.where(live, local_id(cd[...], owned_desc).astype(F32), -1.0),
        lambda: td[...],
        lambda: height[...],
    ]
    source = lax.broadcasted_iota(jnp.int32, (width, width), 0)
    target = lax.broadcasted_iota(jnp.int32, (width, width), 1)
    owner = target // group
    place = target - owner * group
    order = (source == place * na + owner).astype(F32).astype(BF16)
    for f, field in enumerate(fields):
        x = field()
        high = x.astype(BF16)
        rest = x - high.astype(F32)
        middle = rest.astype(BF16)
        low = (rest - middle.astype(F32)).astype(BF16)
        turned[f] = (
            jnp.dot(high, order, preferred_element_type=F32)
            + jnp.dot(middle, order, preferred_element_type=F32)
        ) + jnp.dot(low, order, preferred_element_type=F32)
    lane_group = lax.broadcasted_iota(jnp.int32, (rows, width), 1) // group
    for f in range(FIELDS):
        parts = [None] * na
        for k in range(na):
            piece = turned[f, pl.ds(k, rows, stride=na), :]
            for r in range(na):
                amount = ((k - r) * group) % width
                moved = pltpu.roll(piece, amount, 1) if amount else piece
                parts[r] = moved if k == 0 else jnp.where(lane_group == k, moved, parts[r])
        for r in range(na):
            start = (r // nd * FIELDS + f) * rows
            out[r % nd, start : start + rows] = parts[r]


def cos_sin_pi(x):
    turns = jnp.floor(x + 0.5)
    f = x - turns
    sign = 1.0 - 2.0 * (turns - 2.0 * jnp.floor(turns * 0.5))
    u = f * f
    c = COS_TERMS[-1]
    for term in COS_TERMS[-2::-1]:
        c = c * u + term
    s = SIN_TERMS[-1]
    for term in SIN_TERMS[-2::-1]:
        s = s * u + term
    return c * sign, s * (f * sign)


def rows_pair(ref, rows):
    return jnp.concatenate([ref[pl.ds(r, 1), :] for r in rows], axis=1)


def used_rows(ids_ref, chunks, rows, table):
    count = jnp.int32(0)
    level = lax.broadcasted_iota(jnp.int32, (rows, LANES), 0).astype(F32) + 1.0
    for j in range(chunks):
        ids = ids_ref[j * rows : (j + 1) * rows, :]
        used = jnp.max(jnp.where(ids >= 0.0, level, 0.0)).astype(jnp.int32)
        for i in range(rows):
            table[count + i] = j * rows + i
        count = count + used
    for i in range(BLOCK_ROWS):
        table[count + i] = chunks * rows
    table[table.shape[0] - 1] = lax.div(count + (BLOCK_ROWS - 1), BLOCK_ROWS)


def listed_rows(table, first, count):
    return [table[first + i] for i in range(count)]


def over_blocks(table, step):
    blocks = table[table.shape[0] - 1]
    done = jnp.int32(0)
    for size in TURNS:
        turns = lax.div(blocks - done, size)

        def turn(i, carry, done=done, size=size):
            step([done + i * size + u for u in range(size)])
            return carry

        lax.fori_loop(0, turns, turn, 0)
        done = done + turns * size


def stacked(field):
    high, low = split(field)
    top = jnp.concatenate([high, high], axis=1)
    bottom = jnp.concatenate([low, jnp.zeros_like(low)], axis=1)
    return jnp.concatenate([top, bottom], axis=0)


def forward_step(stack, phi, ids_row, row_iota, owned):
    both = jnp.dot(stack, phi, preferred_element_type=F32)
    value = both[:owned] + both[owned:]
    return jnp.sum(jnp.where(row_iota == ids_row, value, 0.0), axis=0, keepdims=True)


def store_rows(ref, rows, value):
    for i, r in enumerate(rows):
        ref[pl.ds(r, 1), :] = value[:, i * LANES : (i + 1) * LANES]


def basis_loop(table, ids_ref, time_ref, coef, phi_ref, value_ref):
    owned, terms = coef.shape
    half = terms // 2
    value_ref[...] = jnp.zeros(value_ref.shape, F32)
    width = STEP_LANES
    stack = stacked(coef)
    row_iota = lax.broadcasted_iota(jnp.int32, (owned, width), 0).astype(F32)
    fine = (lax.broadcasted_iota(jnp.int32, (8, width), 0) + 1).astype(F32)
    coarse = (lax.broadcasted_iota(jnp.int32, (half // 8, width), 0) * 8).astype(F32)

    def step(block, u):
        rows = listed_rows(table, block * BLOCK_ROWS + u * STEP_ROWS, STEP_ROWS)
        times = rows_pair(time_ref, rows)
        cos_fine, sin_fine = cos_sin_pi(fine * times)
        cos_coarse, sin_coarse = cos_sin_pi(coarse * times)
        cos_parts, sin_parts = [], []
        for j in range(half // 8):
            cj = cos_coarse[j : j + 1]
            sj = sin_coarse[j : j + 1]
            cos_parts.append(cj * cos_fine - sj * sin_fine)
            sin_parts.append(sj * cos_fine + cj * sin_fine)
        high, low = split(jnp.concatenate(cos_parts + sin_parts, axis=0))
        phi = jnp.concatenate([high, low], axis=0)
        phi_ref[block, :, u * width : (u + 1) * width] = phi
        value = forward_step(stack, phi, rows_pair(ids_ref, rows), row_iota, owned)
        store_rows(value_ref, rows, value)

    def whole_block(block, carry):
        for u in range(UNROLL):
            step(block, u)
        return carry

    lax.fori_loop(0, table[table.shape[0] - 1], whole_block, 0)


class Role:
    def __init__(self, sign, send, meta, phi, table, z_ref, value_ref, sum_ref, listed=False):
        if not listed:
            rows = (meta.shape[0] - DUMMY_ROWS) // send.shape[0]
            used_rows(meta, send.shape[0], rows, table)
        self.sign = sign
        self.table = table
        self.ids = meta
        self.phi = phi
        self.z_ref = z_ref
        self.value_ref = value_ref
        self.sum_ref = sum_ref
        self.count = meta.shape[0] - DUMMY_ROWS

    def cross(self, mine, other):
        return mine - other if self.sign > 0 else other - mine

    def backward(self, z, owned):
        high = z.astype(BF16).astype(F32)
        self.z_ref[0, : self.count] = high
        self.z_ref[1, : self.count] = z - high
        self.z_ref[:, self.count :] = jnp.zeros((2, DUMMY_ROWS, LANES), F32)
        blocks, double, width = self.phi.shape
        row_iota = lax.broadcasted_iota(jnp.int32, (owned, width), 0).astype(F32)

        def gather(block):
            rows = listed_rows(self.table, block * BLOCK_ROWS, BLOCK_ROWS)
            hit = row_iota == rows_pair(self.ids, rows)
            parts = [
                jnp.where(hit, rows_pair(self.z_ref.at[k], rows), 0.0).astype(BF16)
                for k in range(2)
            ]
            return lax.dot_general(
                jnp.concatenate(parts, axis=0),
                self.phi[block],
                (((1,), (1,)), ((), ())),
                preferred_element_type=F32,
            )

        return self.gathered(gather)

    def gathered(self, gather):
        self.sum_ref[...] = jnp.zeros(self.sum_ref.shape, F32)

        def step(blocks):
            self.sum_ref[...] += sum(gather(block) for block in blocks)

        over_blocks(self.table, step)
        g = self.sum_ref[...]
        owned, terms = g.shape[0] // 2, g.shape[1] // 2
        return self.sign * (g[:owned, :terms] + (g[:owned, terms:] + g[owned:, :terms]))

    def forward(self, field):
        owned = field.shape[0]
        stack = stacked(field)
        row_iota = lax.broadcasted_iota(jnp.int32, (owned, STEP_LANES), 0).astype(F32)
        self.value_ref[...] = jnp.zeros(self.value_ref.shape, F32)

        def ahead(block):
            for u in range(UNROLL):
                rows = listed_rows(self.table, block * BLOCK_ROWS + u * STEP_ROWS, STEP_ROWS)
                phi = self.phi[block, :, u * STEP_LANES : (u + 1) * STEP_LANES]
                value = forward_step(stack, phi, rows_pair(self.ids, rows), row_iota, owned)
                store_rows(self.value_ref, rows, value)

        def step(blocks):
            for block in blocks:
                ahead(block)

        over_blocks(self.table, step)
        return self.value_ref[: self.count]

    def forward_image(self, field, other, weight):
        owned = field.shape[0]
        stack = stacked(field)
        blocks, double, width = self.phi.shape
        row_iota = lax.broadcasted_iota(jnp.int32, (owned, width), 0).astype(F32)
        fill_padded(self.z_ref.at[0], other)
        fill_padded(self.z_ref.at[1], weight)
        self.value_ref[...] = jnp.zeros(self.value_ref.shape, F32)

        def both(block):
            rows = listed_rows(self.table, block * BLOCK_ROWS, BLOCK_ROWS)
            phi = self.phi[block]
            hit = row_iota == rows_pair(self.ids, rows)
            values = []
            for u in range(UNROLL):
                part = slice(u * STEP_LANES, (u + 1) * STEP_LANES)
                product = jnp.dot(stack, phi[:, part], preferred_element_type=F32)
                value = product[:owned] + product[owned:]
                values.append(
                    jnp.sum(jnp.where(hit[:, part], value, 0.0), axis=0, keepdims=True)
                )
            value = jnp.concatenate(values, axis=1)
            store_rows(self.value_ref, rows, value)
            z = rows_pair(self.z_ref.at[1], rows) * self.cross(
                value, rows_pair(self.z_ref.at[0], rows)
            )
            high = z.astype(BF16).astype(F32)
            parts = [jnp.where(hit, x, 0.0).astype(BF16) for x in (high, z - high)]
            return lax.dot_general(
                jnp.concatenate(parts, axis=0),
                phi,
                (((1,), (1,)), ((), ())),
                preferred_element_type=F32,
            )

        image = self.gathered(both)
        return self.value_ref[: self.count], SCALE * (image + damping * field)

    def weigh(self, residual):
        live = self.ids[: self.count] >= 0.0
        misfit = jnp.where(live, residual, 0.0)
        weight = jnp.where(live, 1.0 / (1.0 + misfit * misfit / cauchy_square), 0.0)
        return weight, weight * misfit

    def gradient(self, z, state):
        return self.backward(z, state.shape[0]) - damping * state

    def image(self, z, before):
        return SCALE * (self.backward(z, before.shape[0]) + damping * before)


def write_chunks(send, first, values):
    chunks, rows = send.shape[0], send.shape[2]
    for j in range(chunks):
        send[j, first] = values[j * rows : (j + 1) * rows, :]


def fill_padded(ref, values):
    count = values.shape[0]
    ref[:count] = values
    ref[count:] = jnp.zeros((ref.shape[0] - count,) + values.shape[1:], F32)


def setup_asc_kernel(
    fold, rows, packed, coef, meta, phi, state, short, onward, times, table, value_ref
):
    state[...] = coef[...]
    chunks = packed.shape[0] * fold
    count = chunks * rows
    meta[:count] = flat_first(packed, 0, fold, rows)
    meta[count:] = jnp.full((DUMMY_ROWS, LANES), -1.0, F32)
    fill_padded(times, flat_first(packed, 1, fold, rows))
    used_rows(meta, chunks, rows, table)
    basis_loop(table, meta, times, coef[...], phi, value_ref)
    short[...] = flat_first(packed, 4, fold, rows) - value_ref[:count]
    for j in range(chunks):
        base = j % fold * FIELDS
        for f in range(2):
            start = (base + f + 2) * rows
            onward[j, f * rows : (f + 1) * rows] = packed[j // fold, start : start + rows]
        onward[j, 2 * rows : 3 * rows] = short[j * rows : (j + 1) * rows]


def setup_desc_kernel(
    fold, rows, packed, state, meta, phi, residual, weights, basis_0, value_0, send,
    times, table, z_ref, value_ref, sum_ref,
):
    chunks = packed.shape[0]
    count = chunks * rows
    meta[:count] = flat_second(packed, 0, rows)
    meta[count:] = jnp.full((DUMMY_ROWS, LANES), -1.0, F32)
    fill_padded(times, flat_second(packed, 1, rows))
    used_rows(meta, chunks, rows, table)
    basis_loop(table, meta, times, state[...], phi, value_ref)
    role = Role(-1.0, send, meta, phi, table, z_ref, value_ref, sum_ref, listed=True)
    own = value_ref[:count]
    write_chunks(send, 0, own)
    left = flat_second(packed, 2, rows) + own
    residual[...] = left
    weights[...], z = role.weigh(left)
    basis_0[...] = role.gradient(z, state[...])
    own = role.forward(basis_0[...])
    value_0[...] = own
    write_chunks(send, 1, own)


def first_asc_kernel(
    chunks, got, short, meta, phi, state,
    residual, weights, crossed_0, basis_0, basis_1, value_1, send, table, z_ref, value_ref, sum_ref,
):
    role = Role(1.0, send, meta, phi, table, z_ref, value_ref, sum_ref)
    left = short[...] + flat(got, 0, chunks)
    residual[...] = left
    weights[...], z = role.weigh(left)
    basis_0[...] = role.gradient(z, state[...])
    other = flat(got, 1, chunks)
    own, basis_1[...] = role.forward_image(basis_0[...], other, weights[...])
    write_chunks(send, 0, own)
    crossed_0[...] = role.cross(own, other)
    own = role.forward(basis_1[...])
    value_1[...] = own
    write_chunks(send, 1, own)


def images_kernel(sign, chunks, keep, got, value_0, meta, phi, weights, basis_0, *rest):
    basis_1, basis_2, send, *kept = rest[:-4]
    role = Role(sign, send, meta, phi, *rest[-4:])
    first = role.cross(value_0[...], flat(got, 0, chunks))
    basis_1[...] = role.image(weights[...] * first, basis_0[...])
    other = flat(got, 1, chunks)
    own, basis_2[...] = role.forward_image(basis_1[...], other, weights[...])
    write_chunks(send, 0, own)
    second = role.cross(own, other)
    own = role.forward(basis_2[...])
    write_chunks(send, 1, own)
    if keep:
        crossed_0, crossed_1, value_2 = kept
        crossed_0[...] = first
        crossed_1[...] = second
        value_2[...] = own


def total(x):
    return jnp.sum(jnp.sum(x, axis=0, keepdims=True), axis=1, keepdims=True)


PAIRS = [(0, 0), (0, 1), (0, 2), (1, 1), (1, 2), (2, 2)]


def gram_kernel(
    sign, chunks, keep, got, value_1, meta, phi, weights, crossed_0, basis_0, basis_1,
    other_0, other_1, other_2, *rest,
):
    basis_2, scalars, *kept = rest[:-4]
    role = Role(sign, got, meta, phi, *rest[-4:])
    weight = weights[...]
    crossed = role.cross(value_1[...], flat(got, 0, chunks))
    basis_2[...] = role.image(weight * crossed, basis_1[...])
    own = role.forward(basis_2[...])
    last = role.cross(own, flat(got, 1, chunks))
    if keep:
        crossed_1, crossed_2, value_2 = kept
        crossed_1[...] = crossed
        crossed_2[...] = last
        value_2[...] = own
    values = [crossed_0[...], crossed, last]
    mine = [basis_0[...], basis_1[...], basis_2[...]]
    others = [other_0[...], other_1[...], other_2[...]]
    lane = lax.broadcasted_iota(jnp.int32, (1, LANES), 1)
    line = jnp.zeros((1, LANES), F32)
    for place_in_line, (i, j) in enumerate(PAIRS):
        dots = total(mine[i] * mine[j] + others[i] * others[j])
        curve = total(weight * values[i] * values[j]) + damping * dots
        line = jnp.where(lane == place_in_line, curve, line)
        if i == 0:
            line = jnp.where(lane == len(PAIRS) + j, dots, line)
    for d in range(scalars.shape[0]):
        scalars[d] = line


def solve(scalars):
    summed = scalars[0]
    for d in range(1, scalars.shape[0]):
        summed = summed + scalars[d]
    line = summed
    lane = lax.broadcasted_iota(jnp.int32, (1, LANES), 1)

    def pick(place):
        return jnp.sum(jnp.where(lane == place, line, 0.0), axis=1, keepdims=True)

    g = {pair: pick(place) for place, pair in enumerate(PAIRS)}
    right = [pick(len(PAIRS) + i) for i in range(3)]
    s = [
        jnp.where(g[i, i] > 0.0, lax.rsqrt(jnp.maximum(g[i, i], 1e-37)), 0.0) for i in range(3)
    ]
    l10 = g[0, 1] * s[0] * s[1]
    l20 = g[0, 2] * s[0] * s[2]
    g21 = g[1, 2] * s[1] * s[2]
    c = [right[i] * s[i] for i in range(3)]

    def inverse(pivot):
        good = pivot > PIVOT_FLOOR
        return jnp.where(good, 1.0 / jnp.where(good, pivot, 1.0), 0.0)

    inv1 = inverse(1.0 - l10 * l10)
    t21 = g21 - l20 * l10
    l21 = t21 * inv1
    inv2 = inverse(1.0 - l20 * l20 - l21 * t21)
    u1 = c[1] - l10 * c[0]
    u2 = c[2] - l20 * c[0] - l21 * u1
    x2 = u2 * inv2
    x1 = u1 * inv1 - l21 * x2
    x0 = c[0] - l10 * x1 - l20 * x2
    return [x0 * s[0], x1 * s[1], x2 * s[2]]


def combine(y, parts):
    return y[0] * parts[0] + (y[1] * parts[1] + y[2] * parts[2])


def next_asc_kernel(
    chunks, scalars, meta, phi, residual, crossed_0, crossed_1, crossed_2,
    basis_a0, basis_a1, basis_a2, basis_d0, basis_d1, basis_d2, state_a, state_d, value_2,
    new_a, new_d, shares, weights, basis_0, value_0, send, table, z_ref, value_ref, sum_ref,
):
    role = Role(1.0, send, meta, phi, table, z_ref, value_ref, sum_ref)
    write_chunks(send, 0, value_2[...])
    y = solve(scalars)
    for i in range(3):
        shares[i : i + 1] = jnp.broadcast_to(y[i], (1, LANES))
    left = residual[...] - combine(y, [crossed_0[...], crossed_1[...], crossed_2[...]])
    new_a[...] = state_a[...] + combine(y, [basis_a0[...], basis_a1[...], basis_a2[...]])
    new_d[...] = state_d[...] + combine(y, [basis_d0[...], basis_d1[...], basis_d2[...]])
    weights[...], z = role.weigh(left)
    basis_0[...] = role.gradient(z, new_a[...])
    own = role.forward(basis_0[...])
    value_0[...] = own
    write_chunks(send, 1, own)


def next_desc_kernel(
    chunks, got, shares, meta, phi, residual, crossed_0, crossed_1, value_2, state,
    weights, new_crossed_0, basis_0, basis_1, value_1, send, table, z_ref, value_ref, sum_ref,
):
    role = Role(-1.0, send, meta, phi, table, z_ref, value_ref, sum_ref)
    y = [shares[i : i + 1] for i in range(3)]
    crossed_2 = role.cross(value_2[...], flat(got, 0, chunks))
    left = residual[...] - combine(y, [crossed_0[...], crossed_1[...], crossed_2])
    weights[...], z = role.weigh(left)
    basis_0[...] = role.gradient(z, state[...])
    other = flat(got, 1, chunks)
    own, basis_1[...] = role.forward_image(basis_0[...], other, weights[...])
    write_chunks(send, 0, own)
    new_crossed_0[...] = role.cross(own, other)
    own = role.forward(basis_1[...])
    value_1[...] = own
    write_chunks(send, 1, own)


def final_kernel(scalars, state_a, basis_0, basis_1, basis_2, desc, out_a, out_d):
    y = solve(scalars)
    out_a[...] = state_a[...] + combine(y, [basis_0[...], basis_1[...], basis_2[...]])
    out_d[...] = desc[0] + combine(y, [desc[1], desc[2], desc[3]])


def body(coef_asc, coef_desc, cross_asc, cross_desc, time_asc, time_desc, height, block_fill):
    owned_asc, terms = coef_asc.shape
    owned_desc = coef_desc.shape[0]
    blocks, width = cross_asc.shape
    na = lax.axis_size("asc")
    nd = lax.axis_size("desc")
    fold = na // nd
    rows = blocks * width // na // LANES
    all_rows = na * rows
    all_blocks = -(-all_rows // BLOCK_ROWS)
    shape = jax.ShapeDtypeStruct

    def call(kernel, outs, scratch, *args, in_specs=None, mebibytes=16):
        return pl.pallas_call(
            kernel,
            out_shape=outs,
            in_specs=[place(x) for x in args] if in_specs is None else in_specs,
            out_specs=jax.tree.map(place, outs),
            scratch_shapes=scratch,
            compiler_params=params(mebibytes),
        )(*args)

    to_role = []
    for p in range(na):
        for q in range(nd):
            to_role.append((p * nd + q, (q * fold + p // nd) * nd + p % nd))
    to_native = [(b, a) for a, b in to_role]
    slots = (cross_asc, cross_desc, time_asc, time_desc, height)
    packed = call(
        functools.partial(pack_kernel, na, nd, owned_asc, owned_desc),
        shape((nd, fold * FIELDS * rows, LANES), F32),
        [pltpu.VMEM((blocks, width), x.dtype) for x in slots]
        + [
            pltpu.VMEM((1, blocks), jnp.int32),
            pltpu.VMEM((FIELDS, blocks, width), F32),
            pltpu.SemaphoreType.DMA((len(slots) + 1,)),
        ],
        *slots, block_fill.reshape(1, blocks),
        in_specs=[pl.BlockSpec(memory_space=pltpu.HBM)] * (len(slots) + 1),
        mebibytes=60,
    )
    at_asc = lax.all_to_all(packed, "desc", split_axis=0, concat_axis=0, tiled=True)
    at_asc, leaving = lax.optimization_barrier((at_asc, coef_desc))
    state_d = lax.ppermute(leaving, ("asc", "desc"), to_role)

    padded = all_rows + DUMMY_ROWS
    meta_shape = shape((padded, LANES), F32)
    phi_shape = shape((all_blocks, 2 * terms, BLOCK_ROWS * LANES), BF16)
    role_shapes = [meta_shape, phi_shape]
    table = pltpu.SMEM((all_rows + rows + BLOCK_ROWS + 1,), jnp.int32)
    slot_shape = shape((all_rows, LANES), F32)
    send_shape = shape((na, 2, rows, LANES), F32)
    field_a = shape(coef_asc.shape, F32)
    field_d = shape(coef_desc.shape, F32)
    line_shape = shape((na * nd, 1, LANES), F32)
    times_scratch = pltpu.VMEM((padded, LANES), F32)
    scratch = [
        table, pltpu.VMEM((2, padded, LANES), F32), pltpu.VMEM((padded, LANES), F32),
        pltpu.VMEM((2 * owned_asc, 2 * terms), F32),
    ]

    def exchange(x):
        return lax.all_to_all(x, "asc", split_axis=0, concat_axis=0, tiled=True)

    def share(x):
        return lax.all_to_all(x, ("asc", "desc"), split_axis=0, concat_axis=0, tiled=True)

    *asc, state_a, short, onward = call(
        functools.partial(setup_asc_kernel, fold, rows),
        role_shapes + [field_a, slot_shape, shape((na, 3 * rows, LANES), F32)],
        [times_scratch, table, scratch[2]],
        at_asc, coef_asc,
    )
    *desc, residual_d, weights_d, d0, own_d, send = call(
        functools.partial(setup_desc_kernel, fold, rows),
        role_shapes + [slot_shape, slot_shape, field_d, slot_shape, send_shape],
        [times_scratch] + scratch,
        exchange(onward), state_d,
    )
    residual_a, weights_a, crossed_a0, a0, a1, own_a, send = call(
        functools.partial(first_asc_kernel, na),
        [slot_shape, slot_shape, slot_shape, field_a, field_a, slot_shape, send_shape],
        scratch,
        exchange(send), short, *asc, state_a,
    )
    kept = [slot_shape] * 3
    d1, d2, send, crossed_d0, crossed_d1, own_d = call(
        functools.partial(images_kernel, -1.0, na, True),
        [field_d, field_d, send_shape] + kept,
        scratch,
        exchange(send), own_d, *desc, weights_d, d0,
    )
    a2, scalars, crossed_a1, crossed_a2, own_a = call(
        functools.partial(gram_kernel, 1.0, na, True),
        [field_a, line_shape] + kept,
        scratch,
        exchange(send), own_a, *asc, weights_a, crossed_a0, a0, a1, d0, d1, d2,
    )
    state_a, state_d, shares, weights_a, a0, own_a, send = call(
        functools.partial(next_asc_kernel, na),
        [
            field_a, field_d, shape((8, LANES), F32),
            slot_shape, field_a, slot_shape, send_shape,
        ],
        scratch,
        share(scalars), *asc, residual_a, crossed_a0, crossed_a1, crossed_a2,
        a0, a1, a2, d0, d1, d2, state_a, state_d, own_a,
    )
    weights_d, crossed_d0, d0, d1, own_d, send = call(
        functools.partial(next_desc_kernel, na),
        [slot_shape, slot_shape, field_d, field_d, slot_shape, send_shape],
        scratch,
        exchange(send), shares, *desc, residual_d, crossed_d0, crossed_d1, own_d, state_d,
    )
    a1, a2, send = call(
        functools.partial(images_kernel, 1.0, na, False),
        [field_a, field_a, send_shape],
        scratch,
        exchange(send), own_a, *asc, weights_a, a0,
    )
    d2, scalars = call(
        functools.partial(gram_kernel, -1.0, na, False),
        [field_d, line_shape],
        scratch,
        exchange(send), own_d, *desc, weights_d, crossed_d0, d0, d1, a0, a1, a2,
    )
    leaving = jnp.stack([state_d, d0, d1, d2])
    native = lax.ppermute(leaving, ("asc", "desc"), to_native)
    return tuple(
        call(
            final_kernel,
            [field_a, field_d],
            [],
            share(scalars), state_a, a0, a1, a2, native,
        )
    )


def solution(mesh):
    split_rows = P(("asc", "desc"), None)
    return jax.shard_map(
        body,
        mesh=mesh,
        in_specs=(split_rows,) * 7 + (P(("asc", "desc")),),
        out_specs=(split_rows, split_rows),
        check_vma=False,
    )
```

```python
import functools
import math

import jax
import jax.numpy as jnp
from jax import lax
from jax.experimental import pallas as pl
from jax.experimental.pallas import tpu as pltpu
from jax.sharding import PartitionSpec as P

GN_STEPS = 2
damping = 2.0
cauchy_square = 2.25

LANES = 128
STEP_ROWS = 2
UNROLL = 3
BLOCK_ROWS = STEP_ROWS * UNROLL
STEP_LANES = STEP_ROWS * LANES
DUMMY_ROWS = 8
TURNS = (5, 2, 1)
SCALE = 1.0 / 128.0
FIELDS = 5
PIVOT_FLOOR = 1e-6
F32 = jnp.float32
BF16 = jnp.bfloat16

COS_TERMS = [(-1.0) ** i * math.pi ** (2 * i) / math.factorial(2 * i) for i in range(8)]
SIN_TERMS = [(-1.0) ** i * math.pi ** (2 * i + 1) / math.factorial(2 * i + 1) for i in range(7)]


def params(mebibytes):
    return pltpu.CompilerParams(vmem_limit_bytes=mebibytes * 1024 * 1024)


def place(x):
    return pl.BlockSpec(memory_space=pltpu.VMEM)


def split(x):
    high = x.astype(BF16)
    low = (x - high.astype(F32)).astype(BF16)
    return high, low


def flat_first(ref, field, fold, rows):
    parts = []
    for j in range(ref.shape[0] * fold):
        start = (j % fold * FIELDS + field) * rows
        parts.append(ref[j // fold, start : start + rows])
    return jnp.concatenate(parts, axis=0)


def flat_second(ref, field, rows):
    start = field * rows
    return jnp.concatenate([ref[j, start : start + rows] for j in range(ref.shape[0])], axis=0)


def flat(ref, field, chunks):
    return jnp.concatenate([ref[j, field] for j in range(chunks)], axis=0)


def local_id(ids, owned):
    if owned & (owned - 1) == 0:
        return ids & (owned - 1)
    return lax.rem(ids, owned)


def pack_kernel(
    na, nd, owned_asc, coef_in, ca_in, cd_in, ta_in, td_in, height_in, fill_in, out,
    coef, ca, cd, ta, td, height, fill, turned, sems,
):
    copies = [
        pltpu.make_async_copy(source, target, sems.at[i])
        for i, (source, target) in enumerate(
            [
                (fill_in, fill), (ca_in, ca), (ta_in, ta),
                (cd_in, cd), (td_in, td), (height_in, height), (coef_in, coef),
            ]
        )
    ]
    for copy in copies:
        copy.start()
    for copy in copies:
        copy.wait()
    owned_desc = coef.shape[0]
    blocks, width = ca.shape
    group = width // na
    rows = blocks // na
    fill_row = fill[...]
    row_id = lax.broadcasted_iota(jnp.int32, (blocks, blocks), 0)
    col_id = lax.broadcasted_iota(jnp.int32, (blocks, blocks), 1)
    fill_col = jnp.sum(
        jnp.where(row_id == col_id, fill_row, 0).astype(F32), axis=1, keepdims=True
    )
    lane = lax.broadcasted_iota(jnp.int32, (blocks, width), 1)
    live = lane.astype(F32) < fill_col
    fields = [
        lambda: jnp.where(live, local_id(ca[...], owned_asc).astype(F32), -1.0),
        lambda: ta[...],
        lambda: jnp.where(live, local_id(cd[...], owned_desc).astype(F32), -1.0),
        lambda: td[...],
        lambda: height[...],
    ]
    source = lax.broadcasted_iota(jnp.int32, (width, width), 0)
    target = lax.broadcasted_iota(jnp.int32, (width, width), 1)
    owner = target // group
    place = target - owner * group
    order = (source == place * na + owner).astype(F32).astype(BF16)
    for f, field in enumerate(fields):
        x = field()
        high = x.astype(BF16)
        rest = x - high.astype(F32)
        middle = rest.astype(BF16)
        low = (rest - middle.astype(F32)).astype(BF16)
        turned[f] = (
            jnp.dot(high, order, preferred_element_type=F32)
            + jnp.dot(middle, order, preferred_element_type=F32)
        ) + jnp.dot(low, order, preferred_element_type=F32)
    lane_group = lax.broadcasted_iota(jnp.int32, (rows, width), 1) // group
    for f in range(FIELDS):
        parts = [None] * na
        for k in range(na):
            piece = turned[f, pl.ds(k, rows, stride=na), :]
            for r in range(na):
                amount = ((k - r) * group) % width
                moved = pltpu.roll(piece, amount, 1) if amount else piece
                parts[r] = moved if k == 0 else jnp.where(lane_group == k, moved, parts[r])
        for r in range(na):
            start = (r // nd * FIELDS + f) * rows
            out[r % nd, start : start + rows] = parts[r]
    for q in range(nd):
        out[q, out.shape[1] - owned_desc :] = coef[...]


def cos_sin_pi(x):
    turns = jnp.floor(x + 0.5)
    f = x - turns
    sign = 1.0 - 2.0 * (turns - 2.0 * jnp.floor(turns * 0.5))
    u = f * f
    c = COS_TERMS[-1]
    for term in COS_TERMS[-2::-1]:
        c = c * u + term
    s = SIN_TERMS[-1]
    for term in SIN_TERMS[-2::-1]:
        s = s * u + term
    return c * sign, s * (f * sign)


def rows_pair(ref, rows):
    return jnp.concatenate([ref[pl.ds(r, 1), :] for r in rows], axis=1)


def used_rows(ids_ref, chunks, rows, table):
    count = jnp.int32(0)
    level = lax.broadcasted_iota(jnp.int32, (rows, LANES), 0).astype(F32) + 1.0
    for j in range(chunks):
        ids = ids_ref[j * rows : (j + 1) * rows, :]
        used = jnp.max(jnp.where(ids >= 0.0, level, 0.0)).astype(jnp.int32)
        for i in range(rows):
            table[count + i] = j * rows + i
        count = count + used
    for i in range(BLOCK_ROWS):
        table[count + i] = chunks * rows
    table[table.shape[0] - 1] = lax.div(count + (BLOCK_ROWS - 1), BLOCK_ROWS)


def listed_rows(table, first, count):
    return [table[first + i] for i in range(count)]


def over_blocks(table, step):
    blocks = table[table.shape[0] - 1]
    done = jnp.int32(0)
    for size in TURNS:
        turns = lax.div(blocks - done, size)

        def turn(i, carry, done=done, size=size):
            step([done + i * size + u for u in range(size)])
            return carry

        lax.fori_loop(0, turns, turn, 0)
        done = done + turns * size


def stacked(field):
    high, low = split(field)
    top = jnp.concatenate([high, high], axis=1)
    bottom = jnp.concatenate([low, jnp.zeros_like(low)], axis=1)
    return jnp.concatenate([top, bottom], axis=0)


def forward_step(stack, phi, ids_row, row_iota, owned):
    both = jnp.dot(stack, phi, preferred_element_type=F32)
    value = both[:owned] + both[owned:]
    return jnp.sum(jnp.where(row_iota == ids_row, value, 0.0), axis=0, keepdims=True)


def store_rows(ref, rows, value):
    for i, r in enumerate(rows):
        ref[pl.ds(r, 1), :] = value[:, i * LANES : (i + 1) * LANES]


def basis_loop(table, ids_ref, time_ref, coef, phi_ref, value_ref):
    owned, terms = coef.shape
    half = terms // 2
    value_ref[...] = jnp.zeros(value_ref.shape, F32)
    width = STEP_LANES
    stack = stacked(coef)
    row_iota = lax.broadcasted_iota(jnp.int32, (owned, width), 0).astype(F32)
    fine = (lax.broadcasted_iota(jnp.int32, (8, width), 0) + 1).astype(F32)
    coarse = (lax.broadcasted_iota(jnp.int32, (half // 8, width), 0) * 8).astype(F32)

    def step(block, u):
        rows = listed_rows(table, block * BLOCK_ROWS + u * STEP_ROWS, STEP_ROWS)
        times = rows_pair(time_ref, rows)
        cos_fine, sin_fine = cos_sin_pi(fine * times)
        cos_coarse, sin_coarse = cos_sin_pi(coarse * times)
        cos_parts, sin_parts = [], []
        for j in range(half // 8):
            cj = cos_coarse[j : j + 1]
            sj = sin_coarse[j : j + 1]
            cos_parts.append(cj * cos_fine - sj * sin_fine)
            sin_parts.append(sj * cos_fine + cj * sin_fine)
        high, low = split(jnp.concatenate(cos_parts + sin_parts, axis=0))
        phi = jnp.concatenate([high, low], axis=0)
        phi_ref[block, :, u * width : (u + 1) * width] = phi
        value = forward_step(stack, phi, rows_pair(ids_ref, rows), row_iota, owned)
        store_rows(value_ref, rows, value)

    def whole_block(block, carry):
        for u in range(UNROLL):
            step(block, u)
        return carry

    lax.fori_loop(0, table[table.shape[0] - 1], whole_block, 0)


class Role:
    def __init__(self, sign, send, meta, phi, table, z_ref, value_ref, sum_ref, listed=False):
        if not listed:
            rows = (meta.shape[0] - DUMMY_ROWS) // send.shape[0]
            used_rows(meta, send.shape[0], rows, table)
        self.sign = sign
        self.table = table
        self.ids = meta
        self.phi = phi
        self.z_ref = z_ref
        self.value_ref = value_ref
        self.sum_ref = sum_ref
        self.count = meta.shape[0] - DUMMY_ROWS

    def cross(self, mine, other):
        return mine - other if self.sign > 0 else other - mine

    def backward(self, z, owned):
        high = z.astype(BF16).astype(F32)
        self.z_ref[0, : self.count] = high
        self.z_ref[1, : self.count] = z - high
        self.z_ref[:, self.count :] = jnp.zeros((2, DUMMY_ROWS, LANES), F32)
        blocks, double, width = self.phi.shape
        row_iota = lax.broadcasted_iota(jnp.int32, (owned, width), 0).astype(F32)

        def gather(block):
            rows = listed_rows(self.table, block * BLOCK_ROWS, BLOCK_ROWS)
            hit = row_iota == rows_pair(self.ids, rows)
            parts = [
                jnp.where(hit, rows_pair(self.z_ref.at[k], rows), 0.0).astype(BF16)
                for k in range(2)
            ]
            return lax.dot_general(
                jnp.concatenate(parts, axis=0),
                self.phi[block],
                (((1,), (1,)), ((), ())),
                preferred_element_type=F32,
            )

        return self.gathered(gather)

    def gathered(self, gather):
        self.sum_ref[...] = jnp.zeros(self.sum_ref.shape, F32)

        def step(blocks):
            self.sum_ref[...] += sum(gather(block) for block in blocks)

        over_blocks(self.table, step)
        g = self.sum_ref[...]
        owned, terms = g.shape[0] // 2, g.shape[1] // 2
        return self.sign * (g[:owned, :terms] + (g[:owned, terms:] + g[owned:, :terms]))

    def forward(self, field):
        owned = field.shape[0]
        stack = stacked(field)
        row_iota = lax.broadcasted_iota(jnp.int32, (owned, STEP_LANES), 0).astype(F32)
        self.value_ref[...] = jnp.zeros(self.value_ref.shape, F32)

        def ahead(block):
            for u in range(UNROLL):
                rows = listed_rows(self.table, block * BLOCK_ROWS + u * STEP_ROWS, STEP_ROWS)
                phi = self.phi[block, :, u * STEP_LANES : (u + 1) * STEP_LANES]
                value = forward_step(stack, phi, rows_pair(self.ids, rows), row_iota, owned)
                store_rows(self.value_ref, rows, value)

        def step(blocks):
            for block in blocks:
                ahead(block)

        over_blocks(self.table, step)
        return self.value_ref[: self.count]

    def forward_image(self, field, other, weight):
        owned = field.shape[0]
        stack = stacked(field)
        blocks, double, width = self.phi.shape
        row_iota = lax.broadcasted_iota(jnp.int32, (owned, width), 0).astype(F32)
        fill_padded(self.z_ref.at[0], other)
        fill_padded(self.z_ref.at[1], weight)
        self.value_ref[...] = jnp.zeros(self.value_ref.shape, F32)

        def both(block):
            rows = listed_rows(self.table, block * BLOCK_ROWS, BLOCK_ROWS)
            phi = self.phi[block]
            hit = row_iota == rows_pair(self.ids, rows)
            values = []
            for u in range(UNROLL):
                part = slice(u * STEP_LANES, (u + 1) * STEP_LANES)
                product = jnp.dot(stack, phi[:, part], preferred_element_type=F32)
                value = product[:owned] + product[owned:]
                values.append(
                    jnp.sum(jnp.where(hit[:, part], value, 0.0), axis=0, keepdims=True)
                )
            value = jnp.concatenate(values, axis=1)
            store_rows(self.value_ref, rows, value)
            z = rows_pair(self.z_ref.at[1], rows) * self.cross(
                value, rows_pair(self.z_ref.at[0], rows)
            )
            high = z.astype(BF16).astype(F32)
            parts = [jnp.where(hit, x, 0.0).astype(BF16) for x in (high, z - high)]
            return lax.dot_general(
                jnp.concatenate(parts, axis=0),
                phi,
                (((1,), (1,)), ((), ())),
                preferred_element_type=F32,
            )

        image = self.gathered(both)
        return self.value_ref[: self.count], SCALE * (image + damping * field)

    def weigh(self, residual):
        live = self.ids[: self.count] >= 0.0
        misfit = jnp.where(live, residual, 0.0)
        weight = jnp.where(live, 1.0 / (1.0 + misfit * misfit / cauchy_square), 0.0)
        return weight, weight * misfit

    def gradient(self, z, state):
        return self.backward(z, state.shape[0]) - damping * state

    def image(self, z, before):
        return SCALE * (self.backward(z, before.shape[0]) + damping * before)


def write_chunks(send, first, values):
    chunks, rows = send.shape[0], send.shape[2]
    for j in range(chunks):
        send[j, first] = values[j * rows : (j + 1) * rows, :]


def fill_padded(ref, values):
    count = values.shape[0]
    ref[:count] = values
    ref[count:] = jnp.zeros((ref.shape[0] - count,) + values.shape[1:], F32)


def setup_asc_kernel(
    fold, rows, packed, coef, meta, phi, state, short, onward, times, table, value_ref
):
    state[...] = coef[...]
    chunks = packed.shape[0] * fold
    count = chunks * rows
    meta[:count] = flat_first(packed, 0, fold, rows)
    meta[count:] = jnp.full((DUMMY_ROWS, LANES), -1.0, F32)
    fill_padded(times, flat_first(packed, 1, fold, rows))
    used_rows(meta, chunks, rows, table)
    basis_loop(table, meta, times, coef[...], phi, value_ref)
    short[...] = flat_first(packed, 4, fold, rows) - value_ref[:count]
    for j in range(chunks):
        base = j % fold * FIELDS
        for f in range(2):
            start = (base + f + 2) * rows
            onward[j, f * rows : (f + 1) * rows] = packed[j // fold, start : start + rows]
        onward[j, 2 * rows : 3 * rows] = short[j * rows : (j + 1) * rows]
        onward[j, 3 * rows :] = packed[j // fold, fold * FIELDS * rows :]


def setup_desc_kernel(
    fold, rows, packed, meta, phi, state, residual, weights, basis_0, value_0, send,
    times, table, z_ref, value_ref, sum_ref,
):
    chunks = packed.shape[0]
    count = chunks * rows
    home = lax.rem(lax.axis_index("asc"), fold) * (chunks // fold) + lax.axis_index("desc")
    state[...] = packed[home, 3 * rows :]
    meta[:count] = flat_second(packed, 0, rows)
    meta[count:] = jnp.full((DUMMY_ROWS, LANES), -1.0, F32)
    fill_padded(times, flat_second(packed, 1, rows))
    used_rows(meta, chunks, rows, table)
    basis_loop(table, meta, times, state[...], phi, value_ref)
    role = Role(-1.0, send, meta, phi, table, z_ref, value_ref, sum_ref, listed=True)
    own = value_ref[:count]
    write_chunks(send, 0, own)
    left = flat_second(packed, 2, rows) + own
    residual[...] = left
    weights[...], z = role.weigh(left)
    basis_0[...] = role.gradient(z, state[...])
    own = role.forward(basis_0[...])
    value_0[...] = own
    write_chunks(send, 1, own)


def first_asc_kernel(
    chunks, got, short, meta, phi, state,
    residual, weights, crossed_0, basis_0, basis_1, value_1, send, table, z_ref, value_ref, sum_ref,
):
    role = Role(1.0, send, meta, phi, table, z_ref, value_ref, sum_ref)
    left = short[...] + flat(got, 0, chunks)
    residual[...] = left
    weights[...], z = role.weigh(left)
    basis_0[...] = role.gradient(z, state[...])
    other = flat(got, 1, chunks)
    own, basis_1[...] = role.forward_image(basis_0[...], other, weights[...])
    write_chunks(send, 0, own)
    crossed_0[...] = role.cross(own, other)
    own = role.forward(basis_1[...])
    value_1[...] = own
    write_chunks(send, 1, own)


def images_kernel(sign, chunks, keep, got, value_0, meta, phi, weights, basis_0, *rest):
    basis_1, basis_2, send, *kept = rest[:-4]
    role = Role(sign, send, meta, phi, *rest[-4:])
    first = role.cross(value_0[...], flat(got, 0, chunks))
    basis_1[...] = role.image(weights[...] * first, basis_0[...])
    other = flat(got, 1, chunks)
    own, basis_2[...] = role.forward_image(basis_1[...], other, weights[...])
    write_chunks(send, 0, own)
    second = role.cross(own, other)
    own = role.forward(basis_2[...])
    write_chunks(send, 1, own)
    if keep:
        crossed_0, crossed_1, value_2 = kept
        crossed_0[...] = first
        crossed_1[...] = second
        value_2[...] = own


def total(x):
    return jnp.sum(jnp.sum(x, axis=0, keepdims=True), axis=1, keepdims=True)


PAIRS = [(0, 0), (0, 1), (0, 2), (1, 1), (1, 2), (2, 2)]


def gram_kernel(
    sign, chunks, keep, got, value_1, meta, phi, weights, crossed_0, basis_0, basis_1,
    other_0, other_1, other_2, *rest,
):
    basis_2, scalars, *kept = rest[:-4]
    role = Role(sign, got, meta, phi, *rest[-4:])
    weight = weights[...]
    crossed = role.cross(value_1[...], flat(got, 0, chunks))
    basis_2[...] = role.image(weight * crossed, basis_1[...])
    own = role.forward(basis_2[...])
    last = role.cross(own, flat(got, 1, chunks))
    if keep:
        crossed_1, crossed_2, value_2 = kept
        crossed_1[...] = crossed
        crossed_2[...] = last
        value_2[...] = own
    values = [crossed_0[...], crossed, last]
    mine = [basis_0[...], basis_1[...], basis_2[...]]
    others = [other_0[...], other_1[...], other_2[...]]
    lane = lax.broadcasted_iota(jnp.int32, (1, LANES), 1)
    line = jnp.zeros((1, LANES), F32)
    for place_in_line, (i, j) in enumerate(PAIRS):
        dots = total(mine[i] * mine[j] + others[i] * others[j])
        curve = total(weight * values[i] * values[j]) + damping * dots
        line = jnp.where(lane == place_in_line, curve, line)
        if i == 0:
            line = jnp.where(lane == len(PAIRS) + j, dots, line)
    for d in range(scalars.shape[0]):
        scalars[d] = line


def solve(scalars):
    summed = scalars[0]
    for d in range(1, scalars.shape[0]):
        summed = summed + scalars[d]
    line = summed
    lane = lax.broadcasted_iota(jnp.int32, (1, LANES), 1)

    def pick(place):
        return jnp.sum(jnp.where(lane == place, line, 0.0), axis=1, keepdims=True)

    g = {pair: pick(place) for place, pair in enumerate(PAIRS)}
    right = [pick(len(PAIRS) + i) for i in range(3)]
    s = [
        jnp.where(g[i, i] > 0.0, lax.rsqrt(jnp.maximum(g[i, i], 1e-37)), 0.0) for i in range(3)
    ]
    l10 = g[0, 1] * s[0] * s[1]
    l20 = g[0, 2] * s[0] * s[2]
    g21 = g[1, 2] * s[1] * s[2]
    c = [right[i] * s[i] for i in range(3)]

    def inverse(pivot):
        good = pivot > PIVOT_FLOOR
        return jnp.where(good, 1.0 / jnp.where(good, pivot, 1.0), 0.0)

    inv1 = inverse(1.0 - l10 * l10)
    t21 = g21 - l20 * l10
    l21 = t21 * inv1
    inv2 = inverse(1.0 - l20 * l20 - l21 * t21)
    u1 = c[1] - l10 * c[0]
    u2 = c[2] - l20 * c[0] - l21 * u1
    x2 = u2 * inv2
    x1 = u1 * inv1 - l21 * x2
    x0 = c[0] - l10 * x1 - l20 * x2
    return [x0 * s[0], x1 * s[1], x2 * s[2]]


def combine(y, parts):
    return y[0] * parts[0] + (y[1] * parts[1] + y[2] * parts[2])


def next_asc_kernel(
    chunks, scalars, meta, phi, residual, crossed_0, crossed_1, crossed_2,
    basis_a0, basis_a1, basis_a2, basis_d0, basis_d1, basis_d2, state_a, state_d, value_2,
    new_a, new_d, shares, weights, basis_0, value_0, send, table, z_ref, value_ref, sum_ref,
):
    role = Role(1.0, send, meta, phi, table, z_ref, value_ref, sum_ref)
    write_chunks(send, 0, value_2[...])
    y = solve(scalars)
    for i in range(3):
        shares[i : i + 1] = jnp.broadcast_to(y[i], (1, LANES))
    left = residual[...] - combine(y, [crossed_0[...], crossed_1[...], crossed_2[...]])
    new_a[...] = state_a[...] + combine(y, [basis_a0[...], basis_a1[...], basis_a2[...]])
    new_d[...] = state_d[...] + combine(y, [basis_d0[...], basis_d1[...], basis_d2[...]])
    weights[...], z = role.weigh(left)
    basis_0[...] = role.gradient(z, new_a[...])
    own = role.forward(basis_0[...])
    value_0[...] = own
    write_chunks(send, 1, own)


def next_desc_kernel(
    chunks, got, shares, meta, phi, residual, crossed_0, crossed_1, value_2, state,
    weights, new_crossed_0, basis_0, basis_1, value_1, send, table, z_ref, value_ref, sum_ref,
):
    role = Role(-1.0, send, meta, phi, table, z_ref, value_ref, sum_ref)
    y = [shares[i : i + 1] for i in range(3)]
    crossed_2 = role.cross(value_2[...], flat(got, 0, chunks))
    left = residual[...] - combine(y, [crossed_0[...], crossed_1[...], crossed_2])
    weights[...], z = role.weigh(left)
    basis_0[...] = role.gradient(z, state[...])
    other = flat(got, 1, chunks)
    own, basis_1[...] = role.forward_image(basis_0[...], other, weights[...])
    write_chunks(send, 0, own)
    new_crossed_0[...] = role.cross(own, other)
    own = role.forward(basis_1[...])
    value_1[...] = own
    write_chunks(send, 1, own)


def final_kernel(scalars, state_a, basis_0, basis_1, basis_2, desc, out_a, out_d):
    y = solve(scalars)
    out_a[...] = state_a[...] + combine(y, [basis_0[...], basis_1[...], basis_2[...]])
    out_d[...] = desc[0] + combine(y, [desc[1], desc[2], desc[3]])


def body(coef_asc, coef_desc, cross_asc, cross_desc, time_asc, time_desc, height, block_fill):
    owned_asc, terms = coef_asc.shape
    owned_desc = coef_desc.shape[0]
    blocks, width = cross_asc.shape
    na = lax.axis_size("asc")
    nd = lax.axis_size("desc")
    fold = na // nd
    rows = blocks * width // na // LANES
    all_rows = na * rows
    all_blocks = -(-all_rows // BLOCK_ROWS)
    shape = jax.ShapeDtypeStruct

    def call(kernel, outs, scratch, *args, in_specs=None, mebibytes=16):
        return pl.pallas_call(
            kernel,
            out_shape=outs,
            in_specs=[place(x) for x in args] if in_specs is None else in_specs,
            out_specs=jax.tree.map(place, outs),
            scratch_shapes=scratch,
            compiler_params=params(mebibytes),
        )(*args)

    to_role = []
    for p in range(na):
        for q in range(nd):
            to_role.append((p * nd + q, (q * fold + p // nd) * nd + p % nd))
    to_native = [(b, a) for a, b in to_role]
    slots = (cross_asc, cross_desc, time_asc, time_desc, height)
    packed = call(
        functools.partial(pack_kernel, na, nd, owned_asc),
        shape((nd, fold * FIELDS * rows + owned_desc, LANES), F32),
        [pltpu.VMEM(coef_desc.shape, F32)]
        + [pltpu.VMEM((blocks, width), x.dtype) for x in slots]
        + [
            pltpu.VMEM((1, blocks), jnp.int32),
            pltpu.VMEM((FIELDS, blocks, width), F32),
            pltpu.SemaphoreType.DMA((len(slots) + 2,)),
        ],
        coef_desc, *slots, block_fill.reshape(1, blocks),
        in_specs=[pl.BlockSpec(memory_space=pltpu.HBM)] * (len(slots) + 2),
        mebibytes=60,
    )
    at_asc = lax.all_to_all(packed, "desc", split_axis=0, concat_axis=0, tiled=True)

    padded = all_rows + DUMMY_ROWS
    meta_shape = shape((padded, LANES), F32)
    phi_shape = shape((all_blocks, 2 * terms, BLOCK_ROWS * LANES), BF16)
    role_shapes = [meta_shape, phi_shape]
    table = pltpu.SMEM((all_rows + rows + BLOCK_ROWS + 1,), jnp.int32)
    slot_shape = shape((all_rows, LANES), F32)
    send_shape = shape((na, 2, rows, LANES), F32)
    field_a = shape(coef_asc.shape, F32)
    field_d = shape(coef_desc.shape, F32)
    line_shape = shape((na * nd, 1, LANES), F32)
    times_scratch = pltpu.VMEM((padded, LANES), F32)
    scratch = [
        table, pltpu.VMEM((2, padded, LANES), F32), pltpu.VMEM((padded, LANES), F32),
        pltpu.VMEM((2 * owned_asc, 2 * terms), F32),
    ]

    def exchange(x):
        return lax.all_to_all(x, "asc", split_axis=0, concat_axis=0, tiled=True)

    def share(x):
        return lax.all_to_all(x, ("asc", "desc"), split_axis=0, concat_axis=0, tiled=True)

    *asc, state_a, short, onward = call(
        functools.partial(setup_asc_kernel, fold, rows),
        role_shapes + [field_a, slot_shape, shape((na, 3 * rows + owned_desc, LANES), F32)],
        [times_scratch, table, scratch[2]],
        at_asc, coef_asc,
    )
    *desc, state_d, residual_d, weights_d, d0, own_d, send = call(
        functools.partial(setup_desc_kernel, fold, rows),
        role_shapes + [field_d, slot_shape, slot_shape, field_d, slot_shape, send_shape],
        [times_scratch] + scratch,
        exchange(onward),
    )
    residual_a, weights_a, crossed_a0, a0, a1, own_a, send = call(
        functools.partial(first_asc_kernel, na),
        [slot_shape, slot_shape, slot_shape, field_a, field_a, slot_shape, send_shape],
        scratch,
        exchange(send), short, *asc, state_a,
    )
    kept = [slot_shape] * 3
    d1, d2, send, crossed_d0, crossed_d1, own_d = call(
        functools.partial(images_kernel, -1.0, na, True),
        [field_d, field_d, send_shape] + kept,
        scratch,
        exchange(send), own_d, *desc, weights_d, d0,
    )
    a2, scalars, crossed_a1, crossed_a2, own_a = call(
        functools.partial(gram_kernel, 1.0, na, True),
        [field_a, line_shape] + kept,
        scratch,
        exchange(send), own_a, *asc, weights_a, crossed_a0, a0, a1, d0, d1, d2,
    )
    state_a, state_d, shares, weights_a, a0, own_a, send = call(
        functools.partial(next_asc_kernel, na),
        [
            field_a, field_d, shape((8, LANES), F32),
            slot_shape, field_a, slot_shape, send_shape,
        ],
        scratch,
        share(scalars), *asc, residual_a, crossed_a0, crossed_a1, crossed_a2,
        a0, a1, a2, d0, d1, d2, state_a, state_d, own_a,
    )
    weights_d, crossed_d0, d0, d1, own_d, send = call(
        functools.partial(next_desc_kernel, na),
        [slot_shape, slot_shape, field_d, field_d, slot_shape, send_shape],
        scratch,
        exchange(send), shares, *desc, residual_d, crossed_d0, crossed_d1, own_d, state_d,
    )
    a1, a2, send = call(
        functools.partial(images_kernel, 1.0, na, False),
        [field_a, field_a, send_shape],
        scratch,
        exchange(send), own_a, *asc, weights_a, a0,
    )
    d2, scalars = call(
        functools.partial(gram_kernel, -1.0, na, False),
        [field_d, line_shape],
        scratch,
        exchange(send), own_d, *desc, weights_d, crossed_d0, d0, d1, a0, a1, a2,
    )
    leaving = jnp.stack([state_d, d0, d1, d2])
    native = lax.ppermute(leaving, ("asc", "desc"), to_native)
    return tuple(
        call(
            final_kernel,
            [field_a, field_d],
            [],
            share(scalars), state_a, a0, a1, a2, native,
        )
    )


def solution(mesh):
    split_rows = P(("asc", "desc"), None)
    return jax.shard_map(
        body,
        mesh=mesh,
        in_specs=(split_rows,) * 7 + (P(("asc", "desc")),),
        out_specs=(split_rows, split_rows),
        check_vma=False,
    )
```

```python
import functools
import math

import jax
import jax.numpy as jnp
from jax import lax
from jax.experimental import pallas as pl
from jax.experimental.pallas import tpu as pltpu
from jax.sharding import PartitionSpec as P

GN_STEPS = 2
damping = 2.0
cauchy_square = 2.25

LANES = 128
STEP_ROWS = 2
UNROLL = 3
BLOCK_ROWS = STEP_ROWS * UNROLL
STEP_LANES = STEP_ROWS * LANES
DUMMY_ROWS = 8
TURNS = (5, 2, 1)
SCALE = 1.0 / 128.0
FIELDS = 5
PIVOT_FLOOR = 1e-6
F32 = jnp.float32
BF16 = jnp.bfloat16

COS_TERMS = [(-1.0) ** i * math.pi ** (2 * i) / math.factorial(2 * i) for i in range(8)]
SIN_TERMS = [(-1.0) ** i * math.pi ** (2 * i + 1) / math.factorial(2 * i + 1) for i in range(7)]


def params(mebibytes):
    return pltpu.CompilerParams(vmem_limit_bytes=mebibytes * 1024 * 1024)


def place(x):
    return pl.BlockSpec(memory_space=pltpu.VMEM)


def split(x):
    high = x.astype(BF16)
    low = (x - high.astype(F32)).astype(BF16)
    return high, low


def flat_first(ref, field, fold, rows):
    parts = []
    for j in range(ref.shape[0] * fold):
        start = (j % fold * FIELDS + field) * rows
        parts.append(ref[j // fold, start : start + rows])
    return jnp.concatenate(parts, axis=0)


def flat_second(ref, field, rows):
    start = field * rows
    return jnp.concatenate([ref[j, start : start + rows] for j in range(ref.shape[0])], axis=0)


def flat(ref, field, chunks):
    return jnp.concatenate([ref[j, field] for j in range(chunks)], axis=0)


def local_id(ids, owned):
    if owned & (owned - 1) == 0:
        return ids & (owned - 1)
    return lax.rem(ids, owned)


def pack_kernel(
    na, nd, owned_asc, coef_in, ca_in, cd_in, ta_in, td_in, height_in, fill_in, out,
    coef, ca, cd, ta, td, height, fill, turned, sems,
):
    copies = [
        pltpu.make_async_copy(source, target, sems.at[i])
        for i, (source, target) in enumerate(
            [
                (fill_in, fill), (ca_in, ca), (ta_in, ta),
                (cd_in, cd), (td_in, td), (height_in, height), (coef_in, coef),
            ]
        )
    ]
    for copy in copies:
        copy.start()
    for copy in copies:
        copy.wait()
    owned_desc = coef.shape[0]
    blocks, width = ca.shape
    group = width // na
    rows = blocks // na
    fill_row = fill[...]
    row_id = lax.broadcasted_iota(jnp.int32, (blocks, blocks), 0)
    col_id = lax.broadcasted_iota(jnp.int32, (blocks, blocks), 1)
    fill_col = jnp.sum(
        jnp.where(row_id == col_id, fill_row, 0).astype(F32), axis=1, keepdims=True
    )
    lane = lax.broadcasted_iota(jnp.int32, (blocks, width), 1)
    live = lane.astype(F32) < fill_col
    fields = [
        lambda: jnp.where(live, local_id(ca[...], owned_asc).astype(F32), -1.0),
        lambda: ta[...],
        lambda: jnp.where(live, local_id(cd[...], owned_desc).astype(F32), -1.0),
        lambda: td[...],
        lambda: height[...],
    ]
    source = lax.broadcasted_iota(jnp.int32, (width, width), 0)
    target = lax.broadcasted_iota(jnp.int32, (width, width), 1)
    owner = target // group
    place = target - owner * group
    order = (source == place * na + owner).astype(F32).astype(BF16)
    for f, field in enumerate(fields):
        x = field()
        high = x.astype(BF16)
        rest = x - high.astype(F32)
        middle = rest.astype(BF16)
        low = (rest - middle.astype(F32)).astype(BF16)
        turned[f] = (
            jnp.dot(high, order, preferred_element_type=F32)
            + jnp.dot(middle, order, preferred_element_type=F32)
        ) + jnp.dot(low, order, preferred_element_type=F32)
    lane_group = lax.broadcasted_iota(jnp.int32, (rows, width), 1) // group
    for f in range(FIELDS):
        parts = [None] * na
        for k in range(na):
            piece = turned[f, pl.ds(k, rows, stride=na), :]
            for r in range(na):
                amount = ((k - r) * group) % width
                moved = pltpu.roll(piece, amount, 1) if amount else piece
                parts[r] = moved if k == 0 else jnp.where(lane_group == k, moved, parts[r])
        for r in range(na):
            start = (r // nd * FIELDS + f) * rows
            out[r % nd, start : start + rows] = parts[r]
    for q in range(nd):
        out[q, out.shape[1] - owned_desc :] = coef[...]


def cos_sin_pi(x):
    turns = jnp.floor(x + 0.5)
    f = x - turns
    sign = 1.0 - 2.0 * (turns - 2.0 * jnp.floor(turns * 0.5))
    u = f * f
    c = COS_TERMS[-1]
    for term in COS_TERMS[-2::-1]:
        c = c * u + term
    s = SIN_TERMS[-1]
    for term in SIN_TERMS[-2::-1]:
        s = s * u + term
    return c * sign, s * (f * sign)


def rows_pair(ref, rows):
    return jnp.concatenate([ref[pl.ds(r, 1), :] for r in rows], axis=1)


def used_rows(ids_ref, chunks, rows, table):
    count = jnp.int32(0)
    level = lax.broadcasted_iota(jnp.int32, (rows, LANES), 0).astype(F32) + 1.0
    for j in range(chunks):
        ids = ids_ref[j * rows : (j + 1) * rows, :]
        used = jnp.max(jnp.where(ids >= 0.0, level, 0.0)).astype(jnp.int32)
        for i in range(rows):
            table[count + i] = j * rows + i
        count = count + used
    for i in range(BLOCK_ROWS):
        table[count + i] = chunks * rows
    table[table.shape[0] - 1] = lax.div(count + (BLOCK_ROWS - 1), BLOCK_ROWS)


def listed_rows(table, first, count):
    return [table[first + i] for i in range(count)]


def over_blocks(table, step):
    blocks = table[table.shape[0] - 1]
    done = jnp.int32(0)
    for size in TURNS:
        turns = lax.div(blocks - done, size)

        def turn(i, carry, done=done, size=size):
            step([done + i * size + u for u in range(size)])
            return carry

        lax.fori_loop(0, turns, turn, 0)
        done = done + turns * size


def stacked(field):
    high, low = split(field)
    top = jnp.concatenate([high, high], axis=1)
    bottom = jnp.concatenate([low, jnp.zeros_like(low)], axis=1)
    return jnp.concatenate([top, bottom], axis=0)


def forward_step(stack, phi, ids_row, row_iota, owned):
    both = jnp.dot(stack, phi, preferred_element_type=F32)
    value = both[:owned] + both[owned:]
    return jnp.sum(jnp.where(row_iota == ids_row, value, 0.0), axis=0, keepdims=True)


def store_rows(ref, rows, value):
    for i, r in enumerate(rows):
        ref[pl.ds(r, 1), :] = value[:, i * LANES : (i + 1) * LANES]


def basis_loop(table, ids_ref, time_ref, coef, phi_ref, value_ref):
    owned, terms = coef.shape
    half = terms // 2
    value_ref[...] = jnp.zeros(value_ref.shape, F32)
    width = STEP_LANES
    stack = stacked(coef)
    row_iota = lax.broadcasted_iota(jnp.int32, (owned, width), 0).astype(F32)
    fine = (lax.broadcasted_iota(jnp.int32, (8, width), 0) + 1).astype(F32)
    coarse = (lax.broadcasted_iota(jnp.int32, (half // 8, width), 0) * 8).astype(F32)

    def step(block, u):
        rows = listed_rows(table, block * BLOCK_ROWS + u * STEP_ROWS, STEP_ROWS)
        times = rows_pair(time_ref, rows)
        cos_fine, sin_fine = cos_sin_pi(fine * times)
        cos_coarse, sin_coarse = cos_sin_pi(coarse * times)
        cos_parts, sin_parts = [], []
        for j in range(half // 8):
            cj = cos_coarse[j : j + 1]
            sj = sin_coarse[j : j + 1]
            cos_parts.append(cj * cos_fine - sj * sin_fine)
            sin_parts.append(sj * cos_fine + cj * sin_fine)
        high, low = split(jnp.concatenate(cos_parts + sin_parts, axis=0))
        phi = jnp.concatenate([high, low], axis=0)
        phi_ref[block, :, u * width : (u + 1) * width] = phi
        value = forward_step(stack, phi, rows_pair(ids_ref, rows), row_iota, owned)
        store_rows(value_ref, rows, value)

    def whole_block(block, carry):
        for u in range(UNROLL):
            step(block, u)
        return carry

    lax.fori_loop(0, table[table.shape[0] - 1], whole_block, 0)


class Role:
    def __init__(self, sign, send, meta, phi, table, z_ref, value_ref, sum_ref, listed=False):
        if not listed:
            rows = (meta.shape[0] - DUMMY_ROWS) // send.shape[0]
            used_rows(meta, send.shape[0], rows, table)
        self.sign = sign
        self.table = table
        self.ids = meta
        self.phi = phi
        self.z_ref = z_ref
        self.value_ref = value_ref
        self.sum_ref = sum_ref
        self.count = meta.shape[0] - DUMMY_ROWS

    def cross(self, mine, other):
        return mine - other if self.sign > 0 else other - mine

    def backward(self, z, owned):
        high = z.astype(BF16).astype(F32)
        self.z_ref[0, : self.count] = high
        self.z_ref[1, : self.count] = z - high
        self.z_ref[:, self.count :] = jnp.zeros((2, DUMMY_ROWS, LANES), F32)
        blocks, double, width = self.phi.shape
        row_iota = lax.broadcasted_iota(jnp.int32, (owned, width), 0).astype(F32)

        def gather(block):
            rows = listed_rows(self.table, block * BLOCK_ROWS, BLOCK_ROWS)
            hit = row_iota == rows_pair(self.ids, rows)
            parts = [
                jnp.where(hit, rows_pair(self.z_ref.at[k], rows), 0.0).astype(BF16)
                for k in range(2)
            ]
            return lax.dot_general(
                jnp.concatenate(parts, axis=0),
                self.phi[block],
                (((1,), (1,)), ((), ())),
                preferred_element_type=F32,
            )

        return self.gathered(gather)

    def gathered(self, gather):
        self.sum_ref[...] = jnp.zeros(self.sum_ref.shape, F32)

        def step(blocks):
            self.sum_ref[...] += sum(gather(block) for block in blocks)

        over_blocks(self.table, step)
        g = self.sum_ref[...]
        owned, terms = g.shape[0] // 2, g.shape[1] // 2
        return self.sign * (g[:owned, :terms] + (g[:owned, terms:] + g[owned:, :terms]))

    def forward(self, field):
        owned = field.shape[0]
        stack = stacked(field)
        row_iota = lax.broadcasted_iota(jnp.int32, (owned, STEP_LANES), 0).astype(F32)
        self.value_ref[...] = jnp.zeros(self.value_ref.shape, F32)

        def ahead(block):
            for u in range(UNROLL):
                rows = listed_rows(self.table, block * BLOCK_ROWS + u * STEP_ROWS, STEP_ROWS)
                phi = self.phi[block, :, u * STEP_LANES : (u + 1) * STEP_LANES]
                value = forward_step(stack, phi, rows_pair(self.ids, rows), row_iota, owned)
                store_rows(self.value_ref, rows, value)

        def step(blocks):
            for block in blocks:
                ahead(block)

        over_blocks(self.table, step)
        return self.value_ref[: self.count]

    def forward_image(self, field, other, weight):
        owned = field.shape[0]
        stack = stacked(field)
        blocks, double, width = self.phi.shape
        row_iota = lax.broadcasted_iota(jnp.int32, (owned, width), 0).astype(F32)
        fill_padded(self.z_ref.at[0], other)
        fill_padded(self.z_ref.at[1], weight)
        self.value_ref[...] = jnp.zeros(self.value_ref.shape, F32)

        def both(block):
            rows = listed_rows(self.table, block * BLOCK_ROWS, BLOCK_ROWS)
            phi = self.phi[block]
            hit = row_iota == rows_pair(self.ids, rows)
            values = []
            for u in range(UNROLL):
                part = slice(u * STEP_LANES, (u + 1) * STEP_LANES)
                product = jnp.dot(stack, phi[:, part], preferred_element_type=F32)
                value = product[:owned] + product[owned:]
                values.append(
                    jnp.sum(jnp.where(hit[:, part], value, 0.0), axis=0, keepdims=True)
                )
            value = jnp.concatenate(values, axis=1)
            store_rows(self.value_ref, rows, value)
            z = rows_pair(self.z_ref.at[1], rows) * self.cross(
                value, rows_pair(self.z_ref.at[0], rows)
            )
            high = z.astype(BF16).astype(F32)
            parts = [jnp.where(hit, x, 0.0).astype(BF16) for x in (high, z - high)]
            return lax.dot_general(
                jnp.concatenate(parts, axis=0),
                phi,
                (((1,), (1,)), ((), ())),
                preferred_element_type=F32,
            )

        image = self.gathered(both)
        return self.value_ref[: self.count], SCALE * image

    def weigh(self, residual):
        live = self.ids[: self.count] >= 0.0
        misfit = jnp.where(live, residual, 0.0)
        weight = jnp.where(live, 1.0 / (1.0 + misfit * misfit / cauchy_square), 0.0)
        return weight, weight * misfit

    def gradient(self, z, state):
        return self.backward(z, state.shape[0]) - damping * state

    def image(self, z, before):
        return SCALE * self.backward(z, before.shape[0])


def write_chunks(send, first, values):
    chunks, rows = send.shape[0], send.shape[2]
    for j in range(chunks):
        send[j, first] = values[j * rows : (j + 1) * rows, :]


def fill_padded(ref, values):
    count = values.shape[0]
    ref[:count] = values
    ref[count:] = jnp.zeros((ref.shape[0] - count,) + values.shape[1:], F32)


def setup_asc_kernel(
    fold, rows, packed, coef, meta, phi, state, short, onward, times, table, value_ref
):
    state[...] = coef[...]
    chunks = packed.shape[0] * fold
    count = chunks * rows
    meta[:count] = flat_first(packed, 0, fold, rows)
    meta[count:] = jnp.full((DUMMY_ROWS, LANES), -1.0, F32)
    fill_padded(times, flat_first(packed, 1, fold, rows))
    used_rows(meta, chunks, rows, table)
    basis_loop(table, meta, times, coef[...], phi, value_ref)
    short[...] = flat_first(packed, 4, fold, rows) - value_ref[:count]
    for j in range(chunks):
        base = j % fold * FIELDS
        for f in range(2):
            start = (base + f + 2) * rows
            onward[j, f * rows : (f + 1) * rows] = packed[j // fold, start : start + rows]
        onward[j, 2 * rows : 3 * rows] = short[j * rows : (j + 1) * rows]
        onward[j, 3 * rows :] = packed[j // fold, fold * FIELDS * rows :]


def setup_desc_kernel(
    fold, rows, packed, meta, phi, state, residual, weights, basis_0, value_0, send,
    times, table, z_ref, value_ref, sum_ref,
):
    chunks = packed.shape[0]
    count = chunks * rows
    home = lax.rem(lax.axis_index("asc"), fold) * (chunks // fold) + lax.axis_index("desc")
    state[...] = packed[home, 3 * rows :]
    meta[:count] = flat_second(packed, 0, rows)
    meta[count:] = jnp.full((DUMMY_ROWS, LANES), -1.0, F32)
    fill_padded(times, flat_second(packed, 1, rows))
    used_rows(meta, chunks, rows, table)
    basis_loop(table, meta, times, state[...], phi, value_ref)
    role = Role(-1.0, send, meta, phi, table, z_ref, value_ref, sum_ref, listed=True)
    own = value_ref[:count]
    write_chunks(send, 0, own)
    left = flat_second(packed, 2, rows) + own
    residual[...] = left
    weights[...], z = role.weigh(left)
    basis_0[...] = role.gradient(z, state[...])
    own = role.forward(basis_0[...])
    value_0[...] = own
    write_chunks(send, 1, own)


def first_asc_kernel(
    chunks, got, short, meta, phi, state,
    residual, weights, crossed_0, basis_0, basis_1, value_1, send, table, z_ref, value_ref, sum_ref,
):
    role = Role(1.0, send, meta, phi, table, z_ref, value_ref, sum_ref)
    left = short[...] + flat(got, 0, chunks)
    residual[...] = left
    weights[...], z = role.weigh(left)
    basis_0[...] = role.gradient(z, state[...])
    other = flat(got, 1, chunks)
    own, basis_1[...] = role.forward_image(basis_0[...], other, weights[...])
    write_chunks(send, 0, own)
    crossed_0[...] = role.cross(own, other)
    own = role.forward(basis_1[...])
    value_1[...] = own
    write_chunks(send, 1, own)


def images_kernel(sign, chunks, keep, got, value_0, meta, phi, weights, basis_0, *rest):
    basis_1, basis_2, send, *kept = rest[:-4]
    role = Role(sign, send, meta, phi, *rest[-4:])
    first = role.cross(value_0[...], flat(got, 0, chunks))
    basis_1[...] = role.image(weights[...] * first, basis_0[...])
    other = flat(got, 1, chunks)
    own, basis_2[...] = role.forward_image(basis_1[...], other, weights[...])
    write_chunks(send, 0, own)
    second = role.cross(own, other)
    own = role.forward(basis_2[...])
    write_chunks(send, 1, own)
    if keep:
        crossed_0, crossed_1, value_2 = kept
        crossed_0[...] = first
        crossed_1[...] = second
        value_2[...] = own


def total(x):
    return jnp.sum(jnp.sum(x, axis=0, keepdims=True), axis=1, keepdims=True)


PAIRS = [(0, 0), (0, 1), (0, 2), (1, 1), (1, 2), (2, 2)]


def gram_kernel(
    sign, chunks, keep, got, value_1, meta, phi, weights, crossed_0, basis_0, basis_1,
    other_0, other_1, other_2, *rest,
):
    basis_2, scalars, *kept = rest[:-4]
    role = Role(sign, got, meta, phi, *rest[-4:])
    weight = weights[...]
    crossed = role.cross(value_1[...], flat(got, 0, chunks))
    basis_2[...] = role.image(weight * crossed, basis_1[...])
    own = role.forward(basis_2[...])
    last = role.cross(own, flat(got, 1, chunks))
    if keep:
        crossed_1, crossed_2, value_2 = kept
        crossed_1[...] = crossed
        crossed_2[...] = last
        value_2[...] = own
    values = [crossed_0[...], crossed, last]
    mine = [basis_0[...], basis_1[...], basis_2[...]]
    others = [other_0[...], other_1[...], other_2[...]]
    lane = lax.broadcasted_iota(jnp.int32, (1, LANES), 1)
    line = jnp.zeros((1, LANES), F32)
    for place_in_line, (i, j) in enumerate(PAIRS):
        dots = total(mine[i] * mine[j] + others[i] * others[j])
        curve = total(weight * values[i] * values[j]) + damping * dots
        line = jnp.where(lane == place_in_line, curve, line)
        if i == 0:
            line = jnp.where(lane == len(PAIRS) + j, dots, line)
    for d in range(scalars.shape[0]):
        scalars[d] = line


def solve(scalars):
    summed = scalars[0]
    for d in range(1, scalars.shape[0]):
        summed = summed + scalars[d]
    line = summed
    lane = lax.broadcasted_iota(jnp.int32, (1, LANES), 1)

    def pick(place):
        return jnp.sum(jnp.where(lane == place, line, 0.0), axis=1, keepdims=True)

    g = {pair: pick(place) for place, pair in enumerate(PAIRS)}
    right = [pick(len(PAIRS) + i) for i in range(3)]
    s = [
        jnp.where(g[i, i] > 0.0, lax.rsqrt(jnp.maximum(g[i, i], 1e-37)), 0.0) for i in range(3)
    ]
    l10 = g[0, 1] * s[0] * s[1]
    l20 = g[0, 2] * s[0] * s[2]
    g21 = g[1, 2] * s[1] * s[2]
    c = [right[i] * s[i] for i in range(3)]

    def inverse(pivot):
        good = pivot > PIVOT_FLOOR
        return jnp.where(good, 1.0 / jnp.where(good, pivot, 1.0), 0.0)

    inv1 = inverse(1.0 - l10 * l10)
    t21 = g21 - l20 * l10
    l21 = t21 * inv1
    inv2 = inverse(1.0 - l20 * l20 - l21 * t21)
    u1 = c[1] - l10 * c[0]
    u2 = c[2] - l20 * c[0] - l21 * u1
    x2 = u2 * inv2
    x1 = u1 * inv1 - l21 * x2
    x0 = c[0] - l10 * x1 - l20 * x2
    return [x0 * s[0], x1 * s[1], x2 * s[2]]


def combine(y, parts):
    return y[0] * parts[0] + (y[1] * parts[1] + y[2] * parts[2])


def next_asc_kernel(
    chunks, scalars, meta, phi, residual, crossed_0, crossed_1, crossed_2,
    basis_a0, basis_a1, basis_a2, basis_d0, basis_d1, basis_d2, state_a, state_d, value_2,
    new_a, new_d, shares, weights, basis_0, value_0, send, table, z_ref, value_ref, sum_ref,
):
    role = Role(1.0, send, meta, phi, table, z_ref, value_ref, sum_ref)
    write_chunks(send, 0, value_2[...])
    y = solve(scalars)
    for i in range(3):
        shares[i : i + 1] = jnp.broadcast_to(y[i], (1, LANES))
    left = residual[...] - combine(y, [crossed_0[...], crossed_1[...], crossed_2[...]])
    new_a[...] = state_a[...] + combine(y, [basis_a0[...], basis_a1[...], basis_a2[...]])
    new_d[...] = state_d[...] + combine(y, [basis_d0[...], basis_d1[...], basis_d2[...]])
    weights[...], z = role.weigh(left)
    basis_0[...] = role.gradient(z, new_a[...])
    own = role.forward(basis_0[...])
    value_0[...] = own
    write_chunks(send, 1, own)


def next_desc_kernel(
    chunks, got, shares, meta, phi, residual, crossed_0, crossed_1, value_2, state,
    weights, new_crossed_0, basis_0, basis_1, value_1, send, table, z_ref, value_ref, sum_ref,
):
    role = Role(-1.0, send, meta, phi, table, z_ref, value_ref, sum_ref)
    y = [shares[i : i + 1] for i in range(3)]
    crossed_2 = role.cross(value_2[...], flat(got, 0, chunks))
    left = residual[...] - combine(y, [crossed_0[...], crossed_1[...], crossed_2])
    weights[...], z = role.weigh(left)
    basis_0[...] = role.gradient(z, state[...])
    other = flat(got, 1, chunks)
    own, basis_1[...] = role.forward_image(basis_0[...], other, weights[...])
    write_chunks(send, 0, own)
    new_crossed_0[...] = role.cross(own, other)
    own = role.forward(basis_1[...])
    value_1[...] = own
    write_chunks(send, 1, own)


def final_kernel(scalars, state_a, basis_0, basis_1, basis_2, desc, out_a, out_d):
    y = solve(scalars)
    out_a[...] = state_a[...] + combine(y, [basis_0[...], basis_1[...], basis_2[...]])
    out_d[...] = desc[0] + combine(y, [desc[1], desc[2], desc[3]])


def body(coef_asc, coef_desc, cross_asc, cross_desc, time_asc, time_desc, height, block_fill):
    owned_asc, terms = coef_asc.shape
    owned_desc = coef_desc.shape[0]
    blocks, width = cross_asc.shape
    na = lax.axis_size("asc")
    nd = lax.axis_size("desc")
    fold = na // nd
    rows = blocks * width // na // LANES
    all_rows = na * rows
    all_blocks = -(-all_rows // BLOCK_ROWS)
    shape = jax.ShapeDtypeStruct

    def call(kernel, outs, scratch, *args, in_specs=None, mebibytes=16):
        return pl.pallas_call(
            kernel,
            out_shape=outs,
            in_specs=[place(x) for x in args] if in_specs is None else in_specs,
            out_specs=jax.tree.map(place, outs),
            scratch_shapes=scratch,
            compiler_params=params(mebibytes),
        )(*args)

    to_role = []
    for p in range(na):
        for q in range(nd):
            to_role.append((p * nd + q, (q * fold + p // nd) * nd + p % nd))
    to_native = [(b, a) for a, b in to_role]
    slots = (cross_asc, cross_desc, time_asc, time_desc, height)
    packed = call(
        functools.partial(pack_kernel, na, nd, owned_asc),
        shape((nd, fold * FIELDS * rows + owned_desc, LANES), F32),
        [pltpu.VMEM(coef_desc.shape, F32)]
        + [pltpu.VMEM((blocks, width), x.dtype) for x in slots]
        + [
            pltpu.VMEM((1, blocks), jnp.int32),
            pltpu.VMEM((FIELDS, blocks, width), F32),
            pltpu.SemaphoreType.DMA((len(slots) + 2,)),
        ],
        coef_desc, *slots, block_fill.reshape(1, blocks),
        in_specs=[pl.BlockSpec(memory_space=pltpu.HBM)] * (len(slots) + 2),
        mebibytes=60,
    )
    at_asc = lax.all_to_all(packed, "desc", split_axis=0, concat_axis=0, tiled=True)

    padded = all_rows + DUMMY_ROWS
    meta_shape = shape((padded, LANES), F32)
    phi_shape = shape((all_blocks, 2 * terms, BLOCK_ROWS * LANES), BF16)
    role_shapes = [meta_shape, phi_shape]
    table = pltpu.SMEM((all_rows + rows + BLOCK_ROWS + 1,), jnp.int32)
    slot_shape = shape((all_rows, LANES), F32)
    send_shape = shape((na, 2, rows, LANES), F32)
    field_a = shape(coef_asc.shape, F32)
    field_d = shape(coef_desc.shape, F32)
    line_shape = shape((na * nd, 1, LANES), F32)
    times_scratch = pltpu.VMEM((padded, LANES), F32)
    scratch = [
        table, pltpu.VMEM((2, padded, LANES), F32), pltpu.VMEM((padded, LANES), F32),
        pltpu.VMEM((2 * owned_asc, 2 * terms), F32),
    ]

    def exchange(x):
        return lax.all_to_all(x, "asc", split_axis=0, concat_axis=0, tiled=True)

    def share(x):
        return lax.all_to_all(x, ("asc", "desc"), split_axis=0, concat_axis=0, tiled=True)

    *asc, state_a, short, onward = call(
        functools.partial(setup_asc_kernel, fold, rows),
        role_shapes + [field_a, slot_shape, shape((na, 3 * rows + owned_desc, LANES), F32)],
        [times_scratch, table, scratch[2]],
        at_asc, coef_asc,
    )
    *desc, state_d, residual_d, weights_d, d0, own_d, send = call(
        functools.partial(setup_desc_kernel, fold, rows),
        role_shapes + [field_d, slot_shape, slot_shape, field_d, slot_shape, send_shape],
        [times_scratch] + scratch,
        exchange(onward),
    )
    residual_a, weights_a, crossed_a0, a0, a1, own_a, send = call(
        functools.partial(first_asc_kernel, na),
        [slot_shape, slot_shape, slot_shape, field_a, field_a, slot_shape, send_shape],
        scratch,
        exchange(send), short, *asc, state_a,
    )
    kept = [slot_shape] * 3
    d1, d2, send, crossed_d0, crossed_d1, own_d = call(
        functools.partial(images_kernel, -1.0, na, True),
        [field_d, field_d, send_shape] + kept,
        scratch,
        exchange(send), own_d, *desc, weights_d, d0,
    )
    a2, scalars, crossed_a1, crossed_a2, own_a = call(
        functools.partial(gram_kernel, 1.0, na, True),
        [field_a, line_shape] + kept,
        scratch,
        exchange(send), own_a, *asc, weights_a, crossed_a0, a0, a1, d0, d1, d2,
    )
    state_a, state_d, shares, weights_a, a0, own_a, send = call(
        functools.partial(next_asc_kernel, na),
        [
            field_a, field_d, shape((8, LANES), F32),
            slot_shape, field_a, slot_shape, send_shape,
        ],
        scratch,
        share(scalars), *asc, residual_a, crossed_a0, crossed_a1, crossed_a2,
        a0, a1, a2, d0, d1, d2, state_a, state_d, own_a,
    )
    weights_d, crossed_d0, d0, d1, own_d, send = call(
        functools.partial(next_desc_kernel, na),
        [slot_shape, slot_shape, field_d, field_d, slot_shape, send_shape],
        scratch,
        exchange(send), shares, *desc, residual_d, crossed_d0, crossed_d1, own_d, state_d,
    )
    a1, a2, send = call(
        functools.partial(images_kernel, 1.0, na, False),
        [field_a, field_a, send_shape],
        scratch,
        exchange(send), own_a, *asc, weights_a, a0,
    )
    d2, scalars = call(
        functools.partial(gram_kernel, -1.0, na, False),
        [field_d, line_shape],
        scratch,
        exchange(send), own_d, *desc, weights_d, crossed_d0, d0, d1, a0, a1, a2,
    )
    leaving = jnp.stack([state_d, d0, d1, d2])
    native = lax.ppermute(leaving, ("asc", "desc"), to_native)
    return tuple(
        call(
            final_kernel,
            [field_a, field_d],
            [],
            share(scalars), state_a, a0, a1, a2, native,
        )
    )


def solution(mesh):
    split_rows = P(("asc", "desc"), None)
    return jax.shard_map(
        body,
        mesh=mesh,
        in_specs=(split_rows,) * 7 + (P(("asc", "desc")),),
        out_specs=(split_rows, split_rows),
        check_vma=False,
    )
```

```python
import functools
import math

import jax
import jax.numpy as jnp
from jax import lax
from jax.experimental import pallas as pl
from jax.experimental.pallas import tpu as pltpu
from jax.sharding import PartitionSpec as P

GN_STEPS = 2
damping = 2.0
cauchy_square = 2.25

LANES = 128
STEP_ROWS = 2
UNROLL = 3
BLOCK_ROWS = STEP_ROWS * UNROLL
STEP_LANES = STEP_ROWS * LANES
DUMMY_ROWS = 8
TURNS = (5, 2, 1)
SCALE = 1.0 / 128.0
FIELDS = 5
PIVOT_FLOOR = 1e-6
F32 = jnp.float32
BF16 = jnp.bfloat16

COS_TERMS = [(-1.0) ** i * math.pi ** (2 * i) / math.factorial(2 * i) for i in range(8)]
SIN_TERMS = [(-1.0) ** i * math.pi ** (2 * i + 1) / math.factorial(2 * i + 1) for i in range(7)]


def params(mebibytes):
    return pltpu.CompilerParams(vmem_limit_bytes=mebibytes * 1024 * 1024)


def place(x):
    return pl.BlockSpec(memory_space=pltpu.VMEM)


def split(x):
    high = x.astype(BF16)
    low = (x - high.astype(F32)).astype(BF16)
    return high, low


def flat_first(ref, field, fold, rows):
    parts = []
    for j in range(ref.shape[0] * fold):
        start = (j % fold * FIELDS + field) * rows
        parts.append(ref[j // fold, start : start + rows])
    return jnp.concatenate(parts, axis=0)


def flat_second(ref, field, rows):
    start = field * rows
    return jnp.concatenate([ref[j, start : start + rows] for j in range(ref.shape[0])], axis=0)


def flat(ref, field, chunks):
    return jnp.concatenate([ref[j, field] for j in range(chunks)], axis=0)


def local_id(ids, owned):
    if owned & (owned - 1) == 0:
        return ids & (owned - 1)
    return lax.rem(ids, owned)


def pack_kernel(
    na, nd, owned_asc, coef_in, ca_in, cd_in, ta_in, td_in, height_in, fill_in, out,
    coef, ca, cd, ta, td, height, fill, turned, sems,
):
    copies = [
        pltpu.make_async_copy(source, target, sems.at[i])
        for i, (source, target) in enumerate(
            [
                (fill_in, fill), (ca_in, ca), (ta_in, ta),
                (cd_in, cd), (td_in, td), (height_in, height), (coef_in, coef),
            ]
        )
    ]
    for copy in copies:
        copy.start()
    for copy in copies:
        copy.wait()
    owned_desc = coef.shape[0]
    blocks, width = ca.shape
    group = width // na
    rows = blocks // na
    fill_row = fill[...]
    row_id = lax.broadcasted_iota(jnp.int32, (blocks, blocks), 0)
    col_id = lax.broadcasted_iota(jnp.int32, (blocks, blocks), 1)
    fill_col = jnp.sum(
        jnp.where(row_id == col_id, fill_row, 0).astype(F32), axis=1, keepdims=True
    )
    lane = lax.broadcasted_iota(jnp.int32, (blocks, width), 1)
    live = lane.astype(F32) < fill_col
    fields = [
        lambda: jnp.where(live, local_id(ca[...], owned_asc).astype(F32), -1.0),
        lambda: ta[...],
        lambda: jnp.where(live, local_id(cd[...], owned_desc).astype(F32), -1.0),
        lambda: td[...],
        lambda: height[...],
    ]
    source = lax.broadcasted_iota(jnp.int32, (width, width), 0)
    target = lax.broadcasted_iota(jnp.int32, (width, width), 1)
    owner = target // group
    place = target - owner * group
    order = (source == place * na + owner).astype(F32).astype(BF16)
    pieces = []
    for field in fields:
        x = field()
        high = x.astype(BF16)
        rest = x - high.astype(F32)
        middle = rest.astype(BF16)
        pieces += [high, middle, (rest - middle.astype(F32)).astype(BF16)]
    product = jnp.dot(jnp.concatenate(pieces, axis=0), order, preferred_element_type=F32)
    for f in range(FIELDS):
        high, middle, low = [
            product[(3 * f + k) * blocks : (3 * f + k + 1) * blocks] for k in range(3)
        ]
        turned[f] = (high + middle) + low
    lane_group = lax.broadcasted_iota(jnp.int32, (rows, width), 1) // group
    for f in range(FIELDS):
        parts = [None] * na
        for k in range(na):
            piece = turned[f, pl.ds(k, rows, stride=na), :]
            for r in range(na):
                amount = ((k - r) * group) % width
                moved = pltpu.roll(piece, amount, 1) if amount else piece
                parts[r] = moved if k == 0 else jnp.where(lane_group == k, moved, parts[r])
        for r in range(na):
            start = (r // nd * FIELDS + f) * rows
            out[r % nd, start : start + rows] = parts[r]
    for q in range(nd):
        out[q, out.shape[1] - owned_desc :] = coef[...]


def cos_sin_pi(x):
    turns = jnp.floor(x + 0.5)
    f = x - turns
    sign = 1.0 - 2.0 * (turns - 2.0 * jnp.floor(turns * 0.5))
    u = f * f
    c = COS_TERMS[-1]
    for term in COS_TERMS[-2::-1]:
        c = c * u + term
    s = SIN_TERMS[-1]
    for term in SIN_TERMS[-2::-1]:
        s = s * u + term
    return c * sign, s * (f * sign)


def rows_pair(ref, rows):
    return jnp.concatenate([ref[pl.ds(r, 1), :] for r in rows], axis=1)


def used_rows(ids_ref, chunks, rows, table):
    count = jnp.int32(0)
    level = lax.broadcasted_iota(jnp.int32, (rows, LANES), 0).astype(F32) + 1.0
    for j in range(chunks):
        ids = ids_ref[j * rows : (j + 1) * rows, :]
        used = jnp.max(jnp.where(ids >= 0.0, level, 0.0)).astype(jnp.int32)
        for i in range(rows):
            table[count + i] = j * rows + i
        count = count + used
    for i in range(BLOCK_ROWS):
        table[count + i] = chunks * rows
    table[table.shape[0] - 1] = lax.div(count + (BLOCK_ROWS - 1), BLOCK_ROWS)


def listed_rows(table, first, count):
    return [table[first + i] for i in range(count)]


def over_blocks(table, step):
    blocks = table[table.shape[0] - 1]
    done = jnp.int32(0)
    for size in TURNS:
        turns = lax.div(blocks - done, size)

        def turn(i, carry, done=done, size=size):
            step([done + i * size + u for u in range(size)])
            return carry

        lax.fori_loop(0, turns, turn, 0)
        done = done + turns * size


def stacked(field):
    high, low = split(field)
    top = jnp.concatenate([high, high], axis=1)
    bottom = jnp.concatenate([low, jnp.zeros_like(low)], axis=1)
    return jnp.concatenate([top, bottom], axis=0)


def forward_step(stack, phi, ids_row, row_iota, owned):
    both = jnp.dot(stack, phi, preferred_element_type=F32)
    value = both[:owned] + both[owned:]
    return jnp.sum(jnp.where(row_iota == ids_row, value, 0.0), axis=0, keepdims=True)


def store_rows(ref, rows, value):
    for i, r in enumerate(rows):
        ref[pl.ds(r, 1), :] = value[:, i * LANES : (i + 1) * LANES]


def basis_loop(table, ids_ref, time_ref, coef, phi_ref, value_ref):
    owned, terms = coef.shape
    half = terms // 2
    value_ref[...] = jnp.zeros(value_ref.shape, F32)
    width = STEP_LANES
    stack = stacked(coef)
    row_iota = lax.broadcasted_iota(jnp.int32, (owned, width), 0).astype(F32)
    fine = (lax.broadcasted_iota(jnp.int32, (8, width), 0) + 1).astype(F32)
    coarse = (lax.broadcasted_iota(jnp.int32, (half // 8, width), 0) * 8).astype(F32)

    def step(block, u):
        rows = listed_rows(table, block * BLOCK_ROWS + u * STEP_ROWS, STEP_ROWS)
        times = rows_pair(time_ref, rows)
        cos_fine, sin_fine = cos_sin_pi(fine * times)
        cos_coarse, sin_coarse = cos_sin_pi(coarse * times)
        cos_parts, sin_parts = [], []
        for j in range(half // 8):
            cj = cos_coarse[j : j + 1]
            sj = sin_coarse[j : j + 1]
            cos_parts.append(cj * cos_fine - sj * sin_fine)
            sin_parts.append(sj * cos_fine + cj * sin_fine)
        high, low = split(jnp.concatenate(cos_parts + sin_parts, axis=0))
        phi = jnp.concatenate([high, low], axis=0)
        phi_ref[block, :, u * width : (u + 1) * width] = phi
        value = forward_step(stack, phi, rows_pair(ids_ref, rows), row_iota, owned)
        store_rows(value_ref, rows, value)

    def whole_block(block, carry):
        for u in range(UNROLL):
            step(block, u)
        return carry

    lax.fori_loop(0, table[table.shape[0] - 1], whole_block, 0)


class Role:
    def __init__(self, sign, send, meta, phi, table, z_ref, value_ref, sum_ref, listed=False):
        if not listed:
            rows = (meta.shape[0] - DUMMY_ROWS) // send.shape[0]
            used_rows(meta, send.shape[0], rows, table)
        self.sign = sign
        self.table = table
        self.ids = meta
        self.phi = phi
        self.z_ref = z_ref
        self.value_ref = value_ref
        self.sum_ref = sum_ref
        self.count = meta.shape[0] - DUMMY_ROWS

    def cross(self, mine, other):
        return mine - other if self.sign > 0 else other - mine

    def backward(self, z, owned):
        high = z.astype(BF16).astype(F32)
        self.z_ref[0, : self.count] = high
        self.z_ref[1, : self.count] = z - high
        self.z_ref[:, self.count :] = jnp.zeros((2, DUMMY_ROWS, LANES), F32)
        blocks, double, width = self.phi.shape
        row_iota = lax.broadcasted_iota(jnp.int32, (owned, width), 0).astype(F32)

        def gather(block):
            rows = listed_rows(self.table, block * BLOCK_ROWS, BLOCK_ROWS)
            hit = row_iota == rows_pair(self.ids, rows)
            parts = [
                jnp.where(hit, rows_pair(self.z_ref.at[k], rows), 0.0).astype(BF16)
                for k in range(2)
            ]
            return lax.dot_general(
                jnp.concatenate(parts, axis=0),
                self.phi[block],
                (((1,), (1,)), ((), ())),
                preferred_element_type=F32,
            )

        return self.gathered(gather)

    def gathered(self, gather):
        self.sum_ref[...] = jnp.zeros(self.sum_ref.shape, F32)

        def step(blocks):
            self.sum_ref[...] += sum(gather(block) for block in blocks)

        over_blocks(self.table, step)
        g = self.sum_ref[...]
        owned, terms = g.shape[0] // 2, g.shape[1] // 2
        return self.sign * (g[:owned, :terms] + (g[:owned, terms:] + g[owned:, :terms]))

    def forward(self, field):
        owned = field.shape[0]
        stack = stacked(field)
        row_iota = lax.broadcasted_iota(jnp.int32, (owned, STEP_LANES), 0).astype(F32)
        self.value_ref[...] = jnp.zeros(self.value_ref.shape, F32)

        def ahead(block):
            for u in range(UNROLL):
                rows = listed_rows(self.table, block * BLOCK_ROWS + u * STEP_ROWS, STEP_ROWS)
                phi = self.phi[block, :, u * STEP_LANES : (u + 1) * STEP_LANES]
                value = forward_step(stack, phi, rows_pair(self.ids, rows), row_iota, owned)
                store_rows(self.value_ref, rows, value)

        def step(blocks):
            for block in blocks:
                ahead(block)

        over_blocks(self.table, step)
        return self.value_ref[: self.count]

    def forward_image(self, field, other, weight):
        owned = field.shape[0]
        stack = stacked(field)
        blocks, double, width = self.phi.shape
        row_iota = lax.broadcasted_iota(jnp.int32, (owned, width), 0).astype(F32)
        fill_padded(self.z_ref.at[0], other)
        fill_padded(self.z_ref.at[1], weight)
        self.value_ref[...] = jnp.zeros(self.value_ref.shape, F32)

        def both(block):
            rows = listed_rows(self.table, block * BLOCK_ROWS, BLOCK_ROWS)
            phi = self.phi[block]
            hit = row_iota == rows_pair(self.ids, rows)
            values = []
            for u in range(UNROLL):
                part = slice(u * STEP_LANES, (u + 1) * STEP_LANES)
                product = jnp.dot(stack, phi[:, part], preferred_element_type=F32)
                value = product[:owned] + product[owned:]
                values.append(
                    jnp.sum(jnp.where(hit[:, part], value, 0.0), axis=0, keepdims=True)
                )
            value = jnp.concatenate(values, axis=1)
            store_rows(self.value_ref, rows, value)
            z = rows_pair(self.z_ref.at[1], rows) * self.cross(
                value, rows_pair(self.z_ref.at[0], rows)
            )
            high = z.astype(BF16).astype(F32)
            parts = [jnp.where(hit, x, 0.0).astype(BF16) for x in (high, z - high)]
            return lax.dot_general(
                jnp.concatenate(parts, axis=0),
                phi,
                (((1,), (1,)), ((), ())),
                preferred_element_type=F32,
            )

        image = self.gathered(both)
        return self.value_ref[: self.count], SCALE * image

    def weigh(self, residual):
        live = self.ids[: self.count] >= 0.0
        misfit = jnp.where(live, residual, 0.0)
        weight = jnp.where(live, 1.0 / (1.0 + misfit * misfit / cauchy_square), 0.0)
        return weight, weight * misfit

    def gradient(self, z, state):
        return self.backward(z, state.shape[0]) - damping * state

    def image(self, z, before):
        return SCALE * self.backward(z, before.shape[0])


def write_chunks(send, first, values):
    chunks, rows = send.shape[0], send.shape[2]
    for j in range(chunks):
        send[j, first] = values[j * rows : (j + 1) * rows, :]


def fill_padded(ref, values):
    count = values.shape[0]
    ref[:count] = values
    ref[count:] = jnp.zeros((ref.shape[0] - count,) + values.shape[1:], F32)


def setup_asc_kernel(
    fold, rows, packed, coef, meta, phi, state, short, onward, times, table, value_ref
):
    state[...] = coef[...]
    chunks = packed.shape[0] * fold
    count = chunks * rows
    meta[:count] = flat_first(packed, 0, fold, rows)
    meta[count:] = jnp.full((DUMMY_ROWS, LANES), -1.0, F32)
    fill_padded(times, flat_first(packed, 1, fold, rows))
    used_rows(meta, chunks, rows, table)
    basis_loop(table, meta, times, coef[...], phi, value_ref)
    short[...] = flat_first(packed, 4, fold, rows) - value_ref[:count]
    for j in range(chunks):
        base = j % fold * FIELDS
        for f in range(2):
            start = (base + f + 2) * rows
            onward[j, f * rows : (f + 1) * rows] = packed[j // fold, start : start + rows]
        onward[j, 2 * rows : 3 * rows] = short[j * rows : (j + 1) * rows]
        onward[j, 3 * rows :] = packed[j // fold, fold * FIELDS * rows :]


def setup_desc_kernel(
    fold, rows, packed, meta, phi, state, residual, weights, basis_0, value_0, send,
    times, table, z_ref, value_ref, sum_ref,
):
    chunks = packed.shape[0]
    count = chunks * rows
    home = lax.rem(lax.axis_index("asc"), fold) * (chunks // fold) + lax.axis_index("desc")
    state[...] = packed[home, 3 * rows :]
    meta[:count] = flat_second(packed, 0, rows)
    meta[count:] = jnp.full((DUMMY_ROWS, LANES), -1.0, F32)
    fill_padded(times, flat_second(packed, 1, rows))
    used_rows(meta, chunks, rows, table)
    basis_loop(table, meta, times, state[...], phi, value_ref)
    role = Role(-1.0, send, meta, phi, table, z_ref, value_ref, sum_ref, listed=True)
    own = value_ref[:count]
    write_chunks(send, 0, own)
    left = flat_second(packed, 2, rows) + own
    residual[...] = left
    weights[...], z = role.weigh(left)
    basis_0[...] = role.gradient(z, state[...])
    own = role.forward(basis_0[...])
    value_0[...] = own
    write_chunks(send, 1, own)


def first_asc_kernel(
    chunks, got, short, meta, phi, state,
    residual, weights, crossed_0, basis_0, basis_1, value_1, send, table, z_ref, value_ref, sum_ref,
):
    role = Role(1.0, send, meta, phi, table, z_ref, value_ref, sum_ref)
    left = short[...] + flat(got, 0, chunks)
    residual[...] = left
    weights[...], z = role.weigh(left)
    basis_0[...] = role.gradient(z, state[...])
    other = flat(got, 1, chunks)
    own, basis_1[...] = role.forward_image(basis_0[...], other, weights[...])
    write_chunks(send, 0, own)
    crossed_0[...] = role.cross(own, other)
    own = role.forward(basis_1[...])
    value_1[...] = own
    write_chunks(send, 1, own)


def images_kernel(sign, chunks, keep, got, value_0, meta, phi, weights, basis_0, *rest):
    basis_1, basis_2, send, *kept = rest[:-4]
    role = Role(sign, send, meta, phi, *rest[-4:])
    first = role.cross(value_0[...], flat(got, 0, chunks))
    basis_1[...] = role.image(weights[...] * first, basis_0[...])
    other = flat(got, 1, chunks)
    own, basis_2[...] = role.forward_image(basis_1[...], other, weights[...])
    write_chunks(send, 0, own)
    second = role.cross(own, other)
    own = role.forward(basis_2[...])
    write_chunks(send, 1, own)
    if keep:
        crossed_0, crossed_1, value_2 = kept
        crossed_0[...] = first
        crossed_1[...] = second
        value_2[...] = own


def total(x):
    return jnp.sum(jnp.sum(x, axis=0, keepdims=True), axis=1, keepdims=True)


PAIRS = [(0, 0), (0, 1), (0, 2), (1, 1), (1, 2), (2, 2)]


def gram_kernel(
    sign, chunks, keep, got, value_1, meta, phi, weights, crossed_0, basis_0, basis_1,
    other_0, other_1, other_2, *rest,
):
    basis_2, scalars, *kept = rest[:-4]
    role = Role(sign, got, meta, phi, *rest[-4:])
    weight = weights[...]
    crossed = role.cross(value_1[...], flat(got, 0, chunks))
    basis_2[...] = role.image(weight * crossed, basis_1[...])
    own = role.forward(basis_2[...])
    last = role.cross(own, flat(got, 1, chunks))
    if keep:
        crossed_1, crossed_2, value_2 = kept
        crossed_1[...] = crossed
        crossed_2[...] = last
        value_2[...] = own
    values = [crossed_0[...], crossed, last]
    mine = [basis_0[...], basis_1[...], basis_2[...]]
    others = [other_0[...], other_1[...], other_2[...]]
    lane = lax.broadcasted_iota(jnp.int32, (1, LANES), 1)
    line = jnp.zeros((1, LANES), F32)
    for place_in_line, (i, j) in enumerate(PAIRS):
        dots = total(mine[i] * mine[j] + others[i] * others[j])
        curve = total(weight * values[i] * values[j]) + damping * dots
        line = jnp.where(lane == place_in_line, curve, line)
        if i == 0:
            line = jnp.where(lane == len(PAIRS) + j, dots, line)
    for d in range(scalars.shape[0]):
        scalars[d] = line


def solve(scalars):
    summed = scalars[0]
    for d in range(1, scalars.shape[0]):
        summed = summed + scalars[d]
    line = summed
    lane = lax.broadcasted_iota(jnp.int32, (1, LANES), 1)

    def pick(place):
        return jnp.sum(jnp.where(lane == place, line, 0.0), axis=1, keepdims=True)

    g = {pair: pick(place) for place, pair in enumerate(PAIRS)}
    right = [pick(len(PAIRS) + i) for i in range(3)]
    s = [
        jnp.where(g[i, i] > 0.0, lax.rsqrt(jnp.maximum(g[i, i], 1e-37)), 0.0) for i in range(3)
    ]
    l10 = g[0, 1] * s[0] * s[1]
    l20 = g[0, 2] * s[0] * s[2]
    g21 = g[1, 2] * s[1] * s[2]
    c = [right[i] * s[i] for i in range(3)]

    def inverse(pivot):
        good = pivot > PIVOT_FLOOR
        return jnp.where(good, 1.0 / jnp.where(good, pivot, 1.0), 0.0)

    inv1 = inverse(1.0 - l10 * l10)
    t21 = g21 - l20 * l10
    l21 = t21 * inv1
    inv2 = inverse(1.0 - l20 * l20 - l21 * t21)
    u1 = c[1] - l10 * c[0]
    u2 = c[2] - l20 * c[0] - l21 * u1
    x2 = u2 * inv2
    x1 = u1 * inv1 - l21 * x2
    x0 = c[0] - l10 * x1 - l20 * x2
    return [x0 * s[0], x1 * s[1], x2 * s[2]]


def combine(y, parts):
    return y[0] * parts[0] + (y[1] * parts[1] + y[2] * parts[2])


def next_asc_kernel(
    chunks, scalars, meta, phi, residual, crossed_0, crossed_1, crossed_2,
    basis_a0, basis_a1, basis_a2, basis_d0, basis_d1, basis_d2, state_a, state_d, value_2,
    new_a, new_d, shares, weights, basis_0, value_0, send, table, z_ref, value_ref, sum_ref,
):
    role = Role(1.0, send, meta, phi, table, z_ref, value_ref, sum_ref)
    write_chunks(send, 0, value_2[...])
    y = solve(scalars)
    for i in range(3):
        shares[i : i + 1] = jnp.broadcast_to(y[i], (1, LANES))
    left = residual[...] - combine(y, [crossed_0[...], crossed_1[...], crossed_2[...]])
    new_a[...] = state_a[...] + combine(y, [basis_a0[...], basis_a1[...], basis_a2[...]])
    new_d[...] = state_d[...] + combine(y, [basis_d0[...], basis_d1[...], basis_d2[...]])
    weights[...], z = role.weigh(left)
    basis_0[...] = role.gradient(z, new_a[...])
    own = role.forward(basis_0[...])
    value_0[...] = own
    write_chunks(send, 1, own)


def next_desc_kernel(
    chunks, got, shares, meta, phi, residual, crossed_0, crossed_1, value_2, state,
    weights, new_crossed_0, basis_0, basis_1, value_1, send, table, z_ref, value_ref, sum_ref,
):
    role = Role(-1.0, send, meta, phi, table, z_ref, value_ref, sum_ref)
    y = [shares[i : i + 1] for i in range(3)]
    crossed_2 = role.cross(value_2[...], flat(got, 0, chunks))
    left = residual[...] - combine(y, [crossed_0[...], crossed_1[...], crossed_2])
    weights[...], z = role.weigh(left)
    basis_0[...] = role.gradient(z, state[...])
    other = flat(got, 1, chunks)
    own, basis_1[...] = role.forward_image(basis_0[...], other, weights[...])
    write_chunks(send, 0, own)
    new_crossed_0[...] = role.cross(own, other)
    own = role.forward(basis_1[...])
    value_1[...] = own
    write_chunks(send, 1, own)


def final_kernel(scalars, state_a, basis_0, basis_1, basis_2, desc, out_a, out_d):
    y = solve(scalars)
    out_a[...] = state_a[...] + combine(y, [basis_0[...], basis_1[...], basis_2[...]])
    out_d[...] = desc[0] + combine(y, [desc[1], desc[2], desc[3]])


def body(coef_asc, coef_desc, cross_asc, cross_desc, time_asc, time_desc, height, block_fill):
    owned_asc, terms = coef_asc.shape
    owned_desc = coef_desc.shape[0]
    blocks, width = cross_asc.shape
    na = lax.axis_size("asc")
    nd = lax.axis_size("desc")
    fold = na // nd
    rows = blocks * width // na // LANES
    all_rows = na * rows
    all_blocks = -(-all_rows // BLOCK_ROWS)
    shape = jax.ShapeDtypeStruct

    def call(kernel, outs, scratch, *args, in_specs=None, mebibytes=16):
        return pl.pallas_call(
            kernel,
            out_shape=outs,
            in_specs=[place(x) for x in args] if in_specs is None else in_specs,
            out_specs=jax.tree.map(place, outs),
            scratch_shapes=scratch,
            compiler_params=params(mebibytes),
        )(*args)

    to_role = []
    for p in range(na):
        for q in range(nd):
            to_role.append((p * nd + q, (q * fold + p // nd) * nd + p % nd))
    to_native = [(b, a) for a, b in to_role]
    slots = (cross_asc, cross_desc, time_asc, time_desc, height)
    packed = call(
        functools.partial(pack_kernel, na, nd, owned_asc),
        shape((nd, fold * FIELDS * rows + owned_desc, LANES), F32),
        [pltpu.VMEM(coef_desc.shape, F32)]
        + [pltpu.VMEM((blocks, width), x.dtype) for x in slots]
        + [
            pltpu.VMEM((1, blocks), jnp.int32),
            pltpu.VMEM((FIELDS, blocks, width), F32),
            pltpu.SemaphoreType.DMA((len(slots) + 2,)),
        ],
        coef_desc, *slots, block_fill.reshape(1, blocks),
        in_specs=[pl.BlockSpec(memory_space=pltpu.HBM)] * (len(slots) + 2),
        mebibytes=60,
    )
    at_asc = lax.all_to_all(packed, "desc", split_axis=0, concat_axis=0, tiled=True)

    padded = all_rows + DUMMY_ROWS
    meta_shape = shape((padded, LANES), F32)
    phi_shape = shape((all_blocks, 2 * terms, BLOCK_ROWS * LANES), BF16)
    role_shapes = [meta_shape, phi_shape]
    table = pltpu.SMEM((all_rows + rows + BLOCK_ROWS + 1,), jnp.int32)
    slot_shape = shape((all_rows, LANES), F32)
    send_shape = shape((na, 2, rows, LANES), F32)
    field_a = shape(coef_asc.shape, F32)
    field_d = shape(coef_desc.shape, F32)
    line_shape = shape((na * nd, 1, LANES), F32)
    times_scratch = pltpu.VMEM((padded, LANES), F32)
    scratch = [
        table, pltpu.VMEM((2, padded, LANES), F32), pltpu.VMEM((padded, LANES), F32),
        pltpu.VMEM((2 * owned_asc, 2 * terms), F32),
    ]

    def exchange(x):
        return lax.all_to_all(x, "asc", split_axis=0, concat_axis=0, tiled=True)

    def share(x):
        return lax.all_to_all(x, ("asc", "desc"), split_axis=0, concat_axis=0, tiled=True)

    *asc, state_a, short, onward = call(
        functools.partial(setup_asc_kernel, fold, rows),
        role_shapes + [field_a, slot_shape, shape((na, 3 * rows + owned_desc, LANES), F32)],
        [times_scratch, table, scratch[2]],
        at_asc, coef_asc,
    )
    *desc, state_d, residual_d, weights_d, d0, own_d, send = call(
        functools.partial(setup_desc_kernel, fold, rows),
        role_shapes + [field_d, slot_shape, slot_shape, field_d, slot_shape, send_shape],
        [times_scratch] + scratch,
        exchange(onward),
    )
    residual_a, weights_a, crossed_a0, a0, a1, own_a, send = call(
        functools.partial(first_asc_kernel, na),
        [slot_shape, slot_shape, slot_shape, field_a, field_a, slot_shape, send_shape],
        scratch,
        exchange(send), short, *asc, state_a,
    )
    kept = [slot_shape] * 3
    d1, d2, send, crossed_d0, crossed_d1, own_d = call(
        functools.partial(images_kernel, -1.0, na, True),
        [field_d, field_d, send_shape] + kept,
        scratch,
        exchange(send), own_d, *desc, weights_d, d0,
    )
    a2, scalars, crossed_a1, crossed_a2, own_a = call(
        functools.partial(gram_kernel, 1.0, na, True),
        [field_a, line_shape] + kept,
        scratch,
        exchange(send), own_a, *asc, weights_a, crossed_a0, a0, a1, d0, d1, d2,
    )
    state_a, state_d, shares, weights_a, a0, own_a, send = call(
        functools.partial(next_asc_kernel, na),
        [
            field_a, field_d, shape((8, LANES), F32),
            slot_shape, field_a, slot_shape, send_shape,
        ],
        scratch,
        share(scalars), *asc, residual_a, crossed_a0, crossed_a1, crossed_a2,
        a0, a1, a2, d0, d1, d2, state_a, state_d, own_a,
    )
    weights_d, crossed_d0, d0, d1, own_d, send = call(
        functools.partial(next_desc_kernel, na),
        [slot_shape, slot_shape, field_d, field_d, slot_shape, send_shape],
        scratch,
        exchange(send), shares, *desc, residual_d, crossed_d0, crossed_d1, own_d, state_d,
    )
    a1, a2, send = call(
        functools.partial(images_kernel, 1.0, na, False),
        [field_a, field_a, send_shape],
        scratch,
        exchange(send), own_a, *asc, weights_a, a0,
    )
    d2, scalars = call(
        functools.partial(gram_kernel, -1.0, na, False),
        [field_d, line_shape],
        scratch,
        exchange(send), own_d, *desc, weights_d, crossed_d0, d0, d1, a0, a1, a2,
    )
    leaving = jnp.stack([state_d, d0, d1, d2])
    native = lax.ppermute(leaving, ("asc", "desc"), to_native)
    return tuple(
        call(
            final_kernel,
            [field_a, field_d],
            [],
            share(scalars), state_a, a0, a1, a2, native,
        )
    )


def solution(mesh):
    split_rows = P(("asc", "desc"), None)
    return jax.shard_map(
        body,
        mesh=mesh,
        in_specs=(split_rows,) * 7 + (P(("asc", "desc")),),
        out_specs=(split_rows, split_rows),
        check_vma=False,
    )
```
